32 devices in a mesh: seq: 8 (over z, x), fsdp: 4 (over y, core).
Axes of the slice: x: 2, y: 2, z: 4, core: 2. Of those that a mesh axis runs over, the one named last changes fastest.
Arguments:
- inputs: bfloat16 [4, 2048, 2048], P('fsdp', 'seq'), may hold values from -6 to 6
- out_grad: bfloat16 [4, 2048, 2048], P('fsdp', 'seq'), may hold values from -6 to 6
- norm_gain: float32 [2048], replicated, may hold values from 0.5 to 1.5
- w_in: bfloat16 [2048, 6704], P(('seq', 'fsdp')), may hold values from -0.125 to 0.125
- conv_weight: float32 [4, 3584], replicated, may hold values from -3 to 3
- conv_bias: float32 [3584], replicated, may hold values from -0.5 to 0.5
- dt_bias: float32 [48], replicated, may hold values from -4 to 0
- a_log: float32 [48], replicated, may hold values from -7 to 1
- skip_gain: float32 [48], replicated, may hold values from 0.2 to 1
- gated_gain: float32 [3072], replicated, may hold values from 0.5 to 1.5
- w_out: bfloat16 [3072, 2048], P(('seq', 'fsdp')), may hold values from -0.109375 to 0.109375
- w_q: bfloat16 [2048, 1024], P(('seq', 'fsdp')), may hold values from -0.125 to 0.125
- w_k: bfloat16 [2048, 256], P(('seq', 'fsdp')), may hold values from -0.125 to 0.125
- w_v: bfloat16 [2048, 256], P(('seq', 'fsdp')), may hold values from -0.125 to 0.125
- w_o: bfloat16 [1024, 2048], P(('seq', 'fsdp')), may hold values from -1.5 to 1.5
- mid_gain: float32 [2048], replicated, may hold values from 0.5 to 1.5
- w_gate: bfloat16 [2048, 4096], P(('seq', 'fsdp')), may hold values from -0.125 to 0.125
- w_up: bfloat16 [2048, 4096], P(('seq', 'fsdp')), may hold values from -0.125 to 0.125
- w_down: bfloat16 [4096, 2048], P(('seq', 'fsdp')), may hold values from -0.09375 to 0.09375
Outputs:
- output: bfloat16 [4, 2048, 2048], P('fsdp', 'seq')
- input_grad: float32 [4, 2048, 2048], P('fsdp', 'seq')
- grad_norm_gain: float32 [2048], replicated
- grad_w_in: float32 [2048, 6704], P(('seq', 'fsdp'))
- grad_conv_weight: float32 [4, 3584], replicated
- grad_conv_bias: float32 [3584], replicated
- grad_dt_bias: float32 [48], replicated
- grad_a_log: float32 [48], replicated
- grad_skip_gain: float32 [48], replicated
- grad_gated_gain: float32 [3072], replicated
- grad_w_out: float32 [3072, 2048], P(('seq', 'fsdp'))
- grad_w_q: float32 [2048, 1024], P(('seq', 'fsdp'))
- grad_w_k: float32 [2048, 256], P(('seq', 'fsdp'))
- grad_w_v: float32 [2048, 256], P(('seq', 'fsdp'))
- grad_w_o: float32 [1024, 2048], P(('seq', 'fsdp'))
- grad_mid_gain: float32 [2048], replicated
- grad_w_gate: float32 [2048, 4096], P(('seq', 'fsdp'))
- grad_w_up: float32 [2048, 4096], P(('seq', 'fsdp'))
- grad_w_down: float32 [4096, 2048], P(('seq', 'fsdp'))
The draws below stay inside these ranges and needn't reach their ends.
All inputs are finite; a program needn't handle non-finite values.
Results may differ from the reference program's by a relative error of at most 0.017.
Values may be sent and summed in bfloat16 or wider, within the bound.
No kernel may reach another device: no remote copies, remote signals or barrier semaphores. Data moves between devices by JAX's collectives and lax.ppermute only.
A program may use at most 704 MiB of HBM per device.

```python
import jax
import jax.numpy as jnp
from jax import lax

D = 2048
MAMBA_HEADS = 48
MAMBA_HEAD = 64
STATE = 256
CONV = 4
ATT_HEADS = 8
KV_HEADS = 2
HEAD_DIM = 128
FF = 4096
SPAN = 128
INNER = 3072
CHANNELS = 3584
PROJ = 6704
QW = 1024
KW = 256
SEQ_LEN = 2048
SEQS = 4


def shard_levels(own_key, shape, split, smallest, largest):
    level, own = 1.0, jax.random.fold_in(own_key, 6)
    for axis_at, blocks in split:
        steps = jnp.exp(jax.random.uniform(jax.random.fold_in(own, axis_at), (blocks,), jnp.float32, smallest / len(split), largest / len(split)))
        level = level * jnp.repeat(steps, shape[axis_at] // blocks).reshape([-1 if axis == axis_at else 1 for axis in range(len(shape))])
    return level


def normal_values(own_key, dims, scale, bound, cuts=(), kind=jnp.bfloat16):
    loudness = shard_levels(own_key, dims, cuts, -0.22, 0.18) if cuts else 1.0
    entries = jax.random.normal(own_key, dims, jnp.float32) * scale * loudness
    return jnp.minimum(jnp.maximum(entries, -bound), bound).astype(kind)


def setup_inputs(seed: int = 0) -> dict:
    key_of = jax.random.split(jax.random.key(seed), 20)
    inputs = normal_values(key_of[0], (SEQS, SEQ_LEN, D), 1.0, 6.0, ((0, 4), (1, 8)))
    out_grad = normal_values(key_of[1], (SEQS, SEQ_LEN, D), 1.0, 6.0, ((0, 4), (1, 8)))
    norm_gain = jnp.clip(1.0 + 0.1 * jax.random.normal(key_of[2], (D,), jnp.float32), 0.5, 1.5)
    w_in = normal_values(key_of[3], (D, PROJ), D ** -0.5, 0.125, ((0, 32),))
    conv_weight = normal_values(key_of[4], (CONV, CHANNELS), CONV ** -0.5, 3.0, (), jnp.float32)
    conv_bias = jnp.clip(jax.random.uniform(key_of[5], (CHANNELS,), jnp.float32, -0.5, 0.5), -0.5, 0.5)
    dt_bias = jnp.clip(jax.random.uniform(key_of[6], (MAMBA_HEADS,), jnp.float32, -4.0, 0.0), -4.0, 0.0)
    a_log = jnp.clip(jax.random.uniform(key_of[7], (MAMBA_HEADS,), jnp.float32, -7.0, 1.0), -7.0, 1.0)
    skip_gain = jnp.clip(jax.random.uniform(key_of[8], (MAMBA_HEADS,), jnp.float32, 0.2, 1.0), 0.2, 1.0)
    gated_gain = jnp.clip(1.0 + 0.1 * jax.random.normal(key_of[9], (INNER,), jnp.float32), 0.5, 1.5)
    w_out = normal_values(key_of[10], (INNER, D), INNER ** -0.5, 0.109375, ((0, 32),))
    w_q = normal_values(key_of[11], (D, QW), D ** -0.5, 0.125, ((0, 32),))
    w_k = normal_values(key_of[12], (D, KW), D ** -0.5, 0.125, ((0, 32),))
    w_v = normal_values(key_of[13], (D, KW), D ** -0.5, 0.125, ((0, 32),))
    w_o = normal_values(key_of[14], (QW, D), 16 ** -0.5, 1.5, ((0, 32),))
    mid_gain = jnp.clip(1.0 + 0.1 * jax.random.normal(key_of[15], (D,), jnp.float32), 0.5, 1.5)
    w_gate = normal_values(key_of[16], (D, FF), D ** -0.5, 0.125, ((0, 32),))
    w_up = normal_values(key_of[17], (D, FF), D ** -0.5, 0.125, ((0, 32),))
    w_down = normal_values(key_of[18], (FF, D), FF ** -0.5, 0.09375, ((0, 32),))
    return {"inputs": inputs, "out_grad": out_grad, "norm_gain": norm_gain, "w_in": w_in, "conv_weight": conv_weight, "conv_bias": conv_bias, "dt_bias": dt_bias, "a_log": a_log, "skip_gain": skip_gain, "gated_gain": gated_gain, "w_out": w_out, "w_q": w_q, "w_k": w_k, "w_v": w_v, "w_o": w_o, "mid_gain": mid_gain, "w_gate": w_gate, "w_up": w_up, "w_down": w_down}


@jax.custom_vjp
def low(v):
    return lax.optimization_barrier(v.astype(jnp.bfloat16)).astype(jnp.float32)

@jax.custom_vjp
def low_back(v):
    return v

def low_keep(v):
    return (low(v), None)

def low_pass(kept, grad):
    return (grad,)

def back_keep(v):
    return (v, None)

def back_low(kept, grad):
    return (low(grad),)
low.defvjp(low_keep, low_pass)
low_back.defvjp(back_keep, back_low)
epsilon = 1e-05
rope_base = 100000000000.0
highest = lax.Precision.HIGHEST
block_limit = 512

def mat_high(left, right):
    return jnp.dot(left, right, precision=highest, preferred_element_type=jnp.float32)

def rms_scale(values, gain):
    return values * lax.rsqrt(lax.optimization_barrier(jnp.mean(values * values, axis=-1, keepdims=True)) + epsilon) * gain

def rotate(values, positions):
    half_dim = values.shape[-1] // 2
    frequencies = rope_base ** (-jnp.arange(half_dim, dtype=jnp.float32) / half_dim)
    angles = positions.astype(jnp.float32)[:, None] * frequencies[None, :]
    cosine = jnp.cos(angles)[:, None, :]
    sine_table = jnp.sin(angles)[:, None, :]
    first_half = values[..., :half_dim]
    second = values[..., half_dim:]
    return jnp.concatenate([first_half * cosine - second * sine_table, second * cosine + first_half * sine_table], axis=-1)

def convolve(padded, conv_weight, conv_bias):
    length = padded.shape[0] - conv_weight.shape[0] + 1
    accumulated = conv_bias[None, :] + jnp.zeros((length, padded.shape[1]), jnp.float32)
    for offset in range(conv_weight.shape[0]):
        accumulated = accumulated + padded[offset:offset + length] * conv_weight[offset]
    return jax.nn.silu(accumulated)

def unpack(mixed, dt_raw, dt_bias, a_log):
    length = mixed.shape[0]
    inputs_ssm = mixed[:, :INNER].reshape(length, MAMBA_HEADS, MAMBA_HEAD)
    b_matrix = mixed[:, INNER:INNER + STATE]
    c_matrix = mixed[:, INNER + STATE:]
    step_size = jax.nn.softplus(dt_raw + dt_bias)
    rates = -jnp.exp(a_log)
    return (inputs_ssm, b_matrix, c_matrix, step_size, rates)

def run_spans(inputs_ssm, b_matrix, c_matrix, step_size, rates):
    length = inputs_ssm.shape[0]
    pieces_count = length // SPAN
    places = jnp.arange(SPAN, dtype=jnp.int32)
    causal = places[:, None] >= places[None, :]

    def span_step(state, pieces):
        part_x, part_b, part_c, part_dt = pieces
        cumulative = jnp.cumsum(part_dt * rates, axis=0)
        spread = cumulative.T[:, :, None] - cumulative.T[:, None, :]
        decay = jnp.exp(jnp.where(causal[None], spread, -jnp.inf))
        intersection = mat_high(part_c, part_b.T)
        weights = intersection[None] * decay * part_dt.T[:, None, :]
        inside = jnp.einsum('hts,shp->thp', weights, part_x, precision=highest)
        carried = jnp.exp(cumulative)[:, :, None] * jnp.einsum('tn,hpn->thp', part_c, state, precision=highest)
        tail = jnp.exp(cumulative[-1][None, :] - cumulative) * part_dt
        local_state = jnp.einsum('shp,sn->hpn', tail[:, :, None] * part_x, part_b, precision=highest)
        updated = jnp.exp(cumulative[-1])[:, None, None] * state + local_state
        return (updated, inside + carried)
    start_state = jnp.zeros((MAMBA_HEADS, MAMBA_HEAD, STATE), jnp.float32)
    pieces = (inputs_ssm.reshape(pieces_count, SPAN, MAMBA_HEADS, MAMBA_HEAD), b_matrix.reshape(pieces_count, SPAN, STATE), c_matrix.reshape(pieces_count, SPAN, STATE), step_size.reshape(pieces_count, SPAN, MAMBA_HEADS))
    final_state, outputs = lax.scan(jax.checkpoint(span_step), start_state, pieces)
    return (outputs.reshape(length, MAMBA_HEADS, MAMBA_HEAD), final_state)

def gate_output(values, gate_z, gated_gain):
    flat = values.reshape(values.shape[0], INNER) * jax.nn.silu(gate_z)
    return rms_scale(flat, gated_gain)

def attention(queries, key_rows, value_rows):
    length = queries.shape[0]
    block_size = min(block_limit, length)
    group_size = ATT_HEADS // KV_HEADS
    score_scale = HEAD_DIM ** (-0.5)
    blocks = queries.reshape(length // block_size, block_size, KV_HEADS, group_size, HEAD_DIM)
    starts = jnp.arange(length // block_size, dtype=jnp.int32) * block_size
    key_place = jnp.arange(length, dtype=jnp.int32)

    def query_block(pieces):
        query_part, first_row = pieces
        raw_scores = jnp.einsum('lkgd,jkd->lkgj', query_part, key_rows, precision=highest) * score_scale
        scores = low_back(raw_scores)
        query_place = first_row + jnp.arange(block_size, dtype=jnp.int32)
        allowed = query_place[:, None, None, None] >= key_place
        probs = jax.nn.softmax(jnp.where(allowed, scores, -jnp.inf), axis=-1)
        return jnp.einsum('lkgj,jkd->lkgd', low(probs), value_rows, precision=highest)
    attended = lax.map(jax.checkpoint(query_block), (blocks, starts))
    return low(low_back(attended.reshape(length, ATT_HEADS * HEAD_DIM)))

def forward_pass(resident, params):
    norm_gain, w_in, conv_weight, conv_bias, dt_bias, a_log, skip_gain, gated_gain, w_out, w_q, w_k, w_v, w_o, mid_gain, w_gate, w_up, w_down = params
    length = resident.shape[0]
    positions = jnp.arange(length, dtype=jnp.int32)
    normed = low(rms_scale(resident, norm_gain))
    projected = low_back(mat_high(normed, w_in))
    gate_z = projected[:, :INNER]
    conv_in = projected[:, INNER:2 * INNER + 2 * STATE]
    dt_raw = projected[:, 2 * INNER + 2 * STATE:]
    padded = jnp.concatenate([jnp.zeros((conv_weight.shape[0] - 1, conv_in.shape[1]), jnp.float32), conv_in], 0)
    mixed = convolve(padded, conv_weight, conv_bias)
    inputs_ssm, b_matrix, c_matrix, step_size, rates = unpack(mixed, dt_raw, dt_bias, a_log)
    scanned, final_state = run_spans(inputs_ssm, b_matrix, c_matrix, step_size, rates)
    values_ssm = scanned + skip_gain[:, None] * inputs_ssm
    gated = low(gate_output(values_ssm, gate_z, gated_gain))
    queries = rotate(low_back(mat_high(normed, w_q)).reshape(length, ATT_HEADS, HEAD_DIM), positions)
    key_rows = rotate(low_back(mat_high(normed, w_k)).reshape(length, KV_HEADS, HEAD_DIM), positions)
    value_rows = low(low_back(mat_high(normed, w_v))).reshape(length, KV_HEADS, HEAD_DIM)
    attended = attention(low(queries), low(key_rows), value_rows)
    mixture = low_back(mat_high(attended, w_o) + mat_high(gated, w_out))
    hidden_state = resident + mixture
    middle = low(rms_scale(hidden_state, mid_gain))
    gate_proj = low_back(mat_high(middle, w_gate))
    up_proj = low_back(mat_high(middle, w_up))
    activated = low(jax.nn.silu(gate_proj) * up_proj)
    return hidden_state + mat_high(activated, w_down)

def reference(inputs, out_grad, norm_gain, w_in, conv_weight, conv_bias, dt_bias, a_log, skip_gain, gated_gain, w_out, w_q, w_k, w_v, w_o, mid_gain, w_gate, w_up, w_down):
    params = tuple((item.astype(jnp.float32) for item in (norm_gain, w_in, conv_weight, conv_bias, dt_bias, a_log, skip_gain, gated_gain, w_out, w_q, w_k, w_v, w_o, mid_gain, w_gate, w_up, w_down)))

    def per_sequence(totals, pieces):
        sequence, cotangent = pieces
        result, backward = jax.vjp(forward_pass, sequence.astype(jnp.float32), params)
        input_part, param_grads = backward(cotangent.astype(jnp.float32))
        totals = jax.tree.map(jnp.add, totals, param_grads)
        return (totals, (result.astype(jnp.bfloat16), input_part))
    zero_grads = tuple((jnp.zeros(item.shape, jnp.float32) for item in params))
    totals, (outputs, input_grads) = lax.scan(per_sequence, zero_grads, (inputs, out_grad))
    return (outputs, input_grads, totals[0], totals[1], totals[2], totals[3], totals[4], totals[5], totals[6], totals[7], totals[8], totals[9], totals[10], totals[11], totals[12], totals[13], totals[14], totals[15], totals[16])
```

```python
import jax
import jax.numpy as jnp
from jax import lax
from jax.sharding import Mesh
from jax.sharding import PartitionSpec as P

D = 2048
MAMBA_HEADS = 48
MAMBA_HEAD = 64
STATE = 256
ATT_HEADS = 8
KV_HEADS = 2
HEAD_DIM = 128
SPAN = 128
INNER = 3072

HEADS = MAMBA_HEADS // 4
PART = HEADS * MAMBA_HEAD
BC = 2 * STATE
DT_PAD = 128
QP = 2 * HEAD_DIM
CONV_COLS = PART + BC
AT_DT = CONV_COLS
AT_Q = AT_DT + DT_PAD
AT_K = AT_Q + QP
AT_V = AT_K + HEAD_DIM
AT_Z = AT_V + HEAD_DIM
MIX_COLS = AT_Z + PART

epsilon = 1e-05
rope_base = 100000000000.0
highest = lax.Precision.HIGHEST
GROUP = ("x", "c")
SHARDS = ("z", "y")
EVERY = ("z", "x", "y", "c")
bf16 = jnp.bfloat16
f32 = jnp.float32


def swap(array, axis):
    return lax.ppermute(array, axis, [(0, 1), (1, 0)])


def shifted(array, distance):
    devices = range(lax.axis_size("z"))
    return lax.ppermute(array, "z", [(i - distance, i) for i in devices if i - distance in devices])


def total(array):
    for axis in EVERY:
        size = lax.axis_size(axis)
        bit = 1
        while bit < size:
            array = array + lax.ppermute(array, axis, [(i, i ^ bit) for i in range(size)])
            bit *= 2
    return array


def group_total(array):
    array = array + swap(array[::-1], "c")
    return array + swap(array, "x")


def low_dot(left, right):
    return jnp.dot(left, right, preferred_element_type=f32)


def back_dot(grad_rows, weight):
    return lax.dot_general(grad_rows, weight, (((1,), (1,)), ((), ())), preferred_element_type=f32)


def weight_grad(left, right):
    return lax.dot_general(left, right, (((0,), (0,)), ((), ())), preferred_element_type=f32)


def rms_scale(values, gain):
    return values * lax.rsqrt(jnp.mean(values * values, axis=-1, keepdims=True) + epsilon) * gain


def rope_tables(positions):
    half_dim = HEAD_DIM // 2
    frequencies = rope_base ** (-jnp.arange(half_dim, dtype=f32) / half_dim)
    angles = positions.astype(f32)[:, None] * frequencies[None, :]
    return (jnp.cos(angles), jnp.sin(angles))


def rotate(values, cosine, sine):
    half_dim = HEAD_DIM // 2
    cosine, sine = cosine[:, None, :], sine[:, None, :]
    first, second = values[..., :half_dim], values[..., half_dim:]
    return jnp.concatenate([first * cosine - second * sine, second * cosine + first * sine], axis=-1)


def convolve(padded, conv_weight, conv_bias):
    taps = conv_weight.shape[0]
    length = padded.shape[1] - taps + 1
    accumulated = conv_bias + padded[:, 0:length] * conv_weight[0]
    for offset in range(1, taps):
        accumulated = accumulated + padded[:, offset : offset + length] * conv_weight[offset]
    return jax.nn.silu(accumulated)


def chunk_parts(mixed, dt_raw, dt_bias, a_log):
    seqs, length = mixed.shape[:2]
    n = length // SPAN
    xs = mixed[..., :PART].reshape(seqs, n, SPAN, HEADS, MAMBA_HEAD)
    bs = mixed[..., PART : PART + STATE].reshape(seqs, n, SPAN, STATE)
    cs = mixed[..., PART + STATE :].reshape(seqs, n, SPAN, STATE)
    dt = jax.nn.softplus(dt_raw + dt_bias).reshape(seqs, n, SPAN, HEADS)
    cum = jnp.cumsum(dt * -jnp.exp(a_log), axis=2)
    return (xs, bs, cs, dt, cum)


def span_states(xs, bs, dt, cum):
    tail = jnp.exp(cum[:, :, -1:] - cum) * dt
    return jnp.einsum("bnshp,bnsm->bnhpm", tail[..., None] * xs, bs, precision=highest)


def local_state(mixed, dt_raw, dt_bias, a_log):
    xs, bs, cs, dt, cum = chunk_parts(mixed, dt_raw, dt_bias, a_log)
    local = span_states(xs, bs, dt, cum)
    state = local[:, 0]
    for i in range(1, local.shape[1]):
        state = jnp.exp(cum[:, i, -1])[:, :, None, None] * state + local[:, i]
    return (state, jnp.exp(jnp.sum(cum[:, :, -1], axis=1)))


def scan_all(mixed, dt_raw, dt_bias, a_log, skip_gain, state_in):
    seqs, length = mixed.shape[:2]
    xs, bs, cs, dt, cum = chunk_parts(mixed, dt_raw, dt_bias, a_log)
    n = length // SPAN
    places = jnp.arange(SPAN, dtype=jnp.int32)
    causal = places[:, None] >= places[None, :]
    cum_h = jnp.moveaxis(cum, 3, 2)
    dt_h = jnp.moveaxis(dt, 3, 2)
    spread = cum_h[..., :, None] - cum_h[..., None, :]
    decay = jnp.exp(jnp.where(causal, spread, -jnp.inf))
    meet = jnp.einsum("bntm,bnsm->bnts", cs, bs, precision=highest)
    weights = meet[:, :, None] * decay * dt_h[..., None, :]
    inside = jnp.einsum("bnhts,bnshp->bnthp", weights, xs, precision=highest)
    local = span_states(xs, bs, dt, cum)
    state, carried = state_in, []
    for i in range(n):
        carried.append(jnp.einsum("btm,bhpm->bthp", cs[:, i], state, precision=highest))
        state = jnp.exp(cum[:, i, -1])[:, :, None, None] * state + local[:, i]
    values = inside + jnp.exp(cum)[..., None] * jnp.stack(carried, 1) + skip_gain[:, None] * xs
    return (values.reshape(seqs, length, PART), state)


def swish_product(gate_proj, up_proj):
    return jax.nn.silu(gate_proj) * up_proj


def gather_tokens(block):
    across = swap(block, "x")
    return (block, swap(block, "c"), across, swap(across, "c"))


def scatter_tokens(blocks):
    near, far = blocks[0], blocks[2]
    sent = swap(jnp.stack([blocks[1].astype(bf16), blocks[3].astype(bf16)]), "c")
    near = near + sent[0].astype(f32)
    far = far + sent[1].astype(f32)
    return near + swap(far.astype(bf16), "x").astype(f32)


def body(
    inputs,
    out_grad,
    norm_gain,
    w_in,
    conv_weight,
    conv_bias,
    dt_bias,
    a_log,
    skip_gain,
    gated_gain,
    w_out,
    w_q,
    w_k,
    w_v,
    w_o,
    mid_gain,
    w_gate,
    w_up,
    w_down,
):
    nz, ny = lax.axis_size("z"), lax.axis_size("y")
    zi, xi, ci = (lax.axis_index(name) for name in ("z", "x", "c"))
    length = inputs.shape[1]
    span_all = 2 * length
    rows = w_in.shape[0]
    ff_rows = w_down.shape[0]
    hidden_part = nz * ny * ff_rows
    edge_count = conv_weight.shape[0] - 1
    out_rows, o_rows = w_out.shape[0], w_o.shape[0]
    aligned = ny == 2 and nz == 4 and MAMBA_HEADS % (4 * nz) == 0
    g = nz if aligned else 1
    hp = HEADS // g

    def heads_mine(array, width):
        lead = array.shape[:-1]
        array = array.reshape(lead + (g, 2, 2, hp * width))
        array = lax.dynamic_index_in_dim(array, xi, len(lead) + 1, keepdims=False)
        array = lax.dynamic_index_in_dim(array, ci, len(lead) + 1, keepdims=False)
        return array.reshape(lead + (HEADS * width,))

    def heads_spread(array, width):
        lead = array.shape[:-1]
        array = array.reshape(lead + (g, 1, 1, hp * width))
        whole = jnp.zeros(lead + (g, 2, 2, hp * width), array.dtype)
        start = (0,) * len(lead) + (0, xi, ci, 0)
        return lax.dynamic_update_slice(whole, array, start).reshape(
            lead + (MAMBA_HEADS * width,)
        )

    def heads_split(array, width):
        n = array.shape[0]
        array = array.reshape(n, g, 2, 2, hp * width)
        return jnp.transpose(array, (2, 3, 0, 1, 4)).reshape(4, n, HEADS * width)

    def heads_join(array, width):
        n = array.shape[1]
        array = array.reshape(2, 2, n, g, hp * width)
        return jnp.transpose(array, (2, 3, 0, 1, 4)).reshape(n, MAMBA_HEADS * width)

    def permuted(array):
        lead = array.shape[:-1]
        array = array.reshape(lead + (nz, 2, ny, 2 * rows))
        return jnp.swapaxes(array, -3, -2).reshape(lead + (D,))

    def restored(array):
        lead = array.shape[:-1]
        array = array.reshape(lead + (nz, ny, 2, 2 * rows))
        return jnp.swapaxes(array, -3, -2).reshape(lead + (D,))

    def to_ranks(array):
        return lax.all_to_all(array, GROUP, 0, 0, tiled=True)

    def in_order(own, other):
        return lax.dynamic_slice_in_dim(
            jnp.concatenate([own, other, own], 0), xi * length, span_all, 0
        )

    def gather_sequences(block):
        own, near, across, far = gather_tokens(block)
        return jnp.stack([in_order(own, across), in_order(near, far)])

    def scatter_sequences(partial):
        mine = partial[0] + swap(partial[1].astype(bf16), "c").astype(f32)
        mine = mine.reshape(2, length, mine.shape[-1])
        own = lax.dynamic_index_in_dim(mine, xi, 0, keepdims=False)
        other = lax.dynamic_index_in_dim(mine, 1 - xi, 0, keepdims=False)
        return own + swap(other.astype(bf16), "x").astype(f32)

    split_q = jnp.transpose(w_q.reshape(rows, 2, 2, 2, HEAD_DIM), (3, 1, 0, 2, 4))
    split_k = jnp.transpose(w_k.reshape(rows, 2, HEAD_DIM), (1, 0, 2))
    split_v = jnp.transpose(w_v.reshape(rows, 2, HEAD_DIM), (1, 0, 2))
    two = lambda a: jnp.broadcast_to(a[None], (2,) + a.shape).reshape(4, rows, a.shape[-1])
    packed_mix = jnp.concatenate(
        [
            heads_split(w_in[:, INNER : 2 * INNER], MAMBA_HEAD),
            jnp.broadcast_to(w_in[None, :, 2 * INNER : 2 * INNER + BC], (4, rows, BC)),
            jnp.pad(
                heads_split(w_in[:, 2 * INNER + BC :], 1), ((0, 0), (0, 0), (0, DT_PAD - HEADS))
            ),
            split_q.reshape(4, rows, QP),
            two(split_k),
            two(split_v),
            heads_split(w_in[:, :INNER], MAMBA_HEAD),
        ],
        axis=2,
    )
    full_mix = lax.all_gather(
        to_ranks(packed_mix).reshape(4 * rows, MIX_COLS), SHARDS, axis=0, tiled=True
    )

    if aligned:
        turn = [(2 * y + c, 2 * c + y) for y in range(2) for c in range(2)]
        place = []
        for z in range(4):
            for y in range(2):
                for c in range(2):
                    place.append(((z * 2 + y) * 2 + c, ((z % 2 * 2 + y) * 2 + c) * 2 + z // 2))
        back_place = [(b, a) for a, b in place]
        sent_out = lax.ppermute(w_out, ("y", "c"), turn)
        sent_o = lax.ppermute(w_o, ("z", "y", "c"), place)
        full_rows = lax.all_gather(
            jnp.concatenate([sent_out, sent_o], 0), SHARDS, axis=0, tiled=True
        ).reshape(nz * ny, out_rows + o_rows, D)
        full_out = full_rows[:, :out_rows].reshape(PART, D)
        full_o = full_rows[:, out_rows:].reshape(QP, D)
    else:
        every_out = lax.all_gather(w_out, EVERY, axis=0, tiled=True)
        every_o = lax.all_gather(w_o, EVERY, axis=0, tiled=True)
        full_out = lax.dynamic_slice_in_dim(every_out, (2 * xi + ci) * PART, PART, 0)
        every_o = every_o.reshape(2, 2, 2, HEAD_DIM, D)
        every_o = lax.dynamic_index_in_dim(every_o, xi, 2, keepdims=False)
        full_o = lax.dynamic_index_in_dim(every_o, ci, 0, keepdims=False).reshape(QP, D)

    def split_ff(w):
        w = w.reshape(rows, nz, 2, ny, 2, ff_rows)
        return jnp.transpose(w, (2, 4, 0, 1, 3, 5)).reshape(4, rows, hidden_part)

    def join_ff(w):
        w = w.reshape(2, 2, rows, nz, ny, ff_rows)
        return jnp.transpose(w, (2, 3, 0, 4, 1, 5)).reshape(rows, 4 * hidden_part)

    packed_ff = jnp.concatenate([split_ff(w_gate), split_ff(w_up)], axis=2)
    full_ff = lax.all_gather(
        to_ranks(packed_ff).reshape(4 * rows, 2 * hidden_part), SHARDS, axis=0, tiled=True
    )
    full_down = lax.all_gather(w_down, SHARDS, axis=0, tiled=True)

    resident = inputs[0].astype(f32)
    normed, norm_back = jax.vjp(rms_scale, resident, norm_gain)
    normed16 = gather_sequences(permuted(normed.astype(bf16)))
    tokens = 2 * span_all
    projected = low_dot(normed16.reshape(tokens, D), full_mix).reshape(2, span_all, MIX_COLS)
    conv_in = projected[..., :CONV_COLS]
    dt_raw = projected[..., AT_DT : AT_DT + HEADS]
    gate_z = projected[..., AT_Z:]
    edge_rows = shifted(conv_in[:, span_all - edge_count :].astype(bf16), 1).astype(f32)

    def rank_channels(array):
        return jnp.concatenate(
            [heads_mine(array[..., :INNER], MAMBA_HEAD), array[..., INNER:]], axis=-1
        )

    conv_w, conv_b = rank_channels(conv_weight), rank_channels(conv_bias)
    dt_b, a_l, skip = (heads_mine(v, 1) for v in (dt_bias, a_log, skip_gain))
    gain = heads_mine(gated_gain, MAMBA_HEAD)

    def conv_piece(conv_in, edge_rows, conv_w, conv_b):
        return convolve(jnp.concatenate([edge_rows, conv_in], 1), conv_w, conv_b)

    mixed, conv_back = jax.vjp(conv_piece, conv_in, edge_rows, conv_w, conv_b)
    own_state, own_decay = local_state(mixed, dt_raw, dt_b, a_l)
    own_state16 = own_state.astype(bf16)

    positions = zi * span_all + jnp.arange(span_all, dtype=jnp.int32)
    cosine, sine = rope_tables(positions)
    query16 = rotate(
        projected[..., AT_Q:AT_K].reshape(2, span_all, 2, HEAD_DIM), cosine, sine
    ).astype(bf16)
    key16 = rotate(projected[..., None, AT_K:AT_V], cosine, sine).astype(bf16)[:, :, 0]
    value16 = projected[..., AT_V:AT_Z].astype(bf16)
    kv16 = jnp.stack([key16, value16])
    kv_all = jnp.concatenate([shifted(kv16, d) for d in range(nz - 1, 0, -1)] + [kv16], axis=2)
    key_all, value_all = kv_all[0], kv_all[1]
    decays = [shifted(own_decay, d) for d in range(1, nz)]
    state_in = jnp.zeros(own_state.shape, f32)
    factor = jnp.ones(own_decay.shape, f32)
    for d in range(1, nz):
        arrived = shifted(own_state16, d).astype(f32)
        state_in = state_in + factor[:, :, None, None] * arrived
        factor = factor * decays[d - 1]

    score_scale = HEAD_DIM ** (-0.5)
    key_place = (zi - nz + 1) * span_all + jnp.arange(nz * span_all, dtype=jnp.int32)
    allowed = (key_place >= 0) & (positions[:, None] >= key_place)
    scores = (
        jnp.einsum("bqhd,bkd->bhqk", query16, key_all, preferred_element_type=f32) * score_scale
    )
    scores = jnp.where(allowed, scores, -jnp.inf)
    peak = jnp.max(scores, axis=-1, keepdims=True)
    unscaled = jnp.exp(scores - peak)
    probs = unscaled * (1.0 / jnp.sum(unscaled, axis=-1, keepdims=True))
    probs16 = probs.astype(bf16)
    attended = jnp.einsum("bhqk,bkd->bqhd", probs16, value_all, preferred_element_type=f32)
    attended16 = attended.reshape(tokens, QP).astype(bf16)

    (scanned, state_out), scan_back = jax.vjp(scan_all, mixed, dt_raw, dt_b, a_l, skip, state_in)
    flat, gate_back = jax.vjp(lambda v, z: v * jax.nn.silu(z), scanned, gate_z)
    square = group_total(jnp.sum(flat * flat, axis=-1, keepdims=True))
    root = lax.rsqrt(square / INNER + epsilon)
    gated16 = (flat * root * gain).astype(bf16).reshape(tokens, PART)
    mixture = low_dot(gated16, full_out) + low_dot(attended16, full_o)
    hidden_state = resident + scatter_sequences(mixture.reshape(2, span_all, D))

    middle, mid_back = jax.vjp(rms_scale, hidden_state, mid_gain)
    middle16 = jnp.concatenate(gather_tokens(permuted(middle.astype(bf16))), 0)
    cotangent16 = jnp.concatenate(gather_tokens(out_grad[0]), 0)
    both = low_dot(middle16, full_ff)
    activated, swish_back = jax.vjp(
        swish_product, both[:, :hidden_part], both[:, hidden_part:]
    )
    activated16 = activated.astype(bf16)
    down = low_dot(activated16, full_down).reshape(4, length, D)
    output = (hidden_state + scatter_tokens(down)).astype(bf16)
    gate_grad, up_grad = swish_back(back_dot(cotangent16, full_down))
    both16 = jnp.concatenate([gate_grad, up_grad], axis=1).astype(bf16)
    mid_grad = restored(scatter_tokens(back_dot(both16, full_ff).reshape(4, length, D)))
    hidden_piece, mid_gain_grad = mid_back(mid_grad)
    hidden_grad = out_grad[0].astype(f32) + hidden_piece

    def to_owners(array):
        return lax.psum_scatter(array.astype(bf16), SHARDS, scatter_dimension=0, tiled=True)

    result_down = to_owners(weight_grad(activated16, cotangent16)).astype(f32)
    ff_parts = to_ranks(to_owners(weight_grad(middle16, both16)).reshape(4, rows, 2 * hidden_part))
    result_gate = join_ff(ff_parts[..., :hidden_part]).astype(f32)
    result_up = join_ff(ff_parts[..., hidden_part:]).astype(f32)

    mix16 = gather_sequences(hidden_grad.astype(bf16)).reshape(tokens, D)
    attended_grad16 = back_dot(mix16, full_o).astype(bf16).reshape(2, span_all, 2, HEAD_DIM)
    gated_grad = back_dot(mix16, full_out).reshape(2, span_all, PART)
    grad_out_w = weight_grad(gated16, mix16)
    grad_o = weight_grad(attended16, mix16)
    if aligned:
        rows_parts = to_owners(
            jnp.concatenate(
                [
                    grad_out_w.reshape(nz * ny, out_rows, D),
                    grad_o.reshape(nz * ny, o_rows, D),
                ],
                axis=1,
            ).reshape(nz * ny * (out_rows + o_rows), D)
        )
        result_out = lax.ppermute(rows_parts[:out_rows], ("y", "c"), turn).astype(f32)
        result_o = lax.ppermute(rows_parts[out_rows:], ("z", "y", "c"), back_place).astype(f32)
    else:
        every_out = lax.dynamic_update_slice_in_dim(
            jnp.zeros((INNER, D), f32), grad_out_w, (2 * xi + ci) * PART, 0
        )
        every_o = lax.dynamic_update_slice(
            jnp.zeros((2, 2, 2, HEAD_DIM, D), f32),
            grad_o.reshape(1, 2, 1, HEAD_DIM, D),
            (ci, 0, xi, 0, 0),
        ).reshape(ATT_HEADS * HEAD_DIM, D)
        result_out = lax.psum_scatter(
            every_out.astype(bf16), EVERY, scatter_dimension=0, tiled=True
        ).astype(f32)
        result_o = lax.psum_scatter(
            every_o.astype(bf16), EVERY, scatter_dimension=0, tiled=True
        ).astype(f32)

    normal = flat * root
    gain_grad = jnp.sum(gated_grad * normal, axis=(0, 1))
    wide = gated_grad * gain
    inner_mean = group_total(jnp.sum(wide * normal, axis=-1, keepdims=True)) / INNER
    flat_grad = root * (wide - normal * inner_mean)
    scanned_grad, gate_z_grad = gate_back(flat_grad)
    state_local_grad = scan_back((scanned_grad, jnp.zeros(state_out.shape, f32)))[5]
    state_local16 = state_local_grad.astype(bf16)
    state_out_grad = jnp.zeros(own_state.shape, f32)
    factor = jnp.ones(own_decay.shape, f32)
    for d in range(1, nz):
        arrived = shifted(state_local16, -d).astype(f32)
        state_out_grad = state_out_grad + factor[:, :, None, None] * arrived
        factor = factor * shifted(own_decay, -d)

    attended_grad32 = attended_grad16.astype(f32)
    delta = jnp.moveaxis(jnp.sum(attended_grad32 * attended, axis=-1), 2, 1)
    prob_grad = jnp.einsum("bqhd,bkd->bhqk", attended_grad16, value_all, preferred_element_type=f32)
    score_grad = (probs * (prob_grad - delta[..., None])).astype(bf16)
    query_grad = score_scale * jnp.einsum(
        "bhqk,bkd->bqhd", score_grad, key_all, preferred_element_type=f32
    )
    key_grads = score_scale * jnp.einsum(
        "bhqk,bqhd->bkd", score_grad, query16, preferred_element_type=f32
    )
    value_grads = jnp.einsum(
        "bhqk,bqhd->bkd", probs16, attended_grad16, preferred_element_type=f32
    )
    kv_grads = jnp.stack([key_grads, value_grads]).reshape(2, 2, nz, span_all, HEAD_DIM)
    kv_grad = kv_grads[:, :, nz - 1]
    for d in range(1, nz):
        kv_grad = kv_grad + shifted(kv_grads[:, :, nz - 1 - d].astype(bf16), -d).astype(f32)

    mixed_grad, dt_raw_grad, dt_bias_grad, a_log_grad, skip_grad, _ = scan_back(
        (scanned_grad, state_out_grad)
    )
    conv_in_grad, edge_grad, conv_w_grad, conv_b_grad = conv_back(mixed_grad)
    edge_back = shifted(edge_grad.astype(bf16), -1).astype(f32)
    conv_in_grad = jnp.concatenate(
        [
            conv_in_grad[:, : span_all - edge_count],
            conv_in_grad[:, span_all - edge_count :] + edge_back,
        ],
        axis=1,
    )
    query_back = rotate(query_grad, cosine, -sine).reshape(2, span_all, QP)
    key_back = rotate(kv_grad[0][:, :, None], cosine, -sine)[:, :, 0]
    projected_grad16 = jnp.concatenate(
        [
            conv_in_grad.astype(bf16),
            jnp.pad(dt_raw_grad, ((0, 0), (0, 0), (0, DT_PAD - HEADS))).astype(bf16),
            query_back.astype(bf16),
            key_back.astype(bf16),
            kv_grad[1].astype(bf16),
            gate_z_grad.astype(bf16),
        ],
        axis=-1,
    ).reshape(tokens, MIX_COLS)
    mix_parts = to_ranks(
        to_owners(weight_grad(normed16.reshape(tokens, D), projected_grad16)).reshape(
            4, rows, MIX_COLS
        )
    ).astype(f32)
    normed_grad = restored(
        scatter_sequences(back_dot(projected_grad16, full_mix).reshape(2, span_all, D))
    )
    resident_grad, norm_gain_grad = norm_back(normed_grad)
    input_grad = hidden_grad + resident_grad

    result_in = jnp.concatenate(
        [
            heads_join(mix_parts[..., AT_Z:], MAMBA_HEAD),
            heads_join(mix_parts[..., :PART], MAMBA_HEAD),
            jnp.sum(mix_parts[..., PART:CONV_COLS], axis=0),
            heads_join(mix_parts[..., AT_DT : AT_DT + HEADS], 1),
        ],
        axis=1,
    )
    result_q = jnp.transpose(
        mix_parts[..., AT_Q:AT_K].reshape(2, 2, rows, 2, HEAD_DIM), (2, 1, 3, 0, 4)
    ).reshape(rows, ATT_HEADS * HEAD_DIM)
    kv_parts = jnp.sum(mix_parts[..., AT_K:AT_Z].reshape(2, 2, rows, 2, HEAD_DIM), axis=0)
    result_k = jnp.transpose(kv_parts[:, :, 0], (1, 0, 2)).reshape(rows, KV_HEADS * HEAD_DIM)
    result_v = jnp.transpose(kv_parts[:, :, 1], (1, 0, 2)).reshape(rows, KV_HEADS * HEAD_DIM)

    def all_channels(array):
        return jnp.concatenate(
            [heads_spread(array[..., :PART], MAMBA_HEAD), array[..., PART:]], axis=-1
        )

    small = [
        norm_gain_grad,
        all_channels(conv_w_grad),
        all_channels(conv_b_grad),
        heads_spread(dt_bias_grad, 1),
        heads_spread(a_log_grad, 1),
        heads_spread(skip_grad, 1),
        heads_spread(gain_grad, MAMBA_HEAD),
        mid_gain_grad,
    ]
    summed = total(jnp.concatenate([v.reshape(-1) for v in small]))
    parts, at = [], 0
    for v in small:
        parts.append(summed[at : at + v.size].reshape(v.shape))
        at += v.size
    return (
        output[None],
        input_grad[None],
        parts[0],
        result_in,
        parts[1],
        parts[2],
        parts[3],
        parts[4],
        parts[5],
        parts[6],
        result_out,
        result_q,
        result_k,
        result_v,
        result_o,
        parts[7],
        result_gate,
        result_up,
        result_down,
    )


def solution(mesh):
    seq, fsdp = mesh.shape["seq"], mesh.shape["fsdp"]
    split = Mesh(mesh.devices.reshape(seq // 2, 2, fsdp // 2, 2), EVERY)
    tokens = P(("y", "c"), ("z", "x"), None)
    matrix = P(EVERY, None)
    return jax.shard_map(
        body,
        mesh=split,
        in_specs=(tokens, tokens, P(), matrix)
        + (P(),) * 6
        + (matrix,) * 5
        + (P(),)
        + (matrix,) * 3,
        out_specs=(tokens, tokens, P(), matrix)
        + (P(),) * 6
        + (matrix,) * 5
        + (P(),)
        + (matrix,) * 3,
        check_vma=False,
    )
```

```python
import jax
import jax.numpy as jnp
from jax import lax
from jax.sharding import Mesh
from jax.sharding import PartitionSpec as P

D = 2048
MAMBA_HEADS = 48
MAMBA_HEAD = 64
STATE = 256
ATT_HEADS = 8
KV_HEADS = 2
HEAD_DIM = 128
SPAN = 128
INNER = 3072

HEADS = MAMBA_HEADS // 4
PART = HEADS * MAMBA_HEAD
BC = 2 * STATE
DT_PAD = 128
QP = 2 * HEAD_DIM
CONV_COLS = PART + BC
AT_DT = CONV_COLS
SCAN_COLS = AT_DT + DT_PAD
AT_K = QP
AT_V = AT_K + HEAD_DIM
AT_Z = AT_V + HEAD_DIM
REST_COLS = AT_Z + PART

epsilon = 1e-05
rope_base = 100000000000.0
highest = lax.Precision.DEFAULT
GROUP = ("x", "c")
SHARDS = ("z", "y")
EVERY = ("z", "x", "y", "c")
bf16 = jnp.bfloat16
f32 = jnp.float32


def swap(array, axis):
    return lax.ppermute(array, axis, [(0, 1), (1, 0)])


def shifted(array, distance):
    devices = range(lax.axis_size("z"))
    return lax.ppermute(array, "z", [(i - distance, i) for i in devices if i - distance in devices])


def total(array):
    for axis in EVERY:
        size = lax.axis_size(axis)
        bit = 1
        while bit < size:
            array = array + lax.ppermute(array, axis, [(i, i ^ bit) for i in range(size)])
            bit *= 2
    return array


def group_total(array):
    array = array + swap(array[::-1], "c")
    return array + swap(array, "x")


def low_dot(left, right):
    return jnp.dot(left, right, preferred_element_type=f32)


def back_dot(grad_rows, weight):
    return lax.dot_general(grad_rows, weight, (((1,), (1,)), ((), ())), preferred_element_type=f32)


def weight_grad(left, right):
    return lax.dot_general(left, right, (((0,), (0,)), ((), ())), preferred_element_type=f32)


def rms_scale(values, gain):
    return values * lax.rsqrt(jnp.mean(values * values, axis=-1, keepdims=True) + epsilon) * gain


def rope_tables(positions):
    half_dim = HEAD_DIM // 2
    frequencies = rope_base ** (-jnp.arange(half_dim, dtype=f32) / half_dim)
    angles = positions.astype(f32)[:, None] * frequencies[None, :]
    return (jnp.cos(angles), jnp.sin(angles))


def rotate(values, cosine, sine):
    half_dim = HEAD_DIM // 2
    cosine, sine = cosine[:, None, :], sine[:, None, :]
    first, second = values[..., :half_dim], values[..., half_dim:]
    return jnp.concatenate([first * cosine - second * sine, second * cosine + first * sine], axis=-1)


def convolve(padded, conv_weight, conv_bias):
    taps = conv_weight.shape[0]
    length = padded.shape[1] - taps + 1
    accumulated = conv_bias + padded[:, 0:length] * conv_weight[0]
    for offset in range(1, taps):
        accumulated = accumulated + padded[:, offset : offset + length] * conv_weight[offset]
    return jax.nn.silu(accumulated)


def chunk_parts(mixed, dt_raw, dt_bias, a_log):
    seqs, length = mixed.shape[:2]
    n = length // SPAN
    xs = mixed[..., :PART].reshape(seqs, n, SPAN, HEADS, MAMBA_HEAD)
    bs = mixed[..., PART : PART + STATE].reshape(seqs, n, SPAN, STATE)
    cs = mixed[..., PART + STATE :].reshape(seqs, n, SPAN, STATE)
    dt = jax.nn.softplus(dt_raw + dt_bias).reshape(seqs, n, SPAN, HEADS)
    cum = jnp.cumsum(dt * -jnp.exp(a_log), axis=2)
    return (xs, bs, cs, dt, cum)


def span_states(xs, bs, dt, cum):
    tail = jnp.exp(cum[:, :, -1:] - cum) * dt
    return jnp.einsum("bnshp,bnsm->bnhpm", tail[..., None] * xs, bs, precision=highest)


def local_state(mixed, dt_raw, dt_bias, a_log):
    xs, bs, cs, dt, cum = chunk_parts(mixed, dt_raw, dt_bias, a_log)
    local = span_states(xs, bs, dt, cum)
    state = local[:, 0]
    for i in range(1, local.shape[1]):
        state = jnp.exp(cum[:, i, -1])[:, :, None, None] * state + local[:, i]
    return (state, jnp.exp(jnp.sum(cum[:, :, -1], axis=1)))


def scan_all(mixed, dt_raw, dt_bias, a_log, skip_gain, state_in):
    seqs, length = mixed.shape[:2]
    xs, bs, cs, dt, cum = chunk_parts(mixed, dt_raw, dt_bias, a_log)
    n = length // SPAN
    places = jnp.arange(SPAN, dtype=jnp.int32)
    causal = places[:, None] >= places[None, :]
    cum_h = jnp.moveaxis(cum, 3, 2)
    dt_h = jnp.moveaxis(dt, 3, 2)
    spread = cum_h[..., :, None] - cum_h[..., None, :]
    decay = jnp.exp(jnp.where(causal, spread, -jnp.inf))
    meet = jnp.einsum("bntm,bnsm->bnts", cs, bs, precision=highest)
    weights = meet[:, :, None] * decay * dt_h[..., None, :]
    inside = jnp.einsum("bnhts,bnshp->bnthp", weights, xs, precision=highest)
    local = span_states(xs, bs, dt, cum)
    state, carried = state_in, []
    for i in range(n):
        carried.append(jnp.einsum("btm,bhpm->bthp", cs[:, i], state, precision=highest))
        state = jnp.exp(cum[:, i, -1])[:, :, None, None] * state + local[:, i]
    values = inside + jnp.exp(cum)[..., None] * jnp.stack(carried, 1) + skip_gain[:, None] * xs
    return (values.reshape(seqs, length, PART), state)


def swish_product(gate_proj, up_proj):
    return jax.nn.silu(gate_proj) * up_proj


def gather_tokens(block):
    across = swap(block, "x")
    return (block, swap(block, "c"), across, swap(across, "c"))


def scatter_tokens(blocks):
    near, far = blocks[0], blocks[2]
    sent = swap(jnp.stack([blocks[1].astype(bf16), blocks[3].astype(bf16)]), "c")
    near = near + sent[0].astype(f32)
    far = far + sent[1].astype(f32)
    return near + swap(far.astype(bf16), "x").astype(f32)


def body(
    inputs,
    out_grad,
    norm_gain,
    w_in,
    conv_weight,
    conv_bias,
    dt_bias,
    a_log,
    skip_gain,
    gated_gain,
    w_out,
    w_q,
    w_k,
    w_v,
    w_o,
    mid_gain,
    w_gate,
    w_up,
    w_down,
):
    nz, ny = lax.axis_size("z"), lax.axis_size("y")
    zi, xi, ci = (lax.axis_index(name) for name in ("z", "x", "c"))
    length = inputs.shape[1]
    span_all = 2 * length
    rows = w_in.shape[0]
    ff_rows = w_down.shape[0]
    hidden_part = nz * ny * ff_rows
    edge_count = conv_weight.shape[0] - 1
    out_rows, o_rows = w_out.shape[0], w_o.shape[0]
    aligned = ny == 2 and nz == 4 and MAMBA_HEADS % (4 * nz) == 0
    g = nz if aligned else 1
    hp = HEADS // g

    def heads_mine(array, width):
        lead = array.shape[:-1]
        array = array.reshape(lead + (g, 2, 2, hp * width))
        array = lax.dynamic_index_in_dim(array, xi, len(lead) + 1, keepdims=False)
        array = lax.dynamic_index_in_dim(array, ci, len(lead) + 1, keepdims=False)
        return array.reshape(lead + (HEADS * width,))

    def heads_spread(array, width):
        lead = array.shape[:-1]
        array = array.reshape(lead + (g, 1, 1, hp * width))
        whole = jnp.zeros(lead + (g, 2, 2, hp * width), array.dtype)
        start = (0,) * len(lead) + (0, xi, ci, 0)
        return lax.dynamic_update_slice(whole, array, start).reshape(
            lead + (MAMBA_HEADS * width,)
        )

    def heads_split(array, width):
        n = array.shape[0]
        array = array.reshape(n, g, 2, 2, hp * width)
        return jnp.transpose(array, (2, 3, 0, 1, 4)).reshape(4, n, HEADS * width)

    def heads_join(array, width):
        n = array.shape[1]
        array = array.reshape(2, 2, n, g, hp * width)
        return jnp.transpose(array, (2, 3, 0, 1, 4)).reshape(n, MAMBA_HEADS * width)

    def permuted(array):
        lead = array.shape[:-1]
        array = array.reshape(lead + (nz, 2, ny, 2 * rows))
        return jnp.swapaxes(array, -3, -2).reshape(lead + (D,))

    def restored(array):
        lead = array.shape[:-1]
        array = array.reshape(lead + (nz, ny, 2, 2 * rows))
        return jnp.swapaxes(array, -3, -2).reshape(lead + (D,))

    def to_ranks(array):
        return lax.all_to_all(array, GROUP, 0, 0, tiled=True)

    def in_order(own, other):
        return lax.dynamic_slice_in_dim(
            jnp.concatenate([own, other, own], 0), xi * length, span_all, 0
        )

    def gather_sequences(block):
        own, near, across, far = gather_tokens(block)
        return jnp.stack([in_order(own, across), in_order(near, far)])

    def scatter_sequences(partial):
        mine = partial[0] + swap(partial[1].astype(bf16), "c").astype(f32)
        mine = mine.reshape(2, length, mine.shape[-1])
        own = lax.dynamic_index_in_dim(mine, xi, 0, keepdims=False)
        other = lax.dynamic_index_in_dim(mine, 1 - xi, 0, keepdims=False)
        return own + swap(other.astype(bf16), "x").astype(f32)

    split_q = jnp.transpose(w_q.reshape(rows, 2, 2, 2, HEAD_DIM), (3, 1, 0, 2, 4))
    split_k = jnp.transpose(w_k.reshape(rows, 2, HEAD_DIM), (1, 0, 2))
    split_v = jnp.transpose(w_v.reshape(rows, 2, HEAD_DIM), (1, 0, 2))
    two = lambda a: jnp.broadcast_to(a[None], (2,) + a.shape).reshape(4, rows, a.shape[-1])
    packed_scan = jnp.concatenate(
        [
            heads_split(w_in[:, INNER : 2 * INNER], MAMBA_HEAD),
            jnp.broadcast_to(w_in[None, :, 2 * INNER : 2 * INNER + BC], (4, rows, BC)),
            jnp.pad(
                heads_split(w_in[:, 2 * INNER + BC :], 1), ((0, 0), (0, 0), (0, DT_PAD - HEADS))
            ),
        ],
        axis=2,
    )
    packed_rest = jnp.concatenate(
        [
            split_q.reshape(4, rows, QP),
            two(split_k),
            two(split_v),
            heads_split(w_in[:, :INNER], MAMBA_HEAD),
        ],
        axis=2,
    )

    def gathered(array):
        return lax.all_gather(array, SHARDS, axis=0, tiled=True)

    def after(array, *others):
        return lax.optimization_barrier((array,) + others)[0]

    full_scan = gathered(to_ranks(packed_scan).reshape(4 * rows, SCAN_COLS))
    full_rest = gathered(after(to_ranks(packed_rest).reshape(4 * rows, REST_COLS), full_scan))

    if aligned:
        turn = [(2 * y + c, 2 * c + y) for y in range(2) for c in range(2)]
        place = []
        for z in range(4):
            for y in range(2):
                for c in range(2):
                    place.append(((z * 2 + y) * 2 + c, ((z % 2 * 2 + y) * 2 + c) * 2 + z // 2))
        back_place = [(b, a) for a, b in place]
        sent_out = lax.ppermute(w_out, ("y", "c"), turn)
        sent_o = lax.ppermute(w_o, ("z", "y", "c"), place)
        whole_rows = gathered(after(jnp.concatenate([sent_out, sent_o], 0), full_rest))
        full_rows = whole_rows.reshape(nz * ny, out_rows + o_rows, D)
        full_out = full_rows[:, :out_rows].reshape(PART, D)
        full_o = full_rows[:, out_rows:].reshape(QP, D)
    else:
        every_out = lax.all_gather(w_out, EVERY, axis=0, tiled=True)
        every_o = lax.all_gather(w_o, EVERY, axis=0, tiled=True)
        full_out = lax.dynamic_slice_in_dim(every_out, (2 * xi + ci) * PART, PART, 0)
        every_o = every_o.reshape(2, 2, 2, HEAD_DIM, D)
        every_o = lax.dynamic_index_in_dim(every_o, xi, 2, keepdims=False)
        full_o = lax.dynamic_index_in_dim(every_o, ci, 0, keepdims=False).reshape(QP, D)
        whole_rows = full_out

    def split_ff(w):
        w = w.reshape(rows, nz, 2, ny, 2, ff_rows)
        return jnp.transpose(w, (2, 4, 0, 1, 3, 5)).reshape(4, rows, hidden_part)

    def join_ff(w):
        w = w.reshape(2, 2, rows, nz, ny, ff_rows)
        return jnp.transpose(w, (2, 3, 0, 4, 1, 5)).reshape(rows, 4 * hidden_part)

    packed_ff = jnp.concatenate([split_ff(w_gate), split_ff(w_up)], axis=2)
    full_ff = gathered(
        after(to_ranks(packed_ff).reshape(4 * rows, 2 * hidden_part), whole_rows)
    )
    full_down = gathered(after(w_down, full_ff))

    resident = inputs[0].astype(f32)
    normed, norm_back = jax.vjp(rms_scale, resident, norm_gain)
    normed16 = gather_sequences(permuted(normed.astype(bf16)))
    tokens = 2 * span_all
    edges16 = shifted(normed16[:, span_all - edge_count :], 1).reshape(2 * edge_count, D)
    normed_rows = normed16.reshape(tokens, D)
    scan_in = low_dot(normed_rows, full_scan).reshape(2, span_all, SCAN_COLS)
    edge_rows = low_dot(edges16, full_scan[:, :CONV_COLS]).reshape(2, edge_count, CONV_COLS)
    conv_in = scan_in[..., :CONV_COLS]
    dt_raw = scan_in[..., AT_DT : AT_DT + HEADS]
    rest = low_dot(normed_rows, full_rest).reshape(2, span_all, REST_COLS)
    gate_z = rest[..., AT_Z:]

    def rank_channels(array):
        return jnp.concatenate(
            [heads_mine(array[..., :INNER], MAMBA_HEAD), array[..., INNER:]], axis=-1
        )

    conv_w, conv_b = rank_channels(conv_weight), rank_channels(conv_bias)
    dt_b, a_l, skip = (heads_mine(v, 1) for v in (dt_bias, a_log, skip_gain))
    gain = heads_mine(gated_gain, MAMBA_HEAD)

    def conv_piece(conv_in, edge_rows, conv_w, conv_b):
        return convolve(jnp.concatenate([edge_rows, conv_in], 1), conv_w, conv_b)

    mixed, conv_back = jax.vjp(conv_piece, conv_in, edge_rows, conv_w, conv_b)
    own_state, own_decay = local_state(mixed, dt_raw, dt_b, a_l)

    def chained(local, decay, step):
        entering = []
        for s in range(2):
            held = jnp.zeros(local.shape[1:], f32)
            for hop in range(nz - 1):
                at = hop if step == 1 else nz - 1 - hop
                leaving = local[s] + decay[s][:, None, None] * held if hop else local[s]
                held = held + lax.ppermute(
                    leaving.astype(bf16), "z", [(at, at + step)]
                ).astype(f32)
            entering.append(held)
        return jnp.stack(entering)

    positions = zi * span_all + jnp.arange(span_all, dtype=jnp.int32)
    cosine, sine = rope_tables(positions)
    query16 = rotate(
        rest[..., :AT_K].reshape(2, span_all, 2, HEAD_DIM), cosine, sine
    ).astype(bf16)
    key16 = rotate(rest[..., None, AT_K:AT_V], cosine, sine).astype(bf16)[:, :, 0]
    value16 = rest[..., AT_V:AT_Z].astype(bf16)
    kv16 = jnp.stack([key16, value16])
    kv_all = jnp.concatenate([shifted(kv16, d) for d in range(nz - 1, 0, -1)] + [kv16], axis=2)
    key_all, value_all = kv_all[0], kv_all[1]
    state_in = chained(own_state, own_decay, 1)

    score_scale = HEAD_DIM ** (-0.5)
    key_place = (zi - nz + 1) * span_all + jnp.arange(nz * span_all, dtype=jnp.int32)
    allowed = (key_place >= 0) & (positions[:, None] >= key_place)
    scores = (
        jnp.einsum("bqhd,bkd->bhqk", query16, key_all, preferred_element_type=f32) * score_scale
    )
    scores = jnp.where(allowed, scores, -jnp.inf)
    peak = jnp.max(scores, axis=-1, keepdims=True)
    unscaled = jnp.exp(scores - peak)
    probs = unscaled * (1.0 / jnp.sum(unscaled, axis=-1, keepdims=True))
    probs16 = probs.astype(bf16)
    attended = jnp.einsum("bhqk,bkd->bqhd", probs16, value_all, preferred_element_type=f32)
    attended16 = attended.reshape(tokens, QP).astype(bf16)

    (scanned, state_out), scan_back = jax.vjp(scan_all, mixed, dt_raw, dt_b, a_l, skip, state_in)
    flat, gate_back = jax.vjp(lambda v, z: v * jax.nn.silu(z), scanned, gate_z)
    square = group_total(jnp.sum(flat * flat, axis=-1, keepdims=True))
    root = lax.rsqrt(square / INNER + epsilon)
    gated16 = (flat * root * gain).astype(bf16).reshape(tokens, PART)
    mixture = low_dot(gated16, full_out) + low_dot(attended16, full_o)
    hidden_state = resident + scatter_sequences(mixture.reshape(2, span_all, D))

    middle, mid_back = jax.vjp(rms_scale, hidden_state, mid_gain)
    middle16 = jnp.concatenate(gather_tokens(permuted(middle.astype(bf16))), 0)
    cotangent16 = jnp.concatenate(gather_tokens(out_grad[0]), 0)
    both = low_dot(middle16, full_ff)
    activated, swish_back = jax.vjp(
        swish_product, both[:, :hidden_part], both[:, hidden_part:]
    )
    activated16 = activated.astype(bf16)
    down = low_dot(activated16, full_down).reshape(4, length, D)
    output = (hidden_state + scatter_tokens(down)).astype(bf16)
    gate_grad, up_grad = swish_back(back_dot(cotangent16, full_down))
    both16 = jnp.concatenate([gate_grad, up_grad], axis=1).astype(bf16)
    mid_grad = restored(scatter_tokens(back_dot(both16, full_ff).reshape(4, length, D)))
    hidden_piece, mid_gain_grad = mid_back(mid_grad)
    hidden_grad = out_grad[0].astype(f32) + hidden_piece

    def to_owners(array):
        return lax.psum_scatter(array.astype(bf16), SHARDS, scatter_dimension=0, tiled=True)

    result_down = to_owners(weight_grad(activated16, cotangent16)).astype(f32)
    ff_parts = to_ranks(to_owners(weight_grad(middle16, both16)).reshape(4, rows, 2 * hidden_part))
    result_gate = join_ff(ff_parts[..., :hidden_part]).astype(f32)
    result_up = join_ff(ff_parts[..., hidden_part:]).astype(f32)

    mix16 = gather_sequences(hidden_grad.astype(bf16)).reshape(tokens, D)
    attended_grad16 = back_dot(mix16, full_o).astype(bf16).reshape(2, span_all, 2, HEAD_DIM)
    gated_grad = back_dot(mix16, full_out).reshape(2, span_all, PART)
    grad_out_w = weight_grad(gated16, mix16)
    grad_o = weight_grad(attended16, mix16)
    if aligned:
        rows_parts = to_owners(
            jnp.concatenate(
                [
                    grad_out_w.reshape(nz * ny, out_rows, D),
                    grad_o.reshape(nz * ny, o_rows, D),
                ],
                axis=1,
            ).reshape(nz * ny * (out_rows + o_rows), D)
        )
        rows_done = rows_parts
        result_out = lax.ppermute(rows_parts[:out_rows], ("y", "c"), turn).astype(f32)
        result_o = lax.ppermute(rows_parts[out_rows:], ("z", "y", "c"), back_place).astype(f32)
    else:
        every_out = lax.dynamic_update_slice_in_dim(
            jnp.zeros((INNER, D), f32), grad_out_w, (2 * xi + ci) * PART, 0
        )
        every_o = lax.dynamic_update_slice(
            jnp.zeros((2, 2, 2, HEAD_DIM, D), f32),
            grad_o.reshape(1, 2, 1, HEAD_DIM, D),
            (ci, 0, xi, 0, 0),
        ).reshape(ATT_HEADS * HEAD_DIM, D)
        result_out = lax.psum_scatter(
            every_out.astype(bf16), EVERY, scatter_dimension=0, tiled=True
        ).astype(f32)
        result_o = lax.psum_scatter(
            every_o.astype(bf16), EVERY, scatter_dimension=0, tiled=True
        ).astype(f32)
        rows_done = result_out

    normal = flat * root
    gain_grad = jnp.sum(gated_grad * normal, axis=(0, 1))
    wide = gated_grad * gain
    inner_mean = group_total(jnp.sum(wide * normal, axis=-1, keepdims=True)) / INNER
    flat_grad = root * (wide - normal * inner_mean)
    scanned_grad, gate_z_grad = gate_back(flat_grad)
    state_local_grad = scan_back((scanned_grad, jnp.zeros(state_out.shape, f32)))[5]
    state_out_grad = chained(state_local_grad, own_decay, -1)

    attended_grad32 = attended_grad16.astype(f32)
    delta = jnp.moveaxis(jnp.sum(attended_grad32 * attended, axis=-1), 2, 1)
    prob_grad = jnp.einsum("bqhd,bkd->bhqk", attended_grad16, value_all, preferred_element_type=f32)
    score_grad = (probs * (prob_grad - delta[..., None])).astype(bf16)
    query_grad = score_scale * jnp.einsum(
        "bhqk,bkd->bqhd", score_grad, key_all, preferred_element_type=f32
    )
    key_grads = score_scale * jnp.einsum(
        "bhqk,bqhd->bkd", score_grad, query16, preferred_element_type=f32
    )
    value_grads = jnp.einsum(
        "bhqk,bqhd->bkd", probs16, attended_grad16, preferred_element_type=f32
    )
    kv_grads = jnp.stack([key_grads, value_grads]).reshape(2, 2, nz, span_all, HEAD_DIM)
    kv_grad = kv_grads[:, :, nz - 1]
    for d in range(1, nz):
        kv_grad = kv_grad + shifted(kv_grads[:, :, nz - 1 - d].astype(bf16), -d).astype(f32)

    mixed_grad, dt_raw_grad, dt_bias_grad, a_log_grad, skip_grad, _ = scan_back(
        (scanned_grad, state_out_grad)
    )
    conv_in_grad, edge_grad, conv_w_grad, conv_b_grad = conv_back(mixed_grad)
    edge_back = shifted(edge_grad.astype(bf16), -1).astype(f32)
    conv_in_grad = jnp.concatenate(
        [
            conv_in_grad[:, : span_all - edge_count],
            conv_in_grad[:, span_all - edge_count :] + edge_back,
        ],
        axis=1,
    )
    query_back = rotate(query_grad, cosine, -sine).reshape(2, span_all, QP)
    key_back = rotate(kv_grad[0][:, :, None], cosine, -sine)[:, :, 0]
    scan_grad16 = jnp.concatenate(
        [
            conv_in_grad.astype(bf16),
            jnp.pad(dt_raw_grad, ((0, 0), (0, 0), (0, DT_PAD - HEADS))).astype(bf16),
        ],
        axis=-1,
    ).reshape(tokens, SCAN_COLS)
    rest_grad16 = jnp.concatenate(
        [
            query_back.astype(bf16),
            key_back.astype(bf16),
            kv_grad[1].astype(bf16),
            gate_z_grad.astype(bf16),
        ],
        axis=-1,
    ).reshape(tokens, REST_COLS)
    rest_owned = to_owners(after(weight_grad(normed_rows, rest_grad16).astype(bf16), rows_done))
    rest_parts = to_ranks(rest_owned.reshape(4, rows, REST_COLS)).astype(f32)
    scan_owned = to_owners(after(weight_grad(normed_rows, scan_grad16).astype(bf16), rest_owned))
    scan_parts = to_ranks(scan_owned.reshape(4, rows, SCAN_COLS)).astype(f32)
    normed_grad = back_dot(scan_grad16, full_scan) + back_dot(rest_grad16, full_rest)
    normed_grad = restored(scatter_sequences(normed_grad.reshape(2, span_all, D)))
    resident_grad, norm_gain_grad = norm_back(normed_grad)
    input_grad = hidden_grad + resident_grad

    result_in = jnp.concatenate(
        [
            heads_join(rest_parts[..., AT_Z:], MAMBA_HEAD),
            heads_join(scan_parts[..., :PART], MAMBA_HEAD),
            jnp.sum(scan_parts[..., PART:CONV_COLS], axis=0),
            heads_join(scan_parts[..., AT_DT : AT_DT + HEADS], 1),
        ],
        axis=1,
    )
    result_q = jnp.transpose(
        rest_parts[..., :AT_K].reshape(2, 2, rows, 2, HEAD_DIM), (2, 1, 3, 0, 4)
    ).reshape(rows, ATT_HEADS * HEAD_DIM)
    kv_parts = jnp.sum(rest_parts[..., AT_K:AT_Z].reshape(2, 2, rows, 2, HEAD_DIM), axis=0)
    result_k = jnp.transpose(kv_parts[:, :, 0], (1, 0, 2)).reshape(rows, KV_HEADS * HEAD_DIM)
    result_v = jnp.transpose(kv_parts[:, :, 1], (1, 0, 2)).reshape(rows, KV_HEADS * HEAD_DIM)

    def all_channels(array):
        return jnp.concatenate(
            [heads_spread(array[..., :PART], MAMBA_HEAD), array[..., PART:]], axis=-1
        )

    small = [
        norm_gain_grad,
        all_channels(conv_w_grad),
        all_channels(conv_b_grad),
        heads_spread(dt_bias_grad, 1),
        heads_spread(a_log_grad, 1),
        heads_spread(skip_grad, 1),
        heads_spread(gain_grad, MAMBA_HEAD),
        mid_gain_grad,
    ]
    summed = total(jnp.concatenate([v.reshape(-1) for v in small]))
    parts, at = [], 0
    for v in small:
        parts.append(summed[at : at + v.size].reshape(v.shape))
        at += v.size
    return (
        output[None],
        input_grad[None],
        parts[0],
        result_in,
        parts[1],
        parts[2],
        parts[3],
        parts[4],
        parts[5],
        parts[6],
        result_out,
        result_q,
        result_k,
        result_v,
        result_o,
        parts[7],
        result_gate,
        result_up,
        result_down,
    )


def solution(mesh):
    seq, fsdp = mesh.shape["seq"], mesh.shape["fsdp"]
    split = Mesh(mesh.devices.reshape(seq // 2, 2, fsdp // 2, 2), EVERY)
    tokens = P(("y", "c"), ("z", "x"), None)
    matrix = P(EVERY, None)
    return jax.shard_map(
        body,
        mesh=split,
        in_specs=(tokens, tokens, P(), matrix)
        + (P(),) * 6
        + (matrix,) * 5
        + (P(),)
        + (matrix,) * 3,
        out_specs=(tokens, tokens, P(), matrix)
        + (P(),) * 6
        + (matrix,) * 5
        + (P(),)
        + (matrix,) * 3,
        check_vma=False,
    )
```

```python
import jax
import jax.numpy as jnp
from jax import lax
from jax.experimental import pallas as pl
from jax.experimental.pallas import tpu as pltpu
from jax.sharding import Mesh
from jax.sharding import PartitionSpec as P

D = 2048
MAMBA_HEADS = 48
MAMBA_HEAD = 64
STATE = 256
ATT_HEADS = 8
KV_HEADS = 2
HEAD_DIM = 128
SPAN = 128
INNER = 3072

HEADS = MAMBA_HEADS // 4
PART = HEADS * MAMBA_HEAD
BC = 2 * STATE
DT_PAD = 128
QP = 2 * HEAD_DIM
CONV_COLS = PART + BC
SCAN_COLS = CONV_COLS + DT_PAD
AT_Q = PART
AT_K = AT_Q + QP
AT_V = AT_K + HEAD_DIM
REST_COLS = AT_V + HEAD_DIM
HALF = D // 2

epsilon = 1e-05
rope_base = 100000000000.0
GROUP = ("x", "c")
SHARDS = ("z", "y")
EVERY = ("z", "x", "y", "c")
bf16 = jnp.bfloat16
f32 = jnp.float32


def swap(array, axis):
    return lax.ppermute(array, axis, [(0, 1), (1, 0)])


def shifted(array, distance):
    devices = range(lax.axis_size("z"))
    return lax.ppermute(array, "z", [(i - distance, i) for i in devices if i - distance in devices])


def total(array):
    for axis in EVERY:
        size = lax.axis_size(axis)
        bit = 1
        while bit < size:
            array = array + lax.ppermute(array, axis, [(i, i ^ bit) for i in range(size)])
            bit *= 2
    return array


def group_total(array):
    array = array + swap(array[::-1], "c")
    return array + swap(array, "x")


def low_dot(left, right):
    return jnp.dot(left, right, preferred_element_type=f32)


def back_dot(grad_rows, weight):
    return lax.dot_general(grad_rows, weight, (((1,), (1,)), ((), ())), preferred_element_type=f32)


def weight_grad(left, right):
    return lax.dot_general(left, right, (((0,), (0,)), ((), ())), preferred_element_type=f32)


def rms_scale(values, gain):
    return values * lax.rsqrt(jnp.mean(values * values, axis=-1, keepdims=True) + epsilon) * gain


def rope_tables(positions):
    half_dim = HEAD_DIM // 2
    frequencies = rope_base ** (-jnp.arange(half_dim, dtype=f32) / half_dim)
    angles = positions.astype(f32)[:, None] * frequencies[None, :]
    return (jnp.cos(angles), jnp.sin(angles))


def rotate(values, cosine, sine):
    half_dim = HEAD_DIM // 2
    cosine, sine = cosine[:, None, :], sine[:, None, :]
    first, second = values[..., :half_dim], values[..., half_dim:]
    return jnp.concatenate([first * cosine - second * sine, second * cosine + first * sine], axis=-1)


def exact(left, right):
    return jnp.dot(left, right, precision=lax.Precision.HIGHEST, preferred_element_type=f32)


def over_lanes(left, right):
    return lax.dot_general(left, right, (((1,), (1,)), ((), ())), preferred_element_type=f32)


def over_rows(left, right):
    return lax.dot_general(left, right, (((0,), (0,)), ((), ())), preferred_element_type=f32)


def widen(values, lift):
    return exact(values, lift)


def narrow(values, lift):
    return lax.dot_general(
        values,
        lift,
        (((1,), (1,)), ((), ())),
        precision=lax.Precision.HIGHEST,
        preferred_element_type=f32,
    )


def sig(values):
    return 1.0 / (1.0 + jnp.exp(-values))


def soft(values):
    return jnp.maximum(values, 0.0) + jnp.log1p(jnp.exp(-jnp.abs(values)))


def square_places():
    return (
        lax.broadcasted_iota(jnp.int32, (SPAN, SPAN), 0),
        lax.broadcasted_iota(jnp.int32, (SPAN, SPAN), 1),
    )


def pre_conv(current, before, taps, bias):
    extended = jnp.concatenate([before, current], axis=0)
    pre = bias + extended[5 : 5 + SPAN] * taps[0:1]
    for k in range(1, 4):
        pre = pre + extended[5 + k : 5 + k + SPAN] * taps[k : k + 1]
    return (pre, extended)


def states_kernel(
    scan_in, before, taps, bias, dt_bias, rates, lift, mixed, steps, starts, prefix, last, held, sofar
):
    @pl.when(pl.program_id(1) == 0)
    def _():
        held[...] = jnp.zeros_like(held)
        sofar[...] = jnp.zeros_like(sofar)

    pre, _ = pre_conv(scan_in[0, :, :CONV_COLS], before[0, 0], taps[...], bias[...])
    mix = pre * sig(pre)
    mixed[0] = mix
    dt = soft(scan_in[0, :, CONV_COLS:] + dt_bias[...])
    row, column = square_places()
    cum = exact(jnp.where(row >= column, 1.0, 0.0), dt * rates[...])
    steps[0, :, :DT_PAD] = dt
    steps[0, :, DT_PAD:] = cum
    starts[0, 0] = sofar[...]
    prefix[0, 0] = held[...]
    end = cum[SPAN - 1 : SPAN]
    tail = jnp.exp(end - cum) * dt
    fed = (mix[:, :PART] * widen(tail, lift[...])).astype(bf16)
    added = over_rows(mix[:, PART : PART + STATE].astype(bf16), fed)
    whole = widen(jnp.broadcast_to(jnp.exp(end), (8, DT_PAD)), lift[...])[0:1]
    held[...] = whole * held[...] + added
    sofar[...] = sofar[...] + end
    last[0] = held[...]


def values_kernel(
    mixed, steps, starts, prefix, state_in, gate, skip, lift, values, flat, square
):
    x = mixed[0, :, :PART]
    b16 = mixed[0, :, PART : PART + STATE].astype(bf16)
    c16 = mixed[0, :, PART + STATE :].astype(bf16)
    dt = steps[0, :, :DT_PAD]
    cum = steps[0, :, DT_PAD:]
    dt_t, cum_t = dt.T, cum.T
    state = prefix[0, 0] + widen(jnp.exp(starts[0, 0]), lift[...])[0:1] * state_in[0]
    meet = over_lanes(c16, b16)
    carried = low_dot(c16, state.astype(bf16)) * widen(jnp.exp(cum), lift[...])
    row, column = square_places()
    first = column < MAMBA_HEAD
    inside = []
    for k in range(HEADS // 2):
        pair = x[:, 2 * MAMBA_HEAD * k : 2 * MAMBA_HEAD * (k + 1)]
        weights = []
        for h in (2 * k, 2 * k + 1):
            spread = cum[:, h : h + 1] - cum_t[h : h + 1, :]
            decay = jnp.exp(jnp.where(row >= column, spread, -1e30))
            weights.append((meet * decay * dt_t[h : h + 1, :]).astype(bf16))
        split = [
            jnp.where(first, pair, 0.0).astype(bf16),
            jnp.where(first, 0.0, pair).astype(bf16),
        ]
        inside.append(low_dot(jnp.concatenate(weights, 1), jnp.concatenate(split, 0)))
    value = jnp.concatenate(inside, 1) + carried + skip[...] * x
    values[0] = value
    z = gate[0]
    product = value * (z * sig(z))
    flat[0] = product
    square[0] = jnp.broadcast_to(
        jnp.sum(product * product, axis=1, keepdims=True), (SPAN, 128)
    )


def gate_back_kernel(
    gated_grad, values, gate, root, mean, gain, c_part, steps, lift,
    value_grad, gate_grad, gain_grad, suffix, first_grad, held,
):
    @pl.when(pl.program_id(1) == 0)
    def _():
        held[...] = jnp.zeros_like(held)

    @pl.when((pl.program_id(0) == 0) & (pl.program_id(1) == 0))
    def _():
        gain_grad[...] = jnp.zeros_like(gain_grad)

    z, value, grad = gate[0], values[0], gated_grad[0]
    s = sig(z)
    silu = z * s
    scale = root[0, :, 0:1]
    normal = value * silu * scale
    flat_grad = scale * (grad * gain[...] - normal * mean[0, :, 0:1])
    d_value = flat_grad * silu
    value_grad[0] = d_value
    gate_grad[0] = (flat_grad * value * (s * (1.0 + z * (1.0 - s)))).astype(bf16)
    gain_grad[0:1] = gain_grad[0:1] + jnp.sum(grad * normal, axis=0, keepdims=True)
    grown = widen(jnp.exp(steps[0, :, DT_PAD:]), lift[...])
    suffix[0, 0] = held[...]
    held[...] = grown[SPAN - 1 : SPAN] * held[...] + over_rows(
        c_part[0].astype(bf16), (grown * d_value).astype(bf16)
    )
    first_grad[0] = held[...]


def scan_back_kernel(
    scan_in, before, mixed, steps, starts, prefix, state_in, suffix, state_grad, value_grad,
    skip, taps, bias, dt_bias, rates, lift,
    scan_grad, edge_grad, conv_grad, small_grad,
    later, after_pre, columns,
):
    @pl.when(pl.program_id(1) == 0)
    def _():
        later[...] = jnp.zeros_like(later)
        after_pre[...] = jnp.zeros_like(after_pre)

    @pl.when((pl.program_id(0) == 0) & (pl.program_id(1) == 0))
    def _():
        conv_grad[...] = jnp.zeros_like(conv_grad)
        small_grad[...] = jnp.zeros_like(small_grad)
        columns[...] = jnp.zeros_like(columns)

    up = lift[...]
    x = mixed[0, :, :PART]
    b16 = mixed[0, :, PART : PART + STATE].astype(bf16)
    c16 = mixed[0, :, PART + STATE :].astype(bf16)
    dt = steps[0, :, :DT_PAD]
    cum = steps[0, :, DT_PAD:]
    dt_t, cum_t = dt.T, cum.T
    end = cum[SPAN - 1 : SPAN]
    dy = value_grad[0]
    state = prefix[0, 0] + widen(jnp.exp(starts[0, 0]), up)[0:1] * state_in[0]
    ending = suffix[0, 0] + widen(jnp.exp(later[...]), up)[0:1] * state_grad[0]
    later[...] = later[...] + end
    state16, ending16 = state.astype(bf16), ending.astype(bf16)
    grown = widen(jnp.exp(cum), up)
    tail_wide = widen(jnp.exp(end - cum), up)
    dt_wide = widen(dt, up)
    grown_dy = grown * dy
    reach = low_dot(c16, state16)
    pull = tail_wide * low_dot(b16, ending16)
    d_c = over_lanes(grown_dy.astype(bf16), state16)
    d_b = over_lanes((tail_wide * dt_wide * x).astype(bf16), ending16)
    meet = over_lanes(c16, b16)
    row, column = square_places()
    first = column < MAMBA_HEAD
    d_meet = jnp.zeros((SPAN, SPAN), f32)
    rows_sum = jnp.zeros((SPAN, DT_PAD), f32)
    back = []
    for k in range(HEADS // 2):
        at = slice(2 * MAMBA_HEAD * k, 2 * MAMBA_HEAD * (k + 1))
        x16, dy_pair = x[:, at].astype(bf16), dy[:, at]
        split = [
            jnp.where(first, dy_pair, 0.0).astype(bf16),
            jnp.where(first, 0.0, dy_pair).astype(bf16),
        ]
        weights = []
        for j in range(2):
            h = 2 * k + j
            spread = cum[:, h : h + 1] - cum_t[h : h + 1, :]
            decay = jnp.exp(jnp.where(row >= column, spread, -1e30))
            d_weight = over_lanes(split[j], x16) * decay
            scaled = d_weight * dt_t[h : h + 1, :]
            d_meet = d_meet + scaled
            rows_sum = rows_sum + jnp.where(
                column == h, jnp.sum(scaled * meet, axis=1, keepdims=True), 0.0
            )
            columns[h : h + 1, :] = jnp.sum(d_weight * meet, axis=0, keepdims=True)
            weights.append((meet * decay).astype(bf16))
        back.append(over_rows(jnp.concatenate(weights, 0), jnp.concatenate(split, 0)))
    d_meet16 = d_meet.astype(bf16)
    d_c = d_c + low_dot(d_meet16, b16)
    d_b = d_b + over_rows(d_meet16, c16)
    d_x = dt_wide * (jnp.concatenate(back, 1) + pull) + skip[...] * dy
    tail_dt = narrow(x * pull, up)
    inner_dt = columns[...].T
    d_cum = rows_sum + narrow(grown_dy * reach, up) - dt * (inner_dt + tail_dt)
    kept = narrow(
        jnp.broadcast_to(jnp.sum(state * ending, axis=0, keepdims=True), (8, PART)), up
    )[0:1]
    extra = jnp.sum(dt * tail_dt, axis=0, keepdims=True) + jnp.exp(end) * kept
    d_log = exact(jnp.where(row <= column, 1.0, 0.0), d_cum) + extra
    rate = rates[...]
    d_raw = (inner_dt + tail_dt + d_log * rate) * sig(
        scan_in[0, :, CONV_COLS:] + dt_bias[...]
    )
    small_grad[0:1] = small_grad[0:1] + jnp.sum(d_raw, axis=0, keepdims=True)
    small_grad[1:2] = small_grad[1:2] + jnp.sum(d_log * dt * rate, axis=0, keepdims=True)
    small_grad[2:3] = small_grad[2:3] + jnp.sum(narrow(dy * x, up), axis=0, keepdims=True)

    pre, extended = pre_conv(scan_in[0, :, :CONV_COLS], before[0, 0], taps[...], bias[...])
    s = sig(pre)
    d_pre = jnp.concatenate([d_x, d_b, d_c], axis=1) * (s * (1.0 + pre * (1.0 - s)))
    for k in range(4):
        conv_grad[k : k + 1] = conv_grad[k : k + 1] + jnp.sum(
            d_pre * extended[5 + k : 5 + k + SPAN], axis=0, keepdims=True
        )
    conv_grad[4:5] = conv_grad[4:5] + jnp.sum(d_pre, axis=0, keepdims=True)
    following = jnp.concatenate([d_pre, after_pre[...]], axis=0)
    d_in = following[0:SPAN] * taps[3:4]
    for k in range(3):
        d_in = d_in + following[3 - k : 3 - k + SPAN] * taps[k : k + 1]
    scan_grad[0, :, :CONV_COLS] = d_in.astype(bf16)
    scan_grad[0, :, CONV_COLS:] = d_raw.astype(bf16)
    front = d_pre[0:8]
    after_pre[...] = front
    padded = jnp.concatenate([jnp.zeros((8, CONV_COLS), f32), front, jnp.zeros((8, CONV_COLS), f32)], 0)
    edge = padded[0:8] * taps[3:4]
    for k in range(3):
        edge = edge + padded[3 - k : 11 - k] * taps[k : k + 1]
    edge_grad[0] = edge


def one(shape):
    return pl.BlockSpec(shape, lambda b, i: (0,) * len(shape))


def by_span(width, column=0, reverse=None):
    if reverse is None:
        return pl.BlockSpec((1, SPAN, width), lambda b, i: (b, i, column))
    return pl.BlockSpec((1, SPAN, width), lambda b, i: (b, reverse - 1 - i, column))


def by_piece(rows, width, reverse=None):
    if reverse is None:
        return pl.BlockSpec((1, 1, rows, width), lambda b, i: (b, i, 0, 0))
    return pl.BlockSpec((1, 1, rows, width), lambda b, i: (b, reverse - 1 - i, 0, 0))


def by_sequence(rows, width):
    return pl.BlockSpec((1, rows, width), lambda b, i: (b, 0, 0))


def grid_call(kernel, spans, ins, outs, scratch, flops, moved):
    return pl.pallas_call(
        kernel,
        grid=(2, spans),
        in_specs=ins,
        out_specs=[spec for spec, _ in outs],
        out_shape=[shape for _, shape in outs],
        scratch_shapes=scratch,
        compiler_params=pltpu.CompilerParams(
            dimension_semantics=("arbitrary", "arbitrary"), vmem_limit_bytes=50 * 2**20
        ),
        cost_estimate=pl.CostEstimate(flops=flops, bytes_accessed=moved, transcendentals=0),
    )


def like(shape, kind=f32):
    return jax.ShapeDtypeStruct(shape, kind)


def scan_states(scan_in, before, taps, bias, dt_bias, rates, lift):
    length = scan_in.shape[1]
    n = length // SPAN
    return grid_call(
        states_kernel,
        n,
        [
            by_span(SCAN_COLS),
            by_piece(8, CONV_COLS),
            one((4, CONV_COLS)),
            one((1, CONV_COLS)),
            one((1, DT_PAD)),
            one((1, DT_PAD)),
            one((DT_PAD, PART)),
        ],
        [
            (by_span(CONV_COLS), like((2, length, CONV_COLS))),
            (by_span(2 * DT_PAD), like((2, length, 2 * DT_PAD))),
            (by_piece(8, DT_PAD), like((2, n, 8, DT_PAD))),
            (by_piece(STATE, PART), like((2, n, STATE, PART))),
            (by_sequence(STATE, PART), like((2, STATE, PART))),
        ],
        [pltpu.VMEM((STATE, PART), f32), pltpu.VMEM((8, DT_PAD), f32)],
        8 * 10**9,
        30 * 10**6,
    )(scan_in, before, taps, bias, dt_bias, rates, lift)


def scan_values(mixed, steps, starts, prefix, state_in, rest, gate_at, skip, lift):
    length = mixed.shape[1]
    n = length // SPAN
    return grid_call(
        values_kernel,
        n,
        [
            by_span(CONV_COLS),
            by_span(2 * DT_PAD),
            by_piece(8, DT_PAD),
            by_piece(STATE, PART),
            by_sequence(STATE, PART),
            by_span(PART, gate_at),
            one((1, PART)),
            one((DT_PAD, PART)),
        ],
        [
            (by_span(PART), like((2, length, PART))),
            (by_span(PART), like((2, length, PART))),
            (by_span(128), like((2, length, 128))),
        ],
        [],
        12 * 10**9,
        30 * 10**6,
    )(mixed, steps, starts, prefix, state_in, rest, skip, lift)


def gate_backward(gated_grad, values, rest, gate_at, root, mean, gain, mixed, steps, lift):
    length = mixed.shape[1]
    n = length // SPAN
    return grid_call(
        gate_back_kernel,
        n,
        [
            by_span(PART, 0, n),
            by_span(PART, 0, n),
            by_span(PART, gate_at, n),
            by_span(128, 0, n),
            by_span(128, 0, n),
            one((1, PART)),
            by_span(STATE, (PART + STATE) // STATE, n),
            by_span(2 * DT_PAD, 0, n),
            one((DT_PAD, PART)),
        ],
        [
            (by_span(PART, 0, n), like((2, length, PART))),
            (by_span(PART, 0, n), like((2, length, PART), bf16)),
            (one((8, PART)), like((8, PART))),
            (by_piece(STATE, PART, n), like((2, n, STATE, PART))),
            (by_sequence(STATE, PART), like((2, STATE, PART))),
        ],
        [pltpu.VMEM((STATE, PART), f32)],
        8 * 10**9,
        30 * 10**6,
    )(gated_grad, values, rest, root, mean, gain, mixed, steps, lift)


def scan_backward(
    scan_in, before, mixed, steps, starts, prefix, state_in, suffix, state_grad, value_grad,
    skip, taps, bias, dt_bias, rates, lift,
):
    length = mixed.shape[1]
    n = length // SPAN
    return grid_call(
        scan_back_kernel,
        n,
        [
            by_span(SCAN_COLS, 0, n),
            by_piece(8, CONV_COLS, n),
            by_span(CONV_COLS, 0, n),
            by_span(2 * DT_PAD, 0, n),
            by_piece(8, DT_PAD, n),
            by_piece(STATE, PART, n),
            by_sequence(STATE, PART),
            by_piece(STATE, PART, n),
            by_sequence(STATE, PART),
            by_span(PART, 0, n),
            one((1, PART)),
            one((4, CONV_COLS)),
            one((1, CONV_COLS)),
            one((1, DT_PAD)),
            one((1, DT_PAD)),
            one((DT_PAD, PART)),
        ],
        [
            (by_span(SCAN_COLS, 0, n), like((2, length, SCAN_COLS), bf16)),
            (by_sequence(8, CONV_COLS), like((2, 8, CONV_COLS))),
            (one((8, CONV_COLS)), like((8, CONV_COLS))),
            (one((8, DT_PAD)), like((8, DT_PAD))),
        ],
        [
            pltpu.VMEM((8, DT_PAD), f32),
            pltpu.VMEM((8, CONV_COLS), f32),
            pltpu.VMEM((SPAN, SPAN), f32),
        ],
        30 * 10**9,
        50 * 10**6,
    )(
        scan_in, before, mixed, steps, starts, prefix, state_in, suffix, state_grad, value_grad,
        skip, taps, bias, dt_bias, rates, lift,
    )


def attend_kernel(query, key, value, query_place, key_place, attended, log_sum):
    scores = over_lanes(query[0], key[0]) * HEAD_DIM ** (-0.5)
    seen = (key_place[0:1] >= 0) & (query_place[:, 0:1] >= key_place[0:1])
    scores = jnp.where(seen, scores, -1e30)
    peak = jnp.max(scores, axis=1, keepdims=True)
    unscaled = jnp.exp(scores - peak)
    whole = jnp.sum(unscaled, axis=1, keepdims=True)
    probs = (unscaled * (1.0 / whole)).astype(bf16)
    attended[0] = low_dot(probs, value[0])
    log_sum[0] = jnp.broadcast_to(peak + jnp.log(whole), log_sum.shape[1:])


def attend_back_kernel(
    query, key, value, grad, attended, log_sum, query_place, key_place, query_grad, kv_grad
):
    @pl.when((pl.program_id(1) == 0) & (pl.program_id(2) == 0))
    def _():
        kv_grad[...] = jnp.zeros_like(kv_grad)

    scale = HEAD_DIM ** (-0.5)
    scores = over_lanes(query[0], key[0]) * scale
    seen = (key_place[0:1] >= 0) & (query_place[:, 0:1] >= key_place[0:1])
    probs = jnp.exp(jnp.where(seen, scores, -1e30) - log_sum[0, :, 0:1])
    delta = jnp.sum(grad[0].astype(f32) * attended[0], axis=1, keepdims=True)
    score_grad = (probs * (over_lanes(grad[0], value[0]) - delta)).astype(bf16)
    query_grad[0] = low_dot(score_grad, key[0]) * scale
    kv_grad[0, 0] = kv_grad[0, 0] + over_rows(score_grad, query[0]) * scale
    kv_grad[1, 0] = kv_grad[1, 0] + over_rows(probs.astype(bf16), grad[0])


def attend_specs(block, keys):
    by_query = pl.BlockSpec((1, block, HEAD_DIM), lambda b, h, i: (b, i, h))
    whole_key = pl.BlockSpec((1, keys, HEAD_DIM), lambda b, h, i: (b, 0, 0))
    place = pl.BlockSpec((block, 128), lambda b, h, i: (i, 0))
    key_at = pl.BlockSpec((8, keys), lambda b, h, i: (0, 0))
    return (by_query, whole_key, place, key_at)


def attend(query, key, value, query_place, key_place):
    length, keys = query.shape[1], key.shape[1]
    block = 256 if keys <= 4096 else 128
    by_query, whole_key, place, key_at = attend_specs(block, keys)
    return pl.pallas_call(
        attend_kernel,
        grid=(2, 2, length // block),
        in_specs=[by_query, whole_key, whole_key, place, key_at],
        out_specs=[by_query, by_query],
        out_shape=[like((2, length, QP)), like((2, length, QP))],
        compiler_params=pltpu.CompilerParams(
            dimension_semantics=("arbitrary",) * 3, vmem_limit_bytes=50 * 2**20
        ),
        cost_estimate=pl.CostEstimate(
            flops=12 * 10**9, bytes_accessed=20 * 10**6, transcendentals=0
        ),
    )(query, key, value, query_place, key_place)


def attend_backward(query, key, value, grad, attended, log_sum, query_place, key_place):
    length, keys = query.shape[1], key.shape[1]
    block = 256 if keys <= 4096 else 128
    by_query, whole_key, place, key_at = attend_specs(block, keys)
    return pl.pallas_call(
        attend_back_kernel,
        grid=(2, 2, length // block),
        in_specs=[by_query, whole_key, whole_key, by_query, by_query, by_query, place, key_at],
        out_specs=[
            by_query,
            pl.BlockSpec((2, 1, keys, HEAD_DIM), lambda b, h, i: (0, b, 0, 0)),
        ],
        out_shape=[like((2, length, QP)), like((2, 2, keys, HEAD_DIM))],
        compiler_params=pltpu.CompilerParams(
            dimension_semantics=("arbitrary",) * 3, vmem_limit_bytes=50 * 2**20
        ),
        cost_estimate=pl.CostEstimate(
            flops=20 * 10**9, bytes_accessed=30 * 10**6, transcendentals=0
        ),
    )(query, key, value, grad, attended, log_sum, query_place, key_place)


def swish_product(gate_proj, up_proj):
    return jax.nn.silu(gate_proj) * up_proj


def gather_tokens(block):
    across = swap(block, "x")
    return (block, swap(block, "c"), across, swap(across, "c"))


def scatter_tokens(blocks):
    near, far = blocks[0], blocks[2]
    sent = swap(jnp.stack([blocks[1].astype(bf16), blocks[3].astype(bf16)]), "c")
    near = near + sent[0].astype(f32)
    far = far + sent[1].astype(f32)
    return near + swap(far.astype(bf16), "x").astype(f32)


def body(
    inputs,
    out_grad,
    norm_gain,
    w_in,
    conv_weight,
    conv_bias,
    dt_bias,
    a_log,
    skip_gain,
    gated_gain,
    w_out,
    w_q,
    w_k,
    w_v,
    w_o,
    mid_gain,
    w_gate,
    w_up,
    w_down,
):
    nz, ny = lax.axis_size("z"), lax.axis_size("y")
    zi, xi, ci = (lax.axis_index(name) for name in ("z", "x", "c"))
    length = inputs.shape[1]
    span_all = 2 * length
    rows = w_in.shape[0]
    ff_rows = w_down.shape[0]
    hidden_part = nz * ny * ff_rows
    edge_count = conv_weight.shape[0] - 1
    out_rows, o_rows = w_out.shape[0], w_o.shape[0]
    aligned = ny == 2 and nz == 4 and MAMBA_HEADS % (4 * nz) == 0
    g = nz if aligned else 1
    hp = HEADS // g

    def heads_mine(array, width):
        lead = array.shape[:-1]
        array = array.reshape(lead + (g, 2, 2, hp * width))
        array = lax.dynamic_index_in_dim(array, xi, len(lead) + 1, keepdims=False)
        array = lax.dynamic_index_in_dim(array, ci, len(lead) + 1, keepdims=False)
        return array.reshape(lead + (HEADS * width,))

    def heads_spread(array, width):
        lead = array.shape[:-1]
        array = array.reshape(lead + (g, 1, 1, hp * width))
        whole = jnp.zeros(lead + (g, 2, 2, hp * width), array.dtype)
        start = (0,) * len(lead) + (0, xi, ci, 0)
        return lax.dynamic_update_slice(whole, array, start).reshape(
            lead + (MAMBA_HEADS * width,)
        )

    def heads_split(array, width):
        n = array.shape[0]
        array = array.reshape(n, g, 2, 2, hp * width)
        return jnp.transpose(array, (2, 3, 0, 1, 4)).reshape(4, n, HEADS * width)

    def heads_join(array, width):
        n = array.shape[1]
        array = array.reshape(2, 2, n, g, hp * width)
        return jnp.transpose(array, (2, 3, 0, 1, 4)).reshape(n, MAMBA_HEADS * width)

    def reordered(array, first, second):
        width = 2 * rows
        return jnp.concatenate(
            [
                array[..., at * width : (at + 1) * width]
                for z in range(nz)
                for at in (
                    (z * first + i) * second + j for j in range(second) for i in range(first)
                )
            ],
            axis=-1,
        )

    def permuted(array):
        return reordered(array, 2, ny)

    def restored(array):
        return reordered(array, ny, 2)

    def to_ranks(array):
        return lax.all_to_all(array, GROUP, 0, 0, tiled=True)

    def in_order(own, other):
        return lax.dynamic_slice_in_dim(
            jnp.concatenate([own, other, own], 0), xi * length, span_all, 0
        )

    def gather_sequences(block):
        own, near, across, far = gather_tokens(block)
        return jnp.stack([in_order(own, across), in_order(near, far)])

    def scatter_sequences(partial):
        mine = partial[0] + swap(partial[1].astype(bf16), "c").astype(f32)
        mine = mine.reshape(2, length, mine.shape[-1])
        own = lax.dynamic_index_in_dim(mine, xi, 0, keepdims=False)
        other = lax.dynamic_index_in_dim(mine, 1 - xi, 0, keepdims=False)
        return own + swap(other.astype(bf16), "x").astype(f32)

    split_q = jnp.transpose(w_q.reshape(rows, 2, 2, 2, HEAD_DIM), (3, 1, 0, 2, 4))
    split_k = jnp.transpose(w_k.reshape(rows, 2, HEAD_DIM), (1, 0, 2))
    split_v = jnp.transpose(w_v.reshape(rows, 2, HEAD_DIM), (1, 0, 2))
    two = lambda a: jnp.broadcast_to(a[None], (2,) + a.shape).reshape(4, rows, a.shape[-1])
    packed_scan = jnp.concatenate(
        [
            heads_split(w_in[:, INNER : 2 * INNER], MAMBA_HEAD),
            jnp.broadcast_to(w_in[None, :, 2 * INNER : 2 * INNER + BC], (4, rows, BC)),
            jnp.pad(
                heads_split(w_in[:, 2 * INNER + BC :], 1), ((0, 0), (0, 0), (0, DT_PAD - HEADS))
            ),
        ],
        axis=2,
    )
    packed_rest = jnp.concatenate(
        [
            heads_split(w_in[:, :INNER], MAMBA_HEAD),
            split_q.reshape(4, rows, QP),
            two(split_k),
            two(split_v),
        ],
        axis=2,
    )

    def gathered(array):
        return lax.all_gather(array, SHARDS, axis=0, tiled=True)

    def after(array, *others):
        return lax.optimization_barrier((array,) + others)[0]

    def split_ff(w):
        w = w.reshape(rows, nz, 2, ny, 2, ff_rows)
        return jnp.transpose(w, (2, 4, 0, 1, 3, 5)).reshape(4, rows, hidden_part)

    def join_ff(w):
        w = w.reshape(2, 2, rows, nz, ny, ff_rows)
        return jnp.transpose(w, (2, 3, 0, 4, 1, 5)).reshape(rows, 4 * hidden_part)

    full_scan = gathered(to_ranks(packed_scan).reshape(4 * rows, SCAN_COLS))

    tokens = 2 * span_all
    resident = inputs[0].astype(f32)
    normed, norm_back = jax.vjp(rms_scale, resident, norm_gain)
    normed16 = gather_sequences(permuted(normed.astype(bf16)))
    edges16 = shifted(normed16[:, span_all - 8 :], 1).reshape(16, D)
    normed_rows = normed16.reshape(tokens, D)

    rest_mine = to_ranks(packed_rest).reshape(4 * rows, REST_COLS)
    if aligned:
        turn = [(2 * y + c, 2 * c + y) for y in range(2) for c in range(2)]
        place = []
        for z in range(4):
            for y in range(2):
                for c in range(2):
                    place.append(((z * 2 + y) * 2 + c, ((z % 2 * 2 + y) * 2 + c) * 2 + z // 2))
        back_place = [(b, a) for a, b in place]
        sent_out = lax.ppermute(w_out, ("y", "c"), turn)
        sent_o = lax.ppermute(w_o, ("z", "y", "c"), place)
        sent_rows = jnp.concatenate([sent_out, sent_o], 0).reshape(2 * rows, 2, HALF)
        second = jnp.concatenate(
            [rest_mine, jnp.swapaxes(sent_rows, 0, 1).reshape(4 * rows, HALF)], axis=1
        )
        whole_second = gathered(after(second, normed_rows, edges16))
        full_rest = whole_second[:, :REST_COLS]
        full_rows = jnp.swapaxes(
            whole_second[:, REST_COLS:].reshape(nz * ny, 2, 2 * rows, HALF), 1, 2
        ).reshape(nz * ny, 2 * rows, D)
        full_out = full_rows[:, :out_rows].reshape(PART, D)
        full_o = full_rows[:, out_rows:].reshape(QP, D)
    else:
        full_rest = gathered(after(rest_mine, normed_rows, edges16))
        every_out = lax.all_gather(w_out, EVERY, axis=0, tiled=True)
        every_o = lax.all_gather(w_o, EVERY, axis=0, tiled=True)
        full_out = lax.dynamic_slice_in_dim(every_out, (2 * xi + ci) * PART, PART, 0)
        every_o = every_o.reshape(2, 2, 2, HEAD_DIM, D)
        every_o = lax.dynamic_index_in_dim(every_o, xi, 2, keepdims=False)
        full_o = lax.dynamic_index_in_dim(every_o, ci, 0, keepdims=False).reshape(QP, D)

    scan_in = low_dot(normed_rows, full_scan).reshape(2, span_all, SCAN_COLS)
    edge_rows = low_dot(edges16, full_scan).reshape(2, 1, 8, SCAN_COLS)
    n = span_all // SPAN
    before = jnp.concatenate(
        [edge_rows, scan_in.reshape(2, n, SPAN, SCAN_COLS)[:, : n - 1, SPAN - 8 :]], axis=1
    )[..., :CONV_COLS]

    def rank_channels(array):
        return jnp.concatenate(
            [heads_mine(array[..., :INNER], MAMBA_HEAD), array[..., INNER:]], axis=-1
        )

    def per_head(array):
        return jnp.pad(heads_mine(array, 1), (0, DT_PAD - HEADS))[None]

    taps, bias = rank_channels(conv_weight), rank_channels(conv_bias)[None]
    dt_b, rates = per_head(dt_bias), per_head(-jnp.exp(a_log))
    skip = jnp.repeat(heads_mine(skip_gain, 1), MAMBA_HEAD)[None]
    gain = heads_mine(gated_gain, MAMBA_HEAD)[None]
    lift = (
        jnp.arange(DT_PAD, dtype=jnp.int32)[:, None]
        == jnp.arange(PART, dtype=jnp.int32)[None] // MAMBA_HEAD
    ).astype(f32)
    mixed, steps, starts, prefix, own_state = scan_states(
        scan_in, before, taps, bias, dt_b, rates, lift
    )
    log_decay = starts[:, n - 1, 0] + steps[:, span_all - 1, DT_PAD:]
    own_decay = jnp.repeat(jnp.exp(log_decay[:, :HEADS]), MAMBA_HEAD, axis=-1)

    def chained(local, step):
        entering = []
        for s in range(2):
            held = jnp.zeros(local.shape[1:], f32)
            for hop in range(nz - 1):
                at = hop if step == 1 else nz - 1 - hop
                leaving = local[s] + own_decay[s][None] * held if hop else local[s]
                held = held + lax.ppermute(
                    leaving.astype(bf16), "z", [(at, at + step)]
                ).astype(f32)
            entering.append(held)
        return jnp.stack(entering)

    state_in = chained(own_state, 1)
    packed_ff = jnp.concatenate([split_ff(w_gate), split_ff(w_up)], axis=2)
    rest = low_dot(normed_rows, full_rest).reshape(2, span_all, REST_COLS)

    positions = zi * span_all + jnp.arange(span_all, dtype=jnp.int32)
    cosine, sine = rope_tables(positions)
    query16 = (
        rotate(rest[..., AT_Q:AT_K].reshape(2, span_all, 2, HEAD_DIM), cosine, sine)
        .astype(bf16)
        .reshape(2, span_all, QP)
    )
    key16 = rotate(rest[..., None, AT_K:AT_V], cosine, sine).astype(bf16)[:, :, 0]
    kv16 = jnp.stack([key16, rest[..., AT_V:].astype(bf16)])
    kv_all = jnp.concatenate([shifted(kv16, d) for d in range(nz - 1, 0, -1)] + [kv16], axis=2)
    keys_at = (zi - nz + 1) * span_all + jnp.arange(nz * span_all, dtype=jnp.int32)
    query_place = jnp.broadcast_to(positions[:, None], (span_all, 128))
    key_place = jnp.broadcast_to(keys_at[None], (8, nz * span_all))
    attended, log_sum = attend(query16, kv_all[0], kv_all[1], query_place, key_place)
    attended16 = attended.reshape(tokens, QP).astype(bf16)

    values, flat, square = scan_values(
        mixed, steps, starts, prefix, state_in, rest, 0, skip, lift
    )
    root = lax.rsqrt(group_total(square[..., :1]) / INNER + epsilon)
    gated16 = (flat * root * gain).astype(bf16).reshape(tokens, PART)
    third = jnp.concatenate(
        [to_ranks(packed_ff).reshape(4 * rows, 2 * hidden_part), w_down], axis=0
    )
    whole_third = gathered(after(third, flat, attended)).reshape(nz * ny, 4 * rows + ff_rows, D)
    full_ff = whole_third[:, : 4 * rows].reshape(D, 2 * hidden_part)
    full_down = whole_third[:, 4 * rows :].reshape(hidden_part, D)
    mixture = low_dot(gated16, full_out) + low_dot(attended16, full_o)
    hidden_state = resident + scatter_sequences(mixture.reshape(2, span_all, D))

    middle, mid_back = jax.vjp(rms_scale, hidden_state, mid_gain)
    middle16 = jnp.concatenate(gather_tokens(permuted(middle.astype(bf16))), 0)
    cotangent16 = jnp.concatenate(gather_tokens(out_grad[0]), 0)
    both = low_dot(middle16, full_ff)
    activated, swish_back = jax.vjp(
        swish_product, both[:, :hidden_part], both[:, hidden_part:]
    )
    activated16 = activated.astype(bf16)
    down = low_dot(activated16, full_down).reshape(4, length, D)
    output = (hidden_state + scatter_tokens(down)).astype(bf16)
    gate_grad, up_grad = swish_back(back_dot(cotangent16, full_down))
    both16 = jnp.concatenate([gate_grad, up_grad], axis=1).astype(bf16)
    mid_grad = restored(scatter_tokens(back_dot(both16, full_ff).reshape(4, length, D)))
    hidden_piece, mid_gain_grad = mid_back(mid_grad)
    hidden_grad = out_grad[0].astype(f32) + hidden_piece

    def to_owners(array):
        return lax.psum_scatter(array.astype(bf16), SHARDS, scatter_dimension=0, tiled=True)

    down_owned = to_owners(weight_grad(activated16, cotangent16))
    result_down = down_owned.astype(f32)
    ff_owned = to_owners(after(weight_grad(middle16, both16).astype(bf16), down_owned))
    ff_parts = to_ranks(ff_owned.reshape(4, rows, 2 * hidden_part))
    result_gate = join_ff(ff_parts[..., :hidden_part]).astype(f32)
    result_up = join_ff(ff_parts[..., hidden_part:]).astype(f32)

    mix16 = gather_sequences(hidden_grad.astype(bf16)).reshape(tokens, D)
    attended_grad16 = back_dot(mix16, full_o).astype(bf16).reshape(2, span_all, QP)
    gated_grad = back_dot(mix16, full_out).reshape(2, span_all, PART)
    grad_out_w = weight_grad(gated16, mix16).astype(bf16)
    grad_o = weight_grad(attended16, mix16).astype(bf16)

    inner = jnp.sum(gated_grad * gain * flat, axis=-1, keepdims=True) * root
    inner_mean = group_total(inner) / INNER
    wide = (2, span_all, 128)
    value_grad, gate_z_grad, gain_grad, suffix, first_grad = gate_backward(
        gated_grad,
        values,
        rest,
        0,
        jnp.broadcast_to(root, wide),
        jnp.broadcast_to(inner_mean, wide),
        gain,
        mixed,
        steps,
        lift,
    )
    state_grad = chained(first_grad, -1)

    query_grad, kv_grads = attend_backward(
        query16,
        kv_all[0],
        kv_all[1],
        attended_grad16,
        attended,
        log_sum,
        query_place,
        key_place,
    )
    kv_grads = kv_grads.reshape(2, 2, nz, span_all, HEAD_DIM)
    kv_grad = kv_grads[:, :, nz - 1]
    for d in range(1, nz):
        kv_grad = kv_grad + shifted(kv_grads[:, :, nz - 1 - d].astype(bf16), -d).astype(f32)
    query_back = rotate(
        query_grad.reshape(2, span_all, 2, HEAD_DIM), cosine, -sine
    ).reshape(2, span_all, QP)
    key_back = rotate(kv_grad[0][:, :, None], cosine, -sine)[:, :, 0]
    rest_grad16 = jnp.concatenate(
        [
            gate_z_grad,
            query_back.astype(bf16),
            key_back.astype(bf16),
            kv_grad[1].astype(bf16),
        ],
        axis=-1,
    ).reshape(tokens, REST_COLS)

    scan_grad16, edge_grad, conv_grad, small_grad = scan_backward(
        scan_in,
        before,
        mixed,
        steps,
        starts,
        prefix,
        state_in,
        suffix,
        state_grad,
        after(value_grad, down_owned),
        skip,
        taps,
        bias,
        dt_b,
        rates,
        lift,
    )
    edge_back = shifted(edge_grad[:, 8 - edge_count :].astype(bf16), -1).astype(f32)
    last_rows = scan_grad16[:, span_all - edge_count :, :CONV_COLS].astype(f32) + edge_back
    scan_grad16 = lax.dynamic_update_slice(
        scan_grad16, last_rows.astype(bf16), (0, span_all - edge_count, 0)
    ).reshape(tokens, SCAN_COLS)
    grads = [
        weight_grad(normed_rows, scan_grad16).astype(bf16),
        weight_grad(normed_rows, rest_grad16).astype(bf16),
    ]
    if aligned:
        rows_grad = jnp.concatenate(
            [grad_out_w.reshape(nz * ny, out_rows, D), grad_o.reshape(nz * ny, o_rows, D)], axis=1
        ).reshape(nz * ny, 2 * rows, 2, HALF)
        grads.append(jnp.swapaxes(rows_grad, 1, 2).reshape(D, HALF))
    mix_owned = to_owners(after(jnp.concatenate(grads, axis=1), ff_owned))
    scan_parts = to_ranks(mix_owned[:, :SCAN_COLS].reshape(4, rows, SCAN_COLS)).astype(f32)
    rest_parts = to_ranks(
        mix_owned[:, SCAN_COLS : SCAN_COLS + REST_COLS].reshape(4, rows, REST_COLS)
    ).astype(f32)
    if aligned:
        rows_parts = jnp.swapaxes(
            mix_owned[:, SCAN_COLS + REST_COLS :].reshape(2, 2 * rows, HALF), 0, 1
        ).reshape(2 * rows, D)
        result_out = lax.ppermute(rows_parts[:out_rows], ("y", "c"), turn).astype(f32)
        result_o = lax.ppermute(rows_parts[out_rows:], ("z", "y", "c"), back_place).astype(f32)
    else:
        every_out = lax.dynamic_update_slice_in_dim(
            jnp.zeros((INNER, D), bf16), grad_out_w, (2 * xi + ci) * PART, 0
        )
        every_o = lax.dynamic_update_slice(
            jnp.zeros((2, 2, 2, HEAD_DIM, D), bf16),
            grad_o.reshape(1, 2, 1, HEAD_DIM, D),
            (ci, 0, xi, 0, 0),
        ).reshape(ATT_HEADS * HEAD_DIM, D)
        result_out = lax.psum_scatter(every_out, EVERY, scatter_dimension=0, tiled=True)
        result_o = lax.psum_scatter(every_o, EVERY, scatter_dimension=0, tiled=True)
        result_out, result_o = result_out.astype(f32), result_o.astype(f32)

    normed_grad = back_dot(scan_grad16, full_scan) + back_dot(rest_grad16, full_rest)
    normed_grad = restored(scatter_sequences(normed_grad.reshape(2, span_all, D)))
    resident_grad, norm_gain_grad = norm_back(normed_grad)
    input_grad = hidden_grad + resident_grad

    result_in = jnp.concatenate(
        [
            heads_join(rest_parts[..., :PART], MAMBA_HEAD),
            heads_join(scan_parts[..., :PART], MAMBA_HEAD),
            jnp.sum(scan_parts[..., PART:CONV_COLS], axis=0),
            heads_join(scan_parts[..., CONV_COLS : CONV_COLS + HEADS], 1),
        ],
        axis=1,
    )
    result_q = jnp.transpose(
        rest_parts[..., AT_Q:AT_K].reshape(2, 2, rows, 2, HEAD_DIM), (2, 1, 3, 0, 4)
    ).reshape(rows, ATT_HEADS * HEAD_DIM)
    kv_parts = jnp.sum(rest_parts[..., AT_K:].reshape(2, 2, rows, 2, HEAD_DIM), axis=0)
    result_k = jnp.transpose(kv_parts[:, :, 0], (1, 0, 2)).reshape(rows, KV_HEADS * HEAD_DIM)
    result_v = jnp.transpose(kv_parts[:, :, 1], (1, 0, 2)).reshape(rows, KV_HEADS * HEAD_DIM)

    def all_channels(array):
        return jnp.concatenate(
            [heads_spread(array[..., :PART], MAMBA_HEAD), array[..., PART:]], axis=-1
        )

    small = [
        norm_gain_grad,
        all_channels(conv_grad[:4]),
        all_channels(conv_grad[4]),
        heads_spread(small_grad[0, :HEADS], 1),
        heads_spread(small_grad[1, :HEADS], 1),
        heads_spread(small_grad[2, :HEADS], 1),
        heads_spread(gain_grad[0], MAMBA_HEAD),
        mid_gain_grad,
    ]
    summed = total(jnp.concatenate([v.reshape(-1) for v in small]))
    parts, at = [], 0
    for v in small:
        parts.append(summed[at : at + v.size].reshape(v.shape))
        at += v.size
    return (
        output[None],
        input_grad[None],
        parts[0],
        result_in,
        parts[1],
        parts[2],
        parts[3],
        parts[4],
        parts[5],
        parts[6],
        result_out,
        result_q,
        result_k,
        result_v,
        result_o,
        parts[7],
        result_gate,
        result_up,
        result_down,
    )


def solution(mesh):
    seq, fsdp = mesh.shape["seq"], mesh.shape["fsdp"]
    split = Mesh(mesh.devices.reshape(seq // 2, 2, fsdp // 2, 2), EVERY)
    tokens = P(("y", "c"), ("z", "x"), None)
    matrix = P(EVERY, None)
    return jax.shard_map(
        body,
        mesh=split,
        in_specs=(tokens, tokens, P(), matrix)
        + (P(),) * 6
        + (matrix,) * 5
        + (P(),)
        + (matrix,) * 3,
        out_specs=(tokens, tokens, P(), matrix)
        + (P(),) * 6
        + (matrix,) * 5
        + (P(),)
        + (matrix,) * 3,
        check_vma=False,
    )
```

```python
import jax
import jax.numpy as jnp
from jax import lax
from jax.experimental import pallas as pl
from jax.experimental.pallas import tpu as pltpu
from jax.sharding import Mesh
from jax.sharding import PartitionSpec as P

D = 2048
MAMBA_HEADS = 48
MAMBA_HEAD = 64
STATE = 256
ATT_HEADS = 8
KV_HEADS = 2
HEAD_DIM = 128
SPAN = 128
INNER = 3072

HEADS = MAMBA_HEADS // 4
PART = HEADS * MAMBA_HEAD
BC = 2 * STATE
DT_PAD = 128
QP = 2 * HEAD_DIM
CONV_COLS = PART + BC
SCAN_COLS = CONV_COLS + DT_PAD
AT_Q = PART
AT_K = AT_Q + QP
AT_V = AT_K + HEAD_DIM
REST_COLS = AT_V + HEAD_DIM

epsilon = 1e-05
rope_base = 100000000000.0
GROUP = ("x", "c")
SHARDS = ("z", "y")
EVERY = ("z", "x", "y", "c")
bf16 = jnp.bfloat16
f32 = jnp.float32


def swap(array, axis):
    return lax.ppermute(array, axis, [(0, 1), (1, 0)])


def shifted(array, distance):
    devices = range(lax.axis_size("z"))
    return lax.ppermute(array, "z", [(i - distance, i) for i in devices if i - distance in devices])


def total(array):
    for axis in EVERY:
        size = lax.axis_size(axis)
        bit = 1
        while bit < size:
            array = array + lax.ppermute(array, axis, [(i, i ^ bit) for i in range(size)])
            bit *= 2
    return array


def group_total(array):
    array = array + swap(array[::-1], "c")
    return array + swap(array, "x")


def low_dot(left, right):
    return jnp.dot(left, right, preferred_element_type=f32)


def back_dot(grad_rows, weight):
    return lax.dot_general(grad_rows, weight, (((1,), (1,)), ((), ())), preferred_element_type=f32)


def weight_grad(left, right):
    return lax.dot_general(left, right, (((0,), (0,)), ((), ())), preferred_element_type=f32)


def rms_scale(values, gain):
    return values * lax.rsqrt(jnp.mean(values * values, axis=-1, keepdims=True) + epsilon) * gain


def rope_tables(positions):
    half_dim = HEAD_DIM // 2
    frequencies = rope_base ** (-jnp.arange(half_dim, dtype=f32) / half_dim)
    angles = positions.astype(f32)[:, None] * frequencies[None, :]
    return (jnp.cos(angles), jnp.sin(angles))


def rotate(values, cosine, sine):
    half_dim = HEAD_DIM // 2
    cosine, sine = cosine[:, None, :], sine[:, None, :]
    first, second = values[..., :half_dim], values[..., half_dim:]
    return jnp.concatenate([first * cosine - second * sine, second * cosine + first * sine], axis=-1)


def pieces(values, count):
    parts = []
    for _ in range(count):
        part = values.astype(bf16)
        parts.append(part)
        values = values - part.astype(f32)
    return parts


def running(mask, values):
    mask16 = mask.astype(bf16)
    return sum(low_dot(mask16, part) for part in pieces(values, 3))


def over_lanes(left, right):
    return lax.dot_general(left, right, (((1,), (1,)), ((), ())), preferred_element_type=f32)


def over_rows(left, right):
    return lax.dot_general(left, right, (((0,), (0,)), ((), ())), preferred_element_type=f32)


def widen(values, lift):
    return sum(low_dot(part, lift) for part in pieces(values, 2))


def narrow(values, lift):
    return sum(over_lanes(part, lift) for part in pieces(values, 2))


def sig(values):
    return 1.0 / (1.0 + jnp.exp(-values))


def soft(values):
    return jnp.maximum(values, 0.0) + jnp.log1p(jnp.exp(-jnp.abs(values)))


def square_places():
    return (
        lax.broadcasted_iota(jnp.int32, (SPAN, SPAN), 0),
        lax.broadcasted_iota(jnp.int32, (SPAN, SPAN), 1),
    )


def pre_conv(current, before, taps, bias):
    extended = jnp.concatenate([before, current], axis=0)
    pre = bias + extended[5 : 5 + SPAN] * taps[0:1]
    for k in range(1, 4):
        pre = pre + extended[5 + k : 5 + k + SPAN] * taps[k : k + 1]
    return (pre, extended)


def states_kernel(
    scan_in, before, taps, bias, dt_bias, rates, lift, mixed, steps, starts, prefix, last, held, sofar
):
    @pl.when(pl.program_id(1) == 0)
    def _():
        held[...] = jnp.zeros_like(held)
        sofar[...] = jnp.zeros_like(sofar)

    pre, _ = pre_conv(scan_in[0, :, :CONV_COLS], before[0, 0], taps[...], bias[...])
    mix = pre * sig(pre)
    mixed[0] = mix
    dt = soft(scan_in[0, :, CONV_COLS:] + dt_bias[...])
    row, column = square_places()
    cum = running(jnp.where(row >= column, 1.0, 0.0), dt * rates[...])
    steps[0, :, :DT_PAD] = dt
    steps[0, :, DT_PAD:] = cum
    starts[0, 0] = sofar[...]
    prefix[0, 0] = held[...]
    end = cum[SPAN - 1 : SPAN]
    tail = jnp.exp(end - cum) * dt
    fed = (mix[:, :PART] * widen(tail, lift[...])).astype(bf16)
    added = over_rows(mix[:, PART : PART + STATE].astype(bf16), fed)
    whole = widen(jnp.broadcast_to(jnp.exp(end), (8, DT_PAD)), lift[...])[0:1]
    held[...] = whole * held[...] + added
    sofar[...] = sofar[...] + end
    last[0] = held[...]


def values_kernel(
    mixed, steps, starts, prefix, state_in, gate, skip, lift, values, flat, square
):
    x = mixed[0, :, :PART]
    b16 = mixed[0, :, PART : PART + STATE].astype(bf16)
    c16 = mixed[0, :, PART + STATE :].astype(bf16)
    dt = steps[0, :, :DT_PAD]
    cum = steps[0, :, DT_PAD:]
    dt_t, cum_t = dt.T, cum.T
    state = prefix[0, 0] + widen(jnp.exp(starts[0, 0]), lift[...])[0:1] * state_in[0]
    meet = over_lanes(c16, b16)
    carried = low_dot(c16, state.astype(bf16)) * widen(jnp.exp(cum), lift[...])
    row, column = square_places()
    first = column < MAMBA_HEAD
    inside = []
    for k in range(HEADS // 2):
        pair = x[:, 2 * MAMBA_HEAD * k : 2 * MAMBA_HEAD * (k + 1)]
        weights = []
        for h in (2 * k, 2 * k + 1):
            spread = cum[:, h : h + 1] - cum_t[h : h + 1, :]
            decay = jnp.exp(jnp.where(row >= column, spread, -1e30))
            weights.append((meet * decay * dt_t[h : h + 1, :]).astype(bf16))
        split = [
            jnp.where(first, pair, 0.0).astype(bf16),
            jnp.where(first, 0.0, pair).astype(bf16),
        ]
        inside.append(low_dot(jnp.concatenate(weights, 1), jnp.concatenate(split, 0)))
    value = jnp.concatenate(inside, 1) + carried + skip[...] * x
    values[0] = value
    z = gate[0]
    product = value * (z * sig(z))
    flat[0] = product
    square[0] = jnp.broadcast_to(
        jnp.sum(product * product, axis=1, keepdims=True), (SPAN, 128)
    )


def gate_back_kernel(
    gated_grad, values, gate, root, mean, gain, c_part, steps, lift,
    value_grad, gate_grad, gain_grad, suffix, first_grad, held,
):
    @pl.when(pl.program_id(1) == 0)
    def _():
        held[...] = jnp.zeros_like(held)

    @pl.when((pl.program_id(0) == 0) & (pl.program_id(1) == 0))
    def _():
        gain_grad[...] = jnp.zeros_like(gain_grad)

    z, value, grad = gate[0], values[0], gated_grad[0]
    s = sig(z)
    silu = z * s
    scale = root[0, :, 0:1]
    normal = value * silu * scale
    flat_grad = scale * (grad * gain[...] - normal * mean[0, :, 0:1])
    d_value = flat_grad * silu
    value_grad[0] = d_value
    gate_grad[0] = (flat_grad * value * (s * (1.0 + z * (1.0 - s)))).astype(bf16)
    gain_grad[0:1] = gain_grad[0:1] + jnp.sum(grad * normal, axis=0, keepdims=True)
    grown = widen(jnp.exp(steps[0, :, DT_PAD:]), lift[...])
    suffix[0, 0] = held[...]
    held[...] = grown[SPAN - 1 : SPAN] * held[...] + over_rows(
        c_part[0].astype(bf16), (grown * d_value).astype(bf16)
    )
    first_grad[0] = held[...]


def scan_back_kernel(
    mixed, steps, starts, prefix, state_in, suffix, value_grad, skip, lift,
    mixed_grad, step_grad, skip_grad, columns,
):
    @pl.when((pl.program_id(0) == 0) & (pl.program_id(1) == 0))
    def _():
        skip_grad[...] = jnp.zeros_like(skip_grad)
        columns[...] = jnp.zeros_like(columns)

    up = lift[...]
    x = mixed[0, :, :PART]
    b16 = mixed[0, :, PART : PART + STATE].astype(bf16)
    c16 = mixed[0, :, PART + STATE :].astype(bf16)
    dt = steps[0, :, :DT_PAD]
    cum = steps[0, :, DT_PAD:]
    dt_t, cum_t = dt.T, cum.T
    end = cum[SPAN - 1 : SPAN]
    dy = value_grad[0]
    state = prefix[0, 0] + widen(jnp.exp(starts[0, 0]), up)[0:1] * state_in[0]
    ending = suffix[0, 0]
    state16, ending16 = state.astype(bf16), ending.astype(bf16)
    grown_dy = widen(jnp.exp(cum), up) * dy
    tail_wide = widen(jnp.exp(end - cum), up)
    dt_wide = widen(dt, up)
    reach = low_dot(c16, state16)
    pull = tail_wide * low_dot(b16, ending16)
    d_c = over_lanes(grown_dy.astype(bf16), state16)
    d_b = over_lanes((tail_wide * dt_wide * x).astype(bf16), ending16)
    meet = over_lanes(c16, b16)
    row, column = square_places()
    first = column < MAMBA_HEAD
    d_meet = jnp.zeros((SPAN, SPAN), f32)
    rows_sum = jnp.zeros((SPAN, DT_PAD), f32)
    back = []
    for k in range(HEADS // 2):
        at = slice(2 * MAMBA_HEAD * k, 2 * MAMBA_HEAD * (k + 1))
        x16, dy_pair = x[:, at].astype(bf16), dy[:, at]
        split = [
            jnp.where(first, dy_pair, 0.0).astype(bf16),
            jnp.where(first, 0.0, dy_pair).astype(bf16),
        ]
        weights = []
        for j in range(2):
            h = 2 * k + j
            spread = cum[:, h : h + 1] - cum_t[h : h + 1, :]
            decay = jnp.exp(jnp.where(row >= column, spread, -1e30))
            d_weight = over_lanes(split[j], x16) * decay
            scaled = d_weight * dt_t[h : h + 1, :]
            d_meet = d_meet + scaled
            rows_sum = rows_sum + jnp.where(
                column == h, jnp.sum(scaled * meet, axis=1, keepdims=True), 0.0
            )
            columns[h : h + 1, :] = jnp.sum(d_weight * meet, axis=0, keepdims=True)
            weights.append((meet * decay).astype(bf16))
        back.append(over_rows(jnp.concatenate(weights, 0), jnp.concatenate(split, 0)))
    d_meet16 = d_meet.astype(bf16)
    mixed_grad[0, :, :PART] = dt_wide * (jnp.concatenate(back, 1) + pull) + skip[...] * dy
    mixed_grad[0, :, PART : PART + STATE] = d_b + over_rows(d_meet16, c16)
    mixed_grad[0, :, PART + STATE :] = d_c + low_dot(d_meet16, b16)
    tail_dt = narrow(x * pull, up)
    inner_dt = columns[...].T
    d_cum = rows_sum + narrow(grown_dy * reach, up) - dt * (inner_dt + tail_dt)
    kept = narrow(
        jnp.broadcast_to(jnp.sum(state * ending, axis=0, keepdims=True), (8, PART)), up
    )[0:1]
    extra = jnp.sum(dt * tail_dt, axis=0, keepdims=True) + jnp.exp(end) * kept
    step_grad[0, :, :DT_PAD] = inner_dt + tail_dt
    step_grad[0, :, DT_PAD:] = running(jnp.where(row <= column, 1.0, 0.0), d_cum) + extra
    skip_grad[0:1] = skip_grad[0:1] + jnp.sum(narrow(dy * x, up), axis=0, keepdims=True)


def finish_back_kernel(
    scan_in, before, mixed, steps, starts, prefix, state_in, state_grad, mixed_grad, step_grad,
    taps, bias, dt_bias, rates, lift,
    scan_grad, edge_grad, conv_grad, small_grad,
    later, after_pre,
):
    @pl.when(pl.program_id(1) == 0)
    def _():
        later[...] = jnp.zeros_like(later)
        after_pre[...] = jnp.zeros_like(after_pre)

    @pl.when((pl.program_id(0) == 0) & (pl.program_id(1) == 0))
    def _():
        conv_grad[...] = jnp.zeros_like(conv_grad)
        small_grad[...] = jnp.zeros_like(small_grad)

    up = lift[...]
    x = mixed[0, :, :PART]
    b16 = mixed[0, :, PART : PART + STATE].astype(bf16)
    dt = steps[0, :, :DT_PAD]
    cum = steps[0, :, DT_PAD:]
    end = cum[SPAN - 1 : SPAN]
    state = prefix[0, 0] + widen(jnp.exp(starts[0, 0]), up)[0:1] * state_in[0]
    ending = widen(jnp.exp(later[...]), up)[0:1] * state_grad[0]
    later[...] = later[...] + end
    ending16 = ending.astype(bf16)
    tail_wide = widen(jnp.exp(end - cum), up)
    dt_wide = widen(dt, up)
    pull = tail_wide * low_dot(b16, ending16)
    d_x = mixed_grad[0, :, :PART] + dt_wide * pull
    d_b = mixed_grad[0, :, PART : PART + STATE] + over_lanes(
        (tail_wide * dt_wide * x).astype(bf16), ending16
    )
    d_c = mixed_grad[0, :, PART + STATE :]
    tail_dt = narrow(x * pull, up)
    kept = narrow(
        jnp.broadcast_to(jnp.sum(state * ending, axis=0, keepdims=True), (8, PART)), up
    )[0:1]
    row, column = square_places()
    fed = dt * tail_dt
    earlier = running(jnp.where(row > column, 1.0, 0.0), fed)
    d_log = step_grad[0, :, DT_PAD:] + earlier + jnp.exp(end) * kept
    rate = rates[...]
    d_raw = (step_grad[0, :, :DT_PAD] + tail_dt + d_log * rate) * sig(
        scan_in[0, :, CONV_COLS:] + dt_bias[...]
    )
    small_grad[0:1] = small_grad[0:1] + jnp.sum(d_raw, axis=0, keepdims=True)
    small_grad[1:2] = small_grad[1:2] + jnp.sum(d_log * dt * rate, axis=0, keepdims=True)

    pre, extended = pre_conv(scan_in[0, :, :CONV_COLS], before[0, 0], taps[...], bias[...])
    s = sig(pre)
    d_pre = jnp.concatenate([d_x, d_b, d_c], axis=1) * (s * (1.0 + pre * (1.0 - s)))
    for k in range(4):
        conv_grad[k : k + 1] = conv_grad[k : k + 1] + jnp.sum(
            d_pre * extended[5 + k : 5 + k + SPAN], axis=0, keepdims=True
        )
    conv_grad[4:5] = conv_grad[4:5] + jnp.sum(d_pre, axis=0, keepdims=True)
    following = jnp.concatenate([d_pre, after_pre[...]], axis=0)
    d_in = following[0:SPAN] * taps[3:4]
    for k in range(3):
        d_in = d_in + following[3 - k : 3 - k + SPAN] * taps[k : k + 1]
    scan_grad[0, :, :CONV_COLS] = d_in.astype(bf16)
    scan_grad[0, :, CONV_COLS:] = d_raw.astype(bf16)
    front = d_pre[0:8]
    after_pre[...] = front
    nothing = jnp.zeros((8, CONV_COLS), f32)
    padded = jnp.concatenate([nothing, front, nothing], 0)
    edge = padded[0:8] * taps[3:4]
    for k in range(3):
        edge = edge + padded[3 - k : 11 - k] * taps[k : k + 1]
    edge_grad[0] = edge


def one(shape):
    return pl.BlockSpec(shape, lambda b, i: (0,) * len(shape))


def by_span(width, column=0, reverse=None):
    if reverse is None:
        return pl.BlockSpec((1, SPAN, width), lambda b, i: (b, i, column))
    return pl.BlockSpec((1, SPAN, width), lambda b, i: (b, reverse - 1 - i, column))


def by_piece(rows, width, reverse=None):
    if reverse is None:
        return pl.BlockSpec((1, 1, rows, width), lambda b, i: (b, i, 0, 0))
    return pl.BlockSpec((1, 1, rows, width), lambda b, i: (b, reverse - 1 - i, 0, 0))


def by_sequence(rows, width):
    return pl.BlockSpec((1, rows, width), lambda b, i: (b, 0, 0))


def grid_call(kernel, spans, ins, outs, scratch, flops, moved):
    return pl.pallas_call(
        kernel,
        grid=(2, spans),
        in_specs=ins,
        out_specs=[spec for spec, _ in outs],
        out_shape=[shape for _, shape in outs],
        scratch_shapes=scratch,
        compiler_params=pltpu.CompilerParams(
            dimension_semantics=("arbitrary", "arbitrary"), vmem_limit_bytes=50 * 2**20
        ),
        cost_estimate=pl.CostEstimate(flops=flops, bytes_accessed=moved, transcendentals=0),
    )


def like(shape, kind=f32):
    return jax.ShapeDtypeStruct(shape, kind)


def scan_states(scan_in, before, taps, bias, dt_bias, rates, lift):
    length = scan_in.shape[1]
    n = length // SPAN
    return grid_call(
        states_kernel,
        n,
        [
            by_span(SCAN_COLS),
            by_piece(8, CONV_COLS),
            one((4, CONV_COLS)),
            one((1, CONV_COLS)),
            one((1, DT_PAD)),
            one((1, DT_PAD)),
            one((DT_PAD, PART)),
        ],
        [
            (by_span(CONV_COLS), like((2, length, CONV_COLS))),
            (by_span(2 * DT_PAD), like((2, length, 2 * DT_PAD))),
            (by_piece(8, DT_PAD), like((2, n, 8, DT_PAD))),
            (by_piece(STATE, PART), like((2, n, STATE, PART))),
            (by_sequence(STATE, PART), like((2, STATE, PART))),
        ],
        [pltpu.VMEM((STATE, PART), f32), pltpu.VMEM((8, DT_PAD), f32)],
        8 * 10**9,
        30 * 10**6,
    )(scan_in, before, taps, bias, dt_bias, rates, lift)


def scan_values(mixed, steps, starts, prefix, state_in, rest, gate_at, skip, lift):
    length = mixed.shape[1]
    n = length // SPAN
    return grid_call(
        values_kernel,
        n,
        [
            by_span(CONV_COLS),
            by_span(2 * DT_PAD),
            by_piece(8, DT_PAD),
            by_piece(STATE, PART),
            by_sequence(STATE, PART),
            by_span(PART, gate_at),
            one((1, PART)),
            one((DT_PAD, PART)),
        ],
        [
            (by_span(PART), like((2, length, PART))),
            (by_span(PART), like((2, length, PART))),
            (by_span(128), like((2, length, 128))),
        ],
        [],
        12 * 10**9,
        30 * 10**6,
    )(mixed, steps, starts, prefix, state_in, rest, skip, lift)


def gate_backward(gated_grad, values, rest, gate_at, root, mean, gain, mixed, steps, lift):
    length = mixed.shape[1]
    n = length // SPAN
    return grid_call(
        gate_back_kernel,
        n,
        [
            by_span(PART, 0, n),
            by_span(PART, 0, n),
            by_span(PART, gate_at, n),
            by_span(128, 0, n),
            by_span(128, 0, n),
            one((1, PART)),
            by_span(STATE, (PART + STATE) // STATE, n),
            by_span(2 * DT_PAD, 0, n),
            one((DT_PAD, PART)),
        ],
        [
            (by_span(PART, 0, n), like((2, length, PART))),
            (by_span(PART, 0, n), like((2, length, PART), bf16)),
            (one((8, PART)), like((8, PART))),
            (by_piece(STATE, PART, n), like((2, n, STATE, PART))),
            (by_sequence(STATE, PART), like((2, STATE, PART))),
        ],
        [pltpu.VMEM((STATE, PART), f32)],
        8 * 10**9,
        30 * 10**6,
    )(gated_grad, values, rest, root, mean, gain, mixed, steps, lift)


def scan_backward(mixed, steps, starts, prefix, state_in, suffix, value_grad, skip, lift):
    length = mixed.shape[1]
    n = length // SPAN
    return grid_call(
        scan_back_kernel,
        n,
        [
            by_span(CONV_COLS),
            by_span(2 * DT_PAD),
            by_piece(8, DT_PAD),
            by_piece(STATE, PART),
            by_sequence(STATE, PART),
            by_piece(STATE, PART),
            by_span(PART),
            one((1, PART)),
            one((DT_PAD, PART)),
        ],
        [
            (by_span(CONV_COLS), like((2, length, CONV_COLS))),
            (by_span(2 * DT_PAD), like((2, length, 2 * DT_PAD))),
            (one((8, DT_PAD)), like((8, DT_PAD))),
        ],
        [pltpu.VMEM((SPAN, SPAN), f32)],
        30 * 10**9,
        40 * 10**6,
    )(mixed, steps, starts, prefix, state_in, suffix, value_grad, skip, lift)


def finish_backward(
    scan_in, before, mixed, steps, starts, prefix, state_in, state_grad, mixed_grad, step_grad,
    taps, bias, dt_bias, rates, lift,
):
    length = mixed.shape[1]
    n = length // SPAN
    return grid_call(
        finish_back_kernel,
        n,
        [
            by_span(SCAN_COLS, 0, n),
            by_piece(8, CONV_COLS, n),
            by_span(CONV_COLS, 0, n),
            by_span(2 * DT_PAD, 0, n),
            by_piece(8, DT_PAD, n),
            by_piece(STATE, PART, n),
            by_sequence(STATE, PART),
            by_sequence(STATE, PART),
            by_span(CONV_COLS, 0, n),
            by_span(2 * DT_PAD, 0, n),
            one((4, CONV_COLS)),
            one((1, CONV_COLS)),
            one((1, DT_PAD)),
            one((1, DT_PAD)),
            one((DT_PAD, PART)),
        ],
        [
            (by_span(SCAN_COLS, 0, n), like((2, length, SCAN_COLS), bf16)),
            (by_sequence(8, CONV_COLS), like((2, 8, CONV_COLS))),
            (one((8, CONV_COLS)), like((8, CONV_COLS))),
            (one((8, DT_PAD)), like((8, DT_PAD))),
        ],
        [pltpu.VMEM((8, DT_PAD), f32), pltpu.VMEM((8, CONV_COLS), f32)],
        15 * 10**9,
        50 * 10**6,
    )(
        scan_in, before, mixed, steps, starts, prefix, state_in, state_grad, mixed_grad, step_grad,
        taps, bias, dt_bias, rates, lift,
    )


def attend_kernel(query, key, value, query_place, key_place, attended, log_sum):
    scores = over_lanes(query[0], key[0]) * HEAD_DIM ** (-0.5)
    seen = (key_place[0:1] >= 0) & (query_place[:, 0:1] >= key_place[0:1])
    scores = jnp.where(seen, scores, -1e30)
    peak = jnp.max(scores, axis=1, keepdims=True)
    unscaled = jnp.exp(scores - peak)
    whole = jnp.sum(unscaled, axis=1, keepdims=True)
    probs = (unscaled * (1.0 / whole)).astype(bf16)
    attended[0] = low_dot(probs, value[0])
    log_sum[0] = jnp.broadcast_to(peak + jnp.log(whole), log_sum.shape[1:])


def attend_back_kernel(
    query, key, value, grad, attended, log_sum, query_place, key_place, query_grad, kv_grad
):
    @pl.when((pl.program_id(1) == 0) & (pl.program_id(2) == 0))
    def _():
        kv_grad[...] = jnp.zeros_like(kv_grad)

    scale = HEAD_DIM ** (-0.5)
    scores = over_lanes(query[0], key[0]) * scale
    seen = (key_place[0:1] >= 0) & (query_place[:, 0:1] >= key_place[0:1])
    probs = jnp.exp(jnp.where(seen, scores, -1e30) - log_sum[0, :, 0:1])
    delta = jnp.sum(grad[0].astype(f32) * attended[0], axis=1, keepdims=True)
    score_grad = (probs * (over_lanes(grad[0], value[0]) - delta)).astype(bf16)
    query_grad[0] = low_dot(score_grad, key[0]) * scale
    kv_grad[0, 0] = kv_grad[0, 0] + over_rows(score_grad, query[0]) * scale
    kv_grad[1, 0] = kv_grad[1, 0] + over_rows(probs.astype(bf16), grad[0])


def attend_specs(block, keys):
    by_query = pl.BlockSpec((1, block, HEAD_DIM), lambda b, h, i: (b, i, h))
    whole_key = pl.BlockSpec((1, keys, HEAD_DIM), lambda b, h, i: (b, 0, 0))
    place = pl.BlockSpec((block, 128), lambda b, h, i: (i, 0))
    key_at = pl.BlockSpec((8, keys), lambda b, h, i: (0, 0))
    return (by_query, whole_key, place, key_at)


def attend(query, key, value, query_place, key_place):
    length, keys = query.shape[1], key.shape[1]
    block = 256 if keys <= 4096 else 128
    by_query, whole_key, place, key_at = attend_specs(block, keys)
    return pl.pallas_call(
        attend_kernel,
        grid=(2, 2, length // block),
        in_specs=[by_query, whole_key, whole_key, place, key_at],
        out_specs=[by_query, by_query],
        out_shape=[like((2, length, QP)), like((2, length, QP))],
        compiler_params=pltpu.CompilerParams(
            dimension_semantics=("arbitrary",) * 3, vmem_limit_bytes=50 * 2**20
        ),
        cost_estimate=pl.CostEstimate(
            flops=12 * 10**9, bytes_accessed=20 * 10**6, transcendentals=0
        ),
    )(query, key, value, query_place, key_place)


def attend_backward(query, key, value, grad, attended, log_sum, query_place, key_place):
    length, keys = query.shape[1], key.shape[1]
    block = 256 if keys <= 4096 else 128
    by_query, whole_key, place, key_at = attend_specs(block, keys)
    return pl.pallas_call(
        attend_back_kernel,
        grid=(2, 2, length // block),
        in_specs=[by_query, whole_key, whole_key, by_query, by_query, by_query, place, key_at],
        out_specs=[
            by_query,
            pl.BlockSpec((2, 1, keys, HEAD_DIM), lambda b, h, i: (0, b, 0, 0)),
        ],
        out_shape=[like((2, length, QP)), like((2, 2, keys, HEAD_DIM))],
        compiler_params=pltpu.CompilerParams(
            dimension_semantics=("arbitrary",) * 3, vmem_limit_bytes=50 * 2**20
        ),
        cost_estimate=pl.CostEstimate(
            flops=20 * 10**9, bytes_accessed=30 * 10**6, transcendentals=0
        ),
    )(query, key, value, grad, attended, log_sum, query_place, key_place)


def swish_product(gate_proj, up_proj):
    return jax.nn.silu(gate_proj) * up_proj


def gather_tokens(block):
    across = swap(block, "x")
    return (block, swap(block, "c"), across, swap(across, "c"))


def scatter_tokens(blocks):
    near, far = blocks[0], blocks[2]
    sent = swap(jnp.stack([blocks[1].astype(bf16), blocks[3].astype(bf16)]), "c")
    near = near + sent[0].astype(f32)
    far = far + sent[1].astype(f32)
    return near + swap(far.astype(bf16), "x").astype(f32)


def body(
    inputs,
    out_grad,
    norm_gain,
    w_in,
    conv_weight,
    conv_bias,
    dt_bias,
    a_log,
    skip_gain,
    gated_gain,
    w_out,
    w_q,
    w_k,
    w_v,
    w_o,
    mid_gain,
    w_gate,
    w_up,
    w_down,
):
    nz, ny = lax.axis_size("z"), lax.axis_size("y")
    zi, xi, ci = (lax.axis_index(name) for name in ("z", "x", "c"))
    length = inputs.shape[1]
    span_all = 2 * length
    rows = w_in.shape[0]
    ff_rows = w_down.shape[0]
    hidden_part = nz * ny * ff_rows
    edge_count = conv_weight.shape[0] - 1
    out_rows, o_rows = w_out.shape[0], w_o.shape[0]
    aligned = ny == 2 and nz == 4 and MAMBA_HEADS % (4 * nz) == 0
    g = nz if aligned else 1
    hp = HEADS // g

    def heads_mine(array, width):
        lead = array.shape[:-1]
        array = array.reshape(lead + (g, 2, 2, hp * width))
        array = lax.dynamic_index_in_dim(array, xi, len(lead) + 1, keepdims=False)
        array = lax.dynamic_index_in_dim(array, ci, len(lead) + 1, keepdims=False)
        return array.reshape(lead + (HEADS * width,))

    def heads_spread(array, width):
        lead = array.shape[:-1]
        array = array.reshape(lead + (g, 1, 1, hp * width))
        whole = jnp.zeros(lead + (g, 2, 2, hp * width), array.dtype)
        start = (0,) * len(lead) + (0, xi, ci, 0)
        return lax.dynamic_update_slice(whole, array, start).reshape(
            lead + (MAMBA_HEADS * width,)
        )

    def heads_split(array, width):
        n = array.shape[0]
        array = array.reshape(n, g, 2, 2, hp * width)
        return jnp.transpose(array, (2, 3, 0, 1, 4)).reshape(4, n, HEADS * width)

    def heads_join(array, width):
        n = array.shape[1]
        array = array.reshape(2, 2, n, g, hp * width)
        return jnp.transpose(array, (2, 3, 0, 1, 4)).reshape(n, MAMBA_HEADS * width)

    def reordered(array, first, second):
        width = 2 * rows
        return jnp.concatenate(
            [
                array[..., at * width : (at + 1) * width]
                for z in range(nz)
                for at in (
                    (z * first + i) * second + j for j in range(second) for i in range(first)
                )
            ],
            axis=-1,
        )

    def permuted(array):
        return reordered(array, 2, ny)

    def restored(array):
        return reordered(array, ny, 2)

    def to_ranks(array):
        return lax.all_to_all(array, GROUP, 0, 0, tiled=True)

    def in_order(own, other):
        return lax.dynamic_slice_in_dim(
            jnp.concatenate([own, other, own], 0), xi * length, span_all, 0
        )

    def gather_sequences(block):
        own, near, across, far = gather_tokens(block)
        return jnp.stack([in_order(own, across), in_order(near, far)])

    def scatter_sequences(partial):
        mine = partial[0] + swap(partial[1].astype(bf16), "c").astype(f32)
        mine = mine.reshape(2, length, mine.shape[-1])
        own = lax.dynamic_index_in_dim(mine, xi, 0, keepdims=False)
        other = lax.dynamic_index_in_dim(mine, 1 - xi, 0, keepdims=False)
        return own + swap(other.astype(bf16), "x").astype(f32)

    split_q = jnp.transpose(w_q.reshape(rows, 2, 2, 2, HEAD_DIM), (3, 1, 0, 2, 4))
    split_k = jnp.transpose(w_k.reshape(rows, 2, HEAD_DIM), (1, 0, 2))
    split_v = jnp.transpose(w_v.reshape(rows, 2, HEAD_DIM), (1, 0, 2))
    two = lambda a: jnp.broadcast_to(a[None], (2,) + a.shape).reshape(4, rows, a.shape[-1])
    packed_scan = jnp.concatenate(
        [
            heads_split(w_in[:, INNER : 2 * INNER], MAMBA_HEAD),
            jnp.broadcast_to(w_in[None, :, 2 * INNER : 2 * INNER + BC], (4, rows, BC)),
            jnp.pad(
                heads_split(w_in[:, 2 * INNER + BC :], 1), ((0, 0), (0, 0), (0, DT_PAD - HEADS))
            ),
        ],
        axis=2,
    )
    packed_rest = jnp.concatenate(
        [
            heads_split(w_in[:, :INNER], MAMBA_HEAD),
            split_q.reshape(4, rows, QP),
            two(split_k),
            two(split_v),
        ],
        axis=2,
    )

    def gathered(array):
        return lax.all_gather(array, SHARDS, axis=0, tiled=True)

    def after(array, *others):
        return lax.optimization_barrier((array,) + others)[0]

    def split_ff(w):
        w = w.reshape(rows, nz, 2, ny, 2, ff_rows)
        return jnp.transpose(w, (2, 4, 0, 1, 3, 5)).reshape(4, rows, hidden_part)

    def join_ff(w):
        w = w.reshape(2, 2, rows, nz, ny, ff_rows)
        return jnp.transpose(w, (2, 3, 0, 4, 1, 5)).reshape(rows, 4 * hidden_part)

    full_scan = gathered(to_ranks(packed_scan).reshape(4 * rows, SCAN_COLS))

    tokens = 2 * span_all
    resident = inputs[0].astype(f32)
    normed, norm_back = jax.vjp(rms_scale, resident, norm_gain)
    normed16 = gather_sequences(permuted(normed.astype(bf16)))
    edges16 = shifted(normed16[:, span_all - 8 :], 1).reshape(16, D)
    normed_rows = normed16.reshape(tokens, D)

    rest_mine = to_ranks(packed_rest).reshape(4 * rows, REST_COLS)
    if aligned:
        turn = [(2 * y + c, 2 * c + y) for y in range(2) for c in range(2)]
        place = []
        for z in range(4):
            for y in range(2):
                for c in range(2):
                    place.append(((z * 2 + y) * 2 + c, ((z % 2 * 2 + y) * 2 + c) * 2 + z // 2))
        back_place = [(b, a) for a, b in place]
        sent_out = lax.ppermute(w_out, ("y", "c"), turn)
        sent_o = lax.ppermute(w_o, ("z", "y", "c"), place)
        sent_rows = jnp.concatenate([sent_out, sent_o], 0)
    full_rest = gathered(after(rest_mine, normed_rows, edges16))
    cotangent16 = jnp.concatenate(gather_tokens(out_grad[0]), 0)

    scan_in = low_dot(normed_rows, full_scan).reshape(2, span_all, SCAN_COLS)
    edge_rows = low_dot(edges16, full_scan).reshape(2, 1, 8, SCAN_COLS)
    n = span_all // SPAN
    before = jnp.concatenate(
        [edge_rows, scan_in.reshape(2, n, SPAN, SCAN_COLS)[:, : n - 1, SPAN - 8 :]], axis=1
    )[..., :CONV_COLS]

    def rank_channels(array):
        return jnp.concatenate(
            [heads_mine(array[..., :INNER], MAMBA_HEAD), array[..., INNER:]], axis=-1
        )

    def per_head(array):
        return jnp.pad(heads_mine(array, 1), (0, DT_PAD - HEADS))[None]

    taps, bias = rank_channels(conv_weight), rank_channels(conv_bias)[None]
    dt_b, rates = per_head(dt_bias), per_head(-jnp.exp(a_log))
    skip = jnp.repeat(heads_mine(skip_gain, 1), MAMBA_HEAD)[None]
    gain = heads_mine(gated_gain, MAMBA_HEAD)[None]
    lift = (
        jnp.arange(DT_PAD, dtype=jnp.int32)[:, None]
        == jnp.arange(PART, dtype=jnp.int32)[None] // MAMBA_HEAD
    ).astype(bf16)
    mixed, steps, starts, prefix, own_state = scan_states(
        scan_in, before, taps, bias, dt_b, rates, lift
    )
    log_decay = starts[:, n - 1, 0] + steps[:, span_all - 1, DT_PAD:]
    own_decay = jnp.repeat(jnp.exp(log_decay[:, :HEADS]), MAMBA_HEAD, axis=-1)

    if aligned:
        full_rows = gathered(after(sent_rows, mixed, cotangent16)).reshape(nz * ny, 2 * rows, D)
        full_out = full_rows[:, :out_rows].reshape(PART, D)
        full_o = full_rows[:, out_rows:].reshape(QP, D)
    else:
        every_out = lax.all_gather(w_out, EVERY, axis=0, tiled=True)
        every_o = lax.all_gather(w_o, EVERY, axis=0, tiled=True)
        full_out = lax.dynamic_slice_in_dim(every_out, (2 * xi + ci) * PART, PART, 0)
        every_o = every_o.reshape(2, 2, 2, HEAD_DIM, D)
        every_o = lax.dynamic_index_in_dim(every_o, xi, 2, keepdims=False)
        full_o = lax.dynamic_index_in_dim(every_o, ci, 0, keepdims=False).reshape(QP, D)

    def chained(local, step, pin=None):
        entering = []
        for s in range(2):
            held = jnp.zeros(local.shape[1:], f32)
            for hop in range(nz - 1):
                at = hop if step == 1 else nz - 1 - hop
                leaving = local[s] + own_decay[s][None] * held if hop else local[s]
                if pin is not None and hop == nz - 2:
                    leaving = after(leaving, pin)
                held = held + lax.ppermute(
                    leaving.astype(bf16), "z", [(at, at + step)]
                ).astype(f32)
            entering.append(held)
        return jnp.stack(entering)

    packed_ff = jnp.concatenate([split_ff(w_gate), split_ff(w_up)], axis=2)
    rest = low_dot(normed_rows, full_rest).reshape(2, span_all, REST_COLS)

    positions = zi * span_all + jnp.arange(span_all, dtype=jnp.int32)
    cosine, sine = rope_tables(positions)
    query16 = (
        rotate(rest[..., AT_Q:AT_K].reshape(2, span_all, 2, HEAD_DIM), cosine, sine)
        .astype(bf16)
        .reshape(2, span_all, QP)
    )
    key16 = rotate(rest[..., None, AT_K:AT_V], cosine, sine).astype(bf16)[:, :, 0]
    kv16 = jnp.stack([key16, rest[..., AT_V:].astype(bf16)])
    state_in = chained(own_state, 1, kv16)
    kv_all = jnp.concatenate([shifted(kv16, d) for d in range(nz - 1, 0, -1)] + [kv16], axis=2)
    keys_at = (zi - nz + 1) * span_all + jnp.arange(nz * span_all, dtype=jnp.int32)
    query_place = jnp.broadcast_to(positions[:, None], (span_all, 128))
    key_place = jnp.broadcast_to(keys_at[None], (8, nz * span_all))
    attended, log_sum = attend(query16, kv_all[0], kv_all[1], query_place, key_place)
    attended16 = attended.reshape(tokens, QP).astype(bf16)

    values, flat, square = scan_values(
        mixed, steps, starts, prefix, state_in, rest, 0, skip, lift
    )
    root = lax.rsqrt(group_total(square[..., :1]) / INNER + epsilon)
    gated16 = (flat * root * gain).astype(bf16).reshape(tokens, PART)
    full_ff = gathered(
        after(to_ranks(packed_ff).reshape(4 * rows, 2 * hidden_part), flat, attended)
    )
    mixture = low_dot(gated16, full_out) + low_dot(attended16, full_o)
    hidden_state = resident + scatter_sequences(mixture.reshape(2, span_all, D))

    middle, mid_back = jax.vjp(rms_scale, hidden_state, mid_gain)
    middle16 = jnp.concatenate(gather_tokens(permuted(middle.astype(bf16))), 0)
    full_down = gathered(after(w_down, middle16))
    both = low_dot(middle16, full_ff)
    activated, swish_back = jax.vjp(
        swish_product, both[:, :hidden_part], both[:, hidden_part:]
    )
    activated16 = activated.astype(bf16)
    down = low_dot(activated16, full_down).reshape(4, length, D)
    output = (hidden_state + scatter_tokens(down)).astype(bf16)

    def to_owners(array):
        return lax.psum_scatter(array, SHARDS, scatter_dimension=0, tiled=True)

    down_grad = weight_grad(activated16, cotangent16).astype(bf16)
    down_owned = to_owners(down_grad)
    result_down = down_owned.astype(f32)
    gate_grad, up_grad = swish_back(back_dot(after(cotangent16, down_grad), full_down))
    both16 = jnp.concatenate([gate_grad, up_grad], axis=1).astype(bf16)
    mid_grad = restored(scatter_tokens(back_dot(both16, full_ff).reshape(4, length, D)))
    hidden_piece, mid_gain_grad = mid_back(mid_grad)
    hidden_grad = out_grad[0].astype(f32) + hidden_piece
    ff_grad = weight_grad(middle16, both16).astype(bf16)
    ff_owned = to_owners(after(ff_grad, down_owned))
    ff_parts = to_ranks(ff_owned.reshape(4, rows, 2 * hidden_part))
    result_gate = join_ff(ff_parts[..., :hidden_part]).astype(f32)
    result_up = join_ff(ff_parts[..., hidden_part:]).astype(f32)

    mix16 = gather_sequences(after(hidden_grad.astype(bf16), ff_grad)).reshape(tokens, D)
    attended_grad16 = back_dot(mix16, full_o).astype(bf16).reshape(2, span_all, QP)
    gated_grad = back_dot(mix16, full_out).reshape(2, span_all, PART)
    grad_out_w = weight_grad(gated16, mix16).astype(bf16)
    grad_o = weight_grad(attended16, mix16).astype(bf16)

    inner = jnp.sum(gated_grad * gain * flat, axis=-1, keepdims=True) * root
    inner_mean = group_total(inner) / INNER
    wide = (2, span_all, 128)
    value_grad, gate_z_grad, gain_grad, suffix, first_grad = gate_backward(
        after(gated_grad, down_owned),
        values,
        rest,
        0,
        jnp.broadcast_to(root, wide),
        jnp.broadcast_to(inner_mean, wide),
        gain,
        mixed,
        steps,
        lift,
    )
    state_grad = chained(first_grad, -1)

    query_grad, kv_grads = attend_backward(
        query16,
        kv_all[0],
        kv_all[1],
        attended_grad16,
        attended,
        log_sum,
        query_place,
        key_place,
    )
    kv_grads = kv_grads.reshape(2, 2, nz, span_all, HEAD_DIM)
    kv_grad = kv_grads[:, :, nz - 1]
    for d in range(1, nz):
        kv_grad = kv_grad + shifted(kv_grads[:, :, nz - 1 - d].astype(bf16), -d).astype(f32)
    query_back = rotate(
        query_grad.reshape(2, span_all, 2, HEAD_DIM), cosine, -sine
    ).reshape(2, span_all, QP)
    key_back = rotate(kv_grad[0][:, :, None], cosine, -sine)[:, :, 0]
    rest_grad16 = jnp.concatenate(
        [
            gate_z_grad,
            query_back.astype(bf16),
            key_back.astype(bf16),
            kv_grad[1].astype(bf16),
        ],
        axis=-1,
    ).reshape(tokens, REST_COLS)

    mixed_grad, step_grad, skip_grad = scan_backward(
        mixed, steps, starts, prefix, state_in, suffix, value_grad, skip, lift
    )
    scan_grad16, edge_grad, conv_grad, small_grad = finish_backward(
        scan_in,
        before,
        mixed,
        steps,
        starts,
        prefix,
        state_in,
        after(state_grad, ff_owned),
        mixed_grad,
        step_grad,
        taps,
        bias,
        dt_b,
        rates,
        lift,
    )
    edge_back = shifted(edge_grad[:, 8 - edge_count :].astype(bf16), -1).astype(f32)
    last_rows = scan_grad16[:, span_all - edge_count :, :CONV_COLS].astype(f32) + edge_back
    scan_grad16 = lax.dynamic_update_slice(
        scan_grad16, last_rows.astype(bf16), (0, span_all - edge_count, 0)
    ).reshape(tokens, SCAN_COLS)
    if aligned:
        rows_grad = jnp.concatenate(
            [grad_out_w.reshape(nz * ny, out_rows, D), grad_o.reshape(nz * ny, o_rows, D)], axis=1
        ).reshape(nz * ny * 2 * rows, D)
        rows_owned = to_owners(after(rows_grad, ff_owned))
        result_out = lax.ppermute(rows_owned[:out_rows], ("y", "c"), turn).astype(f32)
        result_o = lax.ppermute(rows_owned[out_rows:], ("z", "y", "c"), back_place).astype(f32)
    else:
        every_out = lax.dynamic_update_slice_in_dim(
            jnp.zeros((INNER, D), bf16), grad_out_w, (2 * xi + ci) * PART, 0
        )
        every_o = lax.dynamic_update_slice(
            jnp.zeros((2, 2, 2, HEAD_DIM, D), bf16),
            grad_o.reshape(1, 2, 1, HEAD_DIM, D),
            (ci, 0, xi, 0, 0),
        ).reshape(ATT_HEADS * HEAD_DIM, D)
        result_out = lax.psum_scatter(every_out, EVERY, scatter_dimension=0, tiled=True)
        result_o = lax.psum_scatter(every_o, EVERY, scatter_dimension=0, tiled=True)
        result_out, result_o = result_out.astype(f32), result_o.astype(f32)
        rows_owned = result_out
    rest_owned = to_owners(
        after(weight_grad(normed_rows, rest_grad16).astype(bf16), rows_owned)
    )
    rest_parts = to_ranks(rest_owned.reshape(4, rows, REST_COLS)).astype(f32)
    scan_owned = to_owners(
        after(weight_grad(normed_rows, scan_grad16).astype(bf16), rest_owned)
    )
    scan_parts = to_ranks(scan_owned.reshape(4, rows, SCAN_COLS)).astype(f32)

    normed_grad = back_dot(scan_grad16, full_scan) + back_dot(rest_grad16, full_rest)
    normed_grad = restored(scatter_sequences(normed_grad.reshape(2, span_all, D)))
    resident_grad, norm_gain_grad = norm_back(normed_grad)
    input_grad = hidden_grad + resident_grad

    result_in = jnp.concatenate(
        [
            heads_join(rest_parts[..., :PART], MAMBA_HEAD),
            heads_join(scan_parts[..., :PART], MAMBA_HEAD),
            jnp.sum(scan_parts[..., PART:CONV_COLS], axis=0),
            heads_join(scan_parts[..., CONV_COLS : CONV_COLS + HEADS], 1),
        ],
        axis=1,
    )
    result_q = jnp.transpose(
        rest_parts[..., AT_Q:AT_K].reshape(2, 2, rows, 2, HEAD_DIM), (2, 1, 3, 0, 4)
    ).reshape(rows, ATT_HEADS * HEAD_DIM)
    kv_parts = jnp.sum(rest_parts[..., AT_K:].reshape(2, 2, rows, 2, HEAD_DIM), axis=0)
    result_k = jnp.transpose(kv_parts[:, :, 0], (1, 0, 2)).reshape(rows, KV_HEADS * HEAD_DIM)
    result_v = jnp.transpose(kv_parts[:, :, 1], (1, 0, 2)).reshape(rows, KV_HEADS * HEAD_DIM)

    def all_channels(array):
        return jnp.concatenate(
            [heads_spread(array[..., :PART], MAMBA_HEAD), array[..., PART:]], axis=-1
        )

    small = [
        norm_gain_grad,
        all_channels(conv_grad[:4]),
        all_channels(conv_grad[4]),
        heads_spread(small_grad[0, :HEADS], 1),
        heads_spread(small_grad[1, :HEADS], 1),
        heads_spread(skip_grad[0, :HEADS], 1),
        heads_spread(gain_grad[0], MAMBA_HEAD),
        mid_gain_grad,
    ]
    summed = total(jnp.concatenate([v.reshape(-1) for v in small]))
    parts, at = [], 0
    for v in small:
        parts.append(summed[at : at + v.size].reshape(v.shape))
        at += v.size
    return (
        output[None],
        input_grad[None],
        parts[0],
        result_in,
        parts[1],
        parts[2],
        parts[3],
        parts[4],
        parts[5],
        parts[6],
        result_out,
        result_q,
        result_k,
        result_v,
        result_o,
        parts[7],
        result_gate,
        result_up,
        result_down,
    )


def solution(mesh):
    seq, fsdp = mesh.shape["seq"], mesh.shape["fsdp"]
    split = Mesh(mesh.devices.reshape(seq // 2, 2, fsdp // 2, 2), EVERY)
    tokens = P(("y", "c"), ("z", "x"), None)
    matrix = P(EVERY, None)
    return jax.shard_map(
        body,
        mesh=split,
        in_specs=(tokens, tokens, P(), matrix)
        + (P(),) * 6
        + (matrix,) * 5
        + (P(),)
        + (matrix,) * 3,
        out_specs=(tokens, tokens, P(), matrix)
        + (P(),) * 6
        + (matrix,) * 5
        + (P(),)
        + (matrix,) * 3,
        check_vma=False,
    )
```

```python
import jax
import jax.numpy as jnp
from jax import lax
from jax.experimental import pallas as pl
from jax.experimental.pallas import tpu as pltpu
from jax.sharding import Mesh
from jax.sharding import PartitionSpec as P

D = 2048
MAMBA_HEADS = 48
MAMBA_HEAD = 64
STATE = 256
ATT_HEADS = 8
KV_HEADS = 2
HEAD_DIM = 128
SPAN = 128
INNER = 3072

HEADS = MAMBA_HEADS // 4
PART = HEADS * MAMBA_HEAD
BC = 2 * STATE
DT_PAD = 128
QP = 2 * HEAD_DIM
CONV_COLS = PART + BC
SCAN_COLS = CONV_COLS + DT_PAD
AT_Q = PART
AT_K = AT_Q + QP
AT_V = AT_K + HEAD_DIM
REST_COLS = AT_V + HEAD_DIM

epsilon = 1e-05
rope_base = 100000000000.0
GROUP = ("x", "c")
SHARDS = ("z", "y")
EVERY = ("z", "x", "y", "c")
bf16 = jnp.bfloat16
f32 = jnp.float32


def swap(array, axis):
    return lax.ppermute(array, axis, [(0, 1), (1, 0)])


def shifted(array, distance):
    devices = range(lax.axis_size("z"))
    return lax.ppermute(array, "z", [(i - distance, i) for i in devices if i - distance in devices])


def total(array):
    for axis in EVERY:
        size = lax.axis_size(axis)
        bit = 1
        while bit < size:
            array = array + lax.ppermute(array, axis, [(i, i ^ bit) for i in range(size)])
            bit *= 2
    return array


def group_total(array):
    array = array + swap(array[::-1], "c")
    return array + swap(array, "x")


def low_dot(left, right):
    return jnp.dot(left, right, preferred_element_type=f32)


def back_dot(grad_rows, weight):
    return lax.dot_general(grad_rows, weight, (((1,), (1,)), ((), ())), preferred_element_type=f32)


def weight_grad(left, right):
    return lax.dot_general(left, right, (((0,), (0,)), ((), ())), preferred_element_type=f32)


def rms_scale(values, gain):
    return values * lax.rsqrt(jnp.mean(values * values, axis=-1, keepdims=True) + epsilon) * gain


def rope_tables(positions):
    half_dim = HEAD_DIM // 2
    frequencies = rope_base ** (-jnp.arange(half_dim, dtype=f32) / half_dim)
    angles = positions.astype(f32)[:, None] * frequencies[None, :]
    return (jnp.cos(angles), jnp.sin(angles))


def rotate(values, cosine, sine):
    half_dim = HEAD_DIM // 2
    cosine, sine = cosine[:, None, :], sine[:, None, :]
    first, second = values[..., :half_dim], values[..., half_dim:]
    return jnp.concatenate([first * cosine - second * sine, second * cosine + first * sine], axis=-1)


def pieces(values, count):
    parts = []
    for _ in range(count):
        part = values.astype(bf16)
        parts.append(part)
        values = values - part.astype(f32)
    return parts


def running(mask, values):
    mask16 = mask.astype(bf16)
    return sum(low_dot(mask16, part) for part in pieces(values, 3))


def over_lanes(left, right):
    return lax.dot_general(left, right, (((1,), (1,)), ((), ())), preferred_element_type=f32)


def over_rows(left, right):
    return lax.dot_general(left, right, (((0,), (0,)), ((), ())), preferred_element_type=f32)


def widen(values, lift):
    return sum(low_dot(part, lift) for part in pieces(values, 2))


def narrow(values, lift):
    return sum(over_lanes(part, lift) for part in pieces(values, 2))


def sig(values):
    return 1.0 / (1.0 + jnp.exp(-values))


def soft(values):
    return jnp.maximum(values, 0.0) + jnp.log1p(jnp.exp(-jnp.abs(values)))


def square_places():
    return (
        lax.broadcasted_iota(jnp.int32, (SPAN, SPAN), 0),
        lax.broadcasted_iota(jnp.int32, (SPAN, SPAN), 1),
    )


def pre_conv(current, before, taps, bias):
    extended = jnp.concatenate([before, current], axis=0)
    pre = bias + extended[5 : 5 + SPAN] * taps[0:1]
    for k in range(1, 4):
        pre = pre + extended[5 + k : 5 + k + SPAN] * taps[k : k + 1]
    return (pre, extended)


def states_kernel(
    scan_in, before, taps, bias, dt_bias, rates, lift, mixed, steps, starts, prefix, last, held, sofar
):
    @pl.when(pl.program_id(1) == 0)
    def _():
        held[...] = jnp.zeros_like(held)
        sofar[...] = jnp.zeros_like(sofar)

    pre, _ = pre_conv(scan_in[0, :, :CONV_COLS], before[0, 0], taps[...], bias[...])
    mix = pre * sig(pre)
    mixed[0] = mix
    dt = soft(scan_in[0, :, CONV_COLS:] + dt_bias[...])
    row, column = square_places()
    cum = running(jnp.where(row >= column, 1.0, 0.0), dt * rates[...])
    steps[0, :, :DT_PAD] = dt
    steps[0, :, DT_PAD:] = cum
    starts[0, 0] = sofar[...]
    prefix[0, 0] = held[...]
    end = cum[SPAN - 1 : SPAN]
    tail = jnp.exp(end - cum) * dt
    fed = (mix[:, :PART] * widen(tail, lift[...])).astype(bf16)
    added = over_rows(mix[:, PART : PART + STATE].astype(bf16), fed)
    whole = widen(jnp.broadcast_to(jnp.exp(end), (8, DT_PAD)), lift[...])[0:1]
    held[...] = whole * held[...] + added
    sofar[...] = sofar[...] + end
    last[0] = held[...]


def values_kernel(
    mixed, steps, starts, prefix, state_in, gate, skip, lift, values, flat, square
):
    x = mixed[0, :, :PART]
    b16 = mixed[0, :, PART : PART + STATE].astype(bf16)
    c16 = mixed[0, :, PART + STATE :].astype(bf16)
    dt = steps[0, :, :DT_PAD]
    cum = steps[0, :, DT_PAD:]
    dt_t, cum_t = dt.T, cum.T
    state = prefix[0, 0] + widen(jnp.exp(starts[0, 0]), lift[...])[0:1] * state_in[0]
    meet = over_lanes(c16, b16)
    carried = low_dot(c16, state.astype(bf16)) * widen(jnp.exp(cum), lift[...])
    row, column = square_places()
    first = column < MAMBA_HEAD
    inside = []
    for k in range(HEADS // 2):
        pair = x[:, 2 * MAMBA_HEAD * k : 2 * MAMBA_HEAD * (k + 1)]
        weights = []
        for h in (2 * k, 2 * k + 1):
            spread = cum[:, h : h + 1] - cum_t[h : h + 1, :]
            decay = jnp.exp(jnp.where(row >= column, spread, -1e30))
            weights.append((meet * decay * dt_t[h : h + 1, :]).astype(bf16))
        split = [
            jnp.where(first, pair, 0.0).astype(bf16),
            jnp.where(first, 0.0, pair).astype(bf16),
        ]
        inside.append(low_dot(jnp.concatenate(weights, 1), jnp.concatenate(split, 0)))
    value = jnp.concatenate(inside, 1) + carried + skip[...] * x
    values[0] = value
    z = gate[0]
    product = value * (z * sig(z))
    flat[0] = product
    square[0] = jnp.broadcast_to(
        jnp.sum(product * product, axis=1, keepdims=True), (SPAN, 128)
    )


def gate_back_kernel(
    gated_grad, values, gate, root, mean, gain, c_part, steps, lift,
    value_grad, gate_grad, gain_grad, suffix, first_grad, held,
):
    @pl.when(pl.program_id(1) == 0)
    def _():
        held[...] = jnp.zeros_like(held)

    @pl.when((pl.program_id(0) == 0) & (pl.program_id(1) == 0))
    def _():
        gain_grad[...] = jnp.zeros_like(gain_grad)

    z, value, grad = gate[0], values[0], gated_grad[0]
    s = sig(z)
    silu = z * s
    scale = root[0, :, 0:1]
    normal = value * silu * scale
    flat_grad = scale * (grad * gain[...] - normal * mean[0, :, 0:1])
    d_value = flat_grad * silu
    value_grad[0] = d_value
    gate_grad[0] = (flat_grad * value * (s * (1.0 + z * (1.0 - s)))).astype(bf16)
    gain_grad[0:1] = gain_grad[0:1] + jnp.sum(grad * normal, axis=0, keepdims=True)
    grown = widen(jnp.exp(steps[0, :, DT_PAD:]), lift[...])
    suffix[0, 0] = held[...]
    held[...] = grown[SPAN - 1 : SPAN] * held[...] + over_rows(
        c_part[0].astype(bf16), (grown * d_value).astype(bf16)
    )
    first_grad[0] = held[...]


def scan_back_kernel(
    mixed, steps, starts, prefix, state_in, suffix, value_grad, skip, lift,
    mixed_grad, step_grad, skip_grad, columns,
):
    @pl.when((pl.program_id(0) == 0) & (pl.program_id(1) == 0))
    def _():
        skip_grad[...] = jnp.zeros_like(skip_grad)
        columns[...] = jnp.zeros_like(columns)

    up = lift[...]
    x = mixed[0, :, :PART]
    b16 = mixed[0, :, PART : PART + STATE].astype(bf16)
    c16 = mixed[0, :, PART + STATE :].astype(bf16)
    dt = steps[0, :, :DT_PAD]
    cum = steps[0, :, DT_PAD:]
    dt_t, cum_t = dt.T, cum.T
    end = cum[SPAN - 1 : SPAN]
    dy = value_grad[0]
    state = prefix[0, 0] + widen(jnp.exp(starts[0, 0]), up)[0:1] * state_in[0]
    ending = suffix[0, 0]
    state16, ending16 = state.astype(bf16), ending.astype(bf16)
    grown_dy = widen(jnp.exp(cum), up) * dy
    tail_wide = widen(jnp.exp(end - cum), up)
    dt_wide = widen(dt, up)
    reach = low_dot(c16, state16)
    pull = tail_wide * low_dot(b16, ending16)
    d_c = over_lanes(grown_dy.astype(bf16), state16)
    d_b = over_lanes((tail_wide * dt_wide * x).astype(bf16), ending16)
    meet = over_lanes(c16, b16)
    row, column = square_places()
    first = column < MAMBA_HEAD
    d_meet = jnp.zeros((SPAN, SPAN), f32)
    rows_sum = jnp.zeros((SPAN, DT_PAD), f32)
    back = []
    for k in range(HEADS // 2):
        at = slice(2 * MAMBA_HEAD * k, 2 * MAMBA_HEAD * (k + 1))
        x16, dy_pair = x[:, at].astype(bf16), dy[:, at]
        split = [
            jnp.where(first, dy_pair, 0.0).astype(bf16),
            jnp.where(first, 0.0, dy_pair).astype(bf16),
        ]
        weights = []
        for j in range(2):
            h = 2 * k + j
            spread = cum[:, h : h + 1] - cum_t[h : h + 1, :]
            decay = jnp.exp(jnp.where(row >= column, spread, -1e30))
            d_weight = over_lanes(split[j], x16) * decay
            scaled = d_weight * dt_t[h : h + 1, :]
            d_meet = d_meet + scaled
            rows_sum = rows_sum + jnp.where(
                column == h, jnp.sum(scaled * meet, axis=1, keepdims=True), 0.0
            )
            columns[h : h + 1, :] = jnp.sum(d_weight * meet, axis=0, keepdims=True)
            weights.append((meet * decay).astype(bf16))
        back.append(over_rows(jnp.concatenate(weights, 0), jnp.concatenate(split, 0)))
    d_meet16 = d_meet.astype(bf16)
    mixed_grad[0, :, :PART] = dt_wide * (jnp.concatenate(back, 1) + pull) + skip[...] * dy
    mixed_grad[0, :, PART : PART + STATE] = d_b + over_rows(d_meet16, c16)
    mixed_grad[0, :, PART + STATE :] = d_c + low_dot(d_meet16, b16)
    tail_dt = narrow(x * pull, up)
    inner_dt = columns[...].T
    d_cum = rows_sum + narrow(grown_dy * reach, up) - dt * (inner_dt + tail_dt)
    kept = narrow(
        jnp.broadcast_to(jnp.sum(state * ending, axis=0, keepdims=True), (8, PART)), up
    )[0:1]
    extra = jnp.sum(dt * tail_dt, axis=0, keepdims=True) + jnp.exp(end) * kept
    step_grad[0, :, :DT_PAD] = inner_dt + tail_dt
    step_grad[0, :, DT_PAD:] = running(jnp.where(row <= column, 1.0, 0.0), d_cum) + extra
    skip_grad[0:1] = skip_grad[0:1] + jnp.sum(narrow(dy * x, up), axis=0, keepdims=True)


def finish_back_kernel(
    scan_in, before, mixed, steps, starts, prefix, state_in, state_grad, mixed_grad, step_grad,
    taps, bias, dt_bias, rates, lift,
    scan_grad, edge_grad, conv_grad, small_grad,
    later, after_pre,
):
    @pl.when(pl.program_id(1) == 0)
    def _():
        later[...] = jnp.zeros_like(later)
        after_pre[...] = jnp.zeros_like(after_pre)

    @pl.when((pl.program_id(0) == 0) & (pl.program_id(1) == 0))
    def _():
        conv_grad[...] = jnp.zeros_like(conv_grad)
        small_grad[...] = jnp.zeros_like(small_grad)

    up = lift[...]
    x = mixed[0, :, :PART]
    b16 = mixed[0, :, PART : PART + STATE].astype(bf16)
    dt = steps[0, :, :DT_PAD]
    cum = steps[0, :, DT_PAD:]
    end = cum[SPAN - 1 : SPAN]
    state = prefix[0, 0] + widen(jnp.exp(starts[0, 0]), up)[0:1] * state_in[0]
    ending = widen(jnp.exp(later[...]), up)[0:1] * state_grad[0]
    later[...] = later[...] + end
    ending16 = ending.astype(bf16)
    tail_wide = widen(jnp.exp(end - cum), up)
    dt_wide = widen(dt, up)
    pull = tail_wide * low_dot(b16, ending16)
    d_x = mixed_grad[0, :, :PART] + dt_wide * pull
    d_b = mixed_grad[0, :, PART : PART + STATE] + over_lanes(
        (tail_wide * dt_wide * x).astype(bf16), ending16
    )
    d_c = mixed_grad[0, :, PART + STATE :]
    tail_dt = narrow(x * pull, up)
    kept = narrow(
        jnp.broadcast_to(jnp.sum(state * ending, axis=0, keepdims=True), (8, PART)), up
    )[0:1]
    row, column = square_places()
    fed = dt * tail_dt
    earlier = running(jnp.where(row > column, 1.0, 0.0), fed)
    d_log = step_grad[0, :, DT_PAD:] + earlier + jnp.exp(end) * kept
    rate = rates[...]
    d_raw = (step_grad[0, :, :DT_PAD] + tail_dt + d_log * rate) * sig(
        scan_in[0, :, CONV_COLS:] + dt_bias[...]
    )
    small_grad[0:1] = small_grad[0:1] + jnp.sum(d_raw, axis=0, keepdims=True)
    small_grad[1:2] = small_grad[1:2] + jnp.sum(d_log * dt * rate, axis=0, keepdims=True)

    pre, extended = pre_conv(scan_in[0, :, :CONV_COLS], before[0, 0], taps[...], bias[...])
    s = sig(pre)
    d_pre = jnp.concatenate([d_x, d_b, d_c], axis=1) * (s * (1.0 + pre * (1.0 - s)))
    for k in range(4):
        conv_grad[k : k + 1] = conv_grad[k : k + 1] + jnp.sum(
            d_pre * extended[5 + k : 5 + k + SPAN], axis=0, keepdims=True
        )
    conv_grad[4:5] = conv_grad[4:5] + jnp.sum(d_pre, axis=0, keepdims=True)
    following = jnp.concatenate([d_pre, after_pre[...]], axis=0)
    d_in = following[0:SPAN] * taps[3:4]
    for k in range(3):
        d_in = d_in + following[3 - k : 3 - k + SPAN] * taps[k : k + 1]
    scan_grad[0, :, :CONV_COLS] = d_in.astype(bf16)
    scan_grad[0, :, CONV_COLS:] = d_raw.astype(bf16)
    front = d_pre[0:8]
    after_pre[...] = front
    nothing = jnp.zeros((8, CONV_COLS), f32)
    padded = jnp.concatenate([nothing, front, nothing], 0)
    edge = padded[0:8] * taps[3:4]
    for k in range(3):
        edge = edge + padded[3 - k : 11 - k] * taps[k : k + 1]
    edge_grad[0] = edge


def one(shape):
    return pl.BlockSpec(shape, lambda b, i: (0,) * len(shape))


def by_span(width, column=0, reverse=None):
    if reverse is None:
        return pl.BlockSpec((1, SPAN, width), lambda b, i: (b, i, column))
    return pl.BlockSpec((1, SPAN, width), lambda b, i: (b, reverse - 1 - i, column))


def by_piece(rows, width, reverse=None):
    if reverse is None:
        return pl.BlockSpec((1, 1, rows, width), lambda b, i: (b, i, 0, 0))
    return pl.BlockSpec((1, 1, rows, width), lambda b, i: (b, reverse - 1 - i, 0, 0))


def by_sequence(rows, width):
    return pl.BlockSpec((1, rows, width), lambda b, i: (b, 0, 0))


def grid_call(kernel, spans, ins, outs, scratch, flops, moved):
    return pl.pallas_call(
        kernel,
        grid=(2, spans),
        in_specs=ins,
        out_specs=[spec for spec, _ in outs],
        out_shape=[shape for _, shape in outs],
        scratch_shapes=scratch,
        compiler_params=pltpu.CompilerParams(
            dimension_semantics=("arbitrary", "arbitrary"), vmem_limit_bytes=50 * 2**20
        ),
        cost_estimate=pl.CostEstimate(flops=flops, bytes_accessed=moved, transcendentals=0),
    )


def like(shape, kind=f32):
    return jax.ShapeDtypeStruct(shape, kind)


def scan_states(scan_in, before, taps, bias, dt_bias, rates, lift):
    length = scan_in.shape[1]
    n = length // SPAN
    return grid_call(
        states_kernel,
        n,
        [
            by_span(SCAN_COLS),
            by_piece(8, CONV_COLS),
            one((4, CONV_COLS)),
            one((1, CONV_COLS)),
            one((1, DT_PAD)),
            one((1, DT_PAD)),
            one((DT_PAD, PART)),
        ],
        [
            (by_span(CONV_COLS), like((2, length, CONV_COLS))),
            (by_span(2 * DT_PAD), like((2, length, 2 * DT_PAD))),
            (by_piece(8, DT_PAD), like((2, n, 8, DT_PAD))),
            (by_piece(STATE, PART), like((2, n, STATE, PART))),
            (by_sequence(STATE, PART), like((2, STATE, PART))),
        ],
        [pltpu.VMEM((STATE, PART), f32), pltpu.VMEM((8, DT_PAD), f32)],
        8 * 10**9,
        30 * 10**6,
    )(scan_in, before, taps, bias, dt_bias, rates, lift)


def scan_values(mixed, steps, starts, prefix, state_in, rest, gate_at, skip, lift):
    length = mixed.shape[1]
    n = length // SPAN
    return grid_call(
        values_kernel,
        n,
        [
            by_span(CONV_COLS),
            by_span(2 * DT_PAD),
            by_piece(8, DT_PAD),
            by_piece(STATE, PART),
            by_sequence(STATE, PART),
            by_span(PART, gate_at),
            one((1, PART)),
            one((DT_PAD, PART)),
        ],
        [
            (by_span(PART), like((2, length, PART))),
            (by_span(PART), like((2, length, PART))),
            (by_span(128), like((2, length, 128))),
        ],
        [],
        12 * 10**9,
        30 * 10**6,
    )(mixed, steps, starts, prefix, state_in, rest, skip, lift)


def gate_backward(gated_grad, values, rest, gate_at, root, mean, gain, mixed, steps, lift):
    length = mixed.shape[1]
    n = length // SPAN
    return grid_call(
        gate_back_kernel,
        n,
        [
            by_span(PART, 0, n),
            by_span(PART, 0, n),
            by_span(PART, gate_at, n),
            by_span(128, 0, n),
            by_span(128, 0, n),
            one((1, PART)),
            by_span(STATE, (PART + STATE) // STATE, n),
            by_span(2 * DT_PAD, 0, n),
            one((DT_PAD, PART)),
        ],
        [
            (by_span(PART, 0, n), like((2, length, PART))),
            (by_span(PART, 0, n), like((2, length, PART), bf16)),
            (one((8, PART)), like((8, PART))),
            (by_piece(STATE, PART, n), like((2, n, STATE, PART))),
            (by_sequence(STATE, PART), like((2, STATE, PART))),
        ],
        [pltpu.VMEM((STATE, PART), f32)],
        8 * 10**9,
        30 * 10**6,
    )(gated_grad, values, rest, root, mean, gain, mixed, steps, lift)


def scan_backward(mixed, steps, starts, prefix, state_in, suffix, value_grad, skip, lift):
    length = mixed.shape[1]
    n = length // SPAN
    return grid_call(
        scan_back_kernel,
        n,
        [
            by_span(CONV_COLS),
            by_span(2 * DT_PAD),
            by_piece(8, DT_PAD),
            by_piece(STATE, PART),
            by_sequence(STATE, PART),
            by_piece(STATE, PART),
            by_span(PART),
            one((1, PART)),
            one((DT_PAD, PART)),
        ],
        [
            (by_span(CONV_COLS), like((2, length, CONV_COLS))),
            (by_span(2 * DT_PAD), like((2, length, 2 * DT_PAD))),
            (one((8, DT_PAD)), like((8, DT_PAD))),
        ],
        [pltpu.VMEM((SPAN, SPAN), f32)],
        30 * 10**9,
        40 * 10**6,
    )(mixed, steps, starts, prefix, state_in, suffix, value_grad, skip, lift)


def finish_backward(
    scan_in, before, mixed, steps, starts, prefix, state_in, state_grad, mixed_grad, step_grad,
    taps, bias, dt_bias, rates, lift,
):
    length = mixed.shape[1]
    n = length // SPAN
    return grid_call(
        finish_back_kernel,
        n,
        [
            by_span(SCAN_COLS, 0, n),
            by_piece(8, CONV_COLS, n),
            by_span(CONV_COLS, 0, n),
            by_span(2 * DT_PAD, 0, n),
            by_piece(8, DT_PAD, n),
            by_piece(STATE, PART, n),
            by_sequence(STATE, PART),
            by_sequence(STATE, PART),
            by_span(CONV_COLS, 0, n),
            by_span(2 * DT_PAD, 0, n),
            one((4, CONV_COLS)),
            one((1, CONV_COLS)),
            one((1, DT_PAD)),
            one((1, DT_PAD)),
            one((DT_PAD, PART)),
        ],
        [
            (by_span(SCAN_COLS, 0, n), like((2, length, SCAN_COLS), bf16)),
            (by_sequence(8, CONV_COLS), like((2, 8, CONV_COLS))),
            (one((8, CONV_COLS)), like((8, CONV_COLS))),
            (one((8, DT_PAD)), like((8, DT_PAD))),
        ],
        [pltpu.VMEM((8, DT_PAD), f32), pltpu.VMEM((8, CONV_COLS), f32)],
        15 * 10**9,
        50 * 10**6,
    )(
        scan_in, before, mixed, steps, starts, prefix, state_in, state_grad, mixed_grad, step_grad,
        taps, bias, dt_bias, rates, lift,
    )


def attend_kernel(query, key, value, query_place, key_place, attended, log_sum):
    scores = over_lanes(query[0], key[0]) * HEAD_DIM ** (-0.5)
    seen = (key_place[0:1] >= 0) & (query_place[:, 0:1] >= key_place[0:1])
    scores = jnp.where(seen, scores, -1e30)
    peak = jnp.max(scores, axis=1, keepdims=True)
    unscaled = jnp.exp(scores - peak)
    whole = jnp.sum(unscaled, axis=1, keepdims=True)
    probs = (unscaled * (1.0 / whole)).astype(bf16)
    attended[0] = low_dot(probs, value[0])
    log_sum[0] = jnp.broadcast_to(peak + jnp.log(whole), log_sum.shape[1:])


def attend_back_kernel(
    query, key, value, grad, attended, log_sum, query_place, key_place, query_grad, kv_grad
):
    @pl.when((pl.program_id(1) == 0) & (pl.program_id(2) == 0))
    def _():
        kv_grad[...] = jnp.zeros_like(kv_grad)

    scale = HEAD_DIM ** (-0.5)
    scores = over_lanes(query[0], key[0]) * scale
    seen = (key_place[0:1] >= 0) & (query_place[:, 0:1] >= key_place[0:1])
    probs = jnp.exp(jnp.where(seen, scores, -1e30) - log_sum[0, :, 0:1])
    delta = jnp.sum(grad[0].astype(f32) * attended[0], axis=1, keepdims=True)
    score_grad = (probs * (over_lanes(grad[0], value[0]) - delta)).astype(bf16)
    query_grad[0] = low_dot(score_grad, key[0]) * scale
    kv_grad[0, 0] = kv_grad[0, 0] + over_rows(score_grad, query[0]) * scale
    kv_grad[1, 0] = kv_grad[1, 0] + over_rows(probs.astype(bf16), grad[0])


def attend_specs(block, keys):
    by_query = pl.BlockSpec((1, block, HEAD_DIM), lambda b, h, i: (b, i, h))
    whole_key = pl.BlockSpec((1, keys, HEAD_DIM), lambda b, h, i: (b, 0, 0))
    place = pl.BlockSpec((block, 128), lambda b, h, i: (i, 0))
    key_at = pl.BlockSpec((8, keys), lambda b, h, i: (0, 0))
    return (by_query, whole_key, place, key_at)


def attend(query, key, value, query_place, key_place):
    length, keys = query.shape[1], key.shape[1]
    block = 256 if keys <= 4096 else 128
    by_query, whole_key, place, key_at = attend_specs(block, keys)
    return pl.pallas_call(
        attend_kernel,
        grid=(2, 2, length // block),
        in_specs=[by_query, whole_key, whole_key, place, key_at],
        out_specs=[by_query, by_query],
        out_shape=[like((2, length, QP)), like((2, length, QP))],
        compiler_params=pltpu.CompilerParams(
            dimension_semantics=("arbitrary",) * 3, vmem_limit_bytes=50 * 2**20
        ),
        cost_estimate=pl.CostEstimate(
            flops=12 * 10**9, bytes_accessed=20 * 10**6, transcendentals=0
        ),
    )(query, key, value, query_place, key_place)


def attend_backward(query, key, value, grad, attended, log_sum, query_place, key_place):
    length, keys = query.shape[1], key.shape[1]
    block = 256 if keys <= 4096 else 128
    by_query, whole_key, place, key_at = attend_specs(block, keys)
    return pl.pallas_call(
        attend_back_kernel,
        grid=(2, 2, length // block),
        in_specs=[by_query, whole_key, whole_key, by_query, by_query, by_query, place, key_at],
        out_specs=[
            by_query,
            pl.BlockSpec((2, 1, keys, HEAD_DIM), lambda b, h, i: (0, b, 0, 0)),
        ],
        out_shape=[like((2, length, QP)), like((2, 2, keys, HEAD_DIM))],
        compiler_params=pltpu.CompilerParams(
            dimension_semantics=("arbitrary",) * 3, vmem_limit_bytes=50 * 2**20
        ),
        cost_estimate=pl.CostEstimate(
            flops=20 * 10**9, bytes_accessed=30 * 10**6, transcendentals=0
        ),
    )(query, key, value, grad, attended, log_sum, query_place, key_place)


def swish_product(gate_proj, up_proj):
    return jax.nn.silu(gate_proj) * up_proj


def gather_tokens(block):
    across = swap(block, "x")
    return (block, swap(block, "c"), across, swap(across, "c"))


def scatter_tokens(blocks):
    near, far = blocks[0], blocks[2]
    sent = swap(jnp.stack([blocks[1].astype(bf16), blocks[3].astype(bf16)]), "c")
    near = near + sent[0].astype(f32)
    far = far + sent[1].astype(f32)
    return near + swap(far.astype(bf16), "x").astype(f32)


def body(
    inputs,
    out_grad,
    norm_gain,
    w_in,
    conv_weight,
    conv_bias,
    dt_bias,
    a_log,
    skip_gain,
    gated_gain,
    w_out,
    w_q,
    w_k,
    w_v,
    w_o,
    mid_gain,
    w_gate,
    w_up,
    w_down,
):
    nz, ny = lax.axis_size("z"), lax.axis_size("y")
    zi, xi, yi, ci = (lax.axis_index(name) for name in ("z", "x", "y", "c"))
    length = inputs.shape[1]
    span_all = 2 * length
    rows = w_in.shape[0]
    ff_rows = w_down.shape[0]
    hidden_part = nz * ny * ff_rows
    edge_count = conv_weight.shape[0] - 1
    out_rows, o_rows = w_out.shape[0], w_o.shape[0]
    aligned = ny == 2 and nz == 4 and MAMBA_HEADS % (4 * nz) == 0
    g = nz if aligned else 1
    hp = HEADS // g

    def heads_mine(array, width):
        lead = array.shape[:-1]
        array = array.reshape(lead + (g, 2, 2, hp * width))
        array = lax.dynamic_index_in_dim(array, xi, len(lead) + 1, keepdims=False)
        array = lax.dynamic_index_in_dim(array, ci, len(lead) + 1, keepdims=False)
        return array.reshape(lead + (HEADS * width,))

    def heads_spread(array, width):
        lead = array.shape[:-1]
        array = array.reshape(lead + (g, 1, 1, hp * width))
        whole = jnp.zeros(lead + (g, 2, 2, hp * width), array.dtype)
        start = (0,) * len(lead) + (0, xi, ci, 0)
        return lax.dynamic_update_slice(whole, array, start).reshape(
            lead + (MAMBA_HEADS * width,)
        )

    def heads_split(array, width):
        n = array.shape[0]
        array = array.reshape(n, g, 2, 2, hp * width)
        return jnp.transpose(array, (2, 3, 0, 1, 4)).reshape(4, n, HEADS * width)

    def heads_join(array, width):
        n = array.shape[1]
        array = array.reshape(2, 2, n, g, hp * width)
        return jnp.transpose(array, (2, 3, 0, 1, 4)).reshape(n, MAMBA_HEADS * width)

    def reordered(array, first, second):
        width = 2 * rows
        return jnp.concatenate(
            [
                array[..., at * width : (at + 1) * width]
                for z in range(nz)
                for at in (
                    (z * first + i) * second + j for j in range(second) for i in range(first)
                )
            ],
            axis=-1,
        )

    def permuted(array):
        return reordered(array, 2, ny)

    def restored(array):
        return reordered(array, ny, 2)

    def to_ranks(array):
        return lax.all_to_all(array, GROUP, 0, 0, tiled=True)

    def in_order(own, other):
        return lax.dynamic_slice_in_dim(
            jnp.concatenate([own, other, own], 0), xi * length, span_all, 0
        )

    def gather_sequences(block):
        own, near, across, far = gather_tokens(block)
        return jnp.stack([in_order(own, across), in_order(near, far)])

    def scatter_sequences(partial):
        mine = partial[0] + swap(partial[1].astype(bf16), "c").astype(f32)
        mine = mine.reshape(2, length, mine.shape[-1])
        own = lax.dynamic_index_in_dim(mine, xi, 0, keepdims=False)
        other = lax.dynamic_index_in_dim(mine, 1 - xi, 0, keepdims=False)
        return own + swap(other.astype(bf16), "x").astype(f32)

    split_q = jnp.transpose(w_q.reshape(rows, 2, 2, 2, HEAD_DIM), (3, 1, 0, 2, 4))
    split_k = jnp.transpose(w_k.reshape(rows, 2, HEAD_DIM), (1, 0, 2))
    split_v = jnp.transpose(w_v.reshape(rows, 2, HEAD_DIM), (1, 0, 2))
    two = lambda a: jnp.broadcast_to(a[None], (2,) + a.shape).reshape(4, rows, a.shape[-1])
    packed_scan = jnp.concatenate(
        [
            heads_split(w_in[:, INNER : 2 * INNER], MAMBA_HEAD),
            jnp.broadcast_to(w_in[None, :, 2 * INNER : 2 * INNER + BC], (4, rows, BC)),
            jnp.pad(
                heads_split(w_in[:, 2 * INNER + BC :], 1), ((0, 0), (0, 0), (0, DT_PAD - HEADS))
            ),
        ],
        axis=2,
    )
    packed_rest = jnp.concatenate(
        [
            heads_split(w_in[:, :INNER], MAMBA_HEAD),
            split_q.reshape(4, rows, QP),
            two(split_k),
            two(split_v),
        ],
        axis=2,
    )

    def gathered(array):
        return lax.all_gather(array, SHARDS, axis=0, tiled=True)

    def after(array, *others):
        return lax.optimization_barrier((array,) + others)[0]

    def split_ff(w):
        w = w.reshape(rows, nz, 2, ny, 2, ff_rows)
        return jnp.transpose(w, (2, 4, 0, 1, 3, 5)).reshape(4, rows, hidden_part)

    def join_ff(w):
        w = w.reshape(2, 2, rows, nz, ny, ff_rows)
        return jnp.transpose(w, (2, 3, 0, 4, 1, 5)).reshape(rows, 4 * hidden_part)

    full_scan = gathered(to_ranks(packed_scan).reshape(4 * rows, SCAN_COLS))

    tokens = 2 * span_all
    resident = inputs[0].astype(f32)
    normed, norm_back = jax.vjp(rms_scale, resident, norm_gain)
    normed16 = gather_sequences(permuted(normed.astype(bf16)))
    edges16 = shifted(normed16[:, span_all - 8 :], 1).reshape(16, D)
    normed_rows = normed16.reshape(tokens, D)

    rest_mine = to_ranks(packed_rest).reshape(4 * rows, REST_COLS)
    if aligned:
        turn = [(2 * y + c, 2 * c + y) for y in range(2) for c in range(2)]
        place = []
        for z in range(4):
            for y in range(2):
                for c in range(2):
                    place.append(((z * 2 + y) * 2 + c, ((z % 2 * 2 + y) * 2 + c) * 2 + z // 2))
        back_place = [(b, a) for a, b in place]
        sent_out = lax.ppermute(w_out, ("y", "c"), turn)
        sent_o = lax.ppermute(w_o, ("z", "y", "c"), place)
        sent_rows = jnp.concatenate([sent_out, sent_o], 0)
    full_rest = gathered(after(rest_mine, normed_rows, edges16))
    cotangent16 = jnp.concatenate(gather_tokens(out_grad[0]), 0)

    scan_in = low_dot(normed_rows, full_scan).reshape(2, span_all, SCAN_COLS)
    edge_rows = low_dot(edges16, full_scan).reshape(2, 1, 8, SCAN_COLS)
    n = span_all // SPAN
    before = jnp.concatenate(
        [edge_rows, scan_in.reshape(2, n, SPAN, SCAN_COLS)[:, : n - 1, SPAN - 8 :]], axis=1
    )[..., :CONV_COLS]

    def rank_channels(array):
        return jnp.concatenate(
            [heads_mine(array[..., :INNER], MAMBA_HEAD), array[..., INNER:]], axis=-1
        )

    def per_head(array):
        return jnp.pad(heads_mine(array, 1), (0, DT_PAD - HEADS))[None]

    taps, bias = rank_channels(conv_weight), rank_channels(conv_bias)[None]
    dt_b, rates = per_head(dt_bias), per_head(-jnp.exp(a_log))
    skip = jnp.repeat(heads_mine(skip_gain, 1), MAMBA_HEAD)[None]
    gain = heads_mine(gated_gain, MAMBA_HEAD)[None]
    lift = (
        jnp.arange(DT_PAD, dtype=jnp.int32)[:, None]
        == jnp.arange(PART, dtype=jnp.int32)[None] // MAMBA_HEAD
    ).astype(bf16)
    mixed, steps, starts, prefix, own_state = scan_states(
        scan_in, before, taps, bias, dt_b, rates, lift
    )
    log_decay = starts[:, n - 1, 0] + steps[:, span_all - 1, DT_PAD:]
    own_decay = jnp.repeat(jnp.exp(log_decay[:, :HEADS]), MAMBA_HEAD, axis=-1)

    def turned(array, distance):
        return lax.ppermute(array, "z", [(i, (i + distance) % nz) for i in range(nz)])

    if aligned:
        first_rows = after(sent_rows, full_scan)
        along_z = jnp.stack([turned(first_rows, d) for d in range(nz - 1, 0, -1)] + [first_rows])
        along_z = lax.dynamic_slice_in_dim(
            jnp.concatenate([along_z, along_z], 0), nz - 1 - zi, nz, 0
        )
        other_y = swap(along_z, "y")
        full_rows = jnp.where(
            yi == 0, jnp.stack([along_z, other_y], 1), jnp.stack([other_y, along_z], 1)
        )
        full_out = full_rows[:, :, :out_rows].reshape(PART, D)
        full_o = full_rows[:, :, out_rows:].reshape(QP, D)
    else:
        every_out = lax.all_gather(w_out, EVERY, axis=0, tiled=True)
        every_o = lax.all_gather(w_o, EVERY, axis=0, tiled=True)
        full_out = lax.dynamic_slice_in_dim(every_out, (2 * xi + ci) * PART, PART, 0)
        every_o = every_o.reshape(2, 2, 2, HEAD_DIM, D)
        every_o = lax.dynamic_index_in_dim(every_o, xi, 2, keepdims=False)
        full_o = lax.dynamic_index_in_dim(every_o, ci, 0, keepdims=False).reshape(QP, D)

    def chained(local, step, pin=None):
        entering = []
        for s in range(2):
            held = jnp.zeros(local.shape[1:], f32)
            for hop in range(nz - 1):
                at = hop if step == 1 else nz - 1 - hop
                leaving = local[s] + own_decay[s][None] * held if hop else local[s]
                if pin is not None and hop == nz - 2:
                    leaving = after(leaving, pin)
                held = held + lax.ppermute(
                    leaving.astype(bf16), "z", [(at, at + step)]
                ).astype(f32)
            entering.append(held)
        return jnp.stack(entering)

    packed_ff = jnp.concatenate([split_ff(w_gate), split_ff(w_up)], axis=2)
    rest = low_dot(normed_rows, full_rest).reshape(2, span_all, REST_COLS)

    positions = zi * span_all + jnp.arange(span_all, dtype=jnp.int32)
    cosine, sine = rope_tables(positions)
    query16 = (
        rotate(rest[..., AT_Q:AT_K].reshape(2, span_all, 2, HEAD_DIM), cosine, sine)
        .astype(bf16)
        .reshape(2, span_all, QP)
    )
    key16 = rotate(rest[..., None, AT_K:AT_V], cosine, sine).astype(bf16)[:, :, 0]
    kv16 = jnp.stack([key16, rest[..., AT_V:].astype(bf16)])
    state_in = chained(own_state, 1, kv16)
    kv_all = jnp.concatenate([shifted(kv16, d) for d in range(nz - 1, 0, -1)] + [kv16], axis=2)
    keys_at = (zi - nz + 1) * span_all + jnp.arange(nz * span_all, dtype=jnp.int32)
    query_place = jnp.broadcast_to(positions[:, None], (span_all, 128))
    key_place = jnp.broadcast_to(keys_at[None], (8, nz * span_all))
    values, flat, square = scan_values(
        mixed, steps, starts, prefix, state_in, rest, 0, skip, lift
    )
    attended, log_sum = attend(after(query16, flat), kv_all[0], kv_all[1], query_place, key_place)
    attended16 = attended.reshape(tokens, QP).astype(bf16)

    root = lax.rsqrt(group_total(square[..., :1]) / INNER + epsilon)
    gated16 = (flat * root * gain).astype(bf16).reshape(tokens, PART)
    full_ff = gathered(
        after(to_ranks(packed_ff).reshape(4 * rows, 2 * hidden_part), mixed, cotangent16)
    )
    mixture = low_dot(gated16, full_out) + low_dot(attended16, full_o)
    hidden_state = resident + scatter_sequences(mixture.reshape(2, span_all, D))

    middle, mid_back = jax.vjp(rms_scale, hidden_state, mid_gain)
    middle16 = jnp.concatenate(gather_tokens(permuted(middle.astype(bf16))), 0)
    full_down = gathered(after(w_down, hidden_state))
    both = low_dot(middle16, full_ff)
    activated, swish_back = jax.vjp(
        swish_product, both[:, :hidden_part], both[:, hidden_part:]
    )
    activated16 = activated.astype(bf16)
    down = low_dot(activated16, full_down).reshape(4, length, D)
    output = (hidden_state + scatter_tokens(down)).astype(bf16)

    def to_owners(array):
        return lax.psum_scatter(array, SHARDS, scatter_dimension=0, tiled=True)

    down_grad = weight_grad(activated16, cotangent16).astype(bf16)
    down_owned = to_owners(down_grad)
    result_down = down_owned.astype(f32)
    gate_grad, up_grad = swish_back(back_dot(after(cotangent16, down_grad), full_down))
    both16 = jnp.concatenate([gate_grad, up_grad], axis=1).astype(bf16)
    mid_grad = restored(scatter_tokens(back_dot(both16, full_ff).reshape(4, length, D)))
    hidden_piece, mid_gain_grad = mid_back(mid_grad)
    hidden_grad = out_grad[0].astype(f32) + hidden_piece
    ff_grad = weight_grad(middle16, both16).astype(bf16)
    mix16 = gather_sequences(after(hidden_grad.astype(bf16), ff_grad)).reshape(tokens, D)
    ff_owned = to_owners(after(ff_grad, down_owned, mix16))
    ff_parts = to_ranks(ff_owned.reshape(4, rows, 2 * hidden_part))
    result_gate = join_ff(ff_parts[..., :hidden_part]).astype(f32)
    result_up = join_ff(ff_parts[..., hidden_part:]).astype(f32)
    attended_grad16 = back_dot(mix16, full_o).astype(bf16).reshape(2, span_all, QP)
    gated_grad = back_dot(mix16, full_out).reshape(2, span_all, PART)
    grad_out_w = weight_grad(gated16, mix16).astype(bf16)
    grad_o = weight_grad(attended16, mix16).astype(bf16)

    inner = jnp.sum(gated_grad * gain * flat, axis=-1, keepdims=True) * root
    inner_mean = group_total(inner) / INNER
    wide = (2, span_all, 128)
    value_grad, gate_z_grad, gain_grad, suffix, first_grad = gate_backward(
        after(gated_grad, down_owned),
        values,
        rest,
        0,
        jnp.broadcast_to(root, wide),
        jnp.broadcast_to(inner_mean, wide),
        gain,
        mixed,
        steps,
        lift,
    )
    state_grad = chained(first_grad, -1)

    query_grad, kv_grads = attend_backward(
        after(query16, first_grad),
        kv_all[0],
        kv_all[1],
        attended_grad16,
        attended,
        log_sum,
        query_place,
        key_place,
    )
    kv_grads = kv_grads.reshape(2, 2, nz, span_all, HEAD_DIM)
    kv_grad = kv_grads[:, :, nz - 1]
    for d in range(1, nz):
        kv_grad = kv_grad + shifted(kv_grads[:, :, nz - 1 - d].astype(bf16), -d).astype(f32)
    query_back = rotate(
        query_grad.reshape(2, span_all, 2, HEAD_DIM), cosine, -sine
    ).reshape(2, span_all, QP)
    key_back = rotate(kv_grad[0][:, :, None], cosine, -sine)[:, :, 0]
    rest_grad16 = jnp.concatenate(
        [
            gate_z_grad,
            query_back.astype(bf16),
            key_back.astype(bf16),
            kv_grad[1].astype(bf16),
        ],
        axis=-1,
    ).reshape(tokens, REST_COLS)

    mixed_grad, step_grad, skip_grad = scan_backward(
        mixed, steps, starts, prefix, state_in, suffix, value_grad, skip, lift
    )
    scan_grad16, edge_grad, conv_grad, small_grad = finish_backward(
        scan_in,
        before,
        mixed,
        steps,
        starts,
        prefix,
        state_in,
        after(state_grad, ff_owned),
        mixed_grad,
        step_grad,
        taps,
        bias,
        dt_b,
        rates,
        lift,
    )
    edge_back = shifted(edge_grad[:, 8 - edge_count :].astype(bf16), -1).astype(f32)
    last_rows = scan_grad16[:, span_all - edge_count :, :CONV_COLS].astype(f32) + edge_back
    scan_grad16 = lax.dynamic_update_slice(
        scan_grad16, last_rows.astype(bf16), (0, span_all - edge_count, 0)
    ).reshape(tokens, SCAN_COLS)
    if aligned:
        rows_grad = jnp.concatenate(
            [grad_out_w.reshape(nz, 2, out_rows, D), grad_o.reshape(nz, 2, o_rows, D)], axis=2
        )
        other_y = lax.dynamic_index_in_dim(rows_grad, 1 - yi, 1, keepdims=False)
        both_y = lax.dynamic_index_in_dim(rows_grad, yi, 1, keepdims=False).astype(f32) + swap(
            other_y, "y"
        ).astype(f32)
        rows_owned = lax.dynamic_index_in_dim(both_y, zi, 0, keepdims=False)
        for d in range(1, nz):
            leaving = lax.dynamic_index_in_dim(both_y, (zi + d) % nz, 0, keepdims=False)
            rows_owned = rows_owned + turned(leaving.astype(bf16), d).astype(f32)
        rows_owned = rows_owned.astype(bf16)
        result_out = lax.ppermute(rows_owned[:out_rows], ("y", "c"), turn).astype(f32)
        result_o = lax.ppermute(rows_owned[out_rows:], ("z", "y", "c"), back_place).astype(f32)
    else:
        every_out = lax.dynamic_update_slice_in_dim(
            jnp.zeros((INNER, D), bf16), grad_out_w, (2 * xi + ci) * PART, 0
        )
        every_o = lax.dynamic_update_slice(
            jnp.zeros((2, 2, 2, HEAD_DIM, D), bf16),
            grad_o.reshape(1, 2, 1, HEAD_DIM, D),
            (ci, 0, xi, 0, 0),
        ).reshape(ATT_HEADS * HEAD_DIM, D)
        result_out = lax.psum_scatter(every_out, EVERY, scatter_dimension=0, tiled=True)
        result_o = lax.psum_scatter(every_o, EVERY, scatter_dimension=0, tiled=True)
        result_out, result_o = result_out.astype(f32), result_o.astype(f32)
    rest_owned = to_owners(
        after(weight_grad(normed_rows, rest_grad16).astype(bf16), ff_owned, mixed_grad)
    )
    rest_parts = to_ranks(rest_owned.reshape(4, rows, REST_COLS)).astype(f32)
    scan_owned = to_owners(
        after(weight_grad(normed_rows, scan_grad16).astype(bf16), rest_owned)
    )
    scan_parts = to_ranks(scan_owned.reshape(4, rows, SCAN_COLS)).astype(f32)

    normed_grad = back_dot(scan_grad16, full_scan) + back_dot(rest_grad16, full_rest)
    normed_grad = restored(scatter_sequences(normed_grad.reshape(2, span_all, D)))
    resident_grad, norm_gain_grad = norm_back(normed_grad)
    input_grad = hidden_grad + resident_grad

    result_in = jnp.concatenate(
        [
            heads_join(rest_parts[..., :PART], MAMBA_HEAD),
            heads_join(scan_parts[..., :PART], MAMBA_HEAD),
            jnp.sum(scan_parts[..., PART:CONV_COLS], axis=0),
            heads_join(scan_parts[..., CONV_COLS : CONV_COLS + HEADS], 1),
        ],
        axis=1,
    )
    result_q = jnp.transpose(
        rest_parts[..., AT_Q:AT_K].reshape(2, 2, rows, 2, HEAD_DIM), (2, 1, 3, 0, 4)
    ).reshape(rows, ATT_HEADS * HEAD_DIM)
    kv_parts = jnp.sum(rest_parts[..., AT_K:].reshape(2, 2, rows, 2, HEAD_DIM), axis=0)
    result_k = jnp.transpose(kv_parts[:, :, 0], (1, 0, 2)).reshape(rows, KV_HEADS * HEAD_DIM)
    result_v = jnp.transpose(kv_parts[:, :, 1], (1, 0, 2)).reshape(rows, KV_HEADS * HEAD_DIM)

    def all_channels(array):
        return jnp.concatenate(
            [heads_spread(array[..., :PART], MAMBA_HEAD), array[..., PART:]], axis=-1
        )

    small = [
        norm_gain_grad,
        all_channels(conv_grad[:4]),
        all_channels(conv_grad[4]),
        heads_spread(small_grad[0, :HEADS], 1),
        heads_spread(small_grad[1, :HEADS], 1),
        heads_spread(skip_grad[0, :HEADS], 1),
        heads_spread(gain_grad[0], MAMBA_HEAD),
        mid_gain_grad,
    ]
    summed = total(jnp.concatenate([v.reshape(-1) for v in small]))
    parts, at = [], 0
    for v in small:
        parts.append(summed[at : at + v.size].reshape(v.shape))
        at += v.size
    return (
        output[None],
        input_grad[None],
        parts[0],
        result_in,
        parts[1],
        parts[2],
        parts[3],
        parts[4],
        parts[5],
        parts[6],
        result_out,
        result_q,
        result_k,
        result_v,
        result_o,
        parts[7],
        result_gate,
        result_up,
        result_down,
    )


def solution(mesh):
    seq, fsdp = mesh.shape["seq"], mesh.shape["fsdp"]
    split = Mesh(mesh.devices.reshape(seq // 2, 2, fsdp // 2, 2), EVERY)
    tokens = P(("y", "c"), ("z", "x"), None)
    matrix = P(EVERY, None)
    return jax.shard_map(
        body,
        mesh=split,
        in_specs=(tokens, tokens, P(), matrix)
        + (P(),) * 6
        + (matrix,) * 5
        + (P(),)
        + (matrix,) * 3,
        out_specs=(tokens, tokens, P(), matrix)
        + (P(),) * 6
        + (matrix,) * 5
        + (P(),)
        + (matrix,) * 3,
        check_vma=False,
    )
```

```python
import jax
import jax.numpy as jnp
from jax import lax
from jax.experimental import pallas as pl
from jax.experimental.pallas import tpu as pltpu
from jax.sharding import Mesh
from jax.sharding import PartitionSpec as P

D = 2048
MAMBA_HEADS = 48
MAMBA_HEAD = 64
STATE = 256
ATT_HEADS = 8
KV_HEADS = 2
HEAD_DIM = 128
SPAN = 128
INNER = 3072

HEADS = MAMBA_HEADS // 4
PART = HEADS * MAMBA_HEAD
BC = 2 * STATE
DT_PAD = 128
QP = 2 * HEAD_DIM
CONV_COLS = PART + BC
SCAN_COLS = CONV_COLS + DT_PAD
AT_Q = PART
AT_K = AT_Q + QP
AT_V = AT_K + HEAD_DIM
REST_COLS = AT_V + HEAD_DIM

epsilon = 1e-05
rope_base = 100000000000.0
GROUP = ("x", "c")
SHARDS = ("z", "y")
EVERY = ("z", "x", "y", "c")
bf16 = jnp.bfloat16
f32 = jnp.float32


def swap(array, axis):
    return lax.ppermute(array, axis, [(0, 1), (1, 0)])


def shifted(array, distance):
    devices = range(lax.axis_size("z"))
    return lax.ppermute(array, "z", [(i - distance, i) for i in devices if i - distance in devices])


def total(array):
    for axis in EVERY:
        size = lax.axis_size(axis)
        bit = 1
        while bit < size:
            array = array + lax.ppermute(array, axis, [(i, i ^ bit) for i in range(size)])
            bit *= 2
    return array


def group_total(array):
    array = array + swap(array[::-1], "c")
    return array + swap(array, "x")


def low_dot(left, right):
    return jnp.dot(left, right, preferred_element_type=f32)


def back_dot(grad_rows, weight):
    return lax.dot_general(grad_rows, weight, (((1,), (1,)), ((), ())), preferred_element_type=f32)


def weight_grad(left, right):
    return lax.dot_general(left, right, (((0,), (0,)), ((), ())), preferred_element_type=f32)


def rms_scale(values, gain):
    return values * lax.rsqrt(jnp.mean(values * values, axis=-1, keepdims=True) + epsilon) * gain


def rope_tables(positions):
    half_dim = HEAD_DIM // 2
    frequencies = rope_base ** (-jnp.arange(half_dim, dtype=f32) / half_dim)
    angles = positions.astype(f32)[:, None] * frequencies[None, :]
    return (jnp.cos(angles), jnp.sin(angles))


def rotate(values, cosine, sine):
    half_dim = HEAD_DIM // 2
    cosine, sine = cosine[:, None, :], sine[:, None, :]
    first, second = values[..., :half_dim], values[..., half_dim:]
    return jnp.concatenate([first * cosine - second * sine, second * cosine + first * sine], axis=-1)


def pieces(values, count):
    parts = []
    for _ in range(count):
        part = values.astype(bf16)
        parts.append(part)
        values = values - part.astype(f32)
    return parts


def running(mask, values):
    mask16 = mask.astype(bf16)
    return sum(low_dot(mask16, part) for part in pieces(values, 3))


def over_lanes(left, right):
    return lax.dot_general(left, right, (((1,), (1,)), ((), ())), preferred_element_type=f32)


def over_rows(left, right):
    return lax.dot_general(left, right, (((0,), (0,)), ((), ())), preferred_element_type=f32)


def widen(values, lift):
    return sum(low_dot(part, lift) for part in pieces(values, 2))


def narrow(values, lift):
    return sum(over_lanes(part, lift) for part in pieces(values, 2))


def sig(values):
    return 1.0 / (1.0 + jnp.exp(-values))


def soft(values):
    return jnp.maximum(values, 0.0) + jnp.log1p(jnp.exp(-jnp.abs(values)))


def square_places():
    return (
        lax.broadcasted_iota(jnp.int32, (SPAN, SPAN), 0),
        lax.broadcasted_iota(jnp.int32, (SPAN, SPAN), 1),
    )


def pre_conv(current, before, taps, bias):
    extended = jnp.concatenate([before, current], axis=0)
    pre = bias + extended[5 : 5 + SPAN] * taps[0:1]
    for k in range(1, 4):
        pre = pre + extended[5 + k : 5 + k + SPAN] * taps[k : k + 1]
    return (pre, extended)


def states_kernel(
    scan_in, before, taps, bias, dt_bias, rates, lift, mixed, steps, starts, prefix, last, held, sofar
):
    @pl.when(pl.program_id(1) == 0)
    def _():
        held[...] = jnp.zeros_like(held)
        sofar[...] = jnp.zeros_like(sofar)

    pre, _ = pre_conv(scan_in[0, :, :CONV_COLS], before[0, 0], taps[...], bias[...])
    mix = pre * sig(pre)
    mixed[0] = mix
    dt = soft(scan_in[0, :, CONV_COLS:] + dt_bias[...])
    row, column = square_places()
    cum = running(jnp.where(row >= column, 1.0, 0.0), dt * rates[...])
    steps[0, :, :DT_PAD] = dt
    steps[0, :, DT_PAD:] = cum
    starts[0, 0] = sofar[...]
    prefix[0, 0] = held[...]
    end = cum[SPAN - 1 : SPAN]
    tail = jnp.exp(end - cum) * dt
    fed = (mix[:, :PART] * widen(tail, lift[...])).astype(bf16)
    added = over_rows(mix[:, PART : PART + STATE].astype(bf16), fed)
    whole = widen(jnp.broadcast_to(jnp.exp(end), (8, DT_PAD)), lift[...])[0:1]
    held[...] = whole * held[...] + added
    sofar[...] = sofar[...] + end
    last[0] = held[...]


def values_kernel(
    mixed, steps, starts, prefix, state_in, gate, skip, lift, values, flat, square
):
    x = mixed[0, :, :PART]
    b16 = mixed[0, :, PART : PART + STATE].astype(bf16)
    c16 = mixed[0, :, PART + STATE :].astype(bf16)
    dt = steps[0, :, :DT_PAD]
    cum = steps[0, :, DT_PAD:]
    dt_t, cum_t = dt.T, cum.T
    state = prefix[0, 0] + widen(jnp.exp(starts[0, 0]), lift[...])[0:1] * state_in[0]
    meet = over_lanes(c16, b16)
    carried = low_dot(c16, state.astype(bf16)) * widen(jnp.exp(cum), lift[...])
    row, column = square_places()
    first = column < MAMBA_HEAD
    inside = []
    for k in range(HEADS // 2):
        pair = x[:, 2 * MAMBA_HEAD * k : 2 * MAMBA_HEAD * (k + 1)]
        weights = []
        for h in (2 * k, 2 * k + 1):
            spread = cum[:, h : h + 1] - cum_t[h : h + 1, :]
            decay = jnp.exp(jnp.where(row >= column, spread, -1e30))
            weights.append((meet * decay * dt_t[h : h + 1, :]).astype(bf16))
        split = [
            jnp.where(first, pair, 0.0).astype(bf16),
            jnp.where(first, 0.0, pair).astype(bf16),
        ]
        inside.append(low_dot(jnp.concatenate(weights, 1), jnp.concatenate(split, 0)))
    value = jnp.concatenate(inside, 1) + carried + skip[...] * x
    values[0] = value
    z = gate[0]
    product = value * (z * sig(z))
    flat[0] = product
    square[0] = jnp.broadcast_to(
        jnp.sum(product * product, axis=1, keepdims=True), (SPAN, 128)
    )


def gate_back_kernel(
    gated_grad, values, gate, root, mean, gain, c_part, steps, lift,
    value_grad, gate_grad, gain_grad, suffix, first_grad, held,
):
    @pl.when(pl.program_id(1) == 0)
    def _():
        held[...] = jnp.zeros_like(held)

    @pl.when((pl.program_id(0) == 0) & (pl.program_id(1) == 0))
    def _():
        gain_grad[...] = jnp.zeros_like(gain_grad)

    z, value, grad = gate[0], values[0], gated_grad[0]
    s = sig(z)
    silu = z * s
    scale = root[0, :, 0:1]
    normal = value * silu * scale
    flat_grad = scale * (grad * gain[...] - normal * mean[0, :, 0:1])
    d_value = flat_grad * silu
    value_grad[0] = d_value
    gate_grad[0] = (flat_grad * value * (s * (1.0 + z * (1.0 - s)))).astype(bf16)
    gain_grad[0:1] = gain_grad[0:1] + jnp.sum(grad * normal, axis=0, keepdims=True)
    grown = widen(jnp.exp(steps[0, :, DT_PAD:]), lift[...])
    suffix[0, 0] = held[...]
    held[...] = grown[SPAN - 1 : SPAN] * held[...] + over_rows(
        c_part[0].astype(bf16), (grown * d_value).astype(bf16)
    )
    first_grad[0] = held[...]


def scan_back_kernel(
    mixed, steps, starts, prefix, state_in, suffix, value_grad, skip, lift,
    mixed_grad, step_grad, skip_grad, columns,
):
    @pl.when((pl.program_id(0) == 0) & (pl.program_id(1) == 0))
    def _():
        skip_grad[...] = jnp.zeros_like(skip_grad)
        columns[...] = jnp.zeros_like(columns)

    up = lift[...]
    x = mixed[0, :, :PART]
    b16 = mixed[0, :, PART : PART + STATE].astype(bf16)
    c16 = mixed[0, :, PART + STATE :].astype(bf16)
    dt = steps[0, :, :DT_PAD]
    cum = steps[0, :, DT_PAD:]
    dt_t, cum_t = dt.T, cum.T
    end = cum[SPAN - 1 : SPAN]
    dy = value_grad[0]
    state = prefix[0, 0] + widen(jnp.exp(starts[0, 0]), up)[0:1] * state_in[0]
    ending = suffix[0, 0]
    state16, ending16 = state.astype(bf16), ending.astype(bf16)
    grown_dy = widen(jnp.exp(cum), up) * dy
    tail_wide = widen(jnp.exp(end - cum), up)
    dt_wide = widen(dt, up)
    reach = low_dot(c16, state16)
    pull = tail_wide * low_dot(b16, ending16)
    d_c = over_lanes(grown_dy.astype(bf16), state16)
    d_b = over_lanes((tail_wide * dt_wide * x).astype(bf16), ending16)
    meet = over_lanes(c16, b16)
    row, column = square_places()
    first = column < MAMBA_HEAD
    d_meet = jnp.zeros((SPAN, SPAN), f32)
    rows_sum = jnp.zeros((SPAN, DT_PAD), f32)
    back = []
    for k in range(HEADS // 2):
        at = slice(2 * MAMBA_HEAD * k, 2 * MAMBA_HEAD * (k + 1))
        x16, dy_pair = x[:, at].astype(bf16), dy[:, at]
        split = [
            jnp.where(first, dy_pair, 0.0).astype(bf16),
            jnp.where(first, 0.0, dy_pair).astype(bf16),
        ]
        weights = []
        for j in range(2):
            h = 2 * k + j
            spread = cum[:, h : h + 1] - cum_t[h : h + 1, :]
            decay = jnp.exp(jnp.where(row >= column, spread, -1e30))
            d_weight = over_lanes(split[j], x16) * decay
            scaled = d_weight * dt_t[h : h + 1, :]
            d_meet = d_meet + scaled
            rows_sum = rows_sum + jnp.where(
                column == h, jnp.sum(scaled * meet, axis=1, keepdims=True), 0.0
            )
            columns[h : h + 1, :] = jnp.sum(d_weight * meet, axis=0, keepdims=True)
            weights.append((meet * decay).astype(bf16))
        back.append(over_rows(jnp.concatenate(weights, 0), jnp.concatenate(split, 0)))
    d_meet16 = d_meet.astype(bf16)
    mixed_grad[0, :, :PART] = dt_wide * (jnp.concatenate(back, 1) + pull) + skip[...] * dy
    mixed_grad[0, :, PART : PART + STATE] = d_b + over_rows(d_meet16, c16)
    mixed_grad[0, :, PART + STATE :] = d_c + low_dot(d_meet16, b16)
    tail_dt = narrow(x * pull, up)
    inner_dt = columns[...].T
    d_cum = rows_sum + narrow(grown_dy * reach, up) - dt * (inner_dt + tail_dt)
    kept = narrow(
        jnp.broadcast_to(jnp.sum(state * ending, axis=0, keepdims=True), (8, PART)), up
    )[0:1]
    extra = jnp.sum(dt * tail_dt, axis=0, keepdims=True) + jnp.exp(end) * kept
    step_grad[0, :, :DT_PAD] = inner_dt + tail_dt
    step_grad[0, :, DT_PAD:] = running(jnp.where(row <= column, 1.0, 0.0), d_cum) + extra
    skip_grad[0:1] = skip_grad[0:1] + jnp.sum(narrow(dy * x, up), axis=0, keepdims=True)


def finish_back_kernel(
    scan_in, before, mixed, steps, starts, prefix, state_in, state_grad, mixed_grad, step_grad,
    taps, bias, dt_bias, rates, lift,
    scan_grad, edge_grad, conv_grad, small_grad,
    later, after_pre,
):
    @pl.when(pl.program_id(1) == 0)
    def _():
        later[...] = jnp.zeros_like(later)
        after_pre[...] = jnp.zeros_like(after_pre)

    @pl.when((pl.program_id(0) == 0) & (pl.program_id(1) == 0))
    def _():
        conv_grad[...] = jnp.zeros_like(conv_grad)
        small_grad[...] = jnp.zeros_like(small_grad)

    up = lift[...]
    x = mixed[0, :, :PART]
    b16 = mixed[0, :, PART : PART + STATE].astype(bf16)
    dt = steps[0, :, :DT_PAD]
    cum = steps[0, :, DT_PAD:]
    end = cum[SPAN - 1 : SPAN]
    state = prefix[0, 0] + widen(jnp.exp(starts[0, 0]), up)[0:1] * state_in[0]
    ending = widen(jnp.exp(later[...]), up)[0:1] * state_grad[0]
    later[...] = later[...] + end
    ending16 = ending.astype(bf16)
    tail_wide = widen(jnp.exp(end - cum), up)
    dt_wide = widen(dt, up)
    pull = tail_wide * low_dot(b16, ending16)
    d_x = mixed_grad[0, :, :PART] + dt_wide * pull
    d_b = mixed_grad[0, :, PART : PART + STATE] + over_lanes(
        (tail_wide * dt_wide * x).astype(bf16), ending16
    )
    d_c = mixed_grad[0, :, PART + STATE :]
    tail_dt = narrow(x * pull, up)
    kept = narrow(
        jnp.broadcast_to(jnp.sum(state * ending, axis=0, keepdims=True), (8, PART)), up
    )[0:1]
    row, column = square_places()
    fed = dt * tail_dt
    earlier = running(jnp.where(row > column, 1.0, 0.0), fed)
    d_log = step_grad[0, :, DT_PAD:] + earlier + jnp.exp(end) * kept
    rate = rates[...]
    d_raw = (step_grad[0, :, :DT_PAD] + tail_dt + d_log * rate) * sig(
        scan_in[0, :, CONV_COLS:] + dt_bias[...]
    )
    small_grad[0:1] = small_grad[0:1] + jnp.sum(d_raw, axis=0, keepdims=True)
    small_grad[1:2] = small_grad[1:2] + jnp.sum(d_log * dt * rate, axis=0, keepdims=True)

    pre, extended = pre_conv(scan_in[0, :, :CONV_COLS], before[0, 0], taps[...], bias[...])
    s = sig(pre)
    d_pre = jnp.concatenate([d_x, d_b, d_c], axis=1) * (s * (1.0 + pre * (1.0 - s)))
    for k in range(4):
        conv_grad[k : k + 1] = conv_grad[k : k + 1] + jnp.sum(
            d_pre * extended[5 + k : 5 + k + SPAN], axis=0, keepdims=True
        )
    conv_grad[4:5] = conv_grad[4:5] + jnp.sum(d_pre, axis=0, keepdims=True)
    following = jnp.concatenate([d_pre, after_pre[...]], axis=0)
    d_in = following[0:SPAN] * taps[3:4]
    for k in range(3):
        d_in = d_in + following[3 - k : 3 - k + SPAN] * taps[k : k + 1]
    scan_grad[0, :, :CONV_COLS] = d_in.astype(bf16)
    scan_grad[0, :, CONV_COLS:] = d_raw.astype(bf16)
    front = d_pre[0:8]
    after_pre[...] = front
    nothing = jnp.zeros((8, CONV_COLS), f32)
    padded = jnp.concatenate([nothing, front, nothing], 0)
    edge = padded[0:8] * taps[3:4]
    for k in range(3):
        edge = edge + padded[3 - k : 11 - k] * taps[k : k + 1]
    edge_grad[0] = edge


def one(shape):
    return pl.BlockSpec(shape, lambda b, i: (0,) * len(shape))


def by_span(width, column=0, reverse=None):
    if reverse is None:
        return pl.BlockSpec((1, SPAN, width), lambda b, i: (b, i, column))
    return pl.BlockSpec((1, SPAN, width), lambda b, i: (b, reverse - 1 - i, column))


def by_piece(rows, width, reverse=None):
    if reverse is None:
        return pl.BlockSpec((1, 1, rows, width), lambda b, i: (b, i, 0, 0))
    return pl.BlockSpec((1, 1, rows, width), lambda b, i: (b, reverse - 1 - i, 0, 0))


def by_sequence(rows, width):
    return pl.BlockSpec((1, rows, width), lambda b, i: (b, 0, 0))


def grid_call(kernel, spans, ins, outs, scratch, flops, moved):
    return pl.pallas_call(
        kernel,
        grid=(2, spans),
        in_specs=ins,
        out_specs=[spec for spec, _ in outs],
        out_shape=[shape for _, shape in outs],
        scratch_shapes=scratch,
        compiler_params=pltpu.CompilerParams(
            dimension_semantics=("arbitrary", "arbitrary"), vmem_limit_bytes=50 * 2**20
        ),
        cost_estimate=pl.CostEstimate(flops=flops, bytes_accessed=moved, transcendentals=0),
    )


def like(shape, kind=f32):
    return jax.ShapeDtypeStruct(shape, kind)


def scan_states(scan_in, before, taps, bias, dt_bias, rates, lift):
    length = scan_in.shape[1]
    n = length // SPAN
    return grid_call(
        states_kernel,
        n,
        [
            by_span(SCAN_COLS),
            by_piece(8, CONV_COLS),
            one((4, CONV_COLS)),
            one((1, CONV_COLS)),
            one((1, DT_PAD)),
            one((1, DT_PAD)),
            one((DT_PAD, PART)),
        ],
        [
            (by_span(CONV_COLS), like((2, length, CONV_COLS))),
            (by_span(2 * DT_PAD), like((2, length, 2 * DT_PAD))),
            (by_piece(8, DT_PAD), like((2, n, 8, DT_PAD))),
            (by_piece(STATE, PART), like((2, n, STATE, PART))),
            (by_sequence(STATE, PART), like((2, STATE, PART))),
        ],
        [pltpu.VMEM((STATE, PART), f32), pltpu.VMEM((8, DT_PAD), f32)],
        8 * 10**9,
        30 * 10**6,
    )(scan_in, before, taps, bias, dt_bias, rates, lift)


def scan_values(mixed, steps, starts, prefix, state_in, rest, gate_at, skip, lift):
    length = mixed.shape[1]
    n = length // SPAN
    return grid_call(
        values_kernel,
        n,
        [
            by_span(CONV_COLS),
            by_span(2 * DT_PAD),
            by_piece(8, DT_PAD),
            by_piece(STATE, PART),
            by_sequence(STATE, PART),
            by_span(PART, gate_at),
            one((1, PART)),
            one((DT_PAD, PART)),
        ],
        [
            (by_span(PART), like((2, length, PART))),
            (by_span(PART), like((2, length, PART))),
            (by_span(128), like((2, length, 128))),
        ],
        [],
        12 * 10**9,
        30 * 10**6,
    )(mixed, steps, starts, prefix, state_in, rest, skip, lift)


def gate_backward(gated_grad, values, rest, gate_at, root, mean, gain, mixed, steps, lift):
    length = mixed.shape[1]
    n = length // SPAN
    return grid_call(
        gate_back_kernel,
        n,
        [
            by_span(PART, 0, n),
            by_span(PART, 0, n),
            by_span(PART, gate_at, n),
            by_span(128, 0, n),
            by_span(128, 0, n),
            one((1, PART)),
            by_span(STATE, (PART + STATE) // STATE, n),
            by_span(2 * DT_PAD, 0, n),
            one((DT_PAD, PART)),
        ],
        [
            (by_span(PART, 0, n), like((2, length, PART))),
            (by_span(PART, 0, n), like((2, length, PART), bf16)),
            (one((8, PART)), like((8, PART))),
            (by_piece(STATE, PART, n), like((2, n, STATE, PART))),
            (by_sequence(STATE, PART), like((2, STATE, PART))),
        ],
        [pltpu.VMEM((STATE, PART), f32)],
        8 * 10**9,
        30 * 10**6,
    )(gated_grad, values, rest, root, mean, gain, mixed, steps, lift)


def scan_backward(mixed, steps, starts, prefix, state_in, suffix, value_grad, skip, lift):
    length = mixed.shape[1]
    n = length // SPAN
    return grid_call(
        scan_back_kernel,
        n,
        [
            by_span(CONV_COLS),
            by_span(2 * DT_PAD),
            by_piece(8, DT_PAD),
            by_piece(STATE, PART),
            by_sequence(STATE, PART),
            by_piece(STATE, PART),
            by_span(PART),
            one((1, PART)),
            one((DT_PAD, PART)),
        ],
        [
            (by_span(CONV_COLS), like((2, length, CONV_COLS))),
            (by_span(2 * DT_PAD), like((2, length, 2 * DT_PAD))),
            (one((8, DT_PAD)), like((8, DT_PAD))),
        ],
        [pltpu.VMEM((SPAN, SPAN), f32)],
        30 * 10**9,
        40 * 10**6,
    )(mixed, steps, starts, prefix, state_in, suffix, value_grad, skip, lift)


def finish_backward(
    scan_in, before, mixed, steps, starts, prefix, state_in, state_grad, mixed_grad, step_grad,
    taps, bias, dt_bias, rates, lift,
):
    length = mixed.shape[1]
    n = length // SPAN
    return grid_call(
        finish_back_kernel,
        n,
        [
            by_span(SCAN_COLS, 0, n),
            by_piece(8, CONV_COLS, n),
            by_span(CONV_COLS, 0, n),
            by_span(2 * DT_PAD, 0, n),
            by_piece(8, DT_PAD, n),
            by_piece(STATE, PART, n),
            by_sequence(STATE, PART),
            by_sequence(STATE, PART),
            by_span(CONV_COLS, 0, n),
            by_span(2 * DT_PAD, 0, n),
            one((4, CONV_COLS)),
            one((1, CONV_COLS)),
            one((1, DT_PAD)),
            one((1, DT_PAD)),
            one((DT_PAD, PART)),
        ],
        [
            (by_span(SCAN_COLS, 0, n), like((2, length, SCAN_COLS), bf16)),
            (by_sequence(8, CONV_COLS), like((2, 8, CONV_COLS))),
            (one((8, CONV_COLS)), like((8, CONV_COLS))),
            (one((8, DT_PAD)), like((8, DT_PAD))),
        ],
        [pltpu.VMEM((8, DT_PAD), f32), pltpu.VMEM((8, CONV_COLS), f32)],
        15 * 10**9,
        50 * 10**6,
    )(
        scan_in, before, mixed, steps, starts, prefix, state_in, state_grad, mixed_grad, step_grad,
        taps, bias, dt_bias, rates, lift,
    )


def attend_kernel(query, key, value, query_place, key_place, attended, log_sum):
    scores = over_lanes(query[0], key[0]) * HEAD_DIM ** (-0.5)
    seen = (key_place[0:1] >= 0) & (query_place[:, 0:1] >= key_place[0:1])
    scores = jnp.where(seen, scores, -1e30)
    peak = jnp.max(scores, axis=1, keepdims=True)
    unscaled = jnp.exp(scores - peak)
    whole = jnp.sum(unscaled, axis=1, keepdims=True)
    probs = (unscaled * (1.0 / whole)).astype(bf16)
    attended[0] = low_dot(probs, value[0])
    log_sum[0] = jnp.broadcast_to(peak + jnp.log(whole), log_sum.shape[1:])


def attend_back_kernel(
    query, key, value, grad, attended, log_sum, query_place, key_place, query_grad, kv_grad
):
    @pl.when((pl.program_id(1) == 0) & (pl.program_id(2) == 0))
    def _():
        kv_grad[...] = jnp.zeros_like(kv_grad)

    scale = HEAD_DIM ** (-0.5)
    scores = over_lanes(query[0], key[0]) * scale
    seen = (key_place[0:1] >= 0) & (query_place[:, 0:1] >= key_place[0:1])
    probs = jnp.exp(jnp.where(seen, scores, -1e30) - log_sum[0, :, 0:1])
    delta = jnp.sum(grad[0].astype(f32) * attended[0], axis=1, keepdims=True)
    score_grad = (probs * (over_lanes(grad[0], value[0]) - delta)).astype(bf16)
    query_grad[0] = low_dot(score_grad, key[0]) * scale
    kv_grad[0, 0] = kv_grad[0, 0] + over_rows(score_grad, query[0]) * scale
    kv_grad[1, 0] = kv_grad[1, 0] + over_rows(probs.astype(bf16), grad[0])


def attend_specs(block, keys):
    by_query = pl.BlockSpec((1, block, HEAD_DIM), lambda b, h, i: (b, i, h))
    whole_key = pl.BlockSpec((1, keys, HEAD_DIM), lambda b, h, i: (b, 0, 0))
    place = pl.BlockSpec((block, 128), lambda b, h, i: (i, 0))
    key_at = pl.BlockSpec((8, keys), lambda b, h, i: (0, 0))
    return (by_query, whole_key, place, key_at)


def attend(query, key, value, query_place, key_place):
    length, keys = query.shape[1], key.shape[1]
    block = 256 if keys <= 4096 else 128
    by_query, whole_key, place, key_at = attend_specs(block, keys)
    return pl.pallas_call(
        attend_kernel,
        grid=(2, 2, length // block),
        in_specs=[by_query, whole_key, whole_key, place, key_at],
        out_specs=[by_query, by_query],
        out_shape=[like((2, length, QP)), like((2, length, QP))],
        compiler_params=pltpu.CompilerParams(
            dimension_semantics=("arbitrary",) * 3, vmem_limit_bytes=50 * 2**20
        ),
        cost_estimate=pl.CostEstimate(
            flops=12 * 10**9, bytes_accessed=20 * 10**6, transcendentals=0
        ),
    )(query, key, value, query_place, key_place)


def attend_backward(query, key, value, grad, attended, log_sum, query_place, key_place):
    length, keys = query.shape[1], key.shape[1]
    block = 256 if keys <= 4096 else 128
    by_query, whole_key, place, key_at = attend_specs(block, keys)
    return pl.pallas_call(
        attend_back_kernel,
        grid=(2, 2, length // block),
        in_specs=[by_query, whole_key, whole_key, by_query, by_query, by_query, place, key_at],
        out_specs=[
            by_query,
            pl.BlockSpec((2, 1, keys, HEAD_DIM), lambda b, h, i: (0, b, 0, 0)),
        ],
        out_shape=[like((2, length, QP)), like((2, 2, keys, HEAD_DIM))],
        compiler_params=pltpu.CompilerParams(
            dimension_semantics=("arbitrary",) * 3, vmem_limit_bytes=50 * 2**20
        ),
        cost_estimate=pl.CostEstimate(
            flops=20 * 10**9, bytes_accessed=30 * 10**6, transcendentals=0
        ),
    )(query, key, value, grad, attended, log_sum, query_place, key_place)


def swish_product(gate_proj, up_proj):
    return jax.nn.silu(gate_proj) * up_proj


def gather_tokens(block):
    across = swap(block, "x")
    return (block, swap(block, "c"), across, swap(across, "c"))


def scatter_tokens(blocks):
    near, far = blocks[0], blocks[2]
    sent = swap(jnp.stack([blocks[1].astype(bf16), blocks[3].astype(bf16)]), "c")
    near = near + sent[0].astype(f32)
    far = far + sent[1].astype(f32)
    return near + swap(far.astype(bf16), "x").astype(f32)


def body(
    inputs,
    out_grad,
    norm_gain,
    w_in,
    conv_weight,
    conv_bias,
    dt_bias,
    a_log,
    skip_gain,
    gated_gain,
    w_out,
    w_q,
    w_k,
    w_v,
    w_o,
    mid_gain,
    w_gate,
    w_up,
    w_down,
):
    nz, ny = lax.axis_size("z"), lax.axis_size("y")
    zi, xi, yi, ci = (lax.axis_index(name) for name in ("z", "x", "y", "c"))
    length = inputs.shape[1]
    span_all = 2 * length
    rows = w_in.shape[0]
    ff_rows = w_down.shape[0]
    hidden_part = nz * ny * ff_rows
    edge_count = conv_weight.shape[0] - 1
    out_rows, o_rows = w_out.shape[0], w_o.shape[0]
    aligned = ny == 2 and nz == 4 and MAMBA_HEADS % (4 * nz) == 0
    g = nz if aligned else 1
    hp = HEADS // g

    def heads_mine(array, width):
        lead = array.shape[:-1]
        array = array.reshape(lead + (g, 2, 2, hp * width))
        array = lax.dynamic_index_in_dim(array, xi, len(lead) + 1, keepdims=False)
        array = lax.dynamic_index_in_dim(array, ci, len(lead) + 1, keepdims=False)
        return array.reshape(lead + (HEADS * width,))

    def heads_spread(array, width):
        lead = array.shape[:-1]
        array = array.reshape(lead + (g, 1, 1, hp * width))
        whole = jnp.zeros(lead + (g, 2, 2, hp * width), array.dtype)
        start = (0,) * len(lead) + (0, xi, ci, 0)
        return lax.dynamic_update_slice(whole, array, start).reshape(
            lead + (MAMBA_HEADS * width,)
        )

    def heads_split(array, width):
        n = array.shape[0]
        array = array.reshape(n, g, 2, 2, hp * width)
        return jnp.transpose(array, (2, 3, 0, 1, 4)).reshape(4, n, HEADS * width)

    def heads_join(array, width):
        n = array.shape[1]
        array = array.reshape(2, 2, n, g, hp * width)
        return jnp.transpose(array, (2, 3, 0, 1, 4)).reshape(n, MAMBA_HEADS * width)

    def reordered(array, first, second):
        width = 2 * rows
        return jnp.concatenate(
            [
                array[..., at * width : (at + 1) * width]
                for z in range(nz)
                for at in (
                    (z * first + i) * second + j for j in range(second) for i in range(first)
                )
            ],
            axis=-1,
        )

    def permuted(array):
        return reordered(array, 2, ny)

    def restored(array):
        return reordered(array, ny, 2)

    def to_ranks(array):
        return lax.all_to_all(array, GROUP, 0, 0, tiled=True)

    def in_order(own, other):
        return lax.dynamic_slice_in_dim(
            jnp.concatenate([own, other, own], 0), xi * length, span_all, 0
        )

    def gather_sequences(block):
        own, near, across, far = gather_tokens(block)
        return jnp.stack([in_order(own, across), in_order(near, far)])

    def scatter_sequences(partial):
        mine = partial[0] + swap(partial[1].astype(bf16), "c").astype(f32)
        mine = mine.reshape(2, length, mine.shape[-1])
        own = lax.dynamic_index_in_dim(mine, xi, 0, keepdims=False)
        other = lax.dynamic_index_in_dim(mine, 1 - xi, 0, keepdims=False)
        return own + swap(other.astype(bf16), "x").astype(f32)

    split_q = jnp.transpose(w_q.reshape(rows, 2, 2, 2, HEAD_DIM), (3, 1, 0, 2, 4))
    split_k = jnp.transpose(w_k.reshape(rows, 2, HEAD_DIM), (1, 0, 2))
    split_v = jnp.transpose(w_v.reshape(rows, 2, HEAD_DIM), (1, 0, 2))
    two = lambda a: jnp.broadcast_to(a[None], (2,) + a.shape).reshape(4, rows, a.shape[-1])
    packed_scan = jnp.concatenate(
        [
            heads_split(w_in[:, INNER : 2 * INNER], MAMBA_HEAD),
            jnp.broadcast_to(w_in[None, :, 2 * INNER : 2 * INNER + BC], (4, rows, BC)),
            jnp.pad(
                heads_split(w_in[:, 2 * INNER + BC :], 1), ((0, 0), (0, 0), (0, DT_PAD - HEADS))
            ),
        ],
        axis=2,
    )
    packed_rest = jnp.concatenate(
        [
            heads_split(w_in[:, :INNER], MAMBA_HEAD),
            split_q.reshape(4, rows, QP),
            two(split_k),
            two(split_v),
        ],
        axis=2,
    )

    def gathered(array):
        return lax.all_gather(array, SHARDS, axis=0, tiled=True)

    def after(array, *others):
        return lax.optimization_barrier((array,) + others)[0]

    def split_ff(w):
        w = w.reshape(rows, nz, 2, ny, 2, ff_rows)
        return jnp.transpose(w, (2, 4, 0, 1, 3, 5)).reshape(4, rows, hidden_part)

    def join_ff(w):
        w = w.reshape(2, 2, rows, nz, ny, ff_rows)
        return jnp.transpose(w, (2, 3, 0, 4, 1, 5)).reshape(rows, 4 * hidden_part)

    full_scan = gathered(to_ranks(packed_scan).reshape(4 * rows, SCAN_COLS))

    tokens = 2 * span_all
    resident = inputs[0].astype(f32)
    normed, norm_back = jax.vjp(rms_scale, resident, norm_gain)
    normed16 = gather_sequences(permuted(normed.astype(bf16)))
    edges16 = shifted(normed16[:, span_all - 8 :], 1).reshape(16, D)
    normed_rows = normed16.reshape(tokens, D)

    rest_mine = to_ranks(packed_rest).reshape(4 * rows, REST_COLS)
    if aligned:
        turn = [(2 * y + c, 2 * c + y) for y in range(2) for c in range(2)]
        place = []
        for z in range(4):
            for y in range(2):
                for c in range(2):
                    place.append(((z * 2 + y) * 2 + c, ((z % 2 * 2 + y) * 2 + c) * 2 + z // 2))
        back_place = [(b, a) for a, b in place]
        sent_out = lax.ppermute(w_out, ("y", "c"), turn)
        sent_o = lax.ppermute(w_o, ("z", "y", "c"), place)
        sent_rows = jnp.concatenate([sent_out, sent_o], 0)
    full_rest = gathered(after(rest_mine, normed_rows, edges16))
    cotangent16 = jnp.concatenate(gather_tokens(out_grad[0]), 0)

    scan_in = low_dot(normed_rows, full_scan).reshape(2, span_all, SCAN_COLS)
    edge_rows = low_dot(edges16, full_scan).reshape(2, 1, 8, SCAN_COLS)
    n = span_all // SPAN
    before = jnp.concatenate(
        [edge_rows, scan_in.reshape(2, n, SPAN, SCAN_COLS)[:, : n - 1, SPAN - 8 :]], axis=1
    )[..., :CONV_COLS]

    def rank_channels(array):
        return jnp.concatenate(
            [heads_mine(array[..., :INNER], MAMBA_HEAD), array[..., INNER:]], axis=-1
        )

    def per_head(array):
        return jnp.pad(heads_mine(array, 1), (0, DT_PAD - HEADS))[None]

    taps, bias = rank_channels(conv_weight), rank_channels(conv_bias)[None]
    dt_b, rates = per_head(dt_bias), per_head(-jnp.exp(a_log))
    skip = jnp.repeat(heads_mine(skip_gain, 1), MAMBA_HEAD)[None]
    gain = heads_mine(gated_gain, MAMBA_HEAD)[None]
    lift = (
        jnp.arange(DT_PAD, dtype=jnp.int32)[:, None]
        == jnp.arange(PART, dtype=jnp.int32)[None] // MAMBA_HEAD
    ).astype(bf16)
    mixed, steps, starts, prefix, own_state = scan_states(
        scan_in, before, taps, bias, dt_b, rates, lift
    )
    log_decay = starts[:, n - 1, 0] + steps[:, span_all - 1, DT_PAD:]
    own_decay = jnp.repeat(jnp.exp(log_decay[:, :HEADS]), MAMBA_HEAD, axis=-1)

    def turned(array, distance):
        return lax.ppermute(array, "z", [(i, (i + distance) % nz) for i in range(nz)])

    if aligned:
        first_rows = after(sent_rows, full_scan)
        along_z = jnp.stack([turned(first_rows, d) for d in range(nz - 1, 0, -1)] + [first_rows])
        along_z = lax.dynamic_slice_in_dim(
            jnp.concatenate([along_z, along_z], 0), nz - 1 - zi, nz, 0
        )
        other_y = swap(along_z, "y")
        full_rows = jnp.where(
            yi == 0, jnp.stack([along_z, other_y], 1), jnp.stack([other_y, along_z], 1)
        )
        full_out = full_rows[:, :, :out_rows].reshape(PART, D)
        full_o = full_rows[:, :, out_rows:].reshape(QP, D)
    else:
        every_out = lax.all_gather(w_out, EVERY, axis=0, tiled=True)
        every_o = lax.all_gather(w_o, EVERY, axis=0, tiled=True)
        full_out = lax.dynamic_slice_in_dim(every_out, (2 * xi + ci) * PART, PART, 0)
        every_o = every_o.reshape(2, 2, 2, HEAD_DIM, D)
        every_o = lax.dynamic_index_in_dim(every_o, xi, 2, keepdims=False)
        full_o = lax.dynamic_index_in_dim(every_o, ci, 0, keepdims=False).reshape(QP, D)

    def chained(local, step, pin=None):
        entering = []
        for s in range(2):
            held = jnp.zeros(local.shape[1:], f32)
            for hop in range(nz - 1):
                at = hop if step == 1 else nz - 1 - hop
                leaving = local[s] + own_decay[s][None] * held if hop else local[s]
                if pin is not None and hop == nz - 2:
                    leaving = after(leaving, pin)
                held = held + lax.ppermute(
                    leaving.astype(bf16), "z", [(at, at + step)]
                ).astype(f32)
            entering.append(held)
        return jnp.stack(entering)

    packed_ff = jnp.concatenate([split_ff(w_gate), split_ff(w_up)], axis=2)
    rest = low_dot(normed_rows, full_rest).reshape(2, span_all, REST_COLS)

    positions = zi * span_all + jnp.arange(span_all, dtype=jnp.int32)
    cosine, sine = rope_tables(positions)
    query16 = (
        rotate(rest[..., AT_Q:AT_K].reshape(2, span_all, 2, HEAD_DIM), cosine, sine)
        .astype(bf16)
        .reshape(2, span_all, QP)
    )
    key16 = rotate(rest[..., None, AT_K:AT_V], cosine, sine).astype(bf16)[:, :, 0]
    kv16 = jnp.stack([key16, rest[..., AT_V:].astype(bf16)])
    state_in = chained(own_state, 1, kv16)
    kv_before = [shifted(kv16, d) for d in range(nz - 1, 0, -1)]
    keys_at = (zi - nz + 1) * span_all + jnp.arange(nz * span_all, dtype=jnp.int32)
    query_place = jnp.broadcast_to(positions[:, None], (span_all, 128))
    key_place = jnp.broadcast_to(keys_at[None], (8, nz * span_all))
    values, flat, square = scan_values(
        mixed, steps, starts, prefix, state_in, rest, 0, skip, lift
    )
    kv_all = jnp.concatenate(list(after(tuple(kv_before), flat)) + [kv16], axis=2)
    attended, log_sum = attend(query16, kv_all[0], kv_all[1], query_place, key_place)
    attended16 = attended.reshape(tokens, QP).astype(bf16)

    root = lax.rsqrt(group_total(square[..., :1]) / INNER + epsilon)
    gated16 = (flat * root * gain).astype(bf16).reshape(tokens, PART)
    full_ff = gathered(
        after(to_ranks(packed_ff).reshape(4 * rows, 2 * hidden_part), mixed, cotangent16)
    )
    mixture = low_dot(gated16, full_out) + low_dot(attended16, full_o)
    hidden_state = resident + scatter_sequences(mixture.reshape(2, span_all, D))

    middle, mid_back = jax.vjp(rms_scale, hidden_state, mid_gain)
    middle16 = jnp.concatenate(gather_tokens(permuted(middle.astype(bf16))), 0)
    full_down = gathered(after(w_down, hidden_state))
    both = low_dot(middle16, full_ff)
    activated, swish_back = jax.vjp(
        swish_product, both[:, :hidden_part], both[:, hidden_part:]
    )
    activated16 = activated.astype(bf16)
    down = low_dot(activated16, full_down).reshape(4, length, D)
    output = (hidden_state + scatter_tokens(down)).astype(bf16)

    def to_owners(array):
        return lax.psum_scatter(array, SHARDS, scatter_dimension=0, tiled=True)

    down_grad = weight_grad(activated16, cotangent16).astype(bf16)
    down_owned = to_owners(down_grad)
    result_down = down_owned.astype(f32)
    gate_grad, up_grad = swish_back(back_dot(after(cotangent16, down_grad), full_down))
    both16 = jnp.concatenate([gate_grad, up_grad], axis=1).astype(bf16)
    mid_grad = restored(scatter_tokens(back_dot(both16, full_ff).reshape(4, length, D)))
    hidden_piece, mid_gain_grad = mid_back(mid_grad)
    hidden_grad = out_grad[0].astype(f32) + hidden_piece
    ff_grad = weight_grad(middle16, both16).astype(bf16)
    mix16 = gather_sequences(after(hidden_grad.astype(bf16), ff_grad)).reshape(tokens, D)
    ff_owned = to_owners(after(ff_grad, down_owned, mix16))
    ff_parts = to_ranks(ff_owned.reshape(4, rows, 2 * hidden_part))
    result_gate = join_ff(ff_parts[..., :hidden_part]).astype(f32)
    result_up = join_ff(ff_parts[..., hidden_part:]).astype(f32)
    attended_grad16 = back_dot(mix16, full_o).astype(bf16).reshape(2, span_all, QP)
    gated_grad = back_dot(mix16, full_out).reshape(2, span_all, PART)
    grad_out_w = weight_grad(gated16, mix16).astype(bf16)
    grad_o = weight_grad(attended16, mix16).astype(bf16)
    if aligned:
        rows_grad = jnp.concatenate(
            [grad_out_w.reshape(nz, 2, out_rows, D), grad_o.reshape(nz, 2, o_rows, D)], axis=2
        )
        other_y = lax.dynamic_index_in_dim(rows_grad, 1 - yi, 1, keepdims=False)
        both_y = lax.dynamic_index_in_dim(rows_grad, yi, 1, keepdims=False).astype(f32) + swap(
            other_y, "y"
        ).astype(f32)
    else:
        both_y = grad_o

    inner = jnp.sum(gated_grad * gain * flat, axis=-1, keepdims=True) * root
    inner_mean = group_total(inner) / INNER
    wide = (2, span_all, 128)
    value_grad, gate_z_grad, gain_grad, suffix, first_grad = gate_backward(
        after(gated_grad, down_owned),
        values,
        rest,
        0,
        jnp.broadcast_to(root, wide),
        jnp.broadcast_to(inner_mean, wide),
        gain,
        mixed,
        steps,
        lift,
    )
    state_grad = chained(first_grad, -1)

    query_grad, kv_grads = attend_backward(
        after(query16, first_grad),
        kv_all[0],
        kv_all[1],
        attended_grad16,
        attended,
        log_sum,
        query_place,
        key_place,
    )
    kv_grads = kv_grads.reshape(2, 2, nz, span_all, HEAD_DIM)
    kv_grad = kv_grads[:, :, nz - 1]
    for d in range(1, nz):
        kv_grad = kv_grad + shifted(kv_grads[:, :, nz - 1 - d].astype(bf16), -d).astype(f32)
    query_back = rotate(
        query_grad.reshape(2, span_all, 2, HEAD_DIM), cosine, -sine
    ).reshape(2, span_all, QP)
    key_back = rotate(kv_grad[0][:, :, None], cosine, -sine)[:, :, 0]
    rest_grad16 = jnp.concatenate(
        [
            gate_z_grad,
            query_back.astype(bf16),
            key_back.astype(bf16),
            kv_grad[1].astype(bf16),
        ],
        axis=-1,
    ).reshape(tokens, REST_COLS)

    mixed_grad, step_grad, skip_grad = scan_backward(
        mixed, steps, starts, prefix, state_in, suffix, value_grad, skip, lift
    )
    scan_grad16, edge_grad, conv_grad, small_grad = finish_backward(
        scan_in,
        before,
        mixed,
        steps,
        starts,
        prefix,
        state_in,
        after(state_grad, ff_owned, both_y),
        mixed_grad,
        step_grad,
        taps,
        bias,
        dt_b,
        rates,
        lift,
    )
    edge_back = shifted(edge_grad[:, 8 - edge_count :].astype(bf16), -1).astype(f32)
    last_rows = scan_grad16[:, span_all - edge_count :, :CONV_COLS].astype(f32) + edge_back
    scan_grad16 = lax.dynamic_update_slice(
        scan_grad16, last_rows.astype(bf16), (0, span_all - edge_count, 0)
    ).reshape(tokens, SCAN_COLS)
    if aligned:
        rows_owned = lax.dynamic_index_in_dim(both_y, zi, 0, keepdims=False)
        waiting = after(both_y.astype(bf16), state_grad)
        for d in range(1, nz):
            leaving = lax.dynamic_index_in_dim(waiting, (zi + d) % nz, 0, keepdims=False)
            rows_owned = rows_owned + turned(leaving, d).astype(f32)
        rows_owned = rows_owned.astype(bf16)
        result_out = lax.ppermute(rows_owned[:out_rows], ("y", "c"), turn).astype(f32)
        result_o = lax.ppermute(rows_owned[out_rows:], ("z", "y", "c"), back_place).astype(f32)
    else:
        every_out = lax.dynamic_update_slice_in_dim(
            jnp.zeros((INNER, D), bf16), grad_out_w, (2 * xi + ci) * PART, 0
        )
        every_o = lax.dynamic_update_slice(
            jnp.zeros((2, 2, 2, HEAD_DIM, D), bf16),
            grad_o.reshape(1, 2, 1, HEAD_DIM, D),
            (ci, 0, xi, 0, 0),
        ).reshape(ATT_HEADS * HEAD_DIM, D)
        result_out = lax.psum_scatter(every_out, EVERY, scatter_dimension=0, tiled=True)
        result_o = lax.psum_scatter(every_o, EVERY, scatter_dimension=0, tiled=True)
        result_out, result_o = result_out.astype(f32), result_o.astype(f32)
    rest_owned = to_owners(
        after(weight_grad(normed_rows, rest_grad16).astype(bf16), ff_owned, state_grad)
    )
    rest_parts = to_ranks(rest_owned.reshape(4, rows, REST_COLS)).astype(f32)
    scan_owned = to_owners(
        after(weight_grad(normed_rows, scan_grad16).astype(bf16), rest_owned)
    )

    normed_grad = back_dot(scan_grad16, full_scan) + back_dot(rest_grad16, full_rest)
    normed_grad = restored(scatter_sequences(normed_grad.reshape(2, span_all, D)))
    resident_grad, norm_gain_grad = norm_back(normed_grad)
    input_grad = hidden_grad + resident_grad

    result_q = jnp.transpose(
        rest_parts[..., AT_Q:AT_K].reshape(2, 2, rows, 2, HEAD_DIM), (2, 1, 3, 0, 4)
    ).reshape(rows, ATT_HEADS * HEAD_DIM)
    kv_parts = jnp.sum(rest_parts[..., AT_K:].reshape(2, 2, rows, 2, HEAD_DIM), axis=0)
    result_k = jnp.transpose(kv_parts[:, :, 0], (1, 0, 2)).reshape(rows, KV_HEADS * HEAD_DIM)
    result_v = jnp.transpose(kv_parts[:, :, 1], (1, 0, 2)).reshape(rows, KV_HEADS * HEAD_DIM)

    def all_channels(array):
        return jnp.concatenate(
            [heads_spread(array[..., :PART], MAMBA_HEAD), array[..., PART:]], axis=-1
        )

    small = [
        norm_gain_grad,
        all_channels(conv_grad[:4]),
        all_channels(conv_grad[4]),
        heads_spread(small_grad[0, :HEADS], 1),
        heads_spread(small_grad[1, :HEADS], 1),
        heads_spread(skip_grad[0, :HEADS], 1),
        heads_spread(gain_grad[0], MAMBA_HEAD),
        mid_gain_grad,
    ]
    summed = total(jnp.concatenate([v.reshape(-1) for v in small]))
    parts, at = [], 0
    for v in small:
        parts.append(summed[at : at + v.size].reshape(v.shape))
        at += v.size
    scan_owned = after(
        scan_owned,
        summed,
        input_grad,
        output,
        rest_parts,
        result_gate,
        result_up,
        result_down,
        result_q,
        result_k,
        result_v,
        result_out,
        result_o,
    )
    scan_parts = to_ranks(scan_owned.reshape(4, rows, SCAN_COLS)).astype(f32)
    result_in = jnp.concatenate(
        [
            heads_join(rest_parts[..., :PART], MAMBA_HEAD),
            heads_join(scan_parts[..., :PART], MAMBA_HEAD),
            jnp.sum(scan_parts[..., PART:CONV_COLS], axis=0),
            heads_join(scan_parts[..., CONV_COLS : CONV_COLS + HEADS], 1),
        ],
        axis=1,
    )
    return (
        output[None],
        input_grad[None],
        parts[0],
        result_in,
        parts[1],
        parts[2],
        parts[3],
        parts[4],
        parts[5],
        parts[6],
        result_out,
        result_q,
        result_k,
        result_v,
        result_o,
        parts[7],
        result_gate,
        result_up,
        result_down,
    )


def solution(mesh):
    seq, fsdp = mesh.shape["seq"], mesh.shape["fsdp"]
    split = Mesh(mesh.devices.reshape(seq // 2, 2, fsdp // 2, 2), EVERY)
    tokens = P(("y", "c"), ("z", "x"), None)
    matrix = P(EVERY, None)
    return jax.shard_map(
        body,
        mesh=split,
        in_specs=(tokens, tokens, P(), matrix)
        + (P(),) * 6
        + (matrix,) * 5
        + (P(),)
        + (matrix,) * 3,
        out_specs=(tokens, tokens, P(), matrix)
        + (P(),) * 6
        + (matrix,) * 5
        + (P(),)
        + (matrix,) * 3,
        check_vma=False,
    )
```

```python
import jax
import jax.numpy as jnp
from jax import lax
from jax.experimental import pallas as pl
from jax.experimental.pallas import tpu as pltpu
from jax.sharding import Mesh
from jax.sharding import PartitionSpec as P

D = 2048
MAMBA_HEADS = 48
MAMBA_HEAD = 64
STATE = 256
ATT_HEADS = 8
KV_HEADS = 2
HEAD_DIM = 128
SPAN = 128
INNER = 3072

HEADS = MAMBA_HEADS // 4
PART = HEADS * MAMBA_HEAD
BC = 2 * STATE
DT_PAD = 128
QP = 2 * HEAD_DIM
CONV_COLS = PART + BC
SCAN_COLS = CONV_COLS + DT_PAD
QUARTER = BC // 4
SENT_COLS = PART + QUARTER + DT_PAD
AT_Q = PART
AT_K = AT_Q + QP
AT_V = AT_K + HEAD_DIM
REST_COLS = AT_V + HEAD_DIM

epsilon = 1e-05
rope_base = 100000000000.0
GROUP = ("x", "c")
SHARDS = ("z", "y")
EVERY = ("z", "x", "y", "c")
bf16 = jnp.bfloat16
f32 = jnp.float32


def swap(array, axis):
    return lax.ppermute(array, axis, [(0, 1), (1, 0)])


def shifted(array, distance):
    devices = range(lax.axis_size("z"))
    return lax.ppermute(array, "z", [(i - distance, i) for i in devices if i - distance in devices])


def total(array):
    for axis in EVERY:
        size = lax.axis_size(axis)
        bit = 1
        while bit < size:
            array = array + lax.ppermute(array, axis, [(i, i ^ bit) for i in range(size)])
            bit *= 2
    return array


def group_total(array):
    array = array + swap(array[::-1], "c")
    return array + swap(array, "x")


def low_dot(left, right):
    return jnp.dot(left, right, preferred_element_type=f32)


def back_dot(grad_rows, weight):
    return lax.dot_general(grad_rows, weight, (((1,), (1,)), ((), ())), preferred_element_type=f32)


def weight_grad(left, right):
    return lax.dot_general(left, right, (((0,), (0,)), ((), ())), preferred_element_type=f32)


def rms_scale(values, gain):
    return values * lax.rsqrt(jnp.mean(values * values, axis=-1, keepdims=True) + epsilon) * gain


def rope_tables(positions):
    half_dim = HEAD_DIM // 2
    frequencies = rope_base ** (-jnp.arange(half_dim, dtype=f32) / half_dim)
    angles = positions.astype(f32)[:, None] * frequencies[None, :]
    return (jnp.cos(angles), jnp.sin(angles))


def rotate(values, cosine, sine):
    half_dim = HEAD_DIM // 2
    cosine, sine = cosine[:, None, :], sine[:, None, :]
    first, second = values[..., :half_dim], values[..., half_dim:]
    return jnp.concatenate([first * cosine - second * sine, second * cosine + first * sine], axis=-1)


def pieces(values, count):
    parts = []
    for _ in range(count):
        part = values.astype(bf16)
        parts.append(part)
        values = values - part.astype(f32)
    return parts


def running(mask, values):
    mask16 = mask.astype(bf16)
    return sum(low_dot(mask16, part) for part in pieces(values, 3))


def over_lanes(left, right):
    return lax.dot_general(left, right, (((1,), (1,)), ((), ())), preferred_element_type=f32)


def over_rows(left, right):
    return lax.dot_general(left, right, (((0,), (0,)), ((), ())), preferred_element_type=f32)


def widen(values, lift):
    return sum(low_dot(part, lift) for part in pieces(values, 2))


def narrow(values, lift):
    return sum(over_lanes(part, lift) for part in pieces(values, 2))


def sig(values):
    return 1.0 / (1.0 + jnp.exp(-values))


def soft(values):
    return jnp.maximum(values, 0.0) + jnp.log1p(jnp.exp(-jnp.abs(values)))


def square_places():
    return (
        lax.broadcasted_iota(jnp.int32, (SPAN, SPAN), 0),
        lax.broadcasted_iota(jnp.int32, (SPAN, SPAN), 1),
    )


def pre_conv(current, before, taps, bias):
    extended = jnp.concatenate([before, current], axis=0)
    pre = bias + extended[5 : 5 + SPAN] * taps[0:1]
    for k in range(1, 4):
        pre = pre + extended[5 + k : 5 + k + SPAN] * taps[k : k + 1]
    return (pre, extended)


def states_kernel(
    scan_in, before, taps, bias, dt_bias, rates, lift, mixed, steps, starts, prefix, last, held, sofar
):
    @pl.when(pl.program_id(1) == 0)
    def _():
        held[...] = jnp.zeros_like(held)
        sofar[...] = jnp.zeros_like(sofar)

    pre, _ = pre_conv(scan_in[0, :, :CONV_COLS], before[0, 0], taps[...], bias[...])
    mix = pre * sig(pre)
    mixed[0] = mix
    dt = soft(scan_in[0, :, CONV_COLS:] + dt_bias[...])
    row, column = square_places()
    cum = running(jnp.where(row >= column, 1.0, 0.0), dt * rates[...])
    steps[0, :, :DT_PAD] = dt
    steps[0, :, DT_PAD:] = cum
    starts[0, 0] = sofar[...]
    prefix[0, 0] = held[...]
    end = cum[SPAN - 1 : SPAN]
    tail = jnp.exp(end - cum) * dt
    fed = (mix[:, :PART] * widen(tail, lift[...])).astype(bf16)
    added = over_rows(mix[:, PART : PART + STATE].astype(bf16), fed)
    whole = widen(jnp.broadcast_to(jnp.exp(end), (8, DT_PAD)), lift[...])[0:1]
    held[...] = whole * held[...] + added
    sofar[...] = sofar[...] + end
    last[0] = held[...]


def values_kernel(
    mixed, steps, starts, prefix, state_in, gate, skip, lift, values, flat, square
):
    x = mixed[0, :, :PART]
    b16 = mixed[0, :, PART : PART + STATE].astype(bf16)
    c16 = mixed[0, :, PART + STATE :].astype(bf16)
    dt = steps[0, :, :DT_PAD]
    cum = steps[0, :, DT_PAD:]
    dt_t, cum_t = dt.T, cum.T
    state = prefix[0, 0] + widen(jnp.exp(starts[0, 0]), lift[...])[0:1] * state_in[0]
    meet = over_lanes(c16, b16)
    carried = low_dot(c16, state.astype(bf16)) * widen(jnp.exp(cum), lift[...])
    row, column = square_places()
    first = column < MAMBA_HEAD
    inside = []
    for k in range(HEADS // 2):
        pair = x[:, 2 * MAMBA_HEAD * k : 2 * MAMBA_HEAD * (k + 1)]
        weights = []
        for h in (2 * k, 2 * k + 1):
            spread = cum[:, h : h + 1] - cum_t[h : h + 1, :]
            decay = jnp.exp(jnp.where(row >= column, spread, -1e30))
            weights.append((meet * decay * dt_t[h : h + 1, :]).astype(bf16))
        split = [
            jnp.where(first, pair, 0.0).astype(bf16),
            jnp.where(first, 0.0, pair).astype(bf16),
        ]
        inside.append(low_dot(jnp.concatenate(weights, 1), jnp.concatenate(split, 0)))
    value = jnp.concatenate(inside, 1) + carried + skip[...] * x
    values[0] = value
    z = gate[0]
    product = value * (z * sig(z))
    flat[0] = product
    square[0] = jnp.broadcast_to(
        jnp.sum(product * product, axis=1, keepdims=True), (SPAN, 128)
    )


def gate_back_kernel(
    gated_grad, values, gate, root, mean, gain, c_part, steps, lift,
    value_grad, gate_grad, gain_grad, suffix, first_grad, held,
):
    @pl.when(pl.program_id(1) == 0)
    def _():
        held[...] = jnp.zeros_like(held)

    @pl.when((pl.program_id(0) == 0) & (pl.program_id(1) == 0))
    def _():
        gain_grad[...] = jnp.zeros_like(gain_grad)

    z, value, grad = gate[0], values[0], gated_grad[0]
    s = sig(z)
    silu = z * s
    scale = root[0, :, 0:1]
    normal = value * silu * scale
    flat_grad = scale * (grad * gain[...] - normal * mean[0, :, 0:1])
    d_value = flat_grad * silu
    value_grad[0] = d_value
    gate_grad[0] = (flat_grad * value * (s * (1.0 + z * (1.0 - s)))).astype(bf16)
    gain_grad[0:1] = gain_grad[0:1] + jnp.sum(grad * normal, axis=0, keepdims=True)
    grown = widen(jnp.exp(steps[0, :, DT_PAD:]), lift[...])
    suffix[0, 0] = held[...]
    held[...] = grown[SPAN - 1 : SPAN] * held[...] + over_rows(
        c_part[0].astype(bf16), (grown * d_value).astype(bf16)
    )
    first_grad[0] = held[...]


def scan_back_kernel(
    mixed, steps, starts, prefix, state_in, suffix, value_grad, skip, lift,
    mixed_grad, step_grad, skip_grad, columns,
):
    @pl.when((pl.program_id(0) == 0) & (pl.program_id(1) == 0))
    def _():
        skip_grad[...] = jnp.zeros_like(skip_grad)
        columns[...] = jnp.zeros_like(columns)

    up = lift[...]
    x = mixed[0, :, :PART]
    b16 = mixed[0, :, PART : PART + STATE].astype(bf16)
    c16 = mixed[0, :, PART + STATE :].astype(bf16)
    dt = steps[0, :, :DT_PAD]
    cum = steps[0, :, DT_PAD:]
    dt_t, cum_t = dt.T, cum.T
    end = cum[SPAN - 1 : SPAN]
    dy = value_grad[0]
    state = prefix[0, 0] + widen(jnp.exp(starts[0, 0]), up)[0:1] * state_in[0]
    ending = suffix[0, 0]
    state16, ending16 = state.astype(bf16), ending.astype(bf16)
    grown_dy = widen(jnp.exp(cum), up) * dy
    tail_wide = widen(jnp.exp(end - cum), up)
    dt_wide = widen(dt, up)
    reach = low_dot(c16, state16)
    pull = tail_wide * low_dot(b16, ending16)
    d_c = over_lanes(grown_dy.astype(bf16), state16)
    d_b = over_lanes((tail_wide * dt_wide * x).astype(bf16), ending16)
    meet = over_lanes(c16, b16)
    row, column = square_places()
    first = column < MAMBA_HEAD
    d_meet = jnp.zeros((SPAN, SPAN), f32)
    rows_sum = jnp.zeros((SPAN, DT_PAD), f32)
    back = []
    for k in range(HEADS // 2):
        at = slice(2 * MAMBA_HEAD * k, 2 * MAMBA_HEAD * (k + 1))
        x16, dy_pair = x[:, at].astype(bf16), dy[:, at]
        split = [
            jnp.where(first, dy_pair, 0.0).astype(bf16),
            jnp.where(first, 0.0, dy_pair).astype(bf16),
        ]
        weights = []
        for j in range(2):
            h = 2 * k + j
            spread = cum[:, h : h + 1] - cum_t[h : h + 1, :]
            decay = jnp.exp(jnp.where(row >= column, spread, -1e30))
            d_weight = over_lanes(split[j], x16) * decay
            scaled = d_weight * dt_t[h : h + 1, :]
            d_meet = d_meet + scaled
            rows_sum = rows_sum + jnp.where(
                column == h, jnp.sum(scaled * meet, axis=1, keepdims=True), 0.0
            )
            columns[h : h + 1, :] = jnp.sum(d_weight * meet, axis=0, keepdims=True)
            weights.append((meet * decay).astype(bf16))
        back.append(over_rows(jnp.concatenate(weights, 0), jnp.concatenate(split, 0)))
    d_meet16 = d_meet.astype(bf16)
    mixed_grad[0, :, :PART] = dt_wide * (jnp.concatenate(back, 1) + pull) + skip[...] * dy
    mixed_grad[0, :, PART : PART + STATE] = d_b + over_rows(d_meet16, c16)
    mixed_grad[0, :, PART + STATE :] = d_c + low_dot(d_meet16, b16)
    tail_dt = narrow(x * pull, up)
    inner_dt = columns[...].T
    d_cum = rows_sum + narrow(grown_dy * reach, up) - dt * (inner_dt + tail_dt)
    kept = narrow(
        jnp.broadcast_to(jnp.sum(state * ending, axis=0, keepdims=True), (8, PART)), up
    )[0:1]
    extra = jnp.sum(dt * tail_dt, axis=0, keepdims=True) + jnp.exp(end) * kept
    step_grad[0, :, :DT_PAD] = inner_dt + tail_dt
    step_grad[0, :, DT_PAD:] = running(jnp.where(row <= column, 1.0, 0.0), d_cum) + extra
    skip_grad[0:1] = skip_grad[0:1] + jnp.sum(narrow(dy * x, up), axis=0, keepdims=True)


def finish_back_kernel(
    scan_in, before, mixed, steps, starts, prefix, state_in, state_grad, mixed_grad, step_grad,
    taps, bias, dt_bias, rates, lift,
    scan_grad, edge_grad, conv_grad, small_grad,
    later, after_pre,
):
    @pl.when(pl.program_id(1) == 0)
    def _():
        later[...] = jnp.zeros_like(later)
        after_pre[...] = jnp.zeros_like(after_pre)

    @pl.when((pl.program_id(0) == 0) & (pl.program_id(1) == 0))
    def _():
        conv_grad[...] = jnp.zeros_like(conv_grad)
        small_grad[...] = jnp.zeros_like(small_grad)

    up = lift[...]
    x = mixed[0, :, :PART]
    b16 = mixed[0, :, PART : PART + STATE].astype(bf16)
    dt = steps[0, :, :DT_PAD]
    cum = steps[0, :, DT_PAD:]
    end = cum[SPAN - 1 : SPAN]
    state = prefix[0, 0] + widen(jnp.exp(starts[0, 0]), up)[0:1] * state_in[0]
    ending = widen(jnp.exp(later[...]), up)[0:1] * state_grad[0]
    later[...] = later[...] + end
    ending16 = ending.astype(bf16)
    tail_wide = widen(jnp.exp(end - cum), up)
    dt_wide = widen(dt, up)
    pull = tail_wide * low_dot(b16, ending16)
    d_x = mixed_grad[0, :, :PART] + dt_wide * pull
    d_b = mixed_grad[0, :, PART : PART + STATE] + over_lanes(
        (tail_wide * dt_wide * x).astype(bf16), ending16
    )
    d_c = mixed_grad[0, :, PART + STATE :]
    tail_dt = narrow(x * pull, up)
    kept = narrow(
        jnp.broadcast_to(jnp.sum(state * ending, axis=0, keepdims=True), (8, PART)), up
    )[0:1]
    row, column = square_places()
    fed = dt * tail_dt
    earlier = running(jnp.where(row > column, 1.0, 0.0), fed)
    d_log = step_grad[0, :, DT_PAD:] + earlier + jnp.exp(end) * kept
    rate = rates[...]
    d_raw = (step_grad[0, :, :DT_PAD] + tail_dt + d_log * rate) * sig(
        scan_in[0, :, CONV_COLS:] + dt_bias[...]
    )
    small_grad[0:1] = small_grad[0:1] + jnp.sum(d_raw, axis=0, keepdims=True)
    small_grad[1:2] = small_grad[1:2] + jnp.sum(d_log * dt * rate, axis=0, keepdims=True)

    pre, extended = pre_conv(scan_in[0, :, :CONV_COLS], before[0, 0], taps[...], bias[...])
    s = sig(pre)
    d_pre = jnp.concatenate([d_x, d_b, d_c], axis=1) * (s * (1.0 + pre * (1.0 - s)))
    for k in range(4):
        conv_grad[k : k + 1] = conv_grad[k : k + 1] + jnp.sum(
            d_pre * extended[5 + k : 5 + k + SPAN], axis=0, keepdims=True
        )
    conv_grad[4:5] = conv_grad[4:5] + jnp.sum(d_pre, axis=0, keepdims=True)
    following = jnp.concatenate([d_pre, after_pre[...]], axis=0)
    d_in = following[0:SPAN] * taps[3:4]
    for k in range(3):
        d_in = d_in + following[3 - k : 3 - k + SPAN] * taps[k : k + 1]
    scan_grad[0, :, :CONV_COLS] = d_in.astype(bf16)
    scan_grad[0, :, CONV_COLS:] = d_raw.astype(bf16)
    front = d_pre[0:8]
    after_pre[...] = front
    nothing = jnp.zeros((8, CONV_COLS), f32)
    padded = jnp.concatenate([nothing, front, nothing], 0)
    edge = padded[0:8] * taps[3:4]
    for k in range(3):
        edge = edge + padded[3 - k : 11 - k] * taps[k : k + 1]
    edge_grad[0] = edge


def one(shape):
    return pl.BlockSpec(shape, lambda b, i: (0,) * len(shape))


def by_span(width, column=0, reverse=None):
    if reverse is None:
        return pl.BlockSpec((1, SPAN, width), lambda b, i: (b, i, column))
    return pl.BlockSpec((1, SPAN, width), lambda b, i: (b, reverse - 1 - i, column))


def by_piece(rows, width, reverse=None):
    if reverse is None:
        return pl.BlockSpec((1, 1, rows, width), lambda b, i: (b, i, 0, 0))
    return pl.BlockSpec((1, 1, rows, width), lambda b, i: (b, reverse - 1 - i, 0, 0))


def by_sequence(rows, width):
    return pl.BlockSpec((1, rows, width), lambda b, i: (b, 0, 0))


def grid_call(kernel, spans, ins, outs, scratch, flops, moved):
    return pl.pallas_call(
        kernel,
        grid=(2, spans),
        in_specs=ins,
        out_specs=[spec for spec, _ in outs],
        out_shape=[shape for _, shape in outs],
        scratch_shapes=scratch,
        compiler_params=pltpu.CompilerParams(
            dimension_semantics=("arbitrary", "arbitrary"), vmem_limit_bytes=50 * 2**20
        ),
        cost_estimate=pl.CostEstimate(flops=flops, bytes_accessed=moved, transcendentals=0),
    )


def like(shape, kind=f32):
    return jax.ShapeDtypeStruct(shape, kind)


def scan_states(scan_in, before, taps, bias, dt_bias, rates, lift):
    length = scan_in.shape[1]
    n = length // SPAN
    return grid_call(
        states_kernel,
        n,
        [
            by_span(SCAN_COLS),
            by_piece(8, CONV_COLS),
            one((4, CONV_COLS)),
            one((1, CONV_COLS)),
            one((1, DT_PAD)),
            one((1, DT_PAD)),
            one((DT_PAD, PART)),
        ],
        [
            (by_span(CONV_COLS), like((2, length, CONV_COLS))),
            (by_span(2 * DT_PAD), like((2, length, 2 * DT_PAD))),
            (by_piece(8, DT_PAD), like((2, n, 8, DT_PAD))),
            (by_piece(STATE, PART), like((2, n, STATE, PART))),
            (by_sequence(STATE, PART), like((2, STATE, PART))),
        ],
        [pltpu.VMEM((STATE, PART), f32), pltpu.VMEM((8, DT_PAD), f32)],
        8 * 10**9,
        30 * 10**6,
    )(scan_in, before, taps, bias, dt_bias, rates, lift)


def scan_values(mixed, steps, starts, prefix, state_in, rest, gate_at, skip, lift):
    length = mixed.shape[1]
    n = length // SPAN
    return grid_call(
        values_kernel,
        n,
        [
            by_span(CONV_COLS),
            by_span(2 * DT_PAD),
            by_piece(8, DT_PAD),
            by_piece(STATE, PART),
            by_sequence(STATE, PART),
            by_span(PART, gate_at),
            one((1, PART)),
            one((DT_PAD, PART)),
        ],
        [
            (by_span(PART), like((2, length, PART))),
            (by_span(PART), like((2, length, PART))),
            (by_span(128), like((2, length, 128))),
        ],
        [],
        12 * 10**9,
        30 * 10**6,
    )(mixed, steps, starts, prefix, state_in, rest, skip, lift)


def gate_backward(gated_grad, values, rest, gate_at, root, mean, gain, mixed, steps, lift):
    length = mixed.shape[1]
    n = length // SPAN
    return grid_call(
        gate_back_kernel,
        n,
        [
            by_span(PART, 0, n),
            by_span(PART, 0, n),
            by_span(PART, gate_at, n),
            by_span(128, 0, n),
            by_span(128, 0, n),
            one((1, PART)),
            by_span(STATE, (PART + STATE) // STATE, n),
            by_span(2 * DT_PAD, 0, n),
            one((DT_PAD, PART)),
        ],
        [
            (by_span(PART, 0, n), like((2, length, PART))),
            (by_span(PART, 0, n), like((2, length, PART), bf16)),
            (one((8, PART)), like((8, PART))),
            (by_piece(STATE, PART, n), like((2, n, STATE, PART))),
            (by_sequence(STATE, PART), like((2, STATE, PART))),
        ],
        [pltpu.VMEM((STATE, PART), f32)],
        8 * 10**9,
        30 * 10**6,
    )(gated_grad, values, rest, root, mean, gain, mixed, steps, lift)


def scan_backward(mixed, steps, starts, prefix, state_in, suffix, value_grad, skip, lift):
    length = mixed.shape[1]
    n = length // SPAN
    return grid_call(
        scan_back_kernel,
        n,
        [
            by_span(CONV_COLS),
            by_span(2 * DT_PAD),
            by_piece(8, DT_PAD),
            by_piece(STATE, PART),
            by_sequence(STATE, PART),
            by_piece(STATE, PART),
            by_span(PART),
            one((1, PART)),
            one((DT_PAD, PART)),
        ],
        [
            (by_span(CONV_COLS), like((2, length, CONV_COLS))),
            (by_span(2 * DT_PAD), like((2, length, 2 * DT_PAD))),
            (one((8, DT_PAD)), like((8, DT_PAD))),
        ],
        [pltpu.VMEM((SPAN, SPAN), f32)],
        30 * 10**9,
        40 * 10**6,
    )(mixed, steps, starts, prefix, state_in, suffix, value_grad, skip, lift)


def finish_backward(
    scan_in, before, mixed, steps, starts, prefix, state_in, state_grad, mixed_grad, step_grad,
    taps, bias, dt_bias, rates, lift,
):
    length = mixed.shape[1]
    n = length // SPAN
    return grid_call(
        finish_back_kernel,
        n,
        [
            by_span(SCAN_COLS, 0, n),
            by_piece(8, CONV_COLS, n),
            by_span(CONV_COLS, 0, n),
            by_span(2 * DT_PAD, 0, n),
            by_piece(8, DT_PAD, n),
            by_piece(STATE, PART, n),
            by_sequence(STATE, PART),
            by_sequence(STATE, PART),
            by_span(CONV_COLS, 0, n),
            by_span(2 * DT_PAD, 0, n),
            one((4, CONV_COLS)),
            one((1, CONV_COLS)),
            one((1, DT_PAD)),
            one((1, DT_PAD)),
            one((DT_PAD, PART)),
        ],
        [
            (by_span(SCAN_COLS, 0, n), like((2, length, SCAN_COLS), bf16)),
            (by_sequence(8, CONV_COLS), like((2, 8, CONV_COLS))),
            (one((8, CONV_COLS)), like((8, CONV_COLS))),
            (one((8, DT_PAD)), like((8, DT_PAD))),
        ],
        [pltpu.VMEM((8, DT_PAD), f32), pltpu.VMEM((8, CONV_COLS), f32)],
        15 * 10**9,
        50 * 10**6,
    )(
        scan_in, before, mixed, steps, starts, prefix, state_in, state_grad, mixed_grad, step_grad,
        taps, bias, dt_bias, rates, lift,
    )


def attend_kernel(query, key, value, query_place, key_place, attended, log_sum):
    scores = over_lanes(query[0], key[0]) * HEAD_DIM ** (-0.5)
    seen = (key_place[0:1] >= 0) & (query_place[:, 0:1] >= key_place[0:1])
    scores = jnp.where(seen, scores, -1e30)
    peak = jnp.max(scores, axis=1, keepdims=True)
    unscaled = jnp.exp(scores - peak)
    whole = jnp.sum(unscaled, axis=1, keepdims=True)
    probs = (unscaled * (1.0 / whole)).astype(bf16)
    attended[0] = low_dot(probs, value[0])
    log_sum[0] = jnp.broadcast_to(peak + jnp.log(whole), log_sum.shape[1:])


def attend_back_kernel(
    query, key, value, grad, attended, log_sum, query_place, key_place, query_grad, kv_grad
):
    @pl.when((pl.program_id(1) == 0) & (pl.program_id(2) == 0))
    def _():
        kv_grad[...] = jnp.zeros_like(kv_grad)

    scale = HEAD_DIM ** (-0.5)
    scores = over_lanes(query[0], key[0]) * scale
    seen = (key_place[0:1] >= 0) & (query_place[:, 0:1] >= key_place[0:1])
    probs = jnp.exp(jnp.where(seen, scores, -1e30) - log_sum[0, :, 0:1])
    delta = jnp.sum(grad[0].astype(f32) * attended[0], axis=1, keepdims=True)
    score_grad = (probs * (over_lanes(grad[0], value[0]) - delta)).astype(bf16)
    query_grad[0] = low_dot(score_grad, key[0]) * scale
    kv_grad[0, 0] = kv_grad[0, 0] + over_rows(score_grad, query[0]) * scale
    kv_grad[1, 0] = kv_grad[1, 0] + over_rows(probs.astype(bf16), grad[0])


def attend_specs(block, keys):
    by_query = pl.BlockSpec((1, block, HEAD_DIM), lambda b, h, i: (b, i, h))
    whole_key = pl.BlockSpec((1, keys, HEAD_DIM), lambda b, h, i: (b, 0, 0))
    place = pl.BlockSpec((block, 128), lambda b, h, i: (i, 0))
    key_at = pl.BlockSpec((8, keys), lambda b, h, i: (0, 0))
    return (by_query, whole_key, place, key_at)


def attend(query, key, value, query_place, key_place):
    length, keys = query.shape[1], key.shape[1]
    block = 256 if keys <= 4096 else 128
    by_query, whole_key, place, key_at = attend_specs(block, keys)
    return pl.pallas_call(
        attend_kernel,
        grid=(2, 2, length // block),
        in_specs=[by_query, whole_key, whole_key, place, key_at],
        out_specs=[by_query, by_query],
        out_shape=[like((2, length, QP)), like((2, length, QP))],
        compiler_params=pltpu.CompilerParams(
            dimension_semantics=("arbitrary",) * 3, vmem_limit_bytes=50 * 2**20
        ),
        cost_estimate=pl.CostEstimate(
            flops=12 * 10**9, bytes_accessed=20 * 10**6, transcendentals=0
        ),
    )(query, key, value, query_place, key_place)


def attend_backward(query, key, value, grad, attended, log_sum, query_place, key_place):
    length, keys = query.shape[1], key.shape[1]
    block = 256 if keys <= 4096 else 128
    by_query, whole_key, place, key_at = attend_specs(block, keys)
    return pl.pallas_call(
        attend_back_kernel,
        grid=(2, 2, length // block),
        in_specs=[by_query, whole_key, whole_key, by_query, by_query, by_query, place, key_at],
        out_specs=[
            by_query,
            pl.BlockSpec((2, 1, keys, HEAD_DIM), lambda b, h, i: (0, b, 0, 0)),
        ],
        out_shape=[like((2, length, QP)), like((2, 2, keys, HEAD_DIM))],
        compiler_params=pltpu.CompilerParams(
            dimension_semantics=("arbitrary",) * 3, vmem_limit_bytes=50 * 2**20
        ),
        cost_estimate=pl.CostEstimate(
            flops=20 * 10**9, bytes_accessed=30 * 10**6, transcendentals=0
        ),
    )(query, key, value, grad, attended, log_sum, query_place, key_place)


def swish_product(gate_proj, up_proj):
    return jax.nn.silu(gate_proj) * up_proj


def gather_tokens(block):
    across = swap(block, "x")
    return (block, swap(block, "c"), across, swap(across, "c"))


def scatter_tokens(blocks):
    near, far = blocks[0], blocks[2]
    sent = swap(jnp.stack([blocks[1].astype(bf16), blocks[3].astype(bf16)]), "c")
    near = near + sent[0].astype(f32)
    far = far + sent[1].astype(f32)
    return near + swap(far.astype(bf16), "x").astype(f32)


def body(
    inputs,
    out_grad,
    norm_gain,
    w_in,
    conv_weight,
    conv_bias,
    dt_bias,
    a_log,
    skip_gain,
    gated_gain,
    w_out,
    w_q,
    w_k,
    w_v,
    w_o,
    mid_gain,
    w_gate,
    w_up,
    w_down,
):
    nz, ny = lax.axis_size("z"), lax.axis_size("y")
    zi, xi, yi, ci = (lax.axis_index(name) for name in ("z", "x", "y", "c"))
    length = inputs.shape[1]
    span_all = 2 * length
    rows = w_in.shape[0]
    ff_rows = w_down.shape[0]
    hidden_part = nz * ny * ff_rows
    edge_count = conv_weight.shape[0] - 1
    out_rows, o_rows = w_out.shape[0], w_o.shape[0]
    aligned = ny == 2 and nz == 4 and MAMBA_HEADS % (4 * nz) == 0
    g = nz if aligned else 1
    hp = HEADS // g

    def heads_mine(array, width):
        lead = array.shape[:-1]
        array = array.reshape(lead + (g, 2, 2, hp * width))
        array = lax.dynamic_index_in_dim(array, xi, len(lead) + 1, keepdims=False)
        array = lax.dynamic_index_in_dim(array, ci, len(lead) + 1, keepdims=False)
        return array.reshape(lead + (HEADS * width,))

    def heads_spread(array, width):
        lead = array.shape[:-1]
        array = array.reshape(lead + (g, 1, 1, hp * width))
        whole = jnp.zeros(lead + (g, 2, 2, hp * width), array.dtype)
        start = (0,) * len(lead) + (0, xi, ci, 0)
        return lax.dynamic_update_slice(whole, array, start).reshape(
            lead + (MAMBA_HEADS * width,)
        )

    def heads_split(array, width):
        n = array.shape[0]
        array = array.reshape(n, g, 2, 2, hp * width)
        return jnp.transpose(array, (2, 3, 0, 1, 4)).reshape(4, n, HEADS * width)

    def heads_join(array, width):
        n = array.shape[1]
        array = array.reshape(2, 2, n, g, hp * width)
        return jnp.transpose(array, (2, 3, 0, 1, 4)).reshape(n, MAMBA_HEADS * width)

    def reordered(array, first, second):
        width = 2 * rows
        return jnp.concatenate(
            [
                array[..., at * width : (at + 1) * width]
                for z in range(nz)
                for at in (
                    (z * first + i) * second + j for j in range(second) for i in range(first)
                )
            ],
            axis=-1,
        )

    def permuted(array):
        return reordered(array, 2, ny)

    def restored(array):
        return reordered(array, ny, 2)

    def to_ranks(array):
        return lax.all_to_all(array, GROUP, 0, 0, tiled=True)

    def in_order(own, other):
        return lax.dynamic_slice_in_dim(
            jnp.concatenate([own, other, own], 0), xi * length, span_all, 0
        )

    def gather_sequences(block):
        own, near, across, far = gather_tokens(block)
        return jnp.stack([in_order(own, across), in_order(near, far)])

    def scatter_sequences(partial):
        mine = partial[0] + swap(partial[1].astype(bf16), "c").astype(f32)
        mine = mine.reshape(2, length, mine.shape[-1])
        own = lax.dynamic_index_in_dim(mine, xi, 0, keepdims=False)
        other = lax.dynamic_index_in_dim(mine, 1 - xi, 0, keepdims=False)
        return own + swap(other.astype(bf16), "x").astype(f32)

    split_q = jnp.transpose(w_q.reshape(rows, 2, 2, 2, HEAD_DIM), (3, 1, 0, 2, 4))
    split_k = jnp.transpose(w_k.reshape(rows, 2, HEAD_DIM), (1, 0, 2))
    split_v = jnp.transpose(w_v.reshape(rows, 2, HEAD_DIM), (1, 0, 2))
    two = lambda a: jnp.broadcast_to(a[None], (2,) + a.shape).reshape(4, rows, a.shape[-1])
    packed_scan = jnp.concatenate(
        [
            heads_split(w_in[:, INNER : 2 * INNER], MAMBA_HEAD),
            jnp.swapaxes(
                w_in[:, 2 * INNER : 2 * INNER + BC].reshape(rows, 4, QUARTER), 0, 1
            ),
            jnp.pad(
                heads_split(w_in[:, 2 * INNER + BC :], 1), ((0, 0), (0, 0), (0, DT_PAD - HEADS))
            ),
        ],
        axis=2,
    )
    packed_rest = jnp.concatenate(
        [
            heads_split(w_in[:, :INNER], MAMBA_HEAD),
            split_q.reshape(4, rows, QP),
            two(split_k),
            two(split_v),
        ],
        axis=2,
    )

    def gathered(array):
        return lax.all_gather(array, SHARDS, axis=0, tiled=True)

    def after(array, *others):
        return lax.optimization_barrier((array,) + others)[0]

    def split_ff(w):
        w = w.reshape(rows, nz, 2, ny, 2, ff_rows)
        return jnp.transpose(w, (2, 4, 0, 1, 3, 5)).reshape(4, rows, hidden_part)

    def join_ff(w):
        w = w.reshape(2, 2, rows, nz, ny, ff_rows)
        return jnp.transpose(w, (2, 3, 0, 4, 1, 5)).reshape(rows, 4 * hidden_part)

    full_scan = gathered(to_ranks(packed_scan).reshape(4 * rows, SENT_COLS))

    tokens = 2 * span_all
    resident = inputs[0].astype(f32)
    normed, norm_back = jax.vjp(rms_scale, resident, norm_gain)
    normed16 = gather_sequences(permuted(normed.astype(bf16)))
    edges16 = shifted(normed16[:, span_all - 8 :], 1).reshape(16, D)
    normed_rows = normed16.reshape(tokens, D)

    rest_mine = to_ranks(packed_rest).reshape(4 * rows, REST_COLS)
    if aligned:
        turn = [(2 * y + c, 2 * c + y) for y in range(2) for c in range(2)]
        place = []
        for z in range(4):
            for y in range(2):
                for c in range(2):
                    place.append(((z * 2 + y) * 2 + c, ((z % 2 * 2 + y) * 2 + c) * 2 + z // 2))
        back_place = [(b, a) for a, b in place]
        sent_out = lax.ppermute(w_out, ("y", "c"), turn)
        sent_o = lax.ppermute(w_o, ("z", "y", "c"), place)
        sent_rows = jnp.concatenate([sent_out, sent_o], 0)
    full_rest = gathered(after(rest_mine, normed_rows, edges16))
    cotangent16 = jnp.concatenate(gather_tokens(out_grad[0]), 0)

    def beside(own, other, index):
        return jnp.where(
            index == 0,
            jnp.concatenate([own, other], axis=-1),
            jnp.concatenate([other, own], axis=-1),
        )

    n = span_all // SPAN
    sent_in = low_dot(normed_rows, full_scan).reshape(2, span_all, SENT_COLS)
    sent_edge = low_dot(edges16, full_scan).reshape(2, 8, SENT_COLS)
    quarter = jnp.concatenate(
        [sent_edge[..., PART : PART + QUARTER], sent_in[..., PART : PART + QUARTER]], axis=1
    ).astype(bf16)
    half = beside(quarter, swap(quarter[::-1], "c"), ci)
    every_bc = beside(half, swap(half, "x"), xi).astype(f32)
    scan_in = jnp.concatenate(
        [sent_in[..., :PART], every_bc[:, 8:], sent_in[..., PART + QUARTER :]], axis=-1
    )
    edge_rows = jnp.concatenate([sent_edge[..., :PART], every_bc[:, :8]], axis=-1)[:, None]
    before = jnp.concatenate(
        [
            edge_rows,
            scan_in.reshape(2, n, SPAN, SCAN_COLS)[:, : n - 1, SPAN - 8 :, :CONV_COLS],
        ],
        axis=1,
    )

    def rank_channels(array):
        return jnp.concatenate(
            [heads_mine(array[..., :INNER], MAMBA_HEAD), array[..., INNER:]], axis=-1
        )

    def per_head(array):
        return jnp.pad(heads_mine(array, 1), (0, DT_PAD - HEADS))[None]

    taps, bias = rank_channels(conv_weight), rank_channels(conv_bias)[None]
    dt_b, rates = per_head(dt_bias), per_head(-jnp.exp(a_log))
    skip = jnp.repeat(heads_mine(skip_gain, 1), MAMBA_HEAD)[None]
    gain = heads_mine(gated_gain, MAMBA_HEAD)[None]
    lift = (
        jnp.arange(DT_PAD, dtype=jnp.int32)[:, None]
        == jnp.arange(PART, dtype=jnp.int32)[None] // MAMBA_HEAD
    ).astype(bf16)
    mixed, steps, starts, prefix, own_state = scan_states(
        scan_in, before, taps, bias, dt_b, rates, lift
    )
    log_decay = starts[:, n - 1, 0] + steps[:, span_all - 1, DT_PAD:]
    own_decay = jnp.repeat(jnp.exp(log_decay[:, :HEADS]), MAMBA_HEAD, axis=-1)

    def turned(array, distance):
        return lax.ppermute(array, "z", [(i, (i + distance) % nz) for i in range(nz)])

    if aligned:
        first_rows = after(sent_rows, full_scan)
        along_z = jnp.stack([turned(first_rows, d) for d in range(nz - 1, 0, -1)] + [first_rows])
        along_z = lax.dynamic_slice_in_dim(
            jnp.concatenate([along_z, along_z], 0), nz - 1 - zi, nz, 0
        )
        other_y = swap(along_z, "y")
        full_rows = jnp.where(
            yi == 0, jnp.stack([along_z, other_y], 1), jnp.stack([other_y, along_z], 1)
        )
        full_out = full_rows[:, :, :out_rows].reshape(PART, D)
        full_o = full_rows[:, :, out_rows:].reshape(QP, D)
    else:
        every_out = lax.all_gather(w_out, EVERY, axis=0, tiled=True)
        every_o = lax.all_gather(w_o, EVERY, axis=0, tiled=True)
        full_out = lax.dynamic_slice_in_dim(every_out, (2 * xi + ci) * PART, PART, 0)
        every_o = every_o.reshape(2, 2, 2, HEAD_DIM, D)
        every_o = lax.dynamic_index_in_dim(every_o, xi, 2, keepdims=False)
        full_o = lax.dynamic_index_in_dim(every_o, ci, 0, keepdims=False).reshape(QP, D)

    def chained(local, step, pin=None):
        entering = []
        for s in range(2):
            held = jnp.zeros(local.shape[1:], f32)
            for hop in range(nz - 1):
                at = hop if step == 1 else nz - 1 - hop
                leaving = local[s] + own_decay[s][None] * held if hop else local[s]
                if pin is not None and hop == nz - 2:
                    leaving = after(leaving, pin)
                held = held + lax.ppermute(
                    leaving.astype(bf16), "z", [(at, at + step)]
                ).astype(f32)
            entering.append(held)
        return jnp.stack(entering)

    packed_ff = jnp.concatenate([split_ff(w_gate), split_ff(w_up)], axis=2)
    rest = low_dot(normed_rows, full_rest).reshape(2, span_all, REST_COLS)

    positions = zi * span_all + jnp.arange(span_all, dtype=jnp.int32)
    cosine, sine = rope_tables(positions)
    query16 = (
        rotate(rest[..., AT_Q:AT_K].reshape(2, span_all, 2, HEAD_DIM), cosine, sine)
        .astype(bf16)
        .reshape(2, span_all, QP)
    )
    key16 = rotate(rest[..., None, AT_K:AT_V], cosine, sine).astype(bf16)[:, :, 0]
    kv16 = jnp.stack([key16, rest[..., AT_V:].astype(bf16)])
    state_in = chained(own_state, 1, kv16)
    kv_before = [shifted(kv16, d) for d in range(nz - 1, 0, -1)]
    keys_at = (zi - nz + 1) * span_all + jnp.arange(nz * span_all, dtype=jnp.int32)
    query_place = jnp.broadcast_to(positions[:, None], (span_all, 128))
    key_place = jnp.broadcast_to(keys_at[None], (8, nz * span_all))
    values, flat, square = scan_values(
        mixed, steps, starts, prefix, state_in, rest, 0, skip, lift
    )
    kv_all = jnp.concatenate(list(after(tuple(kv_before), flat)) + [kv16], axis=2)
    attended, log_sum = attend(query16, kv_all[0], kv_all[1], query_place, key_place)
    attended16 = attended.reshape(tokens, QP).astype(bf16)

    root = lax.rsqrt(group_total(square[..., :1]) / INNER + epsilon)
    gated16 = (flat * root * gain).astype(bf16).reshape(tokens, PART)
    full_ff = gathered(
        after(to_ranks(packed_ff).reshape(4 * rows, 2 * hidden_part), mixed, cotangent16)
    )
    mixture = low_dot(gated16, full_out) + low_dot(attended16, full_o)
    hidden_state = resident + scatter_sequences(mixture.reshape(2, span_all, D))

    middle, mid_back = jax.vjp(rms_scale, hidden_state, mid_gain)
    middle16 = jnp.concatenate(gather_tokens(permuted(middle.astype(bf16))), 0)
    full_down = gathered(after(w_down, hidden_state))
    both = low_dot(middle16, full_ff)
    activated, swish_back = jax.vjp(
        swish_product, both[:, :hidden_part], both[:, hidden_part:]
    )
    activated16 = activated.astype(bf16)
    down = low_dot(activated16, full_down).reshape(4, length, D)
    output = (hidden_state + scatter_tokens(down)).astype(bf16)

    def to_owners(array):
        return lax.psum_scatter(array, SHARDS, scatter_dimension=0, tiled=True)

    down_grad = weight_grad(activated16, cotangent16).astype(bf16)
    down_owned = to_owners(down_grad)
    result_down = down_owned.astype(f32)
    gate_grad, up_grad = swish_back(back_dot(after(cotangent16, down_grad), full_down))
    both16 = jnp.concatenate([gate_grad, up_grad], axis=1).astype(bf16)
    mid_grad = restored(scatter_tokens(back_dot(both16, full_ff).reshape(4, length, D)))
    hidden_piece, mid_gain_grad = mid_back(mid_grad)
    hidden_grad = out_grad[0].astype(f32) + hidden_piece
    ff_grad = weight_grad(middle16, both16).astype(bf16)
    mix16 = gather_sequences(after(hidden_grad.astype(bf16), ff_grad)).reshape(tokens, D)
    ff_owned = to_owners(after(ff_grad, down_owned, mix16))
    ff_parts = to_ranks(ff_owned.reshape(4, rows, 2 * hidden_part))
    result_gate = join_ff(ff_parts[..., :hidden_part]).astype(f32)
    result_up = join_ff(ff_parts[..., hidden_part:]).astype(f32)
    attended_grad16 = back_dot(mix16, full_o).astype(bf16).reshape(2, span_all, QP)
    gated_grad = back_dot(mix16, full_out).reshape(2, span_all, PART)
    grad_out_w = weight_grad(gated16, mix16).astype(bf16)
    grad_o = weight_grad(attended16, mix16).astype(bf16)
    if aligned:
        rows_grad = jnp.concatenate(
            [grad_out_w.reshape(nz, 2, out_rows, D), grad_o.reshape(nz, 2, o_rows, D)], axis=2
        )
        other_y = lax.dynamic_index_in_dim(rows_grad, 1 - yi, 1, keepdims=False)
        both_y = lax.dynamic_index_in_dim(rows_grad, yi, 1, keepdims=False).astype(f32) + swap(
            other_y, "y"
        ).astype(f32)
    else:
        both_y = grad_o

    inner = jnp.sum(gated_grad * gain * flat, axis=-1, keepdims=True) * root
    inner_mean = group_total(inner) / INNER
    wide = (2, span_all, 128)
    value_grad, gate_z_grad, gain_grad, suffix, first_grad = gate_backward(
        after(gated_grad, down_owned),
        values,
        rest,
        0,
        jnp.broadcast_to(root, wide),
        jnp.broadcast_to(inner_mean, wide),
        gain,
        mixed,
        steps,
        lift,
    )
    mixed_grad, step_grad, skip_grad = scan_backward(
        mixed, steps, starts, prefix, state_in, suffix, value_grad, skip, lift
    )
    state_grad = chained(first_grad, -1, mixed_grad)

    query_grad, kv_grads = attend_backward(
        after(query16, first_grad),
        kv_all[0],
        kv_all[1],
        attended_grad16,
        attended,
        log_sum,
        query_place,
        key_place,
    )
    kv_grads = kv_grads.reshape(2, 2, nz, span_all, HEAD_DIM)
    kv_grad = kv_grads[:, :, nz - 1]
    for d in range(1, nz):
        kv_grad = kv_grad + shifted(kv_grads[:, :, nz - 1 - d].astype(bf16), -d).astype(f32)
    query_back = rotate(
        query_grad.reshape(2, span_all, 2, HEAD_DIM), cosine, -sine
    ).reshape(2, span_all, QP)
    key_back = rotate(kv_grad[0][:, :, None], cosine, -sine)[:, :, 0]
    rest_grad16 = jnp.concatenate(
        [
            gate_z_grad,
            query_back.astype(bf16),
            key_back.astype(bf16),
            kv_grad[1].astype(bf16),
        ],
        axis=-1,
    ).reshape(tokens, REST_COLS)

    scan_grad16, edge_grad, conv_grad, small_grad = finish_backward(
        scan_in,
        before,
        mixed,
        steps,
        starts,
        prefix,
        state_in,
        after(state_grad, ff_owned, both_y),
        mixed_grad,
        step_grad,
        taps,
        bias,
        dt_b,
        rates,
        lift,
    )
    edge_back = shifted(edge_grad[:, 8 - edge_count :].astype(bf16), -1).astype(f32)
    last_rows = scan_grad16[:, span_all - edge_count :, :CONV_COLS].astype(f32) + edge_back
    scan_grad16 = lax.dynamic_update_slice(
        scan_grad16, last_rows.astype(bf16), (0, span_all - edge_count, 0)
    )
    bc_grad = scan_grad16[..., PART:CONV_COLS].reshape(2, span_all, 2, 2 * QUARTER)
    half_grad = lax.dynamic_index_in_dim(bc_grad, xi, 2, keepdims=False).astype(f32) + swap(
        lax.dynamic_index_in_dim(bc_grad, 1 - xi, 2, keepdims=False), "x"
    ).astype(f32)
    half_grad = half_grad.reshape(2, span_all, 2, QUARTER)
    leaving = lax.dynamic_index_in_dim(half_grad, 1 - ci, 2, keepdims=False)
    quarter_grad = lax.dynamic_index_in_dim(half_grad, ci, 2, keepdims=False) + swap(
        leaving[::-1].astype(bf16), "c"
    ).astype(f32)
    sent_grad16 = jnp.concatenate(
        [scan_grad16[..., :PART], quarter_grad.astype(bf16), scan_grad16[..., CONV_COLS:]],
        axis=-1,
    ).reshape(tokens, SENT_COLS)
    if aligned:
        rows_owned = lax.dynamic_index_in_dim(both_y, zi, 0, keepdims=False)
        waiting = after(both_y.astype(bf16), state_grad)
        for d in range(1, nz):
            leaving = lax.dynamic_index_in_dim(waiting, (zi + d) % nz, 0, keepdims=False)
            rows_owned = rows_owned + turned(leaving, d).astype(f32)
        rows_owned = rows_owned.astype(bf16)
        result_out = lax.ppermute(rows_owned[:out_rows], ("y", "c"), turn).astype(f32)
        result_o = lax.ppermute(rows_owned[out_rows:], ("z", "y", "c"), back_place).astype(f32)
    else:
        every_out = lax.dynamic_update_slice_in_dim(
            jnp.zeros((INNER, D), bf16), grad_out_w, (2 * xi + ci) * PART, 0
        )
        every_o = lax.dynamic_update_slice(
            jnp.zeros((2, 2, 2, HEAD_DIM, D), bf16),
            grad_o.reshape(1, 2, 1, HEAD_DIM, D),
            (ci, 0, xi, 0, 0),
        ).reshape(ATT_HEADS * HEAD_DIM, D)
        result_out = lax.psum_scatter(every_out, EVERY, scatter_dimension=0, tiled=True)
        result_o = lax.psum_scatter(every_o, EVERY, scatter_dimension=0, tiled=True)
        result_out, result_o = result_out.astype(f32), result_o.astype(f32)
    rest_owned = to_owners(
        after(weight_grad(normed_rows, rest_grad16).astype(bf16), ff_owned, state_grad)
    )
    rest_parts = to_ranks(rest_owned.reshape(4, rows, REST_COLS)).astype(f32)
    scan_owned = to_owners(
        after(weight_grad(normed_rows, sent_grad16).astype(bf16), rest_owned)
    )

    normed_grad = back_dot(sent_grad16, full_scan) + back_dot(rest_grad16, full_rest)
    normed_grad = restored(scatter_sequences(normed_grad.reshape(2, span_all, D)))
    resident_grad, norm_gain_grad = norm_back(normed_grad)
    input_grad = hidden_grad + resident_grad

    result_q = jnp.transpose(
        rest_parts[..., AT_Q:AT_K].reshape(2, 2, rows, 2, HEAD_DIM), (2, 1, 3, 0, 4)
    ).reshape(rows, ATT_HEADS * HEAD_DIM)
    kv_parts = jnp.sum(rest_parts[..., AT_K:].reshape(2, 2, rows, 2, HEAD_DIM), axis=0)
    result_k = jnp.transpose(kv_parts[:, :, 0], (1, 0, 2)).reshape(rows, KV_HEADS * HEAD_DIM)
    result_v = jnp.transpose(kv_parts[:, :, 1], (1, 0, 2)).reshape(rows, KV_HEADS * HEAD_DIM)

    def all_channels(array):
        return jnp.concatenate(
            [heads_spread(array[..., :PART], MAMBA_HEAD), array[..., PART:]], axis=-1
        )

    small = [
        norm_gain_grad,
        all_channels(conv_grad[:4]),
        all_channels(conv_grad[4]),
        heads_spread(small_grad[0, :HEADS], 1),
        heads_spread(small_grad[1, :HEADS], 1),
        heads_spread(skip_grad[0, :HEADS], 1),
        heads_spread(gain_grad[0], MAMBA_HEAD),
        mid_gain_grad,
    ]
    summed = total(jnp.concatenate([v.reshape(-1) for v in small]))
    parts, at = [], 0
    for v in small:
        parts.append(summed[at : at + v.size].reshape(v.shape))
        at += v.size
    scan_owned = after(
        scan_owned,
        summed,
        input_grad,
        output,
        rest_parts,
        result_gate,
        result_up,
        result_down,
        result_q,
        result_k,
        result_v,
        result_out,
        result_o,
    )
    scan_parts = to_ranks(scan_owned.reshape(4, rows, SENT_COLS)).astype(f32)
    result_in = jnp.concatenate(
        [
            heads_join(rest_parts[..., :PART], MAMBA_HEAD),
            heads_join(scan_parts[..., :PART], MAMBA_HEAD),
            jnp.swapaxes(scan_parts[..., PART : PART + QUARTER], 0, 1).reshape(rows, BC),
            heads_join(scan_parts[..., PART + QUARTER : PART + QUARTER + HEADS], 1),
        ],
        axis=1,
    )
    return (
        output[None],
        input_grad[None],
        parts[0],
        result_in,
        parts[1],
        parts[2],
        parts[3],
        parts[4],
        parts[5],
        parts[6],
        result_out,
        result_q,
        result_k,
        result_v,
        result_o,
        parts[7],
        result_gate,
        result_up,
        result_down,
    )


def solution(mesh):
    seq, fsdp = mesh.shape["seq"], mesh.shape["fsdp"]
    split = Mesh(mesh.devices.reshape(seq // 2, 2, fsdp // 2, 2), EVERY)
    tokens = P(("y", "c"), ("z", "x"), None)
    matrix = P(EVERY, None)
    return jax.shard_map(
        body,
        mesh=split,
        in_specs=(tokens, tokens, P(), matrix)
        + (P(),) * 6
        + (matrix,) * 5
        + (P(),)
        + (matrix,) * 3,
        out_specs=(tokens, tokens, P(), matrix)
        + (P(),) * 6
        + (matrix,) * 5
        + (P(),)
        + (matrix,) * 3,
        check_vma=False,
    )
```

```python
import jax
import jax.numpy as jnp
from jax import lax
from jax.experimental import pallas as pl
from jax.experimental.pallas import tpu as pltpu
from jax.sharding import Mesh
from jax.sharding import PartitionSpec as P

D = 2048
MAMBA_HEADS = 48
MAMBA_HEAD = 64
STATE = 256
ATT_HEADS = 8
KV_HEADS = 2
HEAD_DIM = 128
SPAN = 128
INNER = 3072

HEADS = MAMBA_HEADS // 4
PART = HEADS * MAMBA_HEAD
BC = 2 * STATE
DT_PAD = 128
QP = 2 * HEAD_DIM
CONV_COLS = PART + BC
SCAN_COLS = CONV_COLS + DT_PAD
QUARTER = BC // 4
SENT_COLS = PART + QUARTER + DT_PAD
AT_Q = PART
AT_K = AT_Q + QP
AT_V = AT_K + HEAD_DIM
REST_COLS = AT_V + HEAD_DIM

epsilon = 1e-05
rope_base = 100000000000.0
GROUP = ("x", "c")
SHARDS = ("z", "y")
EVERY = ("z", "x", "y", "c")
bf16 = jnp.bfloat16
f32 = jnp.float32


def swap(array, axis):
    return lax.ppermute(array, axis, [(0, 1), (1, 0)])


def shifted(array, distance):
    devices = range(lax.axis_size("z"))
    return lax.ppermute(array, "z", [(i - distance, i) for i in devices if i - distance in devices])


def total(array):
    for axis in EVERY:
        size = lax.axis_size(axis)
        bit = 1
        while bit < size:
            array = array + lax.ppermute(array, axis, [(i, i ^ bit) for i in range(size)])
            bit *= 2
    return array


def group_total(array):
    array = array + swap(array[::-1], "c")
    return array + swap(array, "x")


def low_dot(left, right):
    return jnp.dot(left, right, preferred_element_type=f32)


def back_dot(grad_rows, weight):
    return lax.dot_general(grad_rows, weight, (((1,), (1,)), ((), ())), preferred_element_type=f32)


def weight_grad(left, right):
    return lax.dot_general(left, right, (((0,), (0,)), ((), ())), preferred_element_type=f32)


def rms_scale(values, gain):
    return values * lax.rsqrt(jnp.mean(values * values, axis=-1, keepdims=True) + epsilon) * gain


def rope_tables(positions):
    half_dim = HEAD_DIM // 2
    frequencies = rope_base ** (-jnp.arange(half_dim, dtype=f32) / half_dim)
    angles = positions.astype(f32)[:, None] * frequencies[None, :]
    return (jnp.cos(angles), jnp.sin(angles))


def rotate(values, cosine, sine):
    half_dim = HEAD_DIM // 2
    cosine, sine = cosine[:, None, :], sine[:, None, :]
    first, second = values[..., :half_dim], values[..., half_dim:]
    return jnp.concatenate([first * cosine - second * sine, second * cosine + first * sine], axis=-1)


def pieces(values, count):
    parts = []
    for _ in range(count):
        part = values.astype(bf16)
        parts.append(part)
        values = values - part.astype(f32)
    return parts


def running(mask, values):
    mask16 = mask.astype(bf16)
    return sum(low_dot(mask16, part) for part in pieces(values, 3))


def over_lanes(left, right):
    return lax.dot_general(left, right, (((1,), (1,)), ((), ())), preferred_element_type=f32)


def over_rows(left, right):
    return lax.dot_general(left, right, (((0,), (0,)), ((), ())), preferred_element_type=f32)


def widen(values, lift):
    return sum(low_dot(part, lift) for part in pieces(values, 2))


def narrow(values, lift):
    return sum(over_lanes(part, lift) for part in pieces(values, 2))


def sig(values):
    return 1.0 / (1.0 + jnp.exp(-values))


def soft(values):
    return jnp.maximum(values, 0.0) + jnp.log1p(jnp.exp(-jnp.abs(values)))


def square_places():
    return (
        lax.broadcasted_iota(jnp.int32, (SPAN, SPAN), 0),
        lax.broadcasted_iota(jnp.int32, (SPAN, SPAN), 1),
    )


def pre_conv(current, before, taps, bias):
    extended = jnp.concatenate([before, current], axis=0)
    pre = bias + extended[5 : 5 + SPAN] * taps[0:1]
    for k in range(1, 4):
        pre = pre + extended[5 + k : 5 + k + SPAN] * taps[k : k + 1]
    return (pre, extended)


def states_kernel(
    scan_in, before, taps, bias, dt_bias, rates, lift, mixed, steps, starts, prefix, last, held, sofar
):
    @pl.when(pl.program_id(1) == 0)
    def _():
        held[...] = jnp.zeros_like(held)
        sofar[...] = jnp.zeros_like(sofar)

    pre, _ = pre_conv(scan_in[0, :, :CONV_COLS], before[0, 0], taps[...], bias[...])
    mix = pre * sig(pre)
    mixed[0] = mix
    dt = soft(scan_in[0, :, CONV_COLS:] + dt_bias[...])
    row, column = square_places()
    cum = running(jnp.where(row >= column, 1.0, 0.0), dt * rates[...])
    steps[0, :, :DT_PAD] = dt
    steps[0, :, DT_PAD:] = cum
    starts[0, 0] = sofar[...]
    prefix[0, 0] = held[...]
    end = cum[SPAN - 1 : SPAN]
    tail = jnp.exp(end - cum) * dt
    fed = (mix[:, :PART] * widen(tail, lift[...])).astype(bf16)
    added = over_rows(mix[:, PART : PART + STATE].astype(bf16), fed)
    whole = widen(jnp.broadcast_to(jnp.exp(end), (8, DT_PAD)), lift[...])[0:1]
    held[...] = whole * held[...] + added
    sofar[...] = sofar[...] + end
    last[0] = held[...]


def values_kernel(
    mixed, steps, starts, prefix, state_in, gate, skip, lift, values, flat, square
):
    x = mixed[0, :, :PART]
    b16 = mixed[0, :, PART : PART + STATE].astype(bf16)
    c16 = mixed[0, :, PART + STATE :].astype(bf16)
    dt = steps[0, :, :DT_PAD]
    cum = steps[0, :, DT_PAD:]
    dt_t, cum_t = dt.T, cum.T
    state = prefix[0, 0] + widen(jnp.exp(starts[0, 0]), lift[...])[0:1] * state_in[0]
    meet = over_lanes(c16, b16)
    carried = low_dot(c16, state.astype(bf16)) * widen(jnp.exp(cum), lift[...])
    row, column = square_places()
    first = column < MAMBA_HEAD
    inside = []
    for k in range(HEADS // 2):
        pair = x[:, 2 * MAMBA_HEAD * k : 2 * MAMBA_HEAD * (k + 1)]
        weights = []
        for h in (2 * k, 2 * k + 1):
            spread = cum[:, h : h + 1] - cum_t[h : h + 1, :]
            decay = jnp.exp(jnp.where(row >= column, spread, -1e30))
            weights.append((meet * decay * dt_t[h : h + 1, :]).astype(bf16))
        split = [
            jnp.where(first, pair, 0.0).astype(bf16),
            jnp.where(first, 0.0, pair).astype(bf16),
        ]
        inside.append(low_dot(jnp.concatenate(weights, 1), jnp.concatenate(split, 0)))
    value = jnp.concatenate(inside, 1) + carried + skip[...] * x
    values[0] = value
    z = gate[0]
    product = value * (z * sig(z))
    flat[0] = product
    square[0] = jnp.broadcast_to(
        jnp.sum(product * product, axis=1, keepdims=True), (SPAN, 128)
    )


def gate_back_kernel(
    gated_grad, values, gate, root, mean, gain, c_part, steps, lift,
    value_grad, gate_grad, gain_grad, suffix, first_grad, held,
):
    @pl.when(pl.program_id(1) == 0)
    def _():
        held[...] = jnp.zeros_like(held)

    @pl.when((pl.program_id(0) == 0) & (pl.program_id(1) == 0))
    def _():
        gain_grad[...] = jnp.zeros_like(gain_grad)

    z, value, grad = gate[0], values[0], gated_grad[0]
    s = sig(z)
    silu = z * s
    scale = root[0, :, 0:1]
    normal = value * silu * scale
    flat_grad = scale * (grad * gain[...] - normal * mean[0, :, 0:1])
    d_value = flat_grad * silu
    value_grad[0] = d_value
    gate_grad[0] = (flat_grad * value * (s * (1.0 + z * (1.0 - s)))).astype(bf16)
    gain_grad[0:1] = gain_grad[0:1] + jnp.sum(grad * normal, axis=0, keepdims=True)
    grown = widen(jnp.exp(steps[0, :, DT_PAD:]), lift[...])
    suffix[0, 0] = held[...]
    held[...] = grown[SPAN - 1 : SPAN] * held[...] + over_rows(
        c_part[0].astype(bf16), (grown * d_value).astype(bf16)
    )
    first_grad[0] = held[...]


def scan_back_kernel(
    mixed, steps, starts, prefix, state_in, suffix, value_grad, skip, lift,
    mixed_grad, step_grad, skip_grad, columns,
):
    @pl.when((pl.program_id(0) == 0) & (pl.program_id(1) == 0))
    def _():
        skip_grad[...] = jnp.zeros_like(skip_grad)
        columns[...] = jnp.zeros_like(columns)

    up = lift[...]
    x = mixed[0, :, :PART]
    b16 = mixed[0, :, PART : PART + STATE].astype(bf16)
    c16 = mixed[0, :, PART + STATE :].astype(bf16)
    dt = steps[0, :, :DT_PAD]
    cum = steps[0, :, DT_PAD:]
    dt_t, cum_t = dt.T, cum.T
    end = cum[SPAN - 1 : SPAN]
    dy = value_grad[0]
    state = prefix[0, 0] + widen(jnp.exp(starts[0, 0]), up)[0:1] * state_in[0]
    ending = suffix[0, 0]
    state16, ending16 = state.astype(bf16), ending.astype(bf16)
    grown_dy = widen(jnp.exp(cum), up) * dy
    tail_wide = widen(jnp.exp(end - cum), up)
    dt_wide = widen(dt, up)
    reach = low_dot(c16, state16)
    pull = tail_wide * low_dot(b16, ending16)
    d_c = over_lanes(grown_dy.astype(bf16), state16)
    d_b = over_lanes((tail_wide * dt_wide * x).astype(bf16), ending16)
    meet = over_lanes(c16, b16)
    row, column = square_places()
    first = column < MAMBA_HEAD
    d_meet = jnp.zeros((SPAN, SPAN), f32)
    rows_sum = jnp.zeros((SPAN, DT_PAD), f32)
    back = []
    for k in range(HEADS // 2):
        at = slice(2 * MAMBA_HEAD * k, 2 * MAMBA_HEAD * (k + 1))
        x16, dy_pair = x[:, at].astype(bf16), dy[:, at]
        split = [
            jnp.where(first, dy_pair, 0.0).astype(bf16),
            jnp.where(first, 0.0, dy_pair).astype(bf16),
        ]
        weights = []
        for j in range(2):
            h = 2 * k + j
            spread = cum[:, h : h + 1] - cum_t[h : h + 1, :]
            decay = jnp.exp(jnp.where(row >= column, spread, -1e30))
            d_weight = over_lanes(split[j], x16) * decay
            scaled = d_weight * dt_t[h : h + 1, :]
            d_meet = d_meet + scaled
            rows_sum = rows_sum + jnp.where(
                column == h, jnp.sum(scaled * meet, axis=1, keepdims=True), 0.0
            )
            columns[h : h + 1, :] = jnp.sum(d_weight * meet, axis=0, keepdims=True)
            weights.append((meet * decay).astype(bf16))
        back.append(over_rows(jnp.concatenate(weights, 0), jnp.concatenate(split, 0)))
    d_meet16 = d_meet.astype(bf16)
    mixed_grad[0, :, :PART] = dt_wide * (jnp.concatenate(back, 1) + pull) + skip[...] * dy
    mixed_grad[0, :, PART : PART + STATE] = d_b + over_rows(d_meet16, c16)
    mixed_grad[0, :, PART + STATE :] = d_c + low_dot(d_meet16, b16)
    tail_dt = narrow(x * pull, up)
    inner_dt = columns[...].T
    d_cum = rows_sum + narrow(grown_dy * reach, up) - dt * (inner_dt + tail_dt)
    kept = narrow(
        jnp.broadcast_to(jnp.sum(state * ending, axis=0, keepdims=True), (8, PART)), up
    )[0:1]
    extra = jnp.sum(dt * tail_dt, axis=0, keepdims=True) + jnp.exp(end) * kept
    step_grad[0, :, :DT_PAD] = inner_dt + tail_dt
    step_grad[0, :, DT_PAD:] = running(jnp.where(row <= column, 1.0, 0.0), d_cum) + extra
    skip_grad[0:1] = skip_grad[0:1] + jnp.sum(narrow(dy * x, up), axis=0, keepdims=True)


def finish_back_kernel(
    scan_in, before, mixed, steps, starts, prefix, state_in, state_grad, mixed_grad, step_grad,
    taps, bias, dt_bias, rates, lift,
    scan_grad, edge_grad, conv_grad, small_grad,
    later, after_pre,
):
    @pl.when(pl.program_id(1) == 0)
    def _():
        later[...] = jnp.zeros_like(later)
        after_pre[...] = jnp.zeros_like(after_pre)

    @pl.when((pl.program_id(0) == 0) & (pl.program_id(1) == 0))
    def _():
        conv_grad[...] = jnp.zeros_like(conv_grad)
        small_grad[...] = jnp.zeros_like(small_grad)

    up = lift[...]
    x = mixed[0, :, :PART]
    b16 = mixed[0, :, PART : PART + STATE].astype(bf16)
    dt = steps[0, :, :DT_PAD]
    cum = steps[0, :, DT_PAD:]
    end = cum[SPAN - 1 : SPAN]
    state = prefix[0, 0] + widen(jnp.exp(starts[0, 0]), up)[0:1] * state_in[0]
    ending = widen(jnp.exp(later[...]), up)[0:1] * state_grad[0]
    later[...] = later[...] + end
    ending16 = ending.astype(bf16)
    tail_wide = widen(jnp.exp(end - cum), up)
    dt_wide = widen(dt, up)
    pull = tail_wide * low_dot(b16, ending16)
    d_x = mixed_grad[0, :, :PART] + dt_wide * pull
    d_b = mixed_grad[0, :, PART : PART + STATE] + over_lanes(
        (tail_wide * dt_wide * x).astype(bf16), ending16
    )
    d_c = mixed_grad[0, :, PART + STATE :]
    tail_dt = narrow(x * pull, up)
    kept = narrow(
        jnp.broadcast_to(jnp.sum(state * ending, axis=0, keepdims=True), (8, PART)), up
    )[0:1]
    row, column = square_places()
    fed = dt * tail_dt
    earlier = running(jnp.where(row > column, 1.0, 0.0), fed)
    d_log = step_grad[0, :, DT_PAD:] + earlier + jnp.exp(end) * kept
    rate = rates[...]
    d_raw = (step_grad[0, :, :DT_PAD] + tail_dt + d_log * rate) * sig(
        scan_in[0, :, CONV_COLS:] + dt_bias[...]
    )
    small_grad[0:1] = small_grad[0:1] + jnp.sum(d_raw, axis=0, keepdims=True)
    small_grad[1:2] = small_grad[1:2] + jnp.sum(d_log * dt * rate, axis=0, keepdims=True)

    pre, extended = pre_conv(scan_in[0, :, :CONV_COLS], before[0, 0], taps[...], bias[...])
    s = sig(pre)
    d_pre = jnp.concatenate([d_x, d_b, d_c], axis=1) * (s * (1.0 + pre * (1.0 - s)))
    for k in range(4):
        conv_grad[k : k + 1] = conv_grad[k : k + 1] + jnp.sum(
            d_pre * extended[5 + k : 5 + k + SPAN], axis=0, keepdims=True
        )
    conv_grad[4:5] = conv_grad[4:5] + jnp.sum(d_pre, axis=0, keepdims=True)
    following = jnp.concatenate([d_pre, after_pre[...]], axis=0)
    d_in = following[0:SPAN] * taps[3:4]
    for k in range(3):
        d_in = d_in + following[3 - k : 3 - k + SPAN] * taps[k : k + 1]
    scan_grad[0, :, :CONV_COLS] = d_in.astype(bf16)
    scan_grad[0, :, CONV_COLS:] = d_raw.astype(bf16)
    front = d_pre[0:8]
    after_pre[...] = front
    nothing = jnp.zeros((8, CONV_COLS), f32)
    padded = jnp.concatenate([nothing, front, nothing], 0)
    edge = padded[0:8] * taps[3:4]
    for k in range(3):
        edge = edge + padded[3 - k : 11 - k] * taps[k : k + 1]
    edge_grad[0] = edge


def one(shape):
    return pl.BlockSpec(shape, lambda b, i: (0,) * len(shape))


def by_span(width, column=0, reverse=None):
    if reverse is None:
        return pl.BlockSpec((1, SPAN, width), lambda b, i: (b, i, column))
    return pl.BlockSpec((1, SPAN, width), lambda b, i: (b, reverse - 1 - i, column))


def by_piece(rows, width, reverse=None):
    if reverse is None:
        return pl.BlockSpec((1, 1, rows, width), lambda b, i: (b, i, 0, 0))
    return pl.BlockSpec((1, 1, rows, width), lambda b, i: (b, reverse - 1 - i, 0, 0))


def by_sequence(rows, width):
    return pl.BlockSpec((1, rows, width), lambda b, i: (b, 0, 0))


def grid_call(kernel, spans, ins, outs, scratch, flops, moved):
    return pl.pallas_call(
        kernel,
        grid=(2, spans),
        in_specs=ins,
        out_specs=[spec for spec, _ in outs],
        out_shape=[shape for _, shape in outs],
        scratch_shapes=scratch,
        compiler_params=pltpu.CompilerParams(
            dimension_semantics=("arbitrary", "arbitrary"), vmem_limit_bytes=50 * 2**20
        ),
        cost_estimate=pl.CostEstimate(flops=flops, bytes_accessed=moved, transcendentals=0),
    )


def like(shape, kind=f32):
    return jax.ShapeDtypeStruct(shape, kind)


def scan_states(scan_in, before, taps, bias, dt_bias, rates, lift):
    length = scan_in.shape[1]
    n = length // SPAN
    return grid_call(
        states_kernel,
        n,
        [
            by_span(SCAN_COLS),
            by_piece(8, CONV_COLS),
            one((4, CONV_COLS)),
            one((1, CONV_COLS)),
            one((1, DT_PAD)),
            one((1, DT_PAD)),
            one((DT_PAD, PART)),
        ],
        [
            (by_span(CONV_COLS), like((2, length, CONV_COLS))),
            (by_span(2 * DT_PAD), like((2, length, 2 * DT_PAD))),
            (by_piece(8, DT_PAD), like((2, n, 8, DT_PAD))),
            (by_piece(STATE, PART), like((2, n, STATE, PART))),
            (by_sequence(STATE, PART), like((2, STATE, PART))),
        ],
        [pltpu.VMEM((STATE, PART), f32), pltpu.VMEM((8, DT_PAD), f32)],
        8 * 10**9,
        30 * 10**6,
    )(scan_in, before, taps, bias, dt_bias, rates, lift)


def scan_values(mixed, steps, starts, prefix, state_in, rest, gate_at, skip, lift):
    length = mixed.shape[1]
    n = length // SPAN
    return grid_call(
        values_kernel,
        n,
        [
            by_span(CONV_COLS),
            by_span(2 * DT_PAD),
            by_piece(8, DT_PAD),
            by_piece(STATE, PART),
            by_sequence(STATE, PART),
            by_span(PART, gate_at),
            one((1, PART)),
            one((DT_PAD, PART)),
        ],
        [
            (by_span(PART), like((2, length, PART))),
            (by_span(PART), like((2, length, PART))),
            (by_span(128), like((2, length, 128))),
        ],
        [],
        12 * 10**9,
        30 * 10**6,
    )(mixed, steps, starts, prefix, state_in, rest, skip, lift)


def gate_backward(gated_grad, values, rest, gate_at, root, mean, gain, mixed, steps, lift):
    length = mixed.shape[1]
    n = length // SPAN
    return grid_call(
        gate_back_kernel,
        n,
        [
            by_span(PART, 0, n),
            by_span(PART, 0, n),
            by_span(PART, gate_at, n),
            by_span(128, 0, n),
            by_span(128, 0, n),
            one((1, PART)),
            by_span(STATE, (PART + STATE) // STATE, n),
            by_span(2 * DT_PAD, 0, n),
            one((DT_PAD, PART)),
        ],
        [
            (by_span(PART, 0, n), like((2, length, PART))),
            (by_span(PART, 0, n), like((2, length, PART), bf16)),
            (one((8, PART)), like((8, PART))),
            (by_piece(STATE, PART, n), like((2, n, STATE, PART))),
            (by_sequence(STATE, PART), like((2, STATE, PART))),
        ],
        [pltpu.VMEM((STATE, PART), f32)],
        8 * 10**9,
        30 * 10**6,
    )(gated_grad, values, rest, root, mean, gain, mixed, steps, lift)


def scan_backward(mixed, steps, starts, prefix, state_in, suffix, value_grad, skip, lift):
    length = mixed.shape[1]
    n = length // SPAN
    return grid_call(
        scan_back_kernel,
        n,
        [
            by_span(CONV_COLS),
            by_span(2 * DT_PAD),
            by_piece(8, DT_PAD),
            by_piece(STATE, PART),
            by_sequence(STATE, PART),
            by_piece(STATE, PART),
            by_span(PART),
            one((1, PART)),
            one((DT_PAD, PART)),
        ],
        [
            (by_span(CONV_COLS), like((2, length, CONV_COLS))),
            (by_span(2 * DT_PAD), like((2, length, 2 * DT_PAD))),
            (one((8, DT_PAD)), like((8, DT_PAD))),
        ],
        [pltpu.VMEM((SPAN, SPAN), f32)],
        30 * 10**9,
        40 * 10**6,
    )(mixed, steps, starts, prefix, state_in, suffix, value_grad, skip, lift)


def finish_backward(
    scan_in, before, mixed, steps, starts, prefix, state_in, state_grad, mixed_grad, step_grad,
    taps, bias, dt_bias, rates, lift,
):
    length = mixed.shape[1]
    n = length // SPAN
    return grid_call(
        finish_back_kernel,
        n,
        [
            by_span(SCAN_COLS, 0, n),
            by_piece(8, CONV_COLS, n),
            by_span(CONV_COLS, 0, n),
            by_span(2 * DT_PAD, 0, n),
            by_piece(8, DT_PAD, n),
            by_piece(STATE, PART, n),
            by_sequence(STATE, PART),
            by_sequence(STATE, PART),
            by_span(CONV_COLS, 0, n),
            by_span(2 * DT_PAD, 0, n),
            one((4, CONV_COLS)),
            one((1, CONV_COLS)),
            one((1, DT_PAD)),
            one((1, DT_PAD)),
            one((DT_PAD, PART)),
        ],
        [
            (by_span(SCAN_COLS, 0, n), like((2, length, SCAN_COLS), bf16)),
            (by_sequence(8, CONV_COLS), like((2, 8, CONV_COLS))),
            (one((8, CONV_COLS)), like((8, CONV_COLS))),
            (one((8, DT_PAD)), like((8, DT_PAD))),
        ],
        [pltpu.VMEM((8, DT_PAD), f32), pltpu.VMEM((8, CONV_COLS), f32)],
        15 * 10**9,
        50 * 10**6,
    )(
        scan_in, before, mixed, steps, starts, prefix, state_in, state_grad, mixed_grad, step_grad,
        taps, bias, dt_bias, rates, lift,
    )


def attend_kernel(query, key, value, query_place, key_place, attended, log_sum):
    scores = over_lanes(query[0], key[0]) * HEAD_DIM ** (-0.5)
    seen = (key_place[0:1] >= 0) & (query_place[:, 0:1] >= key_place[0:1])
    scores = jnp.where(seen, scores, -1e30)
    peak = jnp.max(scores, axis=1, keepdims=True)
    unscaled = jnp.exp(scores - peak)
    whole = jnp.sum(unscaled, axis=1, keepdims=True)
    probs = (unscaled * (1.0 / whole)).astype(bf16)
    attended[0] = low_dot(probs, value[0])
    log_sum[0] = jnp.broadcast_to(peak + jnp.log(whole), log_sum.shape[1:])


def attend_back_kernel(
    query, key, value, grad, attended, log_sum, query_place, key_place, query_grad, kv_grad
):
    @pl.when((pl.program_id(1) == 0) & (pl.program_id(2) == 0))
    def _():
        kv_grad[...] = jnp.zeros_like(kv_grad)

    scale = HEAD_DIM ** (-0.5)
    scores = over_lanes(query[0], key[0]) * scale
    seen = (key_place[0:1] >= 0) & (query_place[:, 0:1] >= key_place[0:1])
    probs = jnp.exp(jnp.where(seen, scores, -1e30) - log_sum[0, :, 0:1])
    delta = jnp.sum(grad[0].astype(f32) * attended[0], axis=1, keepdims=True)
    score_grad = (probs * (over_lanes(grad[0], value[0]) - delta)).astype(bf16)
    query_grad[0] = low_dot(score_grad, key[0]) * scale
    kv_grad[0, 0] = kv_grad[0, 0] + over_rows(score_grad, query[0]) * scale
    kv_grad[1, 0] = kv_grad[1, 0] + over_rows(probs.astype(bf16), grad[0])


def attend_specs(block, keys):
    by_query = pl.BlockSpec((1, block, HEAD_DIM), lambda b, h, i: (b, i, h))
    whole_key = pl.BlockSpec((1, keys, HEAD_DIM), lambda b, h, i: (b, 0, 0))
    place = pl.BlockSpec((block, 128), lambda b, h, i: (i, 0))
    key_at = pl.BlockSpec((8, keys), lambda b, h, i: (0, 0))
    return (by_query, whole_key, place, key_at)


def attend(query, key, value, query_place, key_place):
    length, keys = query.shape[1], key.shape[1]
    block = 256 if keys <= 4096 else 128
    by_query, whole_key, place, key_at = attend_specs(block, keys)
    return pl.pallas_call(
        attend_kernel,
        grid=(2, 2, length // block),
        in_specs=[by_query, whole_key, whole_key, place, key_at],
        out_specs=[by_query, by_query],
        out_shape=[like((2, length, QP)), like((2, length, QP))],
        compiler_params=pltpu.CompilerParams(
            dimension_semantics=("arbitrary",) * 3, vmem_limit_bytes=50 * 2**20
        ),
        cost_estimate=pl.CostEstimate(
            flops=12 * 10**9, bytes_accessed=20 * 10**6, transcendentals=0
        ),
    )(query, key, value, query_place, key_place)


def attend_backward(query, key, value, grad, attended, log_sum, query_place, key_place):
    length, keys = query.shape[1], key.shape[1]
    block = 256 if keys <= 4096 else 128
    by_query, whole_key, place, key_at = attend_specs(block, keys)
    return pl.pallas_call(
        attend_back_kernel,
        grid=(2, 2, length // block),
        in_specs=[by_query, whole_key, whole_key, by_query, by_query, by_query, place, key_at],
        out_specs=[
            by_query,
            pl.BlockSpec((2, 1, keys, HEAD_DIM), lambda b, h, i: (0, b, 0, 0)),
        ],
        out_shape=[like((2, length, QP)), like((2, 2, keys, HEAD_DIM))],
        compiler_params=pltpu.CompilerParams(
            dimension_semantics=("arbitrary",) * 3, vmem_limit_bytes=50 * 2**20
        ),
        cost_estimate=pl.CostEstimate(
            flops=20 * 10**9, bytes_accessed=30 * 10**6, transcendentals=0
        ),
    )(query, key, value, grad, attended, log_sum, query_place, key_place)


def swish_product(gate_proj, up_proj):
    return jax.nn.silu(gate_proj) * up_proj


def gather_tokens(block):
    across = swap(block, "x")
    return (block, swap(block, "c"), across, swap(across, "c"))


def scatter_tokens(blocks):
    near, far = blocks[0], blocks[2]
    sent = swap(jnp.stack([blocks[1].astype(bf16), blocks[3].astype(bf16)]), "c")
    near = near + sent[0].astype(f32)
    far = far + sent[1].astype(f32)
    return near + swap(far.astype(bf16), "x").astype(f32)


def body(
    inputs,
    out_grad,
    norm_gain,
    w_in,
    conv_weight,
    conv_bias,
    dt_bias,
    a_log,
    skip_gain,
    gated_gain,
    w_out,
    w_q,
    w_k,
    w_v,
    w_o,
    mid_gain,
    w_gate,
    w_up,
    w_down,
):
    nz, ny = lax.axis_size("z"), lax.axis_size("y")
    zi, xi, yi, ci = (lax.axis_index(name) for name in ("z", "x", "y", "c"))
    length = inputs.shape[1]
    span_all = 2 * length
    rows = w_in.shape[0]
    ff_rows = w_down.shape[0]
    hidden_part = nz * ny * ff_rows
    edge_count = conv_weight.shape[0] - 1
    out_rows, o_rows = w_out.shape[0], w_o.shape[0]
    aligned = ny == 2 and nz == 4 and MAMBA_HEADS % (4 * nz) == 0
    g = nz if aligned else 1
    hp = HEADS // g

    def heads_mine(array, width):
        lead = array.shape[:-1]
        array = array.reshape(lead + (g, 2, 2, hp * width))
        array = lax.dynamic_index_in_dim(array, xi, len(lead) + 1, keepdims=False)
        array = lax.dynamic_index_in_dim(array, ci, len(lead) + 1, keepdims=False)
        return array.reshape(lead + (HEADS * width,))

    def heads_spread(array, width):
        lead = array.shape[:-1]
        array = array.reshape(lead + (g, 1, 1, hp * width))
        whole = jnp.zeros(lead + (g, 2, 2, hp * width), array.dtype)
        start = (0,) * len(lead) + (0, xi, ci, 0)
        return lax.dynamic_update_slice(whole, array, start).reshape(
            lead + (MAMBA_HEADS * width,)
        )

    def heads_split(array, width):
        n = array.shape[0]
        array = array.reshape(n, g, 2, 2, hp * width)
        return jnp.transpose(array, (2, 3, 0, 1, 4)).reshape(4, n, HEADS * width)

    def heads_join(array, width):
        n = array.shape[1]
        array = array.reshape(2, 2, n, g, hp * width)
        return jnp.transpose(array, (2, 3, 0, 1, 4)).reshape(n, MAMBA_HEADS * width)

    def reordered(array, first, second):
        width = 2 * rows
        return jnp.concatenate(
            [
                array[..., at * width : (at + 1) * width]
                for z in range(nz)
                for at in (
                    (z * first + i) * second + j for j in range(second) for i in range(first)
                )
            ],
            axis=-1,
        )

    def permuted(array):
        return reordered(array, 2, ny)

    def restored(array):
        return reordered(array, ny, 2)

    def to_ranks(array):
        return lax.all_to_all(array, GROUP, 0, 0, tiled=True)

    def in_order(own, other):
        return lax.dynamic_slice_in_dim(
            jnp.concatenate([own, other, own], 0), xi * length, span_all, 0
        )

    def gather_sequences(block):
        own, near, across, far = gather_tokens(block)
        return jnp.stack([in_order(own, across), in_order(near, far)])

    def scatter_sequences(partial):
        mine = partial[0] + swap(partial[1].astype(bf16), "c").astype(f32)
        mine = mine.reshape(2, length, mine.shape[-1])
        own = lax.dynamic_index_in_dim(mine, xi, 0, keepdims=False)
        other = lax.dynamic_index_in_dim(mine, 1 - xi, 0, keepdims=False)
        return own + swap(other.astype(bf16), "x").astype(f32)

    split_q = jnp.transpose(w_q.reshape(rows, 2, 2, 2, HEAD_DIM), (3, 1, 0, 2, 4))
    split_k = jnp.transpose(w_k.reshape(rows, 2, HEAD_DIM), (1, 0, 2))
    split_v = jnp.transpose(w_v.reshape(rows, 2, HEAD_DIM), (1, 0, 2))
    two = lambda a: jnp.broadcast_to(a[None], (2,) + a.shape).reshape(4, rows, a.shape[-1])
    packed_scan = jnp.concatenate(
        [
            heads_split(w_in[:, INNER : 2 * INNER], MAMBA_HEAD),
            jnp.swapaxes(
                w_in[:, 2 * INNER : 2 * INNER + BC].reshape(rows, 4, QUARTER), 0, 1
            ),
            jnp.pad(
                heads_split(w_in[:, 2 * INNER + BC :], 1), ((0, 0), (0, 0), (0, DT_PAD - HEADS))
            ),
        ],
        axis=2,
    )
    packed_rest = jnp.concatenate(
        [
            heads_split(w_in[:, :INNER], MAMBA_HEAD),
            split_q.reshape(4, rows, QP),
            two(split_k),
            two(split_v),
        ],
        axis=2,
    )

    def gathered(array):
        return lax.all_gather(array, SHARDS, axis=0, tiled=True)

    def after(array, *others):
        return lax.optimization_barrier((array,) + others)[0]

    def split_ff(w):
        w = w.reshape(rows, nz, 2, ny, 2, ff_rows)
        return jnp.transpose(w, (2, 4, 0, 1, 3, 5)).reshape(4, rows, hidden_part)

    def join_ff(w):
        w = w.reshape(2, 2, rows, nz, ny, ff_rows)
        return jnp.transpose(w, (2, 3, 0, 4, 1, 5)).reshape(rows, 4 * hidden_part)

    full_scan = gathered(to_ranks(packed_scan).reshape(4 * rows, SENT_COLS))

    tokens = 2 * span_all
    resident = inputs[0].astype(f32)
    normed, norm_back = jax.vjp(rms_scale, resident, norm_gain)
    normed16 = gather_sequences(permuted(normed.astype(bf16)))
    edges16 = shifted(normed16[:, span_all - 8 :], 1).reshape(16, D)
    normed_rows = normed16.reshape(tokens, D)

    rest_mine = to_ranks(packed_rest).reshape(4 * rows, REST_COLS)
    if aligned:
        turn = [(2 * y + c, 2 * c + y) for y in range(2) for c in range(2)]
        place = []
        for z in range(4):
            for y in range(2):
                for c in range(2):
                    place.append(((z * 2 + y) * 2 + c, ((z % 2 * 2 + y) * 2 + c) * 2 + z // 2))
        back_place = [(b, a) for a, b in place]
        sent_out = lax.ppermute(w_out, ("y", "c"), turn)
        sent_o = lax.ppermute(w_o, ("z", "y", "c"), place)
        sent_rows = jnp.concatenate([sent_out, sent_o], 0)
    full_rest = gathered(after(rest_mine, normed_rows, edges16))
    def beside(own, other, index):
        return jnp.where(
            index == 0,
            jnp.concatenate([own, other], axis=-1),
            jnp.concatenate([other, own], axis=-1),
        )

    n = span_all // SPAN
    sent_in = low_dot(normed_rows, full_scan).reshape(2, span_all, SENT_COLS)
    sent_edge = low_dot(edges16, full_scan).reshape(2, 8, SENT_COLS)
    quarter = jnp.concatenate(
        [sent_edge[..., PART : PART + QUARTER], sent_in[..., PART : PART + QUARTER]], axis=1
    ).astype(bf16)
    half = beside(quarter, swap(quarter[::-1], "c"), ci)
    every_bc = beside(half, swap(half, "x"), xi).astype(f32)
    scan_in = jnp.concatenate(
        [sent_in[..., :PART], every_bc[:, 8:], sent_in[..., PART + QUARTER :]], axis=-1
    )
    edge_rows = jnp.concatenate([sent_edge[..., :PART], every_bc[:, :8]], axis=-1)[:, None]
    before = jnp.concatenate(
        [
            edge_rows,
            scan_in.reshape(2, n, SPAN, SCAN_COLS)[:, : n - 1, SPAN - 8 :, :CONV_COLS],
        ],
        axis=1,
    )

    def rank_channels(array):
        return jnp.concatenate(
            [heads_mine(array[..., :INNER], MAMBA_HEAD), array[..., INNER:]], axis=-1
        )

    def per_head(array):
        return jnp.pad(heads_mine(array, 1), (0, DT_PAD - HEADS))[None]

    taps, bias = rank_channels(conv_weight), rank_channels(conv_bias)[None]
    dt_b, rates = per_head(dt_bias), per_head(-jnp.exp(a_log))
    skip = jnp.repeat(heads_mine(skip_gain, 1), MAMBA_HEAD)[None]
    gain = heads_mine(gated_gain, MAMBA_HEAD)[None]
    lift = (
        jnp.arange(DT_PAD, dtype=jnp.int32)[:, None]
        == jnp.arange(PART, dtype=jnp.int32)[None] // MAMBA_HEAD
    ).astype(bf16)
    mixed, steps, starts, prefix, own_state = scan_states(
        scan_in, before, taps, bias, dt_b, rates, lift
    )
    log_decay = starts[:, n - 1, 0] + steps[:, span_all - 1, DT_PAD:]
    own_decay = jnp.repeat(jnp.exp(log_decay[:, :HEADS]), MAMBA_HEAD, axis=-1)

    cotangent16 = jnp.concatenate(gather_tokens(after(out_grad[0], mixed)), 0)

    def turned(array, distance):
        return lax.ppermute(array, "z", [(i, (i + distance) % nz) for i in range(nz)])

    if aligned:
        first_rows = after(sent_rows, full_scan)
        along_z = jnp.stack([turned(first_rows, d) for d in range(nz - 1, 0, -1)] + [first_rows])
        along_z = lax.dynamic_slice_in_dim(
            jnp.concatenate([along_z, along_z], 0), nz - 1 - zi, nz, 0
        )
        other_y = swap(along_z, "y")
        full_rows = jnp.where(
            yi == 0, jnp.stack([along_z, other_y], 1), jnp.stack([other_y, along_z], 1)
        )
        full_out = full_rows[:, :, :out_rows].reshape(PART, D)
        full_o = full_rows[:, :, out_rows:].reshape(QP, D)
    else:
        every_out = lax.all_gather(w_out, EVERY, axis=0, tiled=True)
        every_o = lax.all_gather(w_o, EVERY, axis=0, tiled=True)
        full_out = lax.dynamic_slice_in_dim(every_out, (2 * xi + ci) * PART, PART, 0)
        every_o = every_o.reshape(2, 2, 2, HEAD_DIM, D)
        every_o = lax.dynamic_index_in_dim(every_o, xi, 2, keepdims=False)
        full_o = lax.dynamic_index_in_dim(every_o, ci, 0, keepdims=False).reshape(QP, D)

    def chained(local, step, pin=None):
        entering = []
        for s in range(2):
            held = jnp.zeros(local.shape[1:], f32)
            for hop in range(nz - 1):
                at = hop if step == 1 else nz - 1 - hop
                leaving = local[s] + own_decay[s][None] * held if hop else local[s]
                if pin is not None and hop == nz - 2:
                    leaving = after(leaving, pin)
                held = held + lax.ppermute(
                    leaving.astype(bf16), "z", [(at, at + step)]
                ).astype(f32)
            entering.append(held)
        return jnp.stack(entering)

    packed_ff = jnp.concatenate([split_ff(w_gate), split_ff(w_up)], axis=2)
    rest = low_dot(normed_rows, full_rest).reshape(2, span_all, REST_COLS)

    positions = zi * span_all + jnp.arange(span_all, dtype=jnp.int32)
    cosine, sine = rope_tables(positions)
    query16 = (
        rotate(rest[..., AT_Q:AT_K].reshape(2, span_all, 2, HEAD_DIM), cosine, sine)
        .astype(bf16)
        .reshape(2, span_all, QP)
    )
    key16 = rotate(rest[..., None, AT_K:AT_V], cosine, sine).astype(bf16)[:, :, 0]
    kv16 = jnp.stack([key16, rest[..., AT_V:].astype(bf16)])
    state_in = chained(own_state, 1, kv16)
    kv_before = [shifted(kv16, d) for d in range(nz - 1, 0, -1)]
    keys_at = (zi - nz + 1) * span_all + jnp.arange(nz * span_all, dtype=jnp.int32)
    query_place = jnp.broadcast_to(positions[:, None], (span_all, 128))
    key_place = jnp.broadcast_to(keys_at[None], (8, nz * span_all))
    values, flat, square = scan_values(
        mixed, steps, starts, prefix, state_in, rest, 0, skip, lift
    )
    kv_all = jnp.concatenate(list(after(tuple(kv_before), flat, cotangent16)) + [kv16], axis=2)
    attended, log_sum = attend(query16, kv_all[0], kv_all[1], query_place, key_place)
    attended16 = attended.reshape(tokens, QP).astype(bf16)

    root = lax.rsqrt(group_total(square[..., :1]) / INNER + epsilon)
    gated16 = (flat * root * gain).astype(bf16).reshape(tokens, PART)
    full_ff = gathered(
        after(to_ranks(packed_ff).reshape(4 * rows, 2 * hidden_part), mixed)
    )
    mixture = low_dot(gated16, full_out) + low_dot(attended16, full_o)
    hidden_state = resident + scatter_sequences(mixture.reshape(2, span_all, D))

    middle, mid_back = jax.vjp(rms_scale, hidden_state, mid_gain)
    middle16 = jnp.concatenate(gather_tokens(permuted(middle.astype(bf16))), 0)
    full_down = gathered(after(w_down, hidden_state))
    both = low_dot(middle16, full_ff)
    activated, swish_back = jax.vjp(
        swish_product, both[:, :hidden_part], both[:, hidden_part:]
    )
    activated16 = activated.astype(bf16)
    down = low_dot(activated16, full_down).reshape(4, length, D)
    output = (hidden_state + scatter_tokens(down)).astype(bf16)

    def to_owners(array):
        return lax.psum_scatter(array, SHARDS, scatter_dimension=0, tiled=True)

    down_grad = weight_grad(activated16, cotangent16).astype(bf16)
    down_owned = to_owners(down_grad)
    result_down = down_owned.astype(f32)
    gate_grad, up_grad = swish_back(back_dot(after(cotangent16, down_grad), full_down))
    both16 = jnp.concatenate([gate_grad, up_grad], axis=1).astype(bf16)
    mid_grad = restored(scatter_tokens(back_dot(both16, full_ff).reshape(4, length, D)))
    hidden_piece, mid_gain_grad = mid_back(mid_grad)
    hidden_grad = out_grad[0].astype(f32) + hidden_piece
    ff_grad = weight_grad(middle16, both16).astype(bf16)
    mix16 = gather_sequences(after(hidden_grad.astype(bf16), ff_grad)).reshape(tokens, D)
    ff_owned = to_owners(after(ff_grad, down_owned, mix16))
    ff_parts = to_ranks(ff_owned.reshape(4, rows, 2 * hidden_part))
    result_gate = join_ff(ff_parts[..., :hidden_part]).astype(f32)
    result_up = join_ff(ff_parts[..., hidden_part:]).astype(f32)
    attended_grad16 = back_dot(mix16, full_o).astype(bf16).reshape(2, span_all, QP)
    gated_grad = back_dot(mix16, full_out).reshape(2, span_all, PART)
    grad_out_w = weight_grad(gated16, mix16).astype(bf16)
    grad_o = weight_grad(attended16, mix16).astype(bf16)
    if aligned:
        rows_grad = jnp.concatenate(
            [grad_out_w.reshape(nz, 2, out_rows, D), grad_o.reshape(nz, 2, o_rows, D)], axis=2
        )
        other_y = lax.dynamic_index_in_dim(rows_grad, 1 - yi, 1, keepdims=False)
        both_y = lax.dynamic_index_in_dim(rows_grad, yi, 1, keepdims=False).astype(f32) + swap(
            other_y, "y"
        ).astype(f32)
    else:
        both_y = grad_o

    inner = jnp.sum(gated_grad * gain * flat, axis=-1, keepdims=True) * root
    inner_mean = group_total(inner) / INNER
    wide = (2, span_all, 128)
    value_grad, gate_z_grad, gain_grad, suffix, first_grad = gate_backward(
        after(gated_grad, down_owned),
        values,
        rest,
        0,
        jnp.broadcast_to(root, wide),
        jnp.broadcast_to(inner_mean, wide),
        gain,
        mixed,
        steps,
        lift,
    )
    mixed_grad, step_grad, skip_grad = scan_backward(
        mixed, steps, starts, prefix, state_in, suffix, value_grad, skip, lift
    )
    state_grad = chained(first_grad, -1, mixed_grad)

    query_grad, kv_grads = attend_backward(
        after(query16, first_grad),
        kv_all[0],
        kv_all[1],
        attended_grad16,
        attended,
        log_sum,
        query_place,
        key_place,
    )
    kv_grads = kv_grads.reshape(2, 2, nz, span_all, HEAD_DIM)
    kv_grad = kv_grads[:, :, nz - 1]
    for d in range(1, nz):
        kv_grad = kv_grad + shifted(kv_grads[:, :, nz - 1 - d].astype(bf16), -d).astype(f32)
    query_back = rotate(
        query_grad.reshape(2, span_all, 2, HEAD_DIM), cosine, -sine
    ).reshape(2, span_all, QP)
    key_back = rotate(kv_grad[0][:, :, None], cosine, -sine)[:, :, 0]
    rest_grad16 = jnp.concatenate(
        [
            gate_z_grad,
            query_back.astype(bf16),
            key_back.astype(bf16),
            kv_grad[1].astype(bf16),
        ],
        axis=-1,
    ).reshape(tokens, REST_COLS)

    scan_grad16, edge_grad, conv_grad, small_grad = finish_backward(
        scan_in,
        before,
        mixed,
        steps,
        starts,
        prefix,
        state_in,
        after(state_grad, ff_owned, both_y),
        mixed_grad,
        step_grad,
        taps,
        bias,
        dt_b,
        rates,
        lift,
    )
    edge_back = shifted(edge_grad[:, 8 - edge_count :].astype(bf16), -1).astype(f32)
    last_rows = scan_grad16[:, span_all - edge_count :, :CONV_COLS].astype(f32) + edge_back
    scan_grad16 = lax.dynamic_update_slice(
        scan_grad16, last_rows.astype(bf16), (0, span_all - edge_count, 0)
    )
    bc_grad = scan_grad16[..., PART:CONV_COLS].reshape(2, span_all, 2, 2 * QUARTER)
    half_grad = lax.dynamic_index_in_dim(bc_grad, xi, 2, keepdims=False).astype(f32) + swap(
        lax.dynamic_index_in_dim(bc_grad, 1 - xi, 2, keepdims=False), "x"
    ).astype(f32)
    half_grad = half_grad.reshape(2, span_all, 2, QUARTER)
    leaving = lax.dynamic_index_in_dim(half_grad, 1 - ci, 2, keepdims=False)
    quarter_grad = lax.dynamic_index_in_dim(half_grad, ci, 2, keepdims=False) + swap(
        leaving[::-1].astype(bf16), "c"
    ).astype(f32)
    sent_grad16 = jnp.concatenate(
        [scan_grad16[..., :PART], quarter_grad.astype(bf16), scan_grad16[..., CONV_COLS:]],
        axis=-1,
    ).reshape(tokens, SENT_COLS)
    if aligned:
        waiting = after(both_y.astype(bf16), state_grad)
        arriving = tuple(
            turned(lax.dynamic_index_in_dim(waiting, (zi + d) % nz, 0, keepdims=False), d)
            for d in range(1, nz)
        )
    else:
        every_out = lax.dynamic_update_slice_in_dim(
            jnp.zeros((INNER, D), bf16), grad_out_w, (2 * xi + ci) * PART, 0
        )
        every_o = lax.dynamic_update_slice(
            jnp.zeros((2, 2, 2, HEAD_DIM, D), bf16),
            grad_o.reshape(1, 2, 1, HEAD_DIM, D),
            (ci, 0, xi, 0, 0),
        ).reshape(ATT_HEADS * HEAD_DIM, D)
        result_out = lax.psum_scatter(every_out, EVERY, scatter_dimension=0, tiled=True)
        result_o = lax.psum_scatter(every_o, EVERY, scatter_dimension=0, tiled=True)
        result_out, result_o = result_out.astype(f32), result_o.astype(f32)
    rest_owned = to_owners(
        after(weight_grad(normed_rows, rest_grad16).astype(bf16), ff_owned, state_grad)
    )
    rest_parts = to_ranks(rest_owned.reshape(4, rows, REST_COLS)).astype(f32)
    scan_owned = to_owners(
        after(weight_grad(normed_rows, sent_grad16).astype(bf16), rest_owned)
    )

    normed_grad = back_dot(sent_grad16, full_scan) + back_dot(rest_grad16, full_rest)
    normed_grad = scatter_sequences(normed_grad.reshape(2, span_all, D))
    resident_grad, norm_gain_grad = norm_back(restored(after(normed_grad, rest_parts)))
    input_grad = hidden_grad + resident_grad

    result_q = jnp.transpose(
        rest_parts[..., AT_Q:AT_K].reshape(2, 2, rows, 2, HEAD_DIM), (2, 1, 3, 0, 4)
    ).reshape(rows, ATT_HEADS * HEAD_DIM)
    kv_parts = jnp.sum(rest_parts[..., AT_K:].reshape(2, 2, rows, 2, HEAD_DIM), axis=0)
    result_k = jnp.transpose(kv_parts[:, :, 0], (1, 0, 2)).reshape(rows, KV_HEADS * HEAD_DIM)
    result_v = jnp.transpose(kv_parts[:, :, 1], (1, 0, 2)).reshape(rows, KV_HEADS * HEAD_DIM)

    def all_channels(array):
        return jnp.concatenate(
            [heads_spread(array[..., :PART], MAMBA_HEAD), array[..., PART:]], axis=-1
        )

    small = [
        norm_gain_grad,
        all_channels(conv_grad[:4]),
        all_channels(conv_grad[4]),
        heads_spread(small_grad[0, :HEADS], 1),
        heads_spread(small_grad[1, :HEADS], 1),
        heads_spread(skip_grad[0, :HEADS], 1),
        heads_spread(gain_grad[0], MAMBA_HEAD),
        mid_gain_grad,
    ]
    summed = total(
        after(jnp.concatenate([v.reshape(-1) for v in small]), input_grad, output)
    )
    if aligned:
        rows_owned = lax.dynamic_index_in_dim(both_y, zi, 0, keepdims=False)
        for part in after(arriving, summed):
            rows_owned = rows_owned + part.astype(f32)
        rows_owned = rows_owned.astype(bf16)
        result_out = lax.ppermute(rows_owned[:out_rows], ("y", "c"), turn).astype(f32)
        result_o = lax.ppermute(rows_owned[out_rows:], ("z", "y", "c"), back_place).astype(f32)
    parts, at = [], 0
    for v in small:
        parts.append(summed[at : at + v.size].reshape(v.shape))
        at += v.size
    scan_owned = after(
        scan_owned,
        summed,
        input_grad,
        output,
        rest_parts,
        result_gate,
        result_up,
        result_down,
        result_q,
        result_k,
        result_v,
        result_out,
        result_o,
    )
    scan_parts = to_ranks(scan_owned.reshape(4, rows, SENT_COLS)).astype(f32)
    result_in = jnp.concatenate(
        [
            heads_join(rest_parts[..., :PART], MAMBA_HEAD),
            heads_join(scan_parts[..., :PART], MAMBA_HEAD),
            jnp.swapaxes(scan_parts[..., PART : PART + QUARTER], 0, 1).reshape(rows, BC),
            heads_join(scan_parts[..., PART + QUARTER : PART + QUARTER + HEADS], 1),
        ],
        axis=1,
    )
    return (
        output[None],
        input_grad[None],
        parts[0],
        result_in,
        parts[1],
        parts[2],
        parts[3],
        parts[4],
        parts[5],
        parts[6],
        result_out,
        result_q,
        result_k,
        result_v,
        result_o,
        parts[7],
        result_gate,
        result_up,
        result_down,
    )


def solution(mesh):
    seq, fsdp = mesh.shape["seq"], mesh.shape["fsdp"]
    split = Mesh(mesh.devices.reshape(seq // 2, 2, fsdp // 2, 2), EVERY)
    tokens = P(("y", "c"), ("z", "x"), None)
    matrix = P(EVERY, None)
    return jax.shard_map(
        body,
        mesh=split,
        in_specs=(tokens, tokens, P(), matrix)
        + (P(),) * 6
        + (matrix,) * 5
        + (P(),)
        + (matrix,) * 3,
        out_specs=(tokens, tokens, P(), matrix)
        + (P(),) * 6
        + (matrix,) * 5
        + (P(),)
        + (matrix,) * 3,
        check_vma=False,
    )
```

```python
import jax
import jax.numpy as jnp
from jax import lax
from jax.experimental import pallas as pl
from jax.experimental.pallas import tpu as pltpu
from jax.sharding import Mesh
from jax.sharding import PartitionSpec as P

D = 2048
MAMBA_HEADS = 48
MAMBA_HEAD = 64
STATE = 256
ATT_HEADS = 8
KV_HEADS = 2
HEAD_DIM = 128
SPAN = 128
INNER = 3072

HEADS = MAMBA_HEADS // 4
PART = HEADS * MAMBA_HEAD
BC = 2 * STATE
DT_PAD = 128
QP = 2 * HEAD_DIM
CONV_COLS = PART + BC
SCAN_COLS = CONV_COLS + DT_PAD
QUARTER = BC // 4
SENT_COLS = PART + QUARTER + DT_PAD
AT_Q = PART
AT_K = AT_Q + QP
AT_V = AT_K + HEAD_DIM
REST_COLS = AT_V + HEAD_DIM

epsilon = 1e-05
rope_base = 100000000000.0
GROUP = ("x", "c")
SHARDS = ("z", "y")
EVERY = ("z", "x", "y", "c")
bf16 = jnp.bfloat16
f32 = jnp.float32


def swap(array, axis):
    return lax.ppermute(array, axis, [(0, 1), (1, 0)])


def shifted(array, distance):
    devices = range(lax.axis_size("z"))
    return lax.ppermute(array, "z", [(i - distance, i) for i in devices if i - distance in devices])


def total(array):
    for axis in EVERY:
        size = lax.axis_size(axis)
        bit = 1
        while bit < size:
            array = array + lax.ppermute(array, axis, [(i, i ^ bit) for i in range(size)])
            bit *= 2
    return array


def group_total(array):
    array = array + swap(array[::-1], "c")
    return array + swap(array, "x")


def low_dot(left, right):
    return jnp.dot(left, right, preferred_element_type=f32)


def back_dot(grad_rows, weight):
    return lax.dot_general(grad_rows, weight, (((1,), (1,)), ((), ())), preferred_element_type=f32)


def weight_grad(left, right):
    return lax.dot_general(left, right, (((0,), (0,)), ((), ())), preferred_element_type=f32)


def rms_scale(values, gain):
    return values * lax.rsqrt(jnp.mean(values * values, axis=-1, keepdims=True) + epsilon) * gain


def rope_tables(positions):
    half_dim = HEAD_DIM // 2
    frequencies = rope_base ** (-jnp.arange(half_dim, dtype=f32) / half_dim)
    angles = positions.astype(f32)[:, None] * frequencies[None, :]
    return (jnp.cos(angles), jnp.sin(angles))


def rotate(values, cosine, sine):
    half_dim = HEAD_DIM // 2
    cosine, sine = cosine[:, None, :], sine[:, None, :]
    first, second = values[..., :half_dim], values[..., half_dim:]
    return jnp.concatenate([first * cosine - second * sine, second * cosine + first * sine], axis=-1)


def pieces(values, count):
    parts = []
    for _ in range(count):
        part = values.astype(bf16)
        parts.append(part)
        values = values - part.astype(f32)
    return parts


def running(mask, values):
    mask16 = mask.astype(bf16)
    return sum(low_dot(mask16, part) for part in pieces(values, 3))


def over_lanes(left, right):
    return lax.dot_general(left, right, (((1,), (1,)), ((), ())), preferred_element_type=f32)


def over_rows(left, right):
    return lax.dot_general(left, right, (((0,), (0,)), ((), ())), preferred_element_type=f32)


def widen(values, lift):
    return sum(low_dot(part, lift) for part in pieces(values, 2))


def narrow(values, lift):
    return sum(over_lanes(part, lift) for part in pieces(values, 2))


def sig(values):
    return 1.0 / (1.0 + jnp.exp(-values))


def soft(values):
    return jnp.maximum(values, 0.0) + jnp.log1p(jnp.exp(-jnp.abs(values)))


def square_places():
    return (
        lax.broadcasted_iota(jnp.int32, (SPAN, SPAN), 0),
        lax.broadcasted_iota(jnp.int32, (SPAN, SPAN), 1),
    )


def pre_conv(current, before, taps, bias):
    extended = jnp.concatenate([before, current], axis=0)
    pre = bias + extended[5 : 5 + SPAN] * taps[0:1]
    for k in range(1, 4):
        pre = pre + extended[5 + k : 5 + k + SPAN] * taps[k : k + 1]
    return (pre, extended)


def states_kernel(
    scan_in, before, taps, bias, dt_bias, rates, lift, mixed, steps, starts, prefix, last, held, sofar
):
    @pl.when(pl.program_id(1) == 0)
    def _():
        held[...] = jnp.zeros_like(held)
        sofar[...] = jnp.zeros_like(sofar)

    pre, _ = pre_conv(scan_in[0, :, :CONV_COLS], before[0, 0], taps[...], bias[...])
    mix = pre * sig(pre)
    mixed[0] = mix
    dt = soft(scan_in[0, :, CONV_COLS:] + dt_bias[...])
    row, column = square_places()
    cum = running(jnp.where(row >= column, 1.0, 0.0), dt * rates[...])
    steps[0, :, :DT_PAD] = dt
    steps[0, :, DT_PAD:] = cum
    starts[0, 0] = sofar[...]
    prefix[0, 0] = held[...]
    end = cum[SPAN - 1 : SPAN]
    tail = jnp.exp(end - cum) * dt
    fed = (mix[:, :PART] * widen(tail, lift[...])).astype(bf16)
    added = over_rows(mix[:, PART : PART + STATE].astype(bf16), fed)
    whole = widen(jnp.broadcast_to(jnp.exp(end), (8, DT_PAD)), lift[...])[0:1]
    held[...] = whole * held[...] + added
    sofar[...] = sofar[...] + end
    last[0] = held[...]


def values_kernel(
    mixed, steps, starts, prefix, state_in, gate, skip, lift, values, flat, square
):
    x = mixed[0, :, :PART]
    b16 = mixed[0, :, PART : PART + STATE].astype(bf16)
    c16 = mixed[0, :, PART + STATE :].astype(bf16)
    dt = steps[0, :, :DT_PAD]
    cum = steps[0, :, DT_PAD:]
    dt_t, cum_t = dt.T, cum.T
    state = prefix[0, 0] + widen(jnp.exp(starts[0, 0]), lift[...])[0:1] * state_in[0]
    meet = over_lanes(c16, b16)
    carried = low_dot(c16, state.astype(bf16)) * widen(jnp.exp(cum), lift[...])
    row, column = square_places()
    first = column < MAMBA_HEAD
    inside = []
    for k in range(HEADS // 2):
        pair = x[:, 2 * MAMBA_HEAD * k : 2 * MAMBA_HEAD * (k + 1)]
        weights = []
        for h in (2 * k, 2 * k + 1):
            spread = cum[:, h : h + 1] - cum_t[h : h + 1, :]
            decay = jnp.exp(jnp.where(row >= column, spread, -1e30))
            weights.append((meet * decay * dt_t[h : h + 1, :]).astype(bf16))
        split = [
            jnp.where(first, pair, 0.0).astype(bf16),
            jnp.where(first, 0.0, pair).astype(bf16),
        ]
        inside.append(low_dot(jnp.concatenate(weights, 1), jnp.concatenate(split, 0)))
    value = jnp.concatenate(inside, 1) + carried + skip[...] * x
    values[0] = value
    z = gate[0]
    product = value * (z * sig(z))
    flat[0] = product
    square[0] = jnp.broadcast_to(
        jnp.sum(product * product, axis=1, keepdims=True), (SPAN, 128)
    )


def gate_back_kernel(
    gated_grad, values, gate, root, mean, gain, c_part, steps, lift,
    value_grad, gate_grad, gain_grad, suffix, first_grad, held,
):
    @pl.when(pl.program_id(1) == 0)
    def _():
        held[...] = jnp.zeros_like(held)

    @pl.when((pl.program_id(0) == 0) & (pl.program_id(1) == 0))
    def _():
        gain_grad[...] = jnp.zeros_like(gain_grad)

    z, value, grad = gate[0], values[0], gated_grad[0]
    s = sig(z)
    silu = z * s
    scale = root[0, :, 0:1]
    normal = value * silu * scale
    flat_grad = scale * (grad * gain[...] - normal * mean[0, :, 0:1])
    d_value = flat_grad * silu
    value_grad[0] = d_value
    gate_grad[0] = (flat_grad * value * (s * (1.0 + z * (1.0 - s)))).astype(bf16)
    gain_grad[0:1] = gain_grad[0:1] + jnp.sum(grad * normal, axis=0, keepdims=True)
    grown = widen(jnp.exp(steps[0, :, DT_PAD:]), lift[...])
    suffix[0, 0] = held[...]
    held[...] = grown[SPAN - 1 : SPAN] * held[...] + over_rows(
        c_part[0].astype(bf16), (grown * d_value).astype(bf16)
    )
    first_grad[0] = held[...]


def scan_back_kernel(
    mixed, steps, starts, prefix, state_in, suffix, value_grad, skip, lift,
    mixed_grad, step_grad, skip_grad, columns,
):
    @pl.when((pl.program_id(0) == 0) & (pl.program_id(1) == 0))
    def _():
        skip_grad[...] = jnp.zeros_like(skip_grad)
        columns[...] = jnp.zeros_like(columns)

    up = lift[...]
    x = mixed[0, :, :PART]
    b16 = mixed[0, :, PART : PART + STATE].astype(bf16)
    c16 = mixed[0, :, PART + STATE :].astype(bf16)
    dt = steps[0, :, :DT_PAD]
    cum = steps[0, :, DT_PAD:]
    dt_t, cum_t = dt.T, cum.T
    end = cum[SPAN - 1 : SPAN]
    dy = value_grad[0]
    state = prefix[0, 0] + widen(jnp.exp(starts[0, 0]), up)[0:1] * state_in[0]
    ending = suffix[0, 0]
    state16, ending16 = state.astype(bf16), ending.astype(bf16)
    grown_dy = widen(jnp.exp(cum), up) * dy
    tail_wide = widen(jnp.exp(end - cum), up)
    dt_wide = widen(dt, up)
    reach = low_dot(c16, state16)
    pull = tail_wide * low_dot(b16, ending16)
    d_c = over_lanes(grown_dy.astype(bf16), state16)
    d_b = over_lanes((tail_wide * dt_wide * x).astype(bf16), ending16)
    meet = over_lanes(c16, b16)
    row, column = square_places()
    first = column < MAMBA_HEAD
    d_meet = jnp.zeros((SPAN, SPAN), f32)
    rows_sum = jnp.zeros((SPAN, DT_PAD), f32)
    back = []
    for k in range(HEADS // 2):
        at = slice(2 * MAMBA_HEAD * k, 2 * MAMBA_HEAD * (k + 1))
        x16, dy_pair = x[:, at].astype(bf16), dy[:, at]
        split = [
            jnp.where(first, dy_pair, 0.0).astype(bf16),
            jnp.where(first, 0.0, dy_pair).astype(bf16),
        ]
        weights = []
        for j in range(2):
            h = 2 * k + j
            spread = cum[:, h : h + 1] - cum_t[h : h + 1, :]
            decay = jnp.exp(jnp.where(row >= column, spread, -1e30))
            d_weight = over_lanes(split[j], x16) * decay
            scaled = d_weight * dt_t[h : h + 1, :]
            d_meet = d_meet + scaled
            rows_sum = rows_sum + jnp.where(
                column == h, jnp.sum(scaled * meet, axis=1, keepdims=True), 0.0
            )
            columns[h : h + 1, :] = jnp.sum(d_weight * meet, axis=0, keepdims=True)
            weights.append((meet * decay).astype(bf16))
        back.append(over_rows(jnp.concatenate(weights, 0), jnp.concatenate(split, 0)))
    d_meet16 = d_meet.astype(bf16)
    mixed_grad[0, :, :PART] = dt_wide * (jnp.concatenate(back, 1) + pull) + skip[...] * dy
    mixed_grad[0, :, PART : PART + STATE] = d_b + over_rows(d_meet16, c16)
    mixed_grad[0, :, PART + STATE :] = d_c + low_dot(d_meet16, b16)
    tail_dt = narrow(x * pull, up)
    inner_dt = columns[...].T
    d_cum = rows_sum + narrow(grown_dy * reach, up) - dt * (inner_dt + tail_dt)
    kept = narrow(
        jnp.broadcast_to(jnp.sum(state * ending, axis=0, keepdims=True), (8, PART)), up
    )[0:1]
    extra = jnp.sum(dt * tail_dt, axis=0, keepdims=True) + jnp.exp(end) * kept
    step_grad[0, :, :DT_PAD] = inner_dt + tail_dt
    step_grad[0, :, DT_PAD:] = running(jnp.where(row <= column, 1.0, 0.0), d_cum) + extra
    skip_grad[0:1] = skip_grad[0:1] + jnp.sum(narrow(dy * x, up), axis=0, keepdims=True)


def finish_back_kernel(
    scan_in, before, mixed, steps, starts, prefix, state_in, state_grad, mixed_grad, step_grad,
    taps, bias, dt_bias, rates, lift,
    scan_grad, edge_grad, conv_grad, small_grad,
    later, after_pre,
):
    @pl.when(pl.program_id(1) == 0)
    def _():
        later[...] = jnp.zeros_like(later)
        after_pre[...] = jnp.zeros_like(after_pre)

    @pl.when((pl.program_id(0) == 0) & (pl.program_id(1) == 0))
    def _():
        conv_grad[...] = jnp.zeros_like(conv_grad)
        small_grad[...] = jnp.zeros_like(small_grad)

    up = lift[...]
    x = mixed[0, :, :PART]
    b16 = mixed[0, :, PART : PART + STATE].astype(bf16)
    dt = steps[0, :, :DT_PAD]
    cum = steps[0, :, DT_PAD:]
    end = cum[SPAN - 1 : SPAN]
    state = prefix[0, 0] + widen(jnp.exp(starts[0, 0]), up)[0:1] * state_in[0]
    ending = widen(jnp.exp(later[...]), up)[0:1] * state_grad[0]
    later[...] = later[...] + end
    ending16 = ending.astype(bf16)
    tail_wide = widen(jnp.exp(end - cum), up)
    dt_wide = widen(dt, up)
    pull = tail_wide * low_dot(b16, ending16)
    d_x = mixed_grad[0, :, :PART] + dt_wide * pull
    d_b = mixed_grad[0, :, PART : PART + STATE] + over_lanes(
        (tail_wide * dt_wide * x).astype(bf16), ending16
    )
    d_c = mixed_grad[0, :, PART + STATE :]
    tail_dt = narrow(x * pull, up)
    kept = narrow(
        jnp.broadcast_to(jnp.sum(state * ending, axis=0, keepdims=True), (8, PART)), up
    )[0:1]
    row, column = square_places()
    fed = dt * tail_dt
    earlier = running(jnp.where(row > column, 1.0, 0.0), fed)
    d_log = step_grad[0, :, DT_PAD:] + earlier + jnp.exp(end) * kept
    rate = rates[...]
    d_raw = (step_grad[0, :, :DT_PAD] + tail_dt + d_log * rate) * sig(
        scan_in[0, :, CONV_COLS:] + dt_bias[...]
    )
    small_grad[0:1] = small_grad[0:1] + jnp.sum(d_raw, axis=0, keepdims=True)
    small_grad[1:2] = small_grad[1:2] + jnp.sum(d_log * dt * rate, axis=0, keepdims=True)

    pre, extended = pre_conv(scan_in[0, :, :CONV_COLS], before[0, 0], taps[...], bias[...])
    s = sig(pre)
    d_pre = jnp.concatenate([d_x, d_b, d_c], axis=1) * (s * (1.0 + pre * (1.0 - s)))
    for k in range(4):
        conv_grad[k : k + 1] = conv_grad[k : k + 1] + jnp.sum(
            d_pre * extended[5 + k : 5 + k + SPAN], axis=0, keepdims=True
        )
    conv_grad[4:5] = conv_grad[4:5] + jnp.sum(d_pre, axis=0, keepdims=True)
    following = jnp.concatenate([d_pre, after_pre[...]], axis=0)
    d_in = following[0:SPAN] * taps[3:4]
    for k in range(3):
        d_in = d_in + following[3 - k : 3 - k + SPAN] * taps[k : k + 1]
    scan_grad[0, :, :CONV_COLS] = d_in.astype(bf16)
    scan_grad[0, :, CONV_COLS:] = d_raw.astype(bf16)
    front = d_pre[0:8]
    after_pre[...] = front
    nothing = jnp.zeros((8, CONV_COLS), f32)
    padded = jnp.concatenate([nothing, front, nothing], 0)
    edge = padded[0:8] * taps[3:4]
    for k in range(3):
        edge = edge + padded[3 - k : 11 - k] * taps[k : k + 1]
    edge_grad[0] = edge


def one(shape):
    return pl.BlockSpec(shape, lambda b, i: (0,) * len(shape))


def by_span(width, column=0, reverse=None):
    if reverse is None:
        return pl.BlockSpec((1, SPAN, width), lambda b, i: (b, i, column))
    return pl.BlockSpec((1, SPAN, width), lambda b, i: (b, reverse - 1 - i, column))


def by_piece(rows, width, reverse=None):
    if reverse is None:
        return pl.BlockSpec((1, 1, rows, width), lambda b, i: (b, i, 0, 0))
    return pl.BlockSpec((1, 1, rows, width), lambda b, i: (b, reverse - 1 - i, 0, 0))


def by_sequence(rows, width):
    return pl.BlockSpec((1, rows, width), lambda b, i: (b, 0, 0))


def grid_call(kernel, spans, ins, outs, scratch, flops, moved):
    return pl.pallas_call(
        kernel,
        grid=(2, spans),
        in_specs=ins,
        out_specs=[spec for spec, _ in outs],
        out_shape=[shape for _, shape in outs],
        scratch_shapes=scratch,
        compiler_params=pltpu.CompilerParams(
            dimension_semantics=("arbitrary", "arbitrary"), vmem_limit_bytes=50 * 2**20
        ),
        cost_estimate=pl.CostEstimate(flops=flops, bytes_accessed=moved, transcendentals=0),
    )


def like(shape, kind=f32):
    return jax.ShapeDtypeStruct(shape, kind)


def scan_states(scan_in, before, taps, bias, dt_bias, rates, lift):
    length = scan_in.shape[1]
    n = length // SPAN
    return grid_call(
        states_kernel,
        n,
        [
            by_span(SCAN_COLS),
            by_piece(8, CONV_COLS),
            one((4, CONV_COLS)),
            one((1, CONV_COLS)),
            one((1, DT_PAD)),
            one((1, DT_PAD)),
            one((DT_PAD, PART)),
        ],
        [
            (by_span(CONV_COLS), like((2, length, CONV_COLS))),
            (by_span(2 * DT_PAD), like((2, length, 2 * DT_PAD))),
            (by_piece(8, DT_PAD), like((2, n, 8, DT_PAD))),
            (by_piece(STATE, PART), like((2, n, STATE, PART))),
            (by_sequence(STATE, PART), like((2, STATE, PART))),
        ],
        [pltpu.VMEM((STATE, PART), f32), pltpu.VMEM((8, DT_PAD), f32)],
        8 * 10**9,
        30 * 10**6,
    )(scan_in, before, taps, bias, dt_bias, rates, lift)


def scan_values(mixed, steps, starts, prefix, state_in, rest, gate_at, skip, lift):
    length = mixed.shape[1]
    n = length // SPAN
    return grid_call(
        values_kernel,
        n,
        [
            by_span(CONV_COLS),
            by_span(2 * DT_PAD),
            by_piece(8, DT_PAD),
            by_piece(STATE, PART),
            by_sequence(STATE, PART),
            by_span(PART, gate_at),
            one((1, PART)),
            one((DT_PAD, PART)),
        ],
        [
            (by_span(PART), like((2, length, PART))),
            (by_span(PART), like((2, length, PART))),
            (by_span(128), like((2, length, 128))),
        ],
        [],
        12 * 10**9,
        30 * 10**6,
    )(mixed, steps, starts, prefix, state_in, rest, skip, lift)


def gate_backward(gated_grad, values, rest, gate_at, root, mean, gain, mixed, steps, lift):
    length = mixed.shape[1]
    n = length // SPAN
    return grid_call(
        gate_back_kernel,
        n,
        [
            by_span(PART, 0, n),
            by_span(PART, 0, n),
            by_span(PART, gate_at, n),
            by_span(128, 0, n),
            by_span(128, 0, n),
            one((1, PART)),
            by_span(STATE, (PART + STATE) // STATE, n),
            by_span(2 * DT_PAD, 0, n),
            one((DT_PAD, PART)),
        ],
        [
            (by_span(PART, 0, n), like((2, length, PART))),
            (by_span(PART, 0, n), like((2, length, PART), bf16)),
            (one((8, PART)), like((8, PART))),
            (by_piece(STATE, PART, n), like((2, n, STATE, PART))),
            (by_sequence(STATE, PART), like((2, STATE, PART))),
        ],
        [pltpu.VMEM((STATE, PART), f32)],
        8 * 10**9,
        30 * 10**6,
    )(gated_grad, values, rest, root, mean, gain, mixed, steps, lift)


def scan_backward(mixed, steps, starts, prefix, state_in, suffix, value_grad, skip, lift):
    length = mixed.shape[1]
    n = length // SPAN
    return grid_call(
        scan_back_kernel,
        n,
        [
            by_span(CONV_COLS),
            by_span(2 * DT_PAD),
            by_piece(8, DT_PAD),
            by_piece(STATE, PART),
            by_sequence(STATE, PART),
            by_piece(STATE, PART),
            by_span(PART),
            one((1, PART)),
            one((DT_PAD, PART)),
        ],
        [
            (by_span(CONV_COLS), like((2, length, CONV_COLS))),
            (by_span(2 * DT_PAD), like((2, length, 2 * DT_PAD))),
            (one((8, DT_PAD)), like((8, DT_PAD))),
        ],
        [pltpu.VMEM((SPAN, SPAN), f32)],
        30 * 10**9,
        40 * 10**6,
    )(mixed, steps, starts, prefix, state_in, suffix, value_grad, skip, lift)


def finish_backward(
    scan_in, before, mixed, steps, starts, prefix, state_in, state_grad, mixed_grad, step_grad,
    taps, bias, dt_bias, rates, lift,
):
    length = mixed.shape[1]
    n = length // SPAN
    return grid_call(
        finish_back_kernel,
        n,
        [
            by_span(SCAN_COLS, 0, n),
            by_piece(8, CONV_COLS, n),
            by_span(CONV_COLS, 0, n),
            by_span(2 * DT_PAD, 0, n),
            by_piece(8, DT_PAD, n),
            by_piece(STATE, PART, n),
            by_sequence(STATE, PART),
            by_sequence(STATE, PART),
            by_span(CONV_COLS, 0, n),
            by_span(2 * DT_PAD, 0, n),
            one((4, CONV_COLS)),
            one((1, CONV_COLS)),
            one((1, DT_PAD)),
            one((1, DT_PAD)),
            one((DT_PAD, PART)),
        ],
        [
            (by_span(SCAN_COLS, 0, n), like((2, length, SCAN_COLS), bf16)),
            (by_sequence(8, CONV_COLS), like((2, 8, CONV_COLS))),
            (one((8, CONV_COLS)), like((8, CONV_COLS))),
            (one((8, DT_PAD)), like((8, DT_PAD))),
        ],
        [pltpu.VMEM((8, DT_PAD), f32), pltpu.VMEM((8, CONV_COLS), f32)],
        15 * 10**9,
        50 * 10**6,
    )(
        scan_in, before, mixed, steps, starts, prefix, state_in, state_grad, mixed_grad, step_grad,
        taps, bias, dt_bias, rates, lift,
    )


def attend_kernel(query, key, value, query_place, key_place, attended, log_sum):
    scores = over_lanes(query[0], key[0]) * HEAD_DIM ** (-0.5)
    seen = (key_place[0:1] >= 0) & (query_place[:, 0:1] >= key_place[0:1])
    scores = jnp.where(seen, scores, -1e30)
    peak = jnp.max(scores, axis=1, keepdims=True)
    unscaled = jnp.exp(scores - peak)
    whole = jnp.sum(unscaled, axis=1, keepdims=True)
    probs = (unscaled * (1.0 / whole)).astype(bf16)
    attended[0] = low_dot(probs, value[0])
    log_sum[0] = jnp.broadcast_to(peak + jnp.log(whole), log_sum.shape[1:])


def attend_back_kernel(
    query, key, value, grad, attended, log_sum, query_place, key_place, query_grad, kv_grad
):
    @pl.when((pl.program_id(1) == 0) & (pl.program_id(2) == 0))
    def _():
        kv_grad[...] = jnp.zeros_like(kv_grad)

    scale = HEAD_DIM ** (-0.5)
    scores = over_lanes(query[0], key[0]) * scale
    seen = (key_place[0:1] >= 0) & (query_place[:, 0:1] >= key_place[0:1])
    probs = jnp.exp(jnp.where(seen, scores, -1e30) - log_sum[0, :, 0:1])
    delta = jnp.sum(grad[0].astype(f32) * attended[0], axis=1, keepdims=True)
    score_grad = (probs * (over_lanes(grad[0], value[0]) - delta)).astype(bf16)
    query_grad[0] = low_dot(score_grad, key[0]) * scale
    kv_grad[0, 0] = kv_grad[0, 0] + over_rows(score_grad, query[0]) * scale
    kv_grad[1, 0] = kv_grad[1, 0] + over_rows(probs.astype(bf16), grad[0])


def attend_specs(block, keys):
    by_query = pl.BlockSpec((1, block, HEAD_DIM), lambda b, h, i: (b, i, h))
    whole_key = pl.BlockSpec((1, keys, HEAD_DIM), lambda b, h, i: (b, 0, 0))
    place = pl.BlockSpec((block, 128), lambda b, h, i: (i, 0))
    key_at = pl.BlockSpec((8, keys), lambda b, h, i: (0, 0))
    return (by_query, whole_key, place, key_at)


def attend(query, key, value, query_place, key_place):
    length, keys = query.shape[1], key.shape[1]
    block = 256 if keys <= 4096 else 128
    by_query, whole_key, place, key_at = attend_specs(block, keys)
    return pl.pallas_call(
        attend_kernel,
        grid=(2, 2, length // block),
        in_specs=[by_query, whole_key, whole_key, place, key_at],
        out_specs=[by_query, by_query],
        out_shape=[like((2, length, QP)), like((2, length, QP))],
        compiler_params=pltpu.CompilerParams(
            dimension_semantics=("arbitrary",) * 3, vmem_limit_bytes=50 * 2**20
        ),
        cost_estimate=pl.CostEstimate(
            flops=12 * 10**9, bytes_accessed=20 * 10**6, transcendentals=0
        ),
    )(query, key, value, query_place, key_place)


def attend_backward(query, key, value, grad, attended, log_sum, query_place, key_place):
    length, keys = query.shape[1], key.shape[1]
    block = 256 if keys <= 4096 else 128
    by_query, whole_key, place, key_at = attend_specs(block, keys)
    return pl.pallas_call(
        attend_back_kernel,
        grid=(2, 2, length // block),
        in_specs=[by_query, whole_key, whole_key, by_query, by_query, by_query, place, key_at],
        out_specs=[
            by_query,
            pl.BlockSpec((2, 1, keys, HEAD_DIM), lambda b, h, i: (0, b, 0, 0)),
        ],
        out_shape=[like((2, length, QP)), like((2, 2, keys, HEAD_DIM))],
        compiler_params=pltpu.CompilerParams(
            dimension_semantics=("arbitrary",) * 3, vmem_limit_bytes=50 * 2**20
        ),
        cost_estimate=pl.CostEstimate(
            flops=20 * 10**9, bytes_accessed=30 * 10**6, transcendentals=0
        ),
    )(query, key, value, grad, attended, log_sum, query_place, key_place)


def swish_product(gate_proj, up_proj):
    return jax.nn.silu(gate_proj) * up_proj


def gather_tokens(block):
    across = swap(block, "x")
    return (block, swap(block, "c"), across, swap(across, "c"))


def scatter_tokens(blocks):
    near, far = blocks[0], blocks[2]
    sent = swap(jnp.stack([blocks[1].astype(bf16), blocks[3].astype(bf16)]), "c")
    near = near + sent[0].astype(f32)
    far = far + sent[1].astype(f32)
    return near + swap(far.astype(bf16), "x").astype(f32)


def body(
    inputs,
    out_grad,
    norm_gain,
    w_in,
    conv_weight,
    conv_bias,
    dt_bias,
    a_log,
    skip_gain,
    gated_gain,
    w_out,
    w_q,
    w_k,
    w_v,
    w_o,
    mid_gain,
    w_gate,
    w_up,
    w_down,
):
    nz, ny = lax.axis_size("z"), lax.axis_size("y")
    zi, xi, yi, ci = (lax.axis_index(name) for name in ("z", "x", "y", "c"))
    length = inputs.shape[1]
    span_all = 2 * length
    rows = w_in.shape[0]
    ff_rows = w_down.shape[0]
    hidden_part = nz * ny * ff_rows
    edge_count = conv_weight.shape[0] - 1
    out_rows, o_rows = w_out.shape[0], w_o.shape[0]
    aligned = ny == 2 and nz == 4 and MAMBA_HEADS % (4 * nz) == 0
    g = nz if aligned else 1
    hp = HEADS // g

    def heads_mine(array, width):
        lead = array.shape[:-1]
        array = array.reshape(lead + (g, 2, 2, hp * width))
        array = lax.dynamic_index_in_dim(array, xi, len(lead) + 1, keepdims=False)
        array = lax.dynamic_index_in_dim(array, ci, len(lead) + 1, keepdims=False)
        return array.reshape(lead + (HEADS * width,))

    def heads_spread(array, width):
        lead = array.shape[:-1]
        array = array.reshape(lead + (g, 1, 1, hp * width))
        whole = jnp.zeros(lead + (g, 2, 2, hp * width), array.dtype)
        start = (0,) * len(lead) + (0, xi, ci, 0)
        return lax.dynamic_update_slice(whole, array, start).reshape(
            lead + (MAMBA_HEADS * width,)
        )

    def heads_split(array, width):
        n = array.shape[0]
        array = array.reshape(n, g, 2, 2, hp * width)
        return jnp.transpose(array, (2, 3, 0, 1, 4)).reshape(4, n, HEADS * width)

    def heads_join(array, width):
        n = array.shape[1]
        array = array.reshape(2, 2, n, g, hp * width)
        return jnp.transpose(array, (2, 3, 0, 1, 4)).reshape(n, MAMBA_HEADS * width)

    def reordered(array, first, second):
        width = 2 * rows
        return jnp.concatenate(
            [
                array[..., at * width : (at + 1) * width]
                for z in range(nz)
                for at in (
                    (z * first + i) * second + j for j in range(second) for i in range(first)
                )
            ],
            axis=-1,
        )

    def permuted(array):
        return reordered(array, 2, ny)

    def restored(array):
        return reordered(array, ny, 2)

    def to_ranks(array):
        return lax.all_to_all(array, GROUP, 0, 0, tiled=True)

    def in_order(own, other):
        return lax.dynamic_slice_in_dim(
            jnp.concatenate([own, other, own], 0), xi * length, span_all, 0
        )

    def gather_sequences(block):
        own, near, across, far = gather_tokens(block)
        return jnp.stack([in_order(own, across), in_order(near, far)])

    def scatter_sequences(partial):
        mine = partial[0] + swap(partial[1].astype(bf16), "c").astype(f32)
        mine = mine.reshape(2, length, mine.shape[-1])
        own = lax.dynamic_index_in_dim(mine, xi, 0, keepdims=False)
        other = lax.dynamic_index_in_dim(mine, 1 - xi, 0, keepdims=False)
        return own + swap(other.astype(bf16), "x").astype(f32)

    split_q = jnp.transpose(w_q.reshape(rows, 2, 2, 2, HEAD_DIM), (3, 1, 0, 2, 4))
    split_k = jnp.transpose(w_k.reshape(rows, 2, HEAD_DIM), (1, 0, 2))
    split_v = jnp.transpose(w_v.reshape(rows, 2, HEAD_DIM), (1, 0, 2))
    two = lambda a: jnp.broadcast_to(a[None], (2,) + a.shape).reshape(4, rows, a.shape[-1])
    packed_scan = jnp.concatenate(
        [
            heads_split(w_in[:, INNER : 2 * INNER], MAMBA_HEAD),
            jnp.swapaxes(
                w_in[:, 2 * INNER : 2 * INNER + BC].reshape(rows, 4, QUARTER), 0, 1
            ),
            jnp.pad(
                heads_split(w_in[:, 2 * INNER + BC :], 1), ((0, 0), (0, 0), (0, DT_PAD - HEADS))
            ),
        ],
        axis=2,
    )
    packed_rest = jnp.concatenate(
        [
            heads_split(w_in[:, :INNER], MAMBA_HEAD),
            split_q.reshape(4, rows, QP),
            two(split_k),
            two(split_v),
        ],
        axis=2,
    )

    def gathered(array):
        return lax.all_gather(array, SHARDS, axis=0, tiled=True)

    def after(array, *others):
        return lax.optimization_barrier((array,) + others)[0]

    def split_ff(w):
        w = w.reshape(rows, nz, 2, ny, 2, ff_rows)
        return jnp.transpose(w, (2, 4, 0, 1, 3, 5)).reshape(4, rows, hidden_part)

    def join_ff(w):
        w = w.reshape(2, 2, rows, nz, ny, ff_rows)
        return jnp.transpose(w, (2, 3, 0, 4, 1, 5)).reshape(rows, 4 * hidden_part)

    full_scan = gathered(to_ranks(packed_scan).reshape(4 * rows, SENT_COLS))

    tokens = 2 * span_all
    resident = inputs[0].astype(f32)
    normed, norm_back = jax.vjp(rms_scale, resident, norm_gain)
    normed16 = gather_sequences(permuted(normed.astype(bf16)))
    edges16 = shifted(normed16[:, span_all - 8 :], 1).reshape(16, D)
    normed_rows = normed16.reshape(tokens, D)

    rest_mine = to_ranks(packed_rest).reshape(4 * rows, REST_COLS)
    if aligned:
        turn = [(2 * y + c, 2 * c + y) for y in range(2) for c in range(2)]
        place = []
        for z in range(4):
            for y in range(2):
                for c in range(2):
                    place.append(((z * 2 + y) * 2 + c, ((z % 2 * 2 + y) * 2 + c) * 2 + z // 2))
        back_place = [(b, a) for a, b in place]
        sent_out = lax.ppermute(w_out, ("y", "c"), turn)
        sent_o = lax.ppermute(w_o, ("z", "y", "c"), place)
        sent_rows = jnp.concatenate([sent_out, sent_o], 0)
    full_rest = gathered(after(rest_mine, normed_rows, edges16))
    cotangent16 = jnp.concatenate(gather_tokens(out_grad[0]), 0)

    def beside(own, other, index):
        return jnp.where(
            index == 0,
            jnp.concatenate([own, other], axis=-1),
            jnp.concatenate([other, own], axis=-1),
        )

    n = span_all // SPAN
    sent_in = low_dot(normed_rows, full_scan).reshape(2, span_all, SENT_COLS)
    sent_edge = low_dot(edges16, full_scan).reshape(2, 8, SENT_COLS)
    quarter = jnp.concatenate(
        [sent_edge[..., PART : PART + QUARTER], sent_in[..., PART : PART + QUARTER]], axis=1
    ).astype(bf16)
    half = beside(quarter, swap(quarter[::-1], "c"), ci)
    every_bc = beside(half, swap(half, "x"), xi).astype(f32)
    scan_in = jnp.concatenate(
        [sent_in[..., :PART], every_bc[:, 8:], sent_in[..., PART + QUARTER :]], axis=-1
    )
    edge_rows = jnp.concatenate([sent_edge[..., :PART], every_bc[:, :8]], axis=-1)[:, None]
    before = jnp.concatenate(
        [
            edge_rows,
            scan_in.reshape(2, n, SPAN, SCAN_COLS)[:, : n - 1, SPAN - 8 :, :CONV_COLS],
        ],
        axis=1,
    )

    def rank_channels(array):
        return jnp.concatenate(
            [heads_mine(array[..., :INNER], MAMBA_HEAD), array[..., INNER:]], axis=-1
        )

    def per_head(array):
        return jnp.pad(heads_mine(array, 1), (0, DT_PAD - HEADS))[None]

    taps, bias = rank_channels(conv_weight), rank_channels(conv_bias)[None]
    dt_b, rates = per_head(dt_bias), per_head(-jnp.exp(a_log))
    skip = jnp.repeat(heads_mine(skip_gain, 1), MAMBA_HEAD)[None]
    gain = heads_mine(gated_gain, MAMBA_HEAD)[None]
    lift = (
        jnp.arange(DT_PAD, dtype=jnp.int32)[:, None]
        == jnp.arange(PART, dtype=jnp.int32)[None] // MAMBA_HEAD
    ).astype(bf16)
    mixed, steps, starts, prefix, own_state = scan_states(
        scan_in, before, taps, bias, dt_b, rates, lift
    )
    log_decay = starts[:, n - 1, 0] + steps[:, span_all - 1, DT_PAD:]
    own_decay = jnp.repeat(jnp.exp(log_decay[:, :HEADS]), MAMBA_HEAD, axis=-1)

    def turned(array, distance):
        return lax.ppermute(array, "z", [(i, (i + distance) % nz) for i in range(nz)])

    def chained(local, step, pin=None):
        entering = []
        for s in range(2):
            held = jnp.zeros(local.shape[1:], f32)
            for hop in range(nz - 1):
                at = hop if step == 1 else nz - 1 - hop
                leaving = local[s] + own_decay[s][None] * held if hop else local[s]
                if pin is not None and hop == nz - 2:
                    leaving = after(leaving, pin)
                held = held + lax.ppermute(
                    leaving.astype(bf16), "z", [(at, at + step)]
                ).astype(f32)
            entering.append(held)
        return jnp.stack(entering)

    packed_ff = jnp.concatenate([split_ff(w_gate), split_ff(w_up)], axis=2)
    rest = low_dot(normed_rows, full_rest).reshape(2, span_all, REST_COLS)

    positions = zi * span_all + jnp.arange(span_all, dtype=jnp.int32)
    cosine, sine = rope_tables(positions)
    query16 = (
        rotate(rest[..., AT_Q:AT_K].reshape(2, span_all, 2, HEAD_DIM), cosine, sine)
        .astype(bf16)
        .reshape(2, span_all, QP)
    )
    key16 = rotate(rest[..., None, AT_K:AT_V], cosine, sine).astype(bf16)[:, :, 0]
    kv16 = jnp.stack([key16, rest[..., AT_V:].astype(bf16)])
    state_in = chained(own_state, 1, kv16)
    kv_before = [shifted(kv16, d) for d in range(nz - 1, 0, -1)]
    if aligned:
        first_rows = after(sent_rows, kv_before[-1])
        along_z = jnp.stack([turned(first_rows, d) for d in range(nz - 1, 0, -1)] + [first_rows])
        along_z = lax.dynamic_slice_in_dim(
            jnp.concatenate([along_z, along_z], 0), nz - 1 - zi, nz, 0
        )
        other_y = swap(along_z, "y")
        full_rows = jnp.where(
            yi == 0, jnp.stack([along_z, other_y], 1), jnp.stack([other_y, along_z], 1)
        )
        full_out = full_rows[:, :, :out_rows].reshape(PART, D)
        full_o = full_rows[:, :, out_rows:].reshape(QP, D)
    else:
        every_out = lax.all_gather(w_out, EVERY, axis=0, tiled=True)
        every_o = lax.all_gather(w_o, EVERY, axis=0, tiled=True)
        full_out = lax.dynamic_slice_in_dim(every_out, (2 * xi + ci) * PART, PART, 0)
        every_o = every_o.reshape(2, 2, 2, HEAD_DIM, D)
        every_o = lax.dynamic_index_in_dim(every_o, xi, 2, keepdims=False)
        full_o = lax.dynamic_index_in_dim(every_o, ci, 0, keepdims=False).reshape(QP, D)

    keys_at = (zi - nz + 1) * span_all + jnp.arange(nz * span_all, dtype=jnp.int32)
    query_place = jnp.broadcast_to(positions[:, None], (span_all, 128))
    key_place = jnp.broadcast_to(keys_at[None], (8, nz * span_all))
    values, flat, square = scan_values(
        mixed, steps, starts, prefix, state_in, rest, 0, skip, lift
    )
    kv_all = jnp.concatenate(list(after(tuple(kv_before), flat)) + [kv16], axis=2)
    attended, log_sum = attend(query16, kv_all[0], kv_all[1], query_place, key_place)
    attended16 = attended.reshape(tokens, QP).astype(bf16)

    root = lax.rsqrt(group_total(square[..., :1]) / INNER + epsilon)
    gated16 = (flat * root * gain).astype(bf16).reshape(tokens, PART)
    full_ff = gathered(
        after(to_ranks(packed_ff).reshape(4 * rows, 2 * hidden_part), mixed, cotangent16)
    )
    mixture = low_dot(gated16, full_out) + low_dot(attended16, full_o)
    hidden_state = resident + scatter_sequences(mixture.reshape(2, span_all, D))

    middle, mid_back = jax.vjp(rms_scale, hidden_state, mid_gain)
    middle16 = jnp.concatenate(gather_tokens(permuted(middle.astype(bf16))), 0)
    full_down = gathered(after(w_down, flat, attended))
    both = low_dot(middle16, full_ff)
    activated, swish_back = jax.vjp(
        swish_product, both[:, :hidden_part], both[:, hidden_part:]
    )
    activated16 = activated.astype(bf16)
    down = low_dot(activated16, full_down).reshape(4, length, D)
    output = (hidden_state + scatter_tokens(down)).astype(bf16)

    def to_owners(array):
        return lax.psum_scatter(array, SHARDS, scatter_dimension=0, tiled=True)

    down_grad = weight_grad(activated16, cotangent16).astype(bf16)
    down_owned = to_owners(down_grad)
    result_down = down_owned.astype(f32)
    gate_grad, up_grad = swish_back(back_dot(after(cotangent16, down_grad), full_down))
    both16 = jnp.concatenate([gate_grad, up_grad], axis=1).astype(bf16)
    mid_grad = restored(scatter_tokens(back_dot(both16, full_ff).reshape(4, length, D)))
    hidden_piece, mid_gain_grad = mid_back(mid_grad)
    hidden_grad = out_grad[0].astype(f32) + hidden_piece
    ff_grad = weight_grad(middle16, both16).astype(bf16)
    mix16 = gather_sequences(after(hidden_grad.astype(bf16), ff_grad)).reshape(tokens, D)
    ff_owned = to_owners(after(ff_grad, down_owned, mix16))
    ff_parts = to_ranks(ff_owned.reshape(4, rows, 2 * hidden_part))
    result_gate = join_ff(ff_parts[..., :hidden_part]).astype(f32)
    result_up = join_ff(ff_parts[..., hidden_part:]).astype(f32)
    attended_grad16 = back_dot(mix16, full_o).astype(bf16).reshape(2, span_all, QP)
    gated_grad = back_dot(mix16, full_out).reshape(2, span_all, PART)
    grad_out_w = weight_grad(gated16, mix16).astype(bf16)
    grad_o = weight_grad(attended16, mix16).astype(bf16)
    if aligned:
        rows_grad = jnp.concatenate(
            [grad_out_w.reshape(nz, 2, out_rows, D), grad_o.reshape(nz, 2, o_rows, D)], axis=2
        )
        other_y = lax.dynamic_index_in_dim(rows_grad, 1 - yi, 1, keepdims=False)
        both_y = lax.dynamic_index_in_dim(rows_grad, yi, 1, keepdims=False).astype(f32) + swap(
            other_y, "y"
        ).astype(f32)
    else:
        both_y = grad_o

    inner = jnp.sum(gated_grad * gain * flat, axis=-1, keepdims=True) * root
    inner_mean = group_total(inner) / INNER
    wide = (2, span_all, 128)
    value_grad, gate_z_grad, gain_grad, suffix, first_grad = gate_backward(
        after(gated_grad, down_owned),
        values,
        rest,
        0,
        jnp.broadcast_to(root, wide),
        jnp.broadcast_to(inner_mean, wide),
        gain,
        mixed,
        steps,
        lift,
    )
    mixed_grad, step_grad, skip_grad = scan_backward(
        mixed, steps, starts, prefix, state_in, suffix, value_grad, skip, lift
    )
    state_grad = chained(first_grad, -1, mixed_grad)

    query_grad, kv_grads = attend_backward(
        after(query16, first_grad),
        kv_all[0],
        kv_all[1],
        attended_grad16,
        attended,
        log_sum,
        query_place,
        key_place,
    )
    kv_grads = kv_grads.reshape(2, 2, nz, span_all, HEAD_DIM)
    kv_grad = kv_grads[:, :, nz - 1]
    for d in range(1, nz):
        kv_grad = kv_grad + shifted(kv_grads[:, :, nz - 1 - d].astype(bf16), -d).astype(f32)
    query_back = rotate(
        query_grad.reshape(2, span_all, 2, HEAD_DIM), cosine, -sine
    ).reshape(2, span_all, QP)
    key_back = rotate(kv_grad[0][:, :, None], cosine, -sine)[:, :, 0]
    rest_grad16 = jnp.concatenate(
        [
            gate_z_grad,
            query_back.astype(bf16),
            key_back.astype(bf16),
            kv_grad[1].astype(bf16),
        ],
        axis=-1,
    ).reshape(tokens, REST_COLS)

    scan_grad16, edge_grad, conv_grad, small_grad = finish_backward(
        scan_in,
        before,
        mixed,
        steps,
        starts,
        prefix,
        state_in,
        after(state_grad, ff_owned, both_y),
        mixed_grad,
        step_grad,
        taps,
        bias,
        dt_b,
        rates,
        lift,
    )
    edge_back = shifted(edge_grad[:, 8 - edge_count :].astype(bf16), -1).astype(f32)
    last_rows = scan_grad16[:, span_all - edge_count :, :CONV_COLS].astype(f32) + edge_back
    scan_grad16 = lax.dynamic_update_slice(
        scan_grad16, last_rows.astype(bf16), (0, span_all - edge_count, 0)
    )
    bc_grad = scan_grad16[..., PART:CONV_COLS].reshape(2, span_all, 2, 2 * QUARTER)
    half_grad = lax.dynamic_index_in_dim(bc_grad, xi, 2, keepdims=False).astype(f32) + swap(
        lax.dynamic_index_in_dim(bc_grad, 1 - xi, 2, keepdims=False), "x"
    ).astype(f32)
    half_grad = half_grad.reshape(2, span_all, 2, QUARTER)
    leaving = lax.dynamic_index_in_dim(half_grad, 1 - ci, 2, keepdims=False)
    quarter_grad = lax.dynamic_index_in_dim(half_grad, ci, 2, keepdims=False) + swap(
        leaving[::-1].astype(bf16), "c"
    ).astype(f32)
    sent_grad16 = jnp.concatenate(
        [scan_grad16[..., :PART], quarter_grad.astype(bf16), scan_grad16[..., CONV_COLS:]],
        axis=-1,
    ).reshape(tokens, SENT_COLS)
    if aligned:
        rows_owned = lax.dynamic_index_in_dim(both_y, zi, 0, keepdims=False)
        waiting = after(both_y.astype(bf16), state_grad)
        for d in range(1, nz):
            leaving = lax.dynamic_index_in_dim(waiting, (zi + d) % nz, 0, keepdims=False)
            rows_owned = rows_owned + turned(leaving, d).astype(f32)
        rows_owned = rows_owned.astype(bf16)
        result_out = lax.ppermute(rows_owned[:out_rows], ("y", "c"), turn).astype(f32)
        result_o = lax.ppermute(rows_owned[out_rows:], ("z", "y", "c"), back_place).astype(f32)
    else:
        every_out = lax.dynamic_update_slice_in_dim(
            jnp.zeros((INNER, D), bf16), grad_out_w, (2 * xi + ci) * PART, 0
        )
        every_o = lax.dynamic_update_slice(
            jnp.zeros((2, 2, 2, HEAD_DIM, D), bf16),
            grad_o.reshape(1, 2, 1, HEAD_DIM, D),
            (ci, 0, xi, 0, 0),
        ).reshape(ATT_HEADS * HEAD_DIM, D)
        result_out = lax.psum_scatter(every_out, EVERY, scatter_dimension=0, tiled=True)
        result_o = lax.psum_scatter(every_o, EVERY, scatter_dimension=0, tiled=True)
        result_out, result_o = result_out.astype(f32), result_o.astype(f32)
    rest_owned = to_owners(
        after(weight_grad(normed_rows, rest_grad16).astype(bf16), ff_owned, state_grad)
    )
    rest_parts = to_ranks(rest_owned.reshape(4, rows, REST_COLS)).astype(f32)
    scan_owned = to_owners(
        after(weight_grad(normed_rows, sent_grad16).astype(bf16), rest_owned)
    )

    normed_grad = back_dot(sent_grad16, full_scan) + back_dot(rest_grad16, full_rest)
    normed_grad = restored(scatter_sequences(normed_grad.reshape(2, span_all, D)))
    resident_grad, norm_gain_grad = norm_back(normed_grad)
    input_grad = hidden_grad + resident_grad

    result_q = jnp.transpose(
        rest_parts[..., AT_Q:AT_K].reshape(2, 2, rows, 2, HEAD_DIM), (2, 1, 3, 0, 4)
    ).reshape(rows, ATT_HEADS * HEAD_DIM)
    kv_parts = jnp.sum(rest_parts[..., AT_K:].reshape(2, 2, rows, 2, HEAD_DIM), axis=0)
    result_k = jnp.transpose(kv_parts[:, :, 0], (1, 0, 2)).reshape(rows, KV_HEADS * HEAD_DIM)
    result_v = jnp.transpose(kv_parts[:, :, 1], (1, 0, 2)).reshape(rows, KV_HEADS * HEAD_DIM)

    def all_channels(array):
        return jnp.concatenate(
            [heads_spread(array[..., :PART], MAMBA_HEAD), array[..., PART:]], axis=-1
        )

    small = [
        norm_gain_grad,
        all_channels(conv_grad[:4]),
        all_channels(conv_grad[4]),
        heads_spread(small_grad[0, :HEADS], 1),
        heads_spread(small_grad[1, :HEADS], 1),
        heads_spread(skip_grad[0, :HEADS], 1),
        heads_spread(gain_grad[0], MAMBA_HEAD),
        mid_gain_grad,
    ]
    summed = total(jnp.concatenate([v.reshape(-1) for v in small]))
    parts, at = [], 0
    for v in small:
        parts.append(summed[at : at + v.size].reshape(v.shape))
        at += v.size
    scan_owned = after(
        scan_owned,
        summed,
        input_grad,
        output,
        rest_parts,
        result_gate,
        result_up,
        result_down,
        result_q,
        result_k,
        result_v,
        result_out,
        result_o,
    )
    scan_parts = to_ranks(scan_owned.reshape(4, rows, SENT_COLS)).astype(f32)
    result_in = jnp.concatenate(
        [
            heads_join(rest_parts[..., :PART], MAMBA_HEAD),
            heads_join(scan_parts[..., :PART], MAMBA_HEAD),
            jnp.swapaxes(scan_parts[..., PART : PART + QUARTER], 0, 1).reshape(rows, BC),
            heads_join(scan_parts[..., PART + QUARTER : PART + QUARTER + HEADS], 1),
        ],
        axis=1,
    )
    return (
        output[None],
        input_grad[None],
        parts[0],
        result_in,
        parts[1],
        parts[2],
        parts[3],
        parts[4],
        parts[5],
        parts[6],
        result_out,
        result_q,
        result_k,
        result_v,
        result_o,
        parts[7],
        result_gate,
        result_up,
        result_down,
    )


def solution(mesh):
    seq, fsdp = mesh.shape["seq"], mesh.shape["fsdp"]
    split = Mesh(mesh.devices.reshape(seq // 2, 2, fsdp // 2, 2), EVERY)
    tokens = P(("y", "c"), ("z", "x"), None)
    matrix = P(EVERY, None)
    return jax.shard_map(
        body,
        mesh=split,
        in_specs=(tokens, tokens, P(), matrix)
        + (P(),) * 6
        + (matrix,) * 5
        + (P(),)
        + (matrix,) * 3,
        out_specs=(tokens, tokens, P(), matrix)
        + (P(),) * 6
        + (matrix,) * 5
        + (P(),)
        + (matrix,) * 3,
        check_vma=False,
    )
```
